32 devices in a mesh: gx: 8 (over z, y), gy: 4 (over x, core).
Axes of the slice: x: 2, y: 2, z: 4, core: 2. Of those that a mesh axis runs over, the one named last changes fastest.
Arguments:
- tokens: bfloat16 [4, 64, 32, 256], P(None, 'gx', 'gy'), may hold values from -6 to 6
- syndrome: int32 [4, 64, 32], P(None, 'gx', 'gy'), may hold values 0 or 1
- check_plan_step: int32 [4, 64, 32], P(None, 'gx', 'gy'), may hold values from 0 to 7
- offsets: int32 [6, 2], replicated, may hold values from 0 to 8, as said below
- flip_vector: float32 [256], replicated, may hold values from -3 to 3
- plan_step_embedding: float32 [8, 256], replicated, may hold values from -3 to 3
- gain_tanner: float32 [256], replicated, may hold values from 0.5 to 1.5
- w_query: bfloat16 [256, 256], replicated, may hold values from -0.375 to 0.375
- w_key_value: bfloat16 [256, 512], replicated, may hold values from -0.375 to 0.375
- w_merge: bfloat16 [256, 256], replicated, may hold values from -0.375 to 0.375
- gain_time: float32 [256], replicated, may hold values from 0.5 to 1.5
- w_temporal: bfloat16 [256, 768], replicated, may hold values from -0.375 to 0.375
- w_temporal_out: bfloat16 [256, 256], replicated, may hold values from -0.375 to 0.375
- gain_ffn: float32 [256], replicated, may hold values from 0.5 to 1.5
- w_ffn_up: bfloat16 [256, 1024], replicated, may hold values from -0.375 to 0.375
- w_ffn_down: bfloat16 [1024, 256], replicated, may hold values from -0.1875 to 0.1875
- cotangent: bfloat16 [4, 64, 32, 256], P(None, 'gx', 'gy'), may hold values from -6 to 6
Outputs:
- token_grad: bfloat16 [4, 64, 32, 256], P(None, 'gx', 'gy')
- grad_flip: float32 [256], replicated
- plan_step_gradient: float32 [8, 256], replicated
- grad_gain_tanner: float32 [256], replicated
- grad_query: float32 [256, 256], replicated
- grad_key_value: float32 [256, 512], replicated
- grad_merge: float32 [256, 256], replicated
- grad_gain_time: float32 [256], replicated
- grad_temporal: float32 [256, 768], replicated
- grad_temporal_out: float32 [256, 256], replicated
- grad_gain_ffn: float32 [256], replicated
- grad_up: float32 [256, 1024], replicated
- grad_down: float32 [1024, 256], replicated
The draws below stay inside these ranges and needn't reach their ends.
Inputs may be any that keep to these rules, and one draw needn't show every extreme that they name: `offsets`: rows 0, 4 and 5 are (e, 0) and rows 1, 2 and 3 are (0, e), with e from 1 to 8; rows 0 and 3 have e = 8.
All inputs are finite; a program needn't handle non-finite values. No bound on the sum of `syndrome` on one device may be relied on, other than what follows from the above.
Results may differ from the reference program's by a relative error of at most 0.022.
Values may be sent and summed in bfloat16 or wider, within the bound.
No kernel may reach another device: no remote copies, remote signals or barrier semaphores. Data moves between devices by JAX's collectives and lax.ppermute only.
A program may use at most 64 MiB of HBM per device.

```python
import math
import jax
import jax.numpy as jnp
from jax import lax

MODEL_WIDTH = 256
HEADS = 8
HEADDIM = 32
FF = 1024
PLAN_STEP_COUNT = 8
MONOS = 6
MAXEXP = 8
SYNDROME_ROUNDS = 4
FIRST_LOOP_SITES = 64
SECOND_LOOP_SITES = 32
TOKENS = 8192


def draw_offsets(key, part):
    powers = jax.random.randint(key, (MONOS,), 1, MAXEXP + 1)
    along_rows = jnp.array([1, 0, 0, 0, 1, 1], dtype=jnp.int32)
    leading = jnp.array([1, 0, 0, 1, 0, 0], dtype=jnp.int32)
    powers = powers * (1 - leading) + MAXEXP * leading
    return jnp.stack([powers * along_rows, powers * (1 - along_rows)], axis=1).astype(jnp.int32)


def with_ends(result, own_key, smallest, high):
    index_at = [jax.random.randint(jax.random.fold_in(own_key, axis), (), 0, length) for axis, length in enumerate(result.shape)]
    main_axis = result.shape.index(max(result.shape))
    next_to = index_at[:main_axis] + [(index_at[main_axis] + 1) % result.shape[main_axis]] + index_at[main_axis + 1:]
    return result.at[tuple(index_at)].set(smallest).at[tuple(next_to)].set(high)


def levels(own_key, extent, shards, smallest, high):
    level, own = 1.0, jax.random.fold_in(own_key, 6)
    for position, parts in shards:
        steps = jnp.exp(jax.random.uniform(jax.random.fold_in(own, position), (parts,), jnp.float32, smallest / len(shards), high / len(shards)))
        level = level * jnp.repeat(steps, extent[position] // parts).reshape([-1 if axis == position else 1 for axis in range(len(extent))])
    return level


def scatter_about(key, dims, scale, reach, shards=(), kind=jnp.bfloat16):
    values = jax.random.normal(key, dims, jnp.float32) * scale
    if len(shards) > 0:
        values = levels(key, dims, shards, -0.22, 0.18) * values
    return jnp.clip(values, min=-reach, max=reach).astype(kind)


def setup_inputs(seed: int = 0) -> dict:
    seeds = jax.random.split(jax.random.key(seed), 18)
    return {
        "tokens": scatter_about(seeds[0], (SYNDROME_ROUNDS, FIRST_LOOP_SITES, SECOND_LOOP_SITES, MODEL_WIDTH), 1.0, 6.0, ((1, 8), (2, 4))),
        "syndrome": with_ends((jax.random.randint(seeds[1], (SYNDROME_ROUNDS, FIRST_LOOP_SITES, SECOND_LOOP_SITES), 0, 4) < 1).astype(jnp.int32), jax.random.fold_in(seeds[1], 1), 0, 1),
        "check_plan_step": with_ends(jax.random.randint(seeds[2], (SYNDROME_ROUNDS, FIRST_LOOP_SITES, SECOND_LOOP_SITES), 0, PLAN_STEP_COUNT), jax.random.fold_in(seeds[2], 1), 0, PLAN_STEP_COUNT - 1).astype(jnp.int32),
        "offsets": draw_offsets(jax.random.fold_in(seeds[17], 71), 0),
        "flip_vector": scatter_about(seeds[4], (MODEL_WIDTH,), 0.5, 3.0, (), jnp.float32),
        "plan_step_embedding": scatter_about(seeds[5], (PLAN_STEP_COUNT, MODEL_WIDTH), 0.5, 3.0, (), jnp.float32),
        "gain_tanner": jnp.clip(1.0 + 0.1 * jax.random.normal(seeds[6], (MODEL_WIDTH,), jnp.float32), 0.5, 1.5),
        "w_query": scatter_about(seeds[7], (MODEL_WIDTH, MODEL_WIDTH), MODEL_WIDTH ** -0.5, 0.375),
        "w_key_value": scatter_about(seeds[8], (MODEL_WIDTH, 2 * MODEL_WIDTH), MODEL_WIDTH ** -0.5, 0.375),
        "w_merge": scatter_about(seeds[9], (MODEL_WIDTH, MODEL_WIDTH), MODEL_WIDTH ** -0.5, 0.375),
        "gain_time": jnp.clip(1.0 + 0.1 * jax.random.normal(seeds[10], (MODEL_WIDTH,), jnp.float32), 0.5, 1.5),
        "w_temporal": scatter_about(seeds[11], (MODEL_WIDTH, 3 * MODEL_WIDTH), MODEL_WIDTH ** -0.5, 0.375),
        "w_temporal_out": scatter_about(seeds[12], (MODEL_WIDTH, MODEL_WIDTH), MODEL_WIDTH ** -0.5, 0.375),
        "gain_ffn": jnp.clip(1.0 + 0.1 * jax.random.normal(seeds[13], (MODEL_WIDTH,), jnp.float32), 0.5, 1.5),
        "w_ffn_up": scatter_about(seeds[14], (MODEL_WIDTH, FF), MODEL_WIDTH ** -0.5, 0.375),
        "w_ffn_down": scatter_about(seeds[15], (FF, MODEL_WIDTH), FF ** -0.5, 0.1875),
        "cotangent": scatter_about(seeds[16], (SYNDROME_ROUNDS, FIRST_LOOP_SITES, SECOND_LOOP_SITES, MODEL_WIDTH), 1.0, 6.0, ((1, 8), (2, 4))),
    }


EPS = 1e-05
CAP = 4.0
EXACT_PRECISION = lax.Precision.HIGHEST

def rms_norm(stream, gain):
    return stream * lax.rsqrt(lax.optimization_barrier(jnp.mean(stream * stream, axis=-1, keepdims=True)) + EPS) * gain

def matmul(inputs, weight):
    return lax.dot_general(inputs, weight, (((inputs.ndim - 1,), (0,)), ((), ())), preferred_element_type=jnp.float32)

def back_matmul(inputs, weight, grad_result):
    grad_low = grad_result.astype(jnp.bfloat16)
    grad_inputs = lax.dot_general(grad_low, weight, (((grad_low.ndim - 1,), (1,)), ((), ())), preferred_element_type=jnp.float32)
    flat_inputs = inputs.reshape(-1, inputs.shape[-1])
    flat_grad = grad_low.reshape(-1, grad_low.shape[-1])
    grad_weight = lax.dot_general(flat_inputs, flat_grad, (((0,), (0,)), ((), ())), preferred_element_type=jnp.float32)
    return (grad_inputs, grad_weight)

def attend(query, moved):
    head_shape = query.shape[:-1] + (HEADS, HEADDIM)
    queries = query.reshape(head_shape)
    weights = []
    for neighbour in moved:
        score = lax.optimization_barrier(jnp.sum(queries * neighbour[..., :MODEL_WIDTH].reshape(head_shape), axis=-1)) / math.sqrt(HEADDIM)
        weights.append(jnp.exp(CAP * jnp.tanh(score / CAP)))
    normalizer = weights[0]
    for weight in weights[1:]:
        normalizer = normalizer + weight
    mixed = jnp.zeros(head_shape, jnp.float32)
    for weight, neighbour in zip(weights, moved):
        mixed = mixed + (weight / normalizer)[..., None] * neighbour[..., MODEL_WIDTH:].reshape(head_shape)
    return mixed.reshape(query.shape)

def tanner_round(query, key_value, offsets):
    moved = [key_value]
    for index in range(MONOS):
        rolled = jnp.roll(key_value, -offsets[index, 0], axis=0)
        moved.append(jnp.roll(rolled, -offsets[index, 1], axis=1))
    return attend(query, moved)

def time_attend(packed):
    head_shape = packed.shape[:-1] + (HEADS, HEADDIM)
    queries = packed[..., :MODEL_WIDTH].reshape(head_shape)
    keys = packed[..., MODEL_WIDTH:2 * MODEL_WIDTH].reshape(head_shape)
    values = packed[..., 2 * MODEL_WIDTH:].reshape(head_shape)
    scores = jnp.einsum('rxyhe,sxyhe->xyhrs', queries, keys, precision=EXACT_PRECISION) / math.sqrt(HEADDIM)
    capped = CAP * jnp.tanh(scores / CAP)
    rounds = packed.shape[0]
    later = lax.broadcasted_iota(jnp.int32, (rounds, rounds), 0)
    earlier = lax.broadcasted_iota(jnp.int32, (rounds, rounds), 1)
    weights = jnp.where(earlier <= later, jnp.exp(capped), 0.0)
    probs = weights / lax.optimization_barrier(jnp.sum(weights, axis=-1, keepdims=True))
    mixed = jnp.einsum('xyhrs,sxyhe->rxyhe', probs, values, precision=EXACT_PRECISION)
    return mixed.reshape(packed.shape[:-1] + (MODEL_WIDTH,))

def reference(tokens, syndrome, check_plan_step, offsets, flip_vector, plan_step_embedding, gain_tanner, w_query, w_key_value, w_merge, gain_time, w_temporal, w_temporal_out, gain_ffn, w_ffn_up, w_ffn_down, cotangent):
    plan_step_onehot = (check_plan_step[..., None] == jnp.arange(PLAN_STEP_COUNT, dtype=jnp.int32)).astype(jnp.float32)
    syndrome_float = syndrome.astype(jnp.float32)
    embedded = tokens.astype(jnp.float32) + syndrome_float[..., None] * flip_vector + jnp.dot(plan_step_onehot, plan_step_embedding, precision=EXACT_PRECISION)
    normed_one, norm_one_back = jax.vjp(rms_norm, embedded, gain_tanner)
    hidden_one = normed_one.astype(jnp.bfloat16)
    query = matmul(hidden_one, w_query).astype(jnp.bfloat16)
    key_value = matmul(hidden_one, w_key_value).astype(jnp.bfloat16)

    def tanner_forward(items):
        return tanner_round(items[0].astype(jnp.float32), items[1].astype(jnp.float32), offsets).astype(jnp.bfloat16)
    mixed_one = lax.map(tanner_forward, (query, key_value))
    after_tanner = embedded + matmul(mixed_one, w_merge)
    normed_two, norm_two_back = jax.vjp(rms_norm, after_tanner, gain_time)
    hidden_two = normed_two.astype(jnp.bfloat16)
    packed = matmul(hidden_two, w_temporal).astype(jnp.bfloat16)
    packed_rows = jnp.moveaxis(packed, 1, 0)

    def time_forward(item):
        return time_attend(item[:, None].astype(jnp.float32))[:, 0].astype(jnp.bfloat16)
    mixed_two = jnp.moveaxis(lax.map(time_forward, packed_rows), 0, 1)
    after_time = after_tanner + matmul(mixed_two, w_temporal_out)

    def ffn_round(items):
        stream, outer = items
        normed_three, norm_three_back = jax.vjp(rms_norm, stream, gain_ffn)
        hidden_three = normed_three.astype(jnp.bfloat16)
        before_act = matmul(hidden_three, w_ffn_up)
        activated, gelu_back = jax.vjp(jax.nn.gelu, before_act)
        activated = activated.astype(jnp.bfloat16)
        grad_output = outer.astype(jnp.float32)
        grad_act, grad_down = back_matmul(activated, w_ffn_down, grad_output)
        grad_before = gelu_back(grad_act)[0]
        grad_three, grad_up = back_matmul(hidden_three, w_ffn_up, grad_before)
        grad_norm, grad_gain = norm_three_back(grad_three)
        return (grad_output + grad_norm, grad_up, grad_down, grad_gain)
    grad_after_time, grad_up, grad_down, grad_gain_ffn = lax.map(ffn_round, (after_time, cotangent))
    grad_up = lax.optimization_barrier(jnp.sum(grad_up, axis=0))
    grad_down = lax.optimization_barrier(jnp.sum(grad_down, axis=0))
    grad_gain_ffn = lax.optimization_barrier(jnp.sum(grad_gain_ffn, axis=0))
    grad_mixed_two, grad_temporal_out = back_matmul(mixed_two, w_temporal_out, grad_after_time)

    def time_grads(items):
        rows_packed, rows_grad = items
        back = jax.vjp(time_attend, rows_packed[:, None].astype(jnp.float32))[1]
        return back(rows_grad[:, None])[0][:, 0]
    grad_packed = jnp.moveaxis(lax.map(time_grads, (packed_rows, jnp.moveaxis(grad_mixed_two, 1, 0))), 0, 1)
    grad_two, grad_temporal = back_matmul(hidden_two, w_temporal, grad_packed)
    grad_norm_two, grad_gain_time = norm_two_back(grad_two)
    grad_after_tanner = grad_after_time + grad_norm_two
    grad_mixed_one, grad_merge = back_matmul(mixed_one, w_merge, grad_after_tanner)

    def tanner_grads(items):
        query_round, key_round, grad_round = items

        def tanner_fixed(query_in, key_in):
            return tanner_round(query_in, key_in, offsets)
        back = jax.vjp(tanner_fixed, query_round.astype(jnp.float32), key_round.astype(jnp.float32))[1]
        return back(grad_round)
    grad_query_out, grad_key_out = lax.map(tanner_grads, (query, key_value, grad_mixed_one))
    grad_one_query, grad_query = back_matmul(hidden_one, w_query, grad_query_out)
    grad_one_key, grad_key_value = back_matmul(hidden_one, w_key_value, grad_key_out)
    grad_norm_one, grad_gain_tanner = norm_one_back(grad_one_query + grad_one_key)
    embedding_gradient = grad_after_tanner + grad_norm_one
    token_grad = embedding_gradient.astype(jnp.bfloat16)
    grad_flip = lax.optimization_barrier(jnp.sum(syndrome_float[..., None] * embedding_gradient, axis=(0, 1, 2)))
    plan_step_gradient = lax.dot_general(plan_step_onehot.reshape(-1, PLAN_STEP_COUNT), embedding_gradient.reshape(-1, MODEL_WIDTH), (((0,), (0,)), ((), ())), precision=EXACT_PRECISION)
    scale = 1.0 / math.sqrt(TOKENS)
    return (token_grad, grad_flip * scale, plan_step_gradient * scale, grad_gain_tanner * scale, grad_query * scale, grad_key_value * scale, grad_merge * scale, grad_gain_time * scale, grad_temporal * scale, grad_temporal_out * scale, grad_gain_ffn * scale, grad_up * scale, grad_down * scale)
```

```python
import functools
import math

import jax
import jax.numpy as jnp
from jax import lax
from jax.experimental import pallas as pl
from jax.experimental.pallas import tpu as pltpu
from jax.sharding import PartitionSpec as P

WIDTH = 256
HEADDIM = 32
HEADS = WIDTH // HEADDIM
FF = 1024
PLAN_STEP_COUNT = 8
MONOS = 6
MAXEXP = 8
LANES = 128
HALF = WIDTH // 2

EPS = 1e-05
CAP = 4.0
ALONG_ROWS = (0, 4, 5)
BF = jnp.bfloat16
F32 = jnp.float32
SCORE = 1.0 / math.sqrt(HEADDIM)
GELU_A = math.sqrt(2.0 / math.pi)
GELU_B = 0.044715
MIB = 1 << 20


def dot(a, b, dims=((1,), (0,))):
    return lax.dot_general(a, b, (dims, ((), ())), preferred_element_type=F32)


def dot_nt(a, b):
    return dot(a, b, ((1,), (1,)))


def onehot_rows(code):
    tokens = code.shape[1]
    row = lax.broadcasted_iota(jnp.int32, (16, tokens), 0)
    step = jnp.where(row == (code & 7), 1.0, 0.0)
    flip = jnp.where((row == 8) & (code >= 8), 1.0, 0.0)
    return (step + flip).astype(BF)


def embed(tokens, code, plan, flip):
    row = lax.broadcasted_iota(jnp.int32, (8, WIDTH), 0)
    table = jnp.concatenate([plan, jnp.where(row == 0, flip, 0.0)], axis=0)
    high = table.astype(BF)
    rest = table - high.astype(F32)
    middle = rest.astype(BF)
    low = (rest - middle.astype(F32)).astype(BF)
    onehot = onehot_rows(code)
    chosen = dot(
        jnp.concatenate([onehot, onehot, onehot], axis=0),
        jnp.concatenate([high, middle, low], axis=0),
        ((0,), (0,)),
    )
    return tokens.astype(F32) + chosen


def inverse_rms(stream):
    return lax.rsqrt(jnp.mean(stream * stream, axis=-1, keepdims=True) + EPS)


def norm_back(stream, gain, grad):
    inverse = inverse_rms(stream)
    normed = stream * inverse
    scaled = grad * gain
    mean = jnp.mean(scaled * normed, axis=-1, keepdims=True)
    return inverse * (scaled - normed * mean), jnp.sum(grad * normed, axis=0, keepdims=True)


def gather_heads(slot, period):
    feature = lax.broadcasted_iota(jnp.int32, (WIDTH, LANES), 0) // HEADDIM
    lane = lax.broadcasted_iota(jnp.int32, (WIDTH, LANES), 1) % period
    return jnp.where(lane - feature == slot * HEADS, 1.0, 0.0).astype(BF)


def spread_heads(slot, period):
    lane = lax.broadcasted_iota(jnp.int32, (LANES, WIDTH), 0)
    feature = lax.broadcasted_iota(jnp.int32, (LANES, WIDTH), 1) // HEADDIM
    at = (lane < 2 * period) & (lane % period - feature == slot * HEADS)
    return jnp.where(at, 1.0, 0.0).astype(BF)


def two_parts(value, period):
    lane = lax.broadcasted_iota(jnp.int32, value.shape, 1)
    high = value.astype(BF).astype(F32)
    return jnp.where(lane < period, high, value - high).astype(BF)


def slot_total(value, period):
    shift = HEADS
    while shift < period:
        value = value + pltpu.roll(value, shift, 1)
        shift *= 2
    return value


def softmax_parts(scores, valid, period):
    bent = jnp.tanh(scores * (SCORE / CAP))
    weights = jnp.where(valid, jnp.exp(CAP * bent), 0.0)
    return bent, weights / slot_total(weights, period)


def softmax_back(bent, probs, grad, period):
    inner = probs * grad
    return (inner - probs * slot_total(inner, period)) * (1.0 - bent * bent) * SCORE


def tanner_valid(tokens):
    lane = lax.broadcasted_iota(jnp.int32, (tokens, LANES), 1)
    return lane % 64 < HEADS * (MONOS + 1)


def time_valid(tokens, rounds):
    lane = lax.broadcasted_iota(jnp.int32, (tokens, LANES), 1)
    row = lax.broadcasted_iota(jnp.int32, (tokens, LANES), 0)
    return (lane % 32) // HEADS <= row // (tokens // rounds)


def offset_of(offsets, index):
    return offsets[index, 0] if index in ALONG_ROWS else offsets[index, 1]


def neighbour(number, offsets, extended, columns):
    rounds, twice, width, features = extended.shape
    rows = twice // 2
    tokens = rounds * rows * width
    if number == 0:
        return extended[:, :rows].reshape(tokens, features)
    by = offset_of(offsets, number - 1)
    if number - 1 in ALONG_ROWS:
        return extended[:, pl.ds(by, rows)].reshape(tokens, features)
    own = extended[:, :rows].reshape(rounds * rows, width, features)
    place = lax.broadcasted_iota(jnp.int32, own.shape, 1)
    joined = jnp.where(place >= by, own, columns[...])
    return pltpu.roll(joined, width - by, 1).reshape(tokens, features)


def start_kernel(tokens, code, plan, flip, gain, w_query, w_key_value, x_out, hidden_out, query_out, kv_out):
    x = embed(tokens[...], code[...], plan[...], flip[...])
    hidden = (x * inverse_rms(x) * gain[...]).astype(BF)
    x_out[...] = x
    hidden_out[...] = hidden
    query_out[...] = dot(hidden, w_query[...]).astype(BF)
    kv_out[...] = dot(hidden, w_key_value[...]).astype(BF)


def forward_kernel(
    place, offsets, x_in, query_in, kv_in, row_tokens, row_code, col_tokens, col_code, plan, flip,
    gain_tanner, w_key_value, w_merge, gain_time, w_temporal, w_temporal_out, gain_ffn, w_up, w_down, cotangent,
    keep, send, grad_time_out, tanner_out, mixed_one_out, mixed_two_out, packed_out, hidden_two_out,
    row_kv_out, col_kv_out, bent_one_out, probs_one_out, bent_two_out, probs_two_out, grad_gain_out,
    extended, columns, transposed, transposed_act,
):
    rounds, twice, width, features = extended.shape
    rows = twice // 2
    tokens = x_in.shape[0]
    core = place[0]
    borrowed = []
    for tok, code, out in ((row_tokens, row_code, row_kv_out), (col_tokens, col_code, col_kv_out)):
        other = embed(tok[...], code[...], plan[...], flip[...])
        hidden = (other * inverse_rms(other) * gain_tanner[...]).astype(BF)
        kv = dot(hidden, w_key_value[...]).astype(BF)
        out[...] = kv
        borrowed.append(kv.astype(F32))
    extended[:, :rows] = kv_in[...].astype(F32).reshape(rounds, rows, width, features)
    extended[:, rows:] = borrowed[0].reshape(rounds, rows, width, features)
    columns[...] = borrowed[1].reshape(rounds * rows, width, features)
    query = query_in[...].astype(F32)
    scores = None
    for number in range(MONOS + 1):
        keys = neighbour(number, offsets, extended, columns)[:, :WIDTH]
        part = dot((query * keys).astype(BF), gather_heads(number, 64))
        scores = part if scores is None else scores + part
    bent, probs = softmax_parts(scores, tanner_valid(tokens), 64)
    bent_one_out[...] = bent
    probs_one_out[...] = probs
    parts = two_parts(probs, 64)
    mixed = None
    for number in range(MONOS + 1):
        values = neighbour(number, offsets, extended, columns)[:, WIDTH:]
        part = dot(parts, spread_heads(number, 64)) * values
        mixed = part if mixed is None else mixed + part
    mixed_one = mixed.astype(BF)
    mixed_one_out[...] = mixed_one
    after_tanner = x_in[...] + dot(mixed_one, w_merge[...])
    tanner_out[...] = after_tanner

    hidden_two = (after_tanner * inverse_rms(after_tanner) * gain_time[...]).astype(BF)
    hidden_two_out[...] = hidden_two
    packed_low = dot(hidden_two, w_temporal[...]).astype(BF)
    packed_out[...] = packed_low
    packed = packed_low.astype(F32).reshape(rounds, tokens // rounds, 3 * WIDTH)
    sites = tokens // rounds
    scores = None
    for earlier in range(rounds):
        product = packed[earlier:, :, :WIDTH] * packed[earlier][None, :, WIDTH : 2 * WIDTH]
        part = dot(product.reshape(-1, WIDTH).astype(BF), gather_heads(earlier, 32))
        if earlier:
            part = jnp.concatenate([jnp.zeros((earlier * sites, LANES), F32), part], axis=0)
        scores = part if scores is None else scores + part
    bent, probs = softmax_parts(scores, time_valid(tokens, rounds), 32)
    bent_two_out[...] = bent
    probs_two_out[...] = probs
    parts = two_parts(probs, 32)
    mixed = None
    for earlier in range(rounds):
        weight = dot(parts[earlier * sites :], spread_heads(earlier, 32)).reshape(rounds - earlier, sites, WIDTH)
        part = (weight * packed[earlier][None, :, 2 * WIDTH :]).reshape(-1, WIDTH)
        if earlier:
            part = jnp.concatenate([jnp.zeros((earlier * sites, WIDTH), F32), part], axis=0)
        mixed = part if mixed is None else mixed + part
    mixed_two = mixed.astype(BF)
    mixed_two_out[...] = mixed_two
    after_time = after_tanner + dot(mixed_two, w_temporal_out[...])

    hidden = (after_time * inverse_rms(after_time) * gain_ffn[...]).astype(BF)
    outer = cotangent[...]
    transposed[...] = hidden.T
    grad_three = None
    befores = []
    for block in range(FF // WIDTH):
        cols = slice(block * WIDTH, (block + 1) * WIDTH)
        before = dot(hidden, w_up[:, cols])
        square = before * before
        bend = jnp.tanh(GELU_A * before * (1.0 + GELU_B * square))
        upper = 0.5 * (1.0 + bend)
        activated = (before * upper).astype(BF)
        slope = upper + 0.5 * before * (1.0 - bend * bend) * (GELU_A * (1.0 + 3.0 * GELU_B * square))
        grad_before = (dot_nt(outer, w_down[cols, :]) * slope).astype(BF)
        befores.append(grad_before)
        part = dot_nt(grad_before, w_up[:, cols])
        grad_three = part if grad_three is None else grad_three + part
        transposed_act[cols, :] = activated.T
    for ref, which in ((keep, core), (send, 1 - core)):
        half = pl.ds(pl.multiple_of(which * HALF, HALF), HALF)
        lead = transposed[half, :]
        for block in range(FF // WIDTH):
            ref[block * HALF : (block + 1) * HALF, :] = dot(lead, befores[block]).astype(BF)
            part = transposed_act[pl.ds(pl.multiple_of(block * WIDTH + which * HALF, HALF), HALF), :]
            base = (FF // WIDTH + block) * HALF
            ref[base : base + HALF, :] = dot(part, outer).astype(BF)
    grad_norm, grad_gain = norm_back(after_time, gain_ffn[...], grad_three)
    grad_time_out[...] = outer.astype(F32) + grad_norm
    grad_gain_out[...] = grad_gain


def backward_kernel(
    offsets, grad_time_in, tanner_in, packed_in, query_in, kv_in, row_kv, col_kv,
    bent_one, probs_one, bent_two, probs_two, w_merge, gain_time, w_temporal, w_temporal_out,
    grad_query_out, grad_kv_out, grad_rows_out, grad_cols_out, grad_packed_out, grad_tanner_out, grad_gain_out,
    extended, columns, grad_extended,
):
    rounds, twice, width, features = extended.shape
    rows = twice // 2
    tokens = grad_time_in.shape[0]
    sites = tokens // rounds
    grad_time = grad_time_in[...]
    grad_mixed = dot_nt(grad_time.astype(BF), w_temporal_out[...]).reshape(rounds, sites, WIDTH)
    packed = packed_in[...].astype(F32).reshape(rounds, sites, 3 * WIDTH)
    grad_probs = None
    for earlier in range(rounds):
        product = grad_mixed[earlier:] * packed[earlier][None, :, 2 * WIDTH :]
        part = dot(product.reshape(-1, WIDTH).astype(BF), gather_heads(earlier, 32))
        if earlier:
            part = jnp.concatenate([jnp.zeros((earlier * sites, LANES), F32), part], axis=0)
        grad_probs = part if grad_probs is None else grad_probs + part
    probs = probs_two[...]
    prob_parts = two_parts(probs, 32)
    score_parts = two_parts(softmax_back(bent_two[...], probs, grad_probs, 32), 32)
    grad_queries = None
    grad_keys = []
    grad_values = []
    for earlier in range(rounds):
        spread = spread_heads(earlier, 32)
        shape = (rounds - earlier, sites, WIDTH)
        weight = dot(prob_parts[earlier * sites :], spread).reshape(shape)
        slope = dot(score_parts[earlier * sites :], spread).reshape(shape)
        grad_values.append(jnp.sum(weight * grad_mixed[earlier:], axis=0))
        grad_keys.append(jnp.sum(slope * packed[earlier:, :, :WIDTH], axis=0))
        part = (slope * packed[earlier][None, :, WIDTH : 2 * WIDTH]).reshape(-1, WIDTH)
        if earlier:
            part = jnp.concatenate([jnp.zeros((earlier * sites, WIDTH), F32), part], axis=0)
        grad_queries = part if grad_queries is None else grad_queries + part
    grad_packed = jnp.concatenate(
        [grad_queries, jnp.concatenate(grad_keys, axis=0), jnp.concatenate(grad_values, axis=0)], axis=1
    ).astype(BF)
    grad_packed_out[...] = grad_packed
    grad_two = dot_nt(grad_packed, w_temporal[...])
    grad_norm, grad_gain = norm_back(tanner_in[...], gain_time[...], grad_two)
    grad_gain_out[...] = grad_gain
    grad_tanner = grad_time + grad_norm
    grad_tanner_out[...] = grad_tanner

    grad_mixed = dot_nt(grad_tanner.astype(BF), w_merge[...])
    extended[:, :rows] = kv_in[...].astype(F32).reshape(rounds, rows, width, features)
    extended[:, rows:] = row_kv[...].astype(F32).reshape(rounds, rows, width, features)
    columns[...] = col_kv[...].astype(F32).reshape(rounds * rows, width, features)
    grad_probs = None
    for number in range(MONOS + 1):
        values = neighbour(number, offsets, extended, columns)[:, WIDTH:]
        part = dot((grad_mixed * values).astype(BF), gather_heads(number, 64))
        grad_probs = part if grad_probs is None else grad_probs + part
    probs = probs_one[...]
    prob_parts = two_parts(probs, 64)
    score_parts = two_parts(softmax_back(bent_one[...], probs, grad_probs, 64), 64)
    query = query_in[...].astype(F32)
    grad_query = None
    grad_cols = None
    for number in (0,) + tuple(i + 1 for i in range(MONOS)):
        spread = spread_heads(number, 64)
        slope = dot(score_parts, spread)
        weight = dot(prob_parts, spread)
        keys = neighbour(number, offsets, extended, columns)[:, :WIDTH]
        part = slope * keys
        grad_query = part if grad_query is None else grad_query + part
        grad_kv = jnp.concatenate([slope * query, weight * grad_mixed], axis=1)
        if number == 0:
            grad_extended[:, :rows] = grad_kv.reshape(rounds, rows, width, features)
            grad_extended[:, rows:] = jnp.zeros((rounds, rows, width, features), F32)
            continue
        by = offset_of(offsets, number - 1)
        if number - 1 in ALONG_ROWS:
            grad_extended[:, pl.ds(by, rows)] += grad_kv.reshape(rounds, rows, width, features)
            continue
        moved = pltpu.roll(grad_kv.reshape(rounds * rows, width, features), by % width, 1)
        place = lax.broadcasted_iota(jnp.int32, moved.shape, 1)
        own = jnp.where(place >= by, moved, 0.0)
        grad_extended[:, :rows] += own.reshape(rounds, rows, width, features)
        grad_cols = moved - own if grad_cols is None else grad_cols + (moved - own)
    grad_query_out[...] = grad_query.astype(BF)
    grad_kv_out[...] = grad_extended[:, :rows].reshape(tokens, features)
    grad_rows_out[...] = grad_extended[:, rows:].reshape(tokens, features).astype(BF)
    grad_cols_out[...] = grad_cols.reshape(tokens, features).astype(BF)


def weights_kernel(place, mixed_two, grad_time, hidden_two, grad_packed, mixed_one, grad_tanner, keep, send, transposed):
    core = place[0]
    transposed[0] = hidden_two[...].T
    transposed[1] = mixed_two[...].T
    transposed[2] = mixed_one[...].T
    grad_time_low = grad_time[...].astype(BF)
    grad_tanner_low = grad_tanner[...].astype(BF)
    for ref, which in ((keep, core), (send, 1 - core)):
        half = pl.ds(pl.multiple_of(which * HALF, HALF), HALF)
        for block in range(3):
            cols = slice(block * WIDTH, (block + 1) * WIDTH)
            ref[block * HALF : (block + 1) * HALF, :] = dot(transposed[0, half, :], grad_packed[:, cols]).astype(BF)
        ref[3 * HALF : 4 * HALF, :] = dot(transposed[1, half, :], grad_time_low).astype(BF)
        ref[4 * HALF : 5 * HALF, :] = dot(transposed[2, half, :], grad_tanner_low).astype(BF)


def last_kernel(
    place, grad_kv_in, back_rows, back_cols, grad_query_in, hidden_in, x_in, w_query, w_key_value, gain,
    grad_tanner, code, grad_gain_time, grad_gain_ffn, token_grad, keep, send, transposed,
):
    core = place[0]
    grad_kv = (grad_kv_in[...] + back_rows[...].astype(F32) + back_cols[...].astype(F32)).astype(BF)
    grad_query = grad_query_in[...]
    grad_one = dot_nt(grad_kv, w_key_value[...]) + dot_nt(grad_query, w_query[...])
    grad_norm, grad_gain = norm_back(x_in[...], gain[...], grad_one)
    grad_embedded = grad_tanner[...] + grad_norm
    token_grad[...] = grad_embedded.astype(BF)
    onehot = onehot_rows(code[...])
    high = grad_embedded.astype(BF)
    low = (grad_embedded - high.astype(F32)).astype(BF)
    small = dot(onehot, high) + dot(onehot, low)
    row = lax.broadcasted_iota(jnp.int32, small.shape, 0)
    small = jnp.where(row == 9, grad_gain, small)
    small = jnp.where(row == 10, grad_gain_time[...], small)
    small = jnp.where(row == 11, grad_gain_ffn[...], small).astype(BF)
    transposed[...] = hidden_in[...].T
    for ref, which in ((keep, core), (send, 1 - core)):
        lead = transposed[pl.ds(pl.multiple_of(which * HALF, HALF), HALF), :]
        ref[:16, :] = small
        ref[16 : 16 + HALF, :] = dot(lead, grad_query).astype(BF)
        for block in range(2):
            cols = slice(block * WIDTH, (block + 1) * WIDTH)
            base = 16 + (block + 1) * HALF
            ref[base : base + HALF, :] = dot(lead, grad_kv[:, cols]).astype(BF)


def add_kernel(count, parts, extra, which, place, *refs):
    ins, outs, total = refs[:count], refs[count:-1], refs[-1]
    value = ins[0][...].astype(F32)
    for ref in ins[1:]:
        value = value + ref[...].astype(F32)
    total[...] = value
    rows = (total.shape[0] - extra) // parts
    for number in range(parts):
        part = place[which] ^ number
        if extra:
            outs[number][:extra, :] = value[:extra].astype(BF)
        if rows % 8 == 0:
            piece = total[pl.ds(pl.multiple_of(extra + part * rows, 8), rows), :]
        else:
            piece = value[extra : extra + rows]
            for index in range(1, parts):
                start = extra + index * rows
                piece = jnp.where(part == index, value[start : start + rows], piece)
        outs[number][extra:, :] = piece.astype(BF)


def end_kernel(count, scale, *refs):
    ins, outs = refs[:count], refs[count:]
    value = ins[0][...].astype(F32)
    for ref in ins[1:]:
        value = value + ref[...].astype(F32)
    extra = value.shape[0] - outs[0].shape[0]
    outs[0][...] = value[extra:].astype(BF)
    if extra:
        small = value[:extra] * scale
        outs[1][...] = small[:8]
        for number in range(4):
            outs[2 + number][...] = small[8 + number : 9 + number]


def stack_kernel(*refs):
    out = refs[-1]
    for number, ref in enumerate(refs[:-1]):
        out[number] = ref[...]


def unpack_kernel(blocks, scale, place, own, other, *refs):
    outs, halves = refs[:-1], refs[-1]
    core = place[0]
    groups, lines, rows, _ = own.shape
    for ref, which in ((own, core), (other, 1 - core)):
        for group in range(groups):
            for line in range(lines):
                start = (group * lines + line) * rows
                piece = ref[group ^ place[1], line ^ place[2]]
                halves[which, start : start + rows, :] = piece.astype(F32) * scale
    block = 0
    for out, (down, across) in zip(outs, blocks):
        for index in range(down * across):
            for half in range(2):
                top = (index if down > 1 else 0) * WIDTH + half * HALF
                left = (index if across > 1 else 0) * WIDTH
                out[top : top + HALF, left : left + WIDTH] = halves[half, block * HALF : (block + 1) * HALF, :]
            block += 1


def call(kernel, outs, args, scratch=(), smem=0, limit=16):
    vmem = pl.BlockSpec(memory_space=pltpu.VMEM)
    return pl.pallas_call(
        kernel,
        out_shape=[jax.ShapeDtypeStruct(shape, dtype) for shape, dtype in outs],
        in_specs=[pl.BlockSpec(memory_space=pltpu.SMEM)] * smem + [vmem] * (len(args) - smem),
        out_specs=[vmem] * len(outs),
        scratch_shapes=list(scratch),
        compiler_params=pltpu.CompilerParams(vmem_limit_bytes=limit * MIB),
    )(*args)


def shifted(x, axis, by):
    count = lax.axis_size(axis)
    return lax.ppermute(x, axis, [(i, (i + by) % count) for i in range(count)])


class Layout:
    def __init__(self):
        self.nx = lax.axis_size("gx")
        self.ny = lax.axis_size("gy")
        self.groups = self.ny
        self.lines = self.nx // 2

    def place(self):
        gx = lax.axis_index("gx")
        gy = lax.axis_index("gy")
        return jnp.stack([gy % 2, (gy // 2) * 2 + gx % 2, gx // 2]).astype(jnp.int32)

    def swap(self, x, flip_gx, flip_gy):
        pairs = []
        for gx in range(self.nx):
            for gy in range(self.ny):
                pairs.append((gx * self.ny + gy, (gx ^ flip_gx) * self.ny + (gy ^ flip_gy)))
        return lax.ppermute(x, ("gx", "gy"), pairs)

    def core(self, x):
        return self.swap(x, 0, 1)

    def group(self, x, number):
        return self.swap(x, number % 2, (number // 2) * 2)

    def line(self, x, number):
        return self.swap(x, number * 2, 0)


def reduce_group(layout, place, keep, send, extra, scale):
    rows = keep.shape[0] - extra
    received = layout.core(send)
    part = rows // layout.groups
    pieces = call(
        functools.partial(add_kernel, 2, layout.groups, extra, 1),
        [((part + extra, WIDTH), BF)] * layout.groups,
        [place, keep, received],
        [pltpu.VMEM((rows + extra, WIDTH), F32)],
        smem=1,
    )
    received = [layout.group(pieces[k], k) for k in range(1, layout.groups)]
    rows, part = part, part // layout.lines
    pieces = call(
        functools.partial(add_kernel, layout.groups, layout.lines, extra, 2),
        [((part + extra, WIDTH), BF)] * layout.lines,
        [place, pieces[0], *received],
        [pltpu.VMEM((rows + extra, WIDTH), F32)],
        smem=1,
    )
    received = [layout.line(pieces[k], k) for k in range(1, layout.lines)]
    small = [((8, WIDTH), F32)] + [((1, WIDTH), F32)] * 4 if extra else []
    outs = call(
        functools.partial(end_kernel, layout.lines, scale),
        [((part, WIDTH), BF)] + small,
        [pieces[0], *received],
    )
    return outs[0], outs[1:]


def gather_group(layout, place, shard, blocks, scale):
    rows = shard.shape[0]
    pieces = [shard] + [layout.line(shard, k) for k in range(1, layout.lines)]
    lined = call(stack_kernel, [((layout.lines, rows, WIDTH), BF)], pieces)[0]
    pieces = [lined] + [layout.group(lined, k) for k in range(1, layout.groups)]
    own = call(stack_kernel, [((layout.groups, layout.lines, rows, WIDTH), BF)], pieces)[0]
    other = layout.core(own)
    total = sum(down * across for down, across in blocks)
    return call(
        functools.partial(unpack_kernel, blocks, scale),
        [((down * WIDTH, across * WIDTH), F32) for down, across in blocks],
        [place, own, other],
        [pltpu.VMEM((2, total * HALF, WIDTH), F32)],
        smem=1,
    )


def on_device(
    tokens,
    syndrome,
    check_plan_step,
    offsets,
    flip_vector,
    plan_step_embedding,
    gain_tanner,
    w_query,
    w_key_value,
    w_merge,
    gain_time,
    w_temporal,
    w_temporal_out,
    gain_ffn,
    w_ffn_up,
    w_ffn_down,
    cotangent,
):
    layout = Layout()
    place = layout.place()
    rounds, rows, cols = tokens.shape[:3]
    count = rounds * rows * cols
    scale = 1.0 / math.sqrt(count * layout.nx * layout.ny)
    flat = (count, WIDTH)
    row_tokens = shifted(tokens, "gx", -1).reshape(flat)
    col_tokens = shifted(tokens, "gy", -1).reshape(flat)
    code = (syndrome * 8 + check_plan_step).reshape(1, count)
    row_code = shifted(code, "gx", -1)
    col_code = shifted(code, "gy", -1)
    flip = flip_vector.reshape(1, WIDTH)
    gain_one = gain_tanner.reshape(1, WIDTH)
    gain_two = gain_time.reshape(1, WIDTH)
    gain_three = gain_ffn.reshape(1, WIDTH)

    act = (flat, BF)
    stream = (flat, F32)
    wide = ((count, 2 * WIDTH), BF)
    lanes = ((count, LANES), F32)
    row = ((1, WIDTH), F32)
    x, hidden_one, query, key_value = call(
        start_kernel,
        [stream, act, act, wide],
        [tokens.reshape(flat), code, plan_step_embedding, flip, gain_one, w_query, w_key_value],
    )
    extended = pltpu.VMEM((rounds, 2 * rows, cols, 2 * WIDTH), F32)
    columns = pltpu.VMEM((rounds * rows, cols, 2 * WIDTH), F32)
    half_one = ((2 * (FF // WIDTH) * HALF, WIDTH), BF)
    (
        keep_one, send_one, grad_time, after_tanner, mixed_one, mixed_two, packed, hidden_two,
        row_kv, col_kv, bent_one, probs_one, bent_two, probs_two, grad_gain_ffn,
    ) = call(
        forward_kernel,
        [half_one, half_one, stream, stream, act, act, ((count, 3 * WIDTH), BF), act,
         wide, wide, lanes, lanes, lanes, lanes, row],
        [place, offsets, x, query, key_value, row_tokens, row_code, col_tokens, col_code, plan_step_embedding, flip,
         gain_one, w_key_value, w_merge, gain_two, w_temporal, w_temporal_out, gain_three, w_ffn_up, w_ffn_down,
         cotangent.reshape(flat)],
        [extended, columns, pltpu.VMEM((WIDTH, count), BF), pltpu.VMEM((FF, count), BF)],
        smem=2,
        limit=32,
    )
    grad_query, grad_kv, grad_rows, grad_cols, grad_packed, grad_tanner, grad_gain_time = call(
        backward_kernel,
        [act, ((count, 2 * WIDTH), F32), wide, wide, ((count, 3 * WIDTH), BF), stream, row],
        [offsets, grad_time, after_tanner, packed, query, key_value, row_kv, col_kv,
         bent_one, probs_one, bent_two, probs_two, w_merge, gain_two, w_temporal, w_temporal_out],
        [extended, columns, extended],
        smem=1,
        limit=32,
    )
    back_rows = shifted(grad_rows, "gx", 1)
    back_cols = shifted(grad_cols, "gy", 1)
    half_two = ((5 * HALF, WIDTH), BF)
    keep_two, send_two = call(
        weights_kernel,
        [half_two, half_two],
        [place, mixed_two, grad_time, hidden_two, grad_packed, mixed_one, grad_tanner],
        [pltpu.VMEM((3, WIDTH, count), BF)],
        smem=1,
    )
    shard_one, _ = reduce_group(layout, place, keep_one, send_one, 0, scale)
    shard_two, _ = reduce_group(layout, place, keep_two, send_two, 0, scale)
    half_three = ((16 + 3 * HALF, WIDTH), BF)
    token_grad, keep_three, send_three = call(
        last_kernel,
        [act, half_three, half_three],
        [place, grad_kv, back_rows, back_cols, grad_query, hidden_one, x, w_query, w_key_value, gain_one,
         grad_tanner, code, grad_gain_time, grad_gain_ffn],
        [pltpu.VMEM((WIDTH, count), BF)],
        smem=1,
    )
    shard_three, small = reduce_group(layout, place, keep_three, send_three, 16, scale)
    grad_up, grad_down = gather_group(layout, place, shard_one, ((1, FF // WIDTH), (FF // WIDTH, 1)), scale)
    grad_temporal, grad_temporal_out, grad_merge = gather_group(
        layout, place, shard_two, ((1, 3), (1, 1), (1, 1)), scale
    )
    grad_w_query, grad_key_value = gather_group(layout, place, shard_three, ((1, 1), (1, 2)), scale)
    plan_grad, grad_flip, sum_gain_tanner, sum_gain_time, sum_gain_ffn = small
    return (
        token_grad.reshape(tokens.shape),
        grad_flip.reshape(WIDTH),
        plan_grad,
        sum_gain_tanner.reshape(WIDTH),
        grad_w_query,
        grad_key_value,
        grad_merge,
        sum_gain_time.reshape(WIDTH),
        grad_temporal,
        grad_temporal_out,
        sum_gain_ffn.reshape(WIDTH),
        grad_up,
        grad_down,
    )


def solution(mesh):
    tiled = P(None, "gx", "gy", None)
    sites = P(None, "gx", "gy")
    return jax.shard_map(
        on_device,
        mesh=mesh,
        in_specs=(tiled, sites, sites) + (P(),) * 13 + (tiled,),
        out_specs=(tiled,) + (P(),) * 12,
        check_vma=False,
    )
```

```python
import functools
import math

import jax
import jax.numpy as jnp
from jax import lax
from jax.experimental import pallas as pl
from jax.experimental.pallas import tpu as pltpu
from jax.sharding import PartitionSpec as P

WIDTH = 256
HEADDIM = 32
HEADS = WIDTH // HEADDIM
FF = 1024
PLAN_STEP_COUNT = 8
MONOS = 6
MAXEXP = 8
LANES = 128
HALF = WIDTH // 2

EPS = 1e-05
CAP = 4.0
ALONG_ROWS = (0, 4, 5)
BF = jnp.bfloat16
F32 = jnp.float32
SCORE = 1.0 / math.sqrt(HEADDIM)
GELU_A = math.sqrt(2.0 / math.pi)
GELU_B = 0.044715
MIB = 1 << 20


def dot(a, b, dims=((1,), (0,))):
    return lax.dot_general(a, b, (dims, ((), ())), preferred_element_type=F32)


def dot_nt(a, b):
    return dot(a, b, ((1,), (1,)))


def onehot_rows(code):
    tokens = code.shape[1]
    row = lax.broadcasted_iota(jnp.int32, (16, tokens), 0)
    step = jnp.where(row == (code & 7), 1.0, 0.0)
    flip = jnp.where((row == 8) & (code >= 8), 1.0, 0.0)
    return (step + flip).astype(BF)


def embed(tokens, code, plan, flip):
    row = lax.broadcasted_iota(jnp.int32, (8, WIDTH), 0)
    table = jnp.concatenate([plan, jnp.where(row == 0, flip, 0.0)], axis=0)
    high = table.astype(BF)
    rest = table - high.astype(F32)
    middle = rest.astype(BF)
    low = (rest - middle.astype(F32)).astype(BF)
    onehot = onehot_rows(code)
    chosen = dot(
        jnp.concatenate([onehot, onehot, onehot], axis=0),
        jnp.concatenate([high, middle, low], axis=0),
        ((0,), (0,)),
    )
    return tokens.astype(F32) + chosen


def inverse_rms(stream):
    return lax.rsqrt(jnp.mean(stream * stream, axis=-1, keepdims=True) + EPS)


def norm_back(stream, gain, grad):
    inverse = inverse_rms(stream)
    normed = stream * inverse
    scaled = grad * gain
    mean = jnp.mean(scaled * normed, axis=-1, keepdims=True)
    return inverse * (scaled - normed * mean), jnp.sum(grad * normed, axis=0, keepdims=True)


def gather_heads(slot, period):
    feature = lax.broadcasted_iota(jnp.int32, (WIDTH, LANES), 0) // HEADDIM
    lane = lax.broadcasted_iota(jnp.int32, (WIDTH, LANES), 1) % period
    return jnp.where(lane - feature == slot * HEADS, 1.0, 0.0).astype(BF)


def spread_heads(slot, period):
    lane = lax.broadcasted_iota(jnp.int32, (LANES, WIDTH), 0)
    feature = lax.broadcasted_iota(jnp.int32, (LANES, WIDTH), 1) // HEADDIM
    at = (lane < 2 * period) & (lane % period - feature == slot * HEADS)
    return jnp.where(at, 1.0, 0.0).astype(BF)


def two_parts(value, period):
    lane = lax.broadcasted_iota(jnp.int32, value.shape, 1)
    high = value.astype(BF).astype(F32)
    return jnp.where(lane < period, high, value - high).astype(BF)


def slot_total(value, period):
    shift = HEADS
    while shift < period:
        value = value + pltpu.roll(value, shift, 1)
        shift *= 2
    return value


def softmax_parts(scores, valid, period):
    bent = jnp.tanh(scores * (SCORE / CAP))
    weights = jnp.where(valid, jnp.exp(CAP * bent), 0.0)
    return bent, weights / slot_total(weights, period)


def softmax_back(bent, probs, grad, period):
    inner = probs * grad
    return (inner - probs * slot_total(inner, period)) * (1.0 - bent * bent) * SCORE


def tanner_valid(tokens):
    lane = lax.broadcasted_iota(jnp.int32, (tokens, LANES), 1)
    return lane % 64 < HEADS * (MONOS + 1)


def time_valid(tokens, rounds):
    lane = lax.broadcasted_iota(jnp.int32, (tokens, LANES), 1)
    row = lax.broadcasted_iota(jnp.int32, (tokens, LANES), 0)
    return (lane % 32) // HEADS <= row // (tokens // rounds)


def offset_of(offsets, index):
    return offsets[index, 0] if index in ALONG_ROWS else offsets[index, 1]


def neighbour(number, offsets, extended, columns):
    rounds, twice, width, features = extended.shape
    rows = twice // 2
    tokens = rounds * rows * width
    if number == 0:
        return extended[:, :rows].reshape(tokens, features)
    by = offset_of(offsets, number - 1)
    if number - 1 in ALONG_ROWS:
        return extended[:, pl.ds(by, rows)].reshape(tokens, features)
    own = extended[:, :rows].reshape(rounds * rows, width, features)
    place = lax.broadcasted_iota(jnp.int32, own.shape, 1)
    joined = jnp.where(place >= by, own, columns[...])
    return pltpu.roll(joined, width - by, 1).reshape(tokens, features)


def start_kernel(*refs):
    count = (len(refs) - 10) // 2
    tokens, code, plan, flip, gain, *sources = refs[: 5 + count]
    x_out, hidden_out, query_out, kv_out, *copies = refs[5 + count : -1]
    done = refs[-1]
    moves = [pltpu.make_async_copy(source, copy, done.at[i]) for i, (source, copy) in enumerate(zip(sources, copies))]
    for move in moves:
        move.start()
    x = embed(tokens[...], code[...], plan[...], flip[...])
    hidden = (x * inverse_rms(x) * gain[...]).astype(BF)
    x_out[...] = x
    hidden_out[...] = hidden
    for number, out in ((0, query_out), (1, kv_out)):
        moves[number].wait()
        out[...] = dot(hidden, copies[number][...]).astype(BF)
    for move in moves[2:]:
        move.wait()


def forward_kernel(
    place, offsets, x_in, query_in, kv_in, row_tokens, row_code, col_tokens, col_code, plan, flip,
    gain_tanner, w_key_value, w_merge, gain_time, w_temporal, w_temporal_out, gain_ffn, w_up, w_down, cotangent,
    keep, send, grad_time_out, tanner_out, mixed_one_out, mixed_two_out, packed_out, hidden_two_out,
    row_kv_out, col_kv_out, bent_one_out, probs_one_out, bent_two_out, probs_two_out, grad_gain_out,
    extended, columns, transposed, transposed_act,
):
    rounds, twice, width, features = extended.shape
    rows = twice // 2
    tokens = x_in.shape[0]
    core = place[0]
    borrowed = []
    for tok, code, out in ((row_tokens, row_code, row_kv_out), (col_tokens, col_code, col_kv_out)):
        other = embed(tok[...], code[...], plan[...], flip[...])
        hidden = (other * inverse_rms(other) * gain_tanner[...]).astype(BF)
        kv = dot(hidden, w_key_value[...]).astype(BF)
        out[...] = kv
        borrowed.append(kv.astype(F32))
    extended[:, :rows] = kv_in[...].astype(F32).reshape(rounds, rows, width, features)
    extended[:, rows:] = borrowed[0].reshape(rounds, rows, width, features)
    columns[...] = borrowed[1].reshape(rounds * rows, width, features)
    query = query_in[...].astype(F32)
    scores = None
    for number in range(MONOS + 1):
        keys = neighbour(number, offsets, extended, columns)[:, :WIDTH]
        part = dot((query * keys).astype(BF), gather_heads(number, 64))
        scores = part if scores is None else scores + part
    bent, probs = softmax_parts(scores, tanner_valid(tokens), 64)
    bent_one_out[...] = bent
    probs_one_out[...] = probs
    parts = two_parts(probs, 64)
    mixed = None
    for number in range(MONOS + 1):
        values = neighbour(number, offsets, extended, columns)[:, WIDTH:]
        part = dot(parts, spread_heads(number, 64)) * values
        mixed = part if mixed is None else mixed + part
    mixed_one = mixed.astype(BF)
    mixed_one_out[...] = mixed_one
    after_tanner = x_in[...] + dot(mixed_one, w_merge[...])
    tanner_out[...] = after_tanner

    hidden_two = (after_tanner * inverse_rms(after_tanner) * gain_time[...]).astype(BF)
    hidden_two_out[...] = hidden_two
    packed_low = dot(hidden_two, w_temporal[...]).astype(BF)
    packed_out[...] = packed_low
    packed = packed_low.astype(F32).reshape(rounds, tokens // rounds, 3 * WIDTH)
    sites = tokens // rounds
    scores = None
    for earlier in range(rounds):
        product = packed[earlier:, :, :WIDTH] * packed[earlier][None, :, WIDTH : 2 * WIDTH]
        part = dot(product.reshape(-1, WIDTH).astype(BF), gather_heads(earlier, 32))
        if earlier:
            part = jnp.concatenate([jnp.zeros((earlier * sites, LANES), F32), part], axis=0)
        scores = part if scores is None else scores + part
    bent, probs = softmax_parts(scores, time_valid(tokens, rounds), 32)
    bent_two_out[...] = bent
    probs_two_out[...] = probs
    parts = two_parts(probs, 32)
    mixed = None
    for earlier in range(rounds):
        weight = dot(parts[earlier * sites :], spread_heads(earlier, 32)).reshape(rounds - earlier, sites, WIDTH)
        part = (weight * packed[earlier][None, :, 2 * WIDTH :]).reshape(-1, WIDTH)
        if earlier:
            part = jnp.concatenate([jnp.zeros((earlier * sites, WIDTH), F32), part], axis=0)
        mixed = part if mixed is None else mixed + part
    mixed_two = mixed.astype(BF)
    mixed_two_out[...] = mixed_two
    after_time = after_tanner + dot(mixed_two, w_temporal_out[...])

    hidden = (after_time * inverse_rms(after_time) * gain_ffn[...]).astype(BF)
    outer = cotangent[...]
    transposed[...] = hidden.T
    grad_three = None
    befores = []
    for block in range(FF // WIDTH):
        cols = slice(block * WIDTH, (block + 1) * WIDTH)
        before = dot(hidden, w_up[:, cols])
        square = before * before
        bend = jnp.tanh(GELU_A * before * (1.0 + GELU_B * square))
        upper = 0.5 * (1.0 + bend)
        activated = (before * upper).astype(BF)
        slope = upper + 0.5 * before * (1.0 - bend * bend) * (GELU_A * (1.0 + 3.0 * GELU_B * square))
        grad_before = (dot_nt(outer, w_down[cols, :]) * slope).astype(BF)
        befores.append(grad_before)
        part = dot_nt(grad_before, w_up[:, cols])
        grad_three = part if grad_three is None else grad_three + part
        transposed_act[cols, :] = activated.T
    for ref, which in ((keep, core), (send, 1 - core)):
        half = pl.ds(pl.multiple_of(which * HALF, HALF), HALF)
        lead = transposed[half, :]
        for block in range(FF // WIDTH):
            ref[block * HALF : (block + 1) * HALF, :] = dot(lead, befores[block]).astype(BF)
            part = transposed_act[pl.ds(pl.multiple_of(block * WIDTH + which * HALF, HALF), HALF), :]
            base = (FF // WIDTH + block) * HALF
            ref[base : base + HALF, :] = dot(part, outer).astype(BF)
    grad_norm, grad_gain = norm_back(after_time, gain_ffn[...], grad_three)
    grad_time_out[...] = outer.astype(F32) + grad_norm
    grad_gain_out[...] = grad_gain


def backward_kernel(
    offsets, grad_time_in, tanner_in, packed_in, query_in, kv_in, row_kv, col_kv,
    bent_one, probs_one, bent_two, probs_two, w_merge, gain_time, w_temporal, w_temporal_out,
    grad_query_out, grad_kv_out, grad_rows_out, grad_cols_out, grad_packed_out, grad_tanner_out, grad_gain_out,
    extended, columns, grad_extended,
):
    rounds, twice, width, features = extended.shape
    rows = twice // 2
    tokens = grad_time_in.shape[0]
    sites = tokens // rounds
    grad_time = grad_time_in[...]
    grad_mixed = dot_nt(grad_time.astype(BF), w_temporal_out[...]).reshape(rounds, sites, WIDTH)
    packed = packed_in[...].astype(F32).reshape(rounds, sites, 3 * WIDTH)
    grad_probs = None
    for earlier in range(rounds):
        product = grad_mixed[earlier:] * packed[earlier][None, :, 2 * WIDTH :]
        part = dot(product.reshape(-1, WIDTH).astype(BF), gather_heads(earlier, 32))
        if earlier:
            part = jnp.concatenate([jnp.zeros((earlier * sites, LANES), F32), part], axis=0)
        grad_probs = part if grad_probs is None else grad_probs + part
    probs = probs_two[...]
    prob_parts = two_parts(probs, 32)
    score_parts = two_parts(softmax_back(bent_two[...], probs, grad_probs, 32), 32)
    grad_queries = None
    grad_keys = []
    grad_values = []
    for earlier in range(rounds):
        spread = spread_heads(earlier, 32)
        shape = (rounds - earlier, sites, WIDTH)
        weight = dot(prob_parts[earlier * sites :], spread).reshape(shape)
        slope = dot(score_parts[earlier * sites :], spread).reshape(shape)
        grad_values.append(jnp.sum(weight * grad_mixed[earlier:], axis=0))
        grad_keys.append(jnp.sum(slope * packed[earlier:, :, :WIDTH], axis=0))
        part = (slope * packed[earlier][None, :, WIDTH : 2 * WIDTH]).reshape(-1, WIDTH)
        if earlier:
            part = jnp.concatenate([jnp.zeros((earlier * sites, WIDTH), F32), part], axis=0)
        grad_queries = part if grad_queries is None else grad_queries + part
    grad_packed = jnp.concatenate(
        [grad_queries, jnp.concatenate(grad_keys, axis=0), jnp.concatenate(grad_values, axis=0)], axis=1
    ).astype(BF)
    grad_packed_out[...] = grad_packed
    grad_two = dot_nt(grad_packed, w_temporal[...])
    grad_norm, grad_gain = norm_back(tanner_in[...], gain_time[...], grad_two)
    grad_gain_out[...] = grad_gain
    grad_tanner = grad_time + grad_norm
    grad_tanner_out[...] = grad_tanner

    grad_mixed = dot_nt(grad_tanner.astype(BF), w_merge[...])
    extended[:, :rows] = kv_in[...].astype(F32).reshape(rounds, rows, width, features)
    extended[:, rows:] = row_kv[...].astype(F32).reshape(rounds, rows, width, features)
    columns[...] = col_kv[...].astype(F32).reshape(rounds * rows, width, features)
    grad_probs = None
    for number in range(MONOS + 1):
        values = neighbour(number, offsets, extended, columns)[:, WIDTH:]
        part = dot((grad_mixed * values).astype(BF), gather_heads(number, 64))
        grad_probs = part if grad_probs is None else grad_probs + part
    probs = probs_one[...]
    prob_parts = two_parts(probs, 64)
    score_parts = two_parts(softmax_back(bent_one[...], probs, grad_probs, 64), 64)
    query = query_in[...].astype(F32)
    grad_query = None
    grad_cols = None
    for number in (0,) + tuple(i + 1 for i in range(MONOS)):
        spread = spread_heads(number, 64)
        slope = dot(score_parts, spread)
        weight = dot(prob_parts, spread)
        keys = neighbour(number, offsets, extended, columns)[:, :WIDTH]
        part = slope * keys
        grad_query = part if grad_query is None else grad_query + part
        grad_kv = jnp.concatenate([slope * query, weight * grad_mixed], axis=1)
        if number == 0:
            grad_extended[:, :rows] = grad_kv.reshape(rounds, rows, width, features)
            grad_extended[:, rows:] = jnp.zeros((rounds, rows, width, features), F32)
            continue
        by = offset_of(offsets, number - 1)
        if number - 1 in ALONG_ROWS:
            grad_extended[:, pl.ds(by, rows)] += grad_kv.reshape(rounds, rows, width, features)
            continue
        moved = pltpu.roll(grad_kv.reshape(rounds * rows, width, features), by % width, 1)
        place = lax.broadcasted_iota(jnp.int32, moved.shape, 1)
        own = jnp.where(place >= by, moved, 0.0)
        grad_extended[:, :rows] += own.reshape(rounds, rows, width, features)
        grad_cols = moved - own if grad_cols is None else grad_cols + (moved - own)
    grad_query_out[...] = grad_query.astype(BF)
    grad_kv_out[...] = grad_extended[:, :rows].reshape(tokens, features)
    grad_rows_out[...] = grad_extended[:, rows:].reshape(tokens, features).astype(BF)
    grad_cols_out[...] = grad_cols.reshape(tokens, features).astype(BF)


def weights_kernel(place, mixed_two, grad_time, hidden_two, grad_packed, mixed_one, grad_tanner, keep, send, transposed):
    core = place[0]
    transposed[0] = hidden_two[...].T
    transposed[1] = mixed_two[...].T
    transposed[2] = mixed_one[...].T
    grad_time_low = grad_time[...].astype(BF)
    grad_tanner_low = grad_tanner[...].astype(BF)
    for ref, which in ((keep, core), (send, 1 - core)):
        half = pl.ds(pl.multiple_of(which * HALF, HALF), HALF)
        for block in range(3):
            cols = slice(block * WIDTH, (block + 1) * WIDTH)
            ref[block * HALF : (block + 1) * HALF, :] = dot(transposed[0, half, :], grad_packed[:, cols]).astype(BF)
        ref[3 * HALF : 4 * HALF, :] = dot(transposed[1, half, :], grad_time_low).astype(BF)
        ref[4 * HALF : 5 * HALF, :] = dot(transposed[2, half, :], grad_tanner_low).astype(BF)


def last_kernel(
    place, grad_kv_in, back_rows, back_cols, grad_query_in, hidden_in, x_in, w_query, w_key_value, gain,
    grad_tanner, code, grad_gain_time, grad_gain_ffn, token_grad, keep, send, transposed,
):
    core = place[0]
    grad_kv = (grad_kv_in[...] + back_rows[...].astype(F32) + back_cols[...].astype(F32)).astype(BF)
    grad_query = grad_query_in[...]
    grad_one = dot_nt(grad_kv, w_key_value[...]) + dot_nt(grad_query, w_query[...])
    grad_norm, grad_gain = norm_back(x_in[...], gain[...], grad_one)
    grad_embedded = grad_tanner[...] + grad_norm
    token_grad[...] = grad_embedded.astype(BF)
    onehot = onehot_rows(code[...])
    high = grad_embedded.astype(BF)
    low = (grad_embedded - high.astype(F32)).astype(BF)
    small = dot(onehot, high) + dot(onehot, low)
    row = lax.broadcasted_iota(jnp.int32, small.shape, 0)
    small = jnp.where(row == 9, grad_gain, small)
    small = jnp.where(row == 10, grad_gain_time[...], small)
    small = jnp.where(row == 11, grad_gain_ffn[...], small).astype(BF)
    transposed[...] = hidden_in[...].T
    for ref, which in ((keep, core), (send, 1 - core)):
        lead = transposed[pl.ds(pl.multiple_of(which * HALF, HALF), HALF), :]
        ref[:16, :] = small
        ref[16 : 16 + HALF, :] = dot(lead, grad_query).astype(BF)
        for block in range(2):
            cols = slice(block * WIDTH, (block + 1) * WIDTH)
            base = 16 + (block + 1) * HALF
            ref[base : base + HALF, :] = dot(lead, grad_kv[:, cols]).astype(BF)


def add_kernel(extra, *refs):
    ins, out = refs[:-1], refs[-1]
    value = None
    for ref in ins:
        for part in ([ref] if len(ref.shape) == 2 else [ref.at[i] for i in range(ref.shape[0])]):
            part = part[...].astype(F32)
            value = part if value is None else value + part
    rows = (value.shape[0] - extra) // out.shape[0]
    low = value.astype(BF)
    for number in range(out.shape[0]):
        if extra:
            out[number, :extra, :] = low[:extra]
        out[number, extra:, :] = low[extra + number * rows : extra + (number + 1) * rows]


def end_kernel(extra, scale, received, out, *small):
    value = received[0].astype(F32)
    for number in range(1, received.shape[0]):
        value = value + received[number].astype(F32)
    low = value[extra:].astype(BF)
    for number in range(out.shape[0]):
        out[number] = low
    if extra:
        value = value[:extra] * scale
        small[0][...] = value[:8]
        for number in range(4):
            small[1 + number][...] = value[8 + number : 9 + number]


def repeat_kernel(piece, out):
    for number in range(out.shape[0]):
        out[number] = piece[...]


def unpack_kernel(blocks, scale, place, own, other, *refs):
    outs, halves = refs[:-1], refs[-1]
    core = place[0]
    groups, lines, rows, _ = own.shape
    for ref, which in ((own, core), (other, 1 - core)):
        for group in range(groups):
            for line in range(lines):
                start = (group * lines + line) * rows
                halves[which, start : start + rows, :] = ref[group, line].astype(F32) * scale
    block = 0
    for out, (down, across) in zip(outs, blocks):
        for index in range(down * across):
            for half in range(2):
                top = (index if down > 1 else 0) * WIDTH + half * HALF
                left = (index if across > 1 else 0) * WIDTH
                out[top : top + HALF, left : left + WIDTH] = halves[half, block * HALF : (block + 1) * HALF, :]
            block += 1


def call(kernel, outs, args, scratch=(), smem=0, limit=16):
    vmem = pl.BlockSpec(memory_space=pltpu.VMEM)
    return pl.pallas_call(
        kernel,
        out_shape=[jax.ShapeDtypeStruct(shape, dtype) for shape, dtype in outs],
        in_specs=[pl.BlockSpec(memory_space=pltpu.SMEM)] * smem + [vmem] * (len(args) - smem),
        out_specs=[vmem] * len(outs),
        scratch_shapes=list(scratch),
        compiler_params=pltpu.CompilerParams(vmem_limit_bytes=limit * MIB),
    )(*args)


def shifted(x, axis, by):
    count = lax.axis_size(axis)
    return lax.ppermute(x, axis, [(i, (i + by) % count) for i in range(count)])


class Layout:
    def __init__(self):
        self.nx = lax.axis_size("gx")
        self.ny = lax.axis_size("gy")
        self.groups = self.ny
        self.lines = self.nx // 2

    def place(self):
        gx = lax.axis_index("gx")
        gy = lax.axis_index("gy")
        return jnp.stack([gy % 2, (gy // 2) * 2 + gx % 2, gx // 2]).astype(jnp.int32)

    def core(self, x):
        pairs = []
        for gx in range(self.nx):
            for gy in range(self.ny):
                pairs.append((gx * self.ny + gy, gx * self.ny + (gy ^ 1)))
        return lax.ppermute(x, ("gx", "gy"), pairs)

    def device(self, group, line, core):
        return (line * 2 + group % 2) * self.ny + (group // 2) * 2 + core

    def trade(self, x, sets):
        return lax.all_to_all(x, ("gx", "gy"), 0, 0, axis_index_groups=sets)

    def group(self, x):
        return self.trade(
            x,
            [
                [self.device(group, line, core) for group in range(self.groups)]
                for line in range(self.lines)
                for core in range(2)
            ],
        )

    def line(self, x):
        return self.trade(
            x,
            [
                [self.device(group, line, core) for line in range(self.lines)]
                for group in range(self.groups)
                for core in range(2)
            ],
        )


def reduce_group(layout, keep, send, extra, scale):
    rows = keep.shape[0] - extra
    received = layout.core(send)
    part = rows // layout.groups
    pieces = call(
        functools.partial(add_kernel, extra),
        [((layout.groups, part + extra, WIDTH), BF)],
        [keep, received],
    )[0]
    received = layout.group(pieces)
    part = part // layout.lines
    pieces = call(
        functools.partial(add_kernel, extra),
        [((layout.lines, part + extra, WIDTH), BF)],
        [received],
    )[0]
    received = layout.line(pieces)
    small = [((8, WIDTH), F32)] + [((1, WIDTH), F32)] * 4 if extra else []
    outs = call(
        functools.partial(end_kernel, extra, scale),
        [((layout.lines, part, WIDTH), BF)] + small,
        [received],
    )
    return outs[0], outs[1:]


def gather_group(layout, place, shards, blocks, scale):
    lined = layout.line(shards)
    copies = call(repeat_kernel, [((layout.groups,) + lined.shape, BF)], [lined])[0]
    own = layout.group(copies)
    other = layout.core(own)
    total = sum(down * across for down, across in blocks)
    return call(
        functools.partial(unpack_kernel, blocks, scale),
        [((down * WIDTH, across * WIDTH), F32) for down, across in blocks],
        [place, own, other],
        [pltpu.VMEM((2, total * HALF, WIDTH), F32)],
        smem=1,
    )


def on_device(
    tokens,
    syndrome,
    check_plan_step,
    offsets,
    flip_vector,
    plan_step_embedding,
    gain_tanner,
    w_query,
    w_key_value,
    w_merge,
    gain_time,
    w_temporal,
    w_temporal_out,
    gain_ffn,
    w_ffn_up,
    w_ffn_down,
    cotangent,
):
    layout = Layout()
    place = layout.place()
    rounds, rows, cols = tokens.shape[:3]
    count = rounds * rows * cols
    scale = 1.0 / math.sqrt(count * layout.nx * layout.ny)
    flat = (count, WIDTH)
    row_tokens = shifted(tokens, "gx", -1).reshape(flat)
    col_tokens = shifted(tokens, "gy", -1).reshape(flat)
    code = (syndrome * 8 + check_plan_step).reshape(1, count)
    row_code = shifted(code, "gx", -1)
    col_code = shifted(code, "gy", -1)
    flip = flip_vector.reshape(1, WIDTH)
    gain_one = gain_tanner.reshape(1, WIDTH)
    gain_two = gain_time.reshape(1, WIDTH)
    gain_three = gain_ffn.reshape(1, WIDTH)

    act = (flat, BF)
    stream = (flat, F32)
    wide = ((count, 2 * WIDTH), BF)
    lanes = ((count, LANES), F32)
    row = ((1, WIDTH), F32)
    weights = [w_query, w_key_value, w_merge, w_temporal, w_temporal_out, w_ffn_up, w_ffn_down, cotangent.reshape(flat)]
    outs = [stream, act, act, wide] + [(w.shape, w.dtype) for w in weights]
    vmem = pl.BlockSpec(memory_space=pltpu.VMEM)
    (
        x, hidden_one, query, key_value,
        w_query, w_key_value, w_merge, w_temporal, w_temporal_out, w_ffn_up, w_ffn_down, outer,
    ) = pl.pallas_call(
        start_kernel,
        out_shape=[jax.ShapeDtypeStruct(shape, dtype) for shape, dtype in outs],
        in_specs=[vmem] * 5 + [pl.BlockSpec(memory_space=pl.ANY)] * len(weights),
        out_specs=[vmem] * len(outs),
        scratch_shapes=[pltpu.SemaphoreType.DMA((len(weights),))],
        compiler_params=pltpu.CompilerParams(vmem_limit_bytes=16 * MIB),
    )(tokens.reshape(flat), code, plan_step_embedding, flip, gain_one, *weights)
    extended = pltpu.VMEM((rounds, 2 * rows, cols, 2 * WIDTH), F32)
    columns = pltpu.VMEM((rounds * rows, cols, 2 * WIDTH), F32)
    half_one = ((2 * (FF // WIDTH) * HALF, WIDTH), BF)
    (
        keep_one, send_one, grad_time, after_tanner, mixed_one, mixed_two, packed, hidden_two,
        row_kv, col_kv, bent_one, probs_one, bent_two, probs_two, grad_gain_ffn,
    ) = call(
        forward_kernel,
        [half_one, half_one, stream, stream, act, act, ((count, 3 * WIDTH), BF), act,
         wide, wide, lanes, lanes, lanes, lanes, row],
        [place, offsets, x, query, key_value, row_tokens, row_code, col_tokens, col_code, plan_step_embedding, flip,
         gain_one, w_key_value, w_merge, gain_two, w_temporal, w_temporal_out, gain_three, w_ffn_up, w_ffn_down,
         outer],
        [extended, columns, pltpu.VMEM((WIDTH, count), BF), pltpu.VMEM((FF, count), BF)],
        smem=2,
        limit=32,
    )
    grad_query, grad_kv, grad_rows, grad_cols, grad_packed, grad_tanner, grad_gain_time = call(
        backward_kernel,
        [act, ((count, 2 * WIDTH), F32), wide, wide, ((count, 3 * WIDTH), BF), stream, row],
        [offsets, grad_time, after_tanner, packed, query, key_value, row_kv, col_kv,
         bent_one, probs_one, bent_two, probs_two, w_merge, gain_two, w_temporal, w_temporal_out],
        [extended, columns, extended],
        smem=1,
        limit=32,
    )
    back_rows = shifted(grad_rows, "gx", 1)
    back_cols = shifted(grad_cols, "gy", 1)
    half_two = ((5 * HALF, WIDTH), BF)
    keep_two, send_two = call(
        weights_kernel,
        [half_two, half_two],
        [place, mixed_two, grad_time, hidden_two, grad_packed, mixed_one, grad_tanner],
        [pltpu.VMEM((3, WIDTH, count), BF)],
        smem=1,
    )
    shard_one, _ = reduce_group(layout, keep_one, send_one, 0, scale)
    shard_two, _ = reduce_group(layout, keep_two, send_two, 0, scale)
    half_three = ((16 + 3 * HALF, WIDTH), BF)
    token_grad, keep_three, send_three = call(
        last_kernel,
        [act, half_three, half_three],
        [place, grad_kv, back_rows, back_cols, grad_query, hidden_one, x, w_query, w_key_value, gain_one,
         grad_tanner, code, grad_gain_time, grad_gain_ffn],
        [pltpu.VMEM((WIDTH, count), BF)],
        smem=1,
    )
    shard_three, small = reduce_group(layout, keep_three, send_three, 16, scale)
    grad_up, grad_down = gather_group(layout, place, shard_one, ((1, FF // WIDTH), (FF // WIDTH, 1)), scale)
    grad_temporal, grad_temporal_out, grad_merge = gather_group(
        layout, place, shard_two, ((1, 3), (1, 1), (1, 1)), scale
    )
    grad_w_query, grad_key_value = gather_group(layout, place, shard_three, ((1, 1), (1, 2)), scale)
    plan_grad, grad_flip, sum_gain_tanner, sum_gain_time, sum_gain_ffn = small
    return (
        token_grad.reshape(tokens.shape),
        grad_flip.reshape(WIDTH),
        plan_grad,
        sum_gain_tanner.reshape(WIDTH),
        grad_w_query,
        grad_key_value,
        grad_merge,
        sum_gain_time.reshape(WIDTH),
        grad_temporal,
        grad_temporal_out,
        sum_gain_ffn.reshape(WIDTH),
        grad_up,
        grad_down,
    )


def solution(mesh):
    tiled = P(None, "gx", "gy", None)
    sites = P(None, "gx", "gy")
    return jax.shard_map(
        on_device,
        mesh=mesh,
        in_specs=(tiled, sites, sites) + (P(),) * 13 + (tiled,),
        out_specs=(tiled,) + (P(),) * 12,
        check_vma=False,
    )
```

```python
import functools
import math

import jax
import jax.numpy as jnp
from jax import lax
from jax.experimental import pallas as pl
from jax.experimental.pallas import tpu as pltpu
from jax.sharding import PartitionSpec as P

WIDTH = 256
HEADDIM = 32
HEADS = WIDTH // HEADDIM
FF = 1024
PLAN_STEP_COUNT = 8
MONOS = 6
MAXEXP = 8
LANES = 128
HALF = WIDTH // 2

EPS = 1e-05
CAP = 4.0
ALONG_ROWS = (0, 4, 5)
BF = jnp.bfloat16
F32 = jnp.float32
SCORE = 1.0 / math.sqrt(HEADDIM)
GELU_A = math.sqrt(2.0 / math.pi)
GELU_B = 0.044715
MIB = 1 << 20


def dot(a, b, dims=((1,), (0,))):
    return lax.dot_general(a, b, (dims, ((), ())), preferred_element_type=F32)


def dot_nt(a, b):
    return dot(a, b, ((1,), (1,)))


def embed(packed, plan, flip, width):
    count = packed.shape[0]
    lines = count // (width + 1)
    tokens = lines * width
    codes = packed[tokens:, :LANES]
    token = lax.broadcasted_iota(jnp.int32, (tokens, lines), 0)
    line = lax.broadcasted_iota(jnp.int32, (tokens, lines), 1)
    spread = dot(jnp.where(token // width == line, 1.0, 0.0).astype(BF), codes)
    token = lax.broadcasted_iota(jnp.int32, (tokens, LANES), 0)
    lane = lax.broadcasted_iota(jnp.int32, (tokens, LANES), 1)
    picked = jnp.where(token % width == lane, spread, 0.0).astype(BF)
    code = dot(picked, jnp.ones((LANES, LANES), BF))
    flipped = code >= PLAN_STEP_COUNT
    step = jnp.where(flipped, code - PLAN_STEP_COUNT, code)
    slot = lane % 16
    chosen = (slot.astype(F32) == step) | ((slot == PLAN_STEP_COUNT) & flipped)
    onehot = jnp.where(chosen & (lane < 48), 1.0, 0.0).astype(BF)
    row = lax.broadcasted_iota(jnp.int32, (8, WIDTH), 0)
    table = jnp.concatenate([plan, jnp.where(row == 0, flip, 0.0)], axis=0)
    high = table.astype(BF)
    rest = table - high.astype(F32)
    middle = rest.astype(BF)
    low = (rest - middle.astype(F32)).astype(BF)
    empty = jnp.zeros((LANES - 48, WIDTH), BF)
    vectors = dot(onehot, jnp.concatenate([high, middle, low, empty], axis=0))
    return packed[:tokens].astype(F32) + vectors, onehot


def inverse_rms(stream):
    return lax.rsqrt(jnp.mean(stream * stream, axis=-1, keepdims=True) + EPS)


def norm_back(stream, gain, grad):
    inverse = inverse_rms(stream)
    normed = stream * inverse
    scaled = grad * gain
    mean = jnp.mean(scaled * normed, axis=-1, keepdims=True)
    return inverse * (scaled - normed * mean), jnp.sum(grad * normed, axis=0, keepdims=True)


def gather_heads(slot, period):
    feature = lax.broadcasted_iota(jnp.int32, (WIDTH, LANES), 0) // HEADDIM
    lane = lax.broadcasted_iota(jnp.int32, (WIDTH, LANES), 1) % period
    return jnp.where(lane - feature == slot * HEADS, 1.0, 0.0).astype(BF)


def spread_heads(slot, period):
    lane = lax.broadcasted_iota(jnp.int32, (LANES, WIDTH), 0)
    feature = lax.broadcasted_iota(jnp.int32, (LANES, WIDTH), 1) // HEADDIM
    at = (lane < 2 * period) & (lane % period - feature == slot * HEADS)
    return jnp.where(at, 1.0, 0.0).astype(BF)


def two_parts(value, period):
    lane = lax.broadcasted_iota(jnp.int32, value.shape, 1)
    high = value.astype(BF).astype(F32)
    return jnp.where(lane < period, high, value - high).astype(BF)


def slot_total(value, period):
    shift = HEADS
    while shift < period:
        value = value + pltpu.roll(value, shift, 1)
        shift *= 2
    return value


def softmax_parts(scores, valid, period):
    bent = jnp.tanh(scores * (SCORE / CAP))
    weights = jnp.where(valid, jnp.exp(CAP * bent), 0.0)
    return bent, weights / slot_total(weights, period)


def softmax_back(bent, probs, grad, period):
    inner = probs * grad
    return (inner - probs * slot_total(inner, period)) * (1.0 - bent * bent) * SCORE


def tanner_valid(tokens):
    lane = lax.broadcasted_iota(jnp.int32, (tokens, LANES), 1)
    return lane % 64 < HEADS * (MONOS + 1)


def time_valid(tokens, rounds):
    lane = lax.broadcasted_iota(jnp.int32, (tokens, LANES), 1)
    row = lax.broadcasted_iota(jnp.int32, (tokens, LANES), 0)
    return (lane % 32) // HEADS <= row // (tokens // rounds)


def offset_of(offsets, index):
    return offsets[index, 0] if index in ALONG_ROWS else offsets[index, 1]


def neighbour(number, offsets, extended, columns):
    rounds, twice, width, features = extended.shape
    rows = twice // 2
    tokens = rounds * rows * width
    if number == 0:
        return extended[:, :rows].reshape(tokens, features)
    by = offset_of(offsets, number - 1)
    if number - 1 in ALONG_ROWS:
        return extended[:, pl.ds(by, rows)].reshape(tokens, features)
    own = extended[:, :rows].reshape(rounds * rows, width, features)
    place = lax.broadcasted_iota(jnp.int32, own.shape, 1)
    joined = jnp.where(place >= by, own, columns[...])
    return pltpu.roll(joined, width - by, 1).reshape(tokens, features)


def pack_kernel(tokens, syndrome, step, out, flips, steps, done):
    count = tokens.shape[0]
    rounds, rows, width = syndrome.shape
    moves = [
        pltpu.make_async_copy(tokens, out.at[pl.ds(0, count)], done.at[0]),
        pltpu.make_async_copy(syndrome, flips, done.at[1]),
        pltpu.make_async_copy(step, steps, done.at[2]),
    ]
    for move in moves:
        move.start()
    out[count:, :] = jnp.zeros((rounds * rows, WIDTH), BF)
    moves[1].wait()
    moves[2].wait()
    code = flips[...] * PLAN_STEP_COUNT + steps[...]
    out[count:, :width] = code.reshape(rounds * rows, width).astype(F32).astype(BF)
    moves[0].wait()


def start_kernel(width, *refs):
    count = (len(refs) - 7) // 2
    packed, sources = refs[0], refs[1 : 1 + count]
    x_out, onehot_out, hidden_out, query_out, kv_out, *copies = refs[1 + count : -1]
    done = refs[-1]
    moves = [pltpu.make_async_copy(source, copy, done.at[i]) for i, (source, copy) in enumerate(zip(sources, copies))]
    for move in moves:
        move.start()
    for move in moves[:3]:
        move.wait()
    plan, flip, gain, w_query, w_key_value = copies[:5]
    x, onehot = embed(packed[...], plan[...], flip[...], width)
    hidden = (x * inverse_rms(x) * gain[...]).astype(BF)
    x_out[...] = x
    onehot_out[...] = onehot
    hidden_out[...] = hidden
    moves[3].wait()
    query_out[...] = dot(hidden, w_query[...]).astype(BF)
    moves[4].wait()
    kv_out[...] = dot(hidden, w_key_value[...]).astype(BF)
    for move in moves[5:]:
        move.wait()


def forward_kernel(
    place, offsets, x_in, query_in, kv_in, row_packed, col_packed, plan, flip,
    gain_tanner, w_key_value, w_merge, gain_time, w_temporal, w_temporal_out, gain_ffn, w_up, w_down, cotangent,
    keep, send, grad_time_out, tanner_out, mixed_one_out, mixed_two_out, packed_out, hidden_two_out,
    row_kv_out, col_kv_out, row_x_out, col_x_out, row_hidden_out, col_hidden_out, row_onehot_out, col_onehot_out,
    bent_one_out, probs_one_out, bent_two_out, probs_two_out, grad_gain_out,
    extended, columns, transposed, transposed_act,
):
    rounds, twice, width, features = extended.shape
    rows = twice // 2
    tokens = x_in.shape[0]
    core = place[0]
    borrowed = []
    for other, x_out, hidden_out, onehot_out, kv_out in (
        (row_packed, row_x_out, row_hidden_out, row_onehot_out, row_kv_out),
        (col_packed, col_x_out, col_hidden_out, col_onehot_out, col_kv_out),
    ):
        x, onehot = embed(other[...], plan[...], flip[...], width)
        hidden = (x * inverse_rms(x) * gain_tanner[...]).astype(BF)
        kv = dot(hidden, w_key_value[...]).astype(BF)
        x_out[...] = x
        onehot_out[...] = onehot
        hidden_out[...] = hidden
        kv_out[...] = kv
        borrowed.append(kv.astype(F32))
    extended[:, :rows] = kv_in[...].astype(F32).reshape(rounds, rows, width, features)
    extended[:, rows:] = borrowed[0].reshape(rounds, rows, width, features)
    columns[...] = borrowed[1].reshape(rounds * rows, width, features)
    query = query_in[...].astype(F32)
    scores = None
    for number in range(MONOS + 1):
        keys = neighbour(number, offsets, extended, columns)[:, :WIDTH]
        part = dot((query * keys).astype(BF), gather_heads(number, 64))
        scores = part if scores is None else scores + part
    bent, probs = softmax_parts(scores, tanner_valid(tokens), 64)
    bent_one_out[...] = bent
    probs_one_out[...] = probs
    parts = two_parts(probs, 64)
    mixed = None
    for number in range(MONOS + 1):
        values = neighbour(number, offsets, extended, columns)[:, WIDTH:]
        part = dot(parts, spread_heads(number, 64)) * values
        mixed = part if mixed is None else mixed + part
    mixed_one = mixed.astype(BF)
    mixed_one_out[...] = mixed_one
    after_tanner = x_in[...] + dot(mixed_one, w_merge[...])
    tanner_out[...] = after_tanner

    hidden_two = (after_tanner * inverse_rms(after_tanner) * gain_time[...]).astype(BF)
    hidden_two_out[...] = hidden_two
    packed_low = dot(hidden_two, w_temporal[...]).astype(BF)
    packed_out[...] = packed_low
    packed = packed_low.astype(F32).reshape(rounds, tokens // rounds, 3 * WIDTH)
    sites = tokens // rounds
    scores = None
    for earlier in range(rounds):
        product = packed[earlier:, :, :WIDTH] * packed[earlier][None, :, WIDTH : 2 * WIDTH]
        part = dot(product.reshape(-1, WIDTH).astype(BF), gather_heads(earlier, 32))
        if earlier:
            part = jnp.concatenate([jnp.zeros((earlier * sites, LANES), F32), part], axis=0)
        scores = part if scores is None else scores + part
    bent, probs = softmax_parts(scores, time_valid(tokens, rounds), 32)
    bent_two_out[...] = bent
    probs_two_out[...] = probs
    parts = two_parts(probs, 32)
    mixed = None
    for earlier in range(rounds):
        weight = dot(parts[earlier * sites :], spread_heads(earlier, 32)).reshape(rounds - earlier, sites, WIDTH)
        part = (weight * packed[earlier][None, :, 2 * WIDTH :]).reshape(-1, WIDTH)
        if earlier:
            part = jnp.concatenate([jnp.zeros((earlier * sites, WIDTH), F32), part], axis=0)
        mixed = part if mixed is None else mixed + part
    mixed_two = mixed.astype(BF)
    mixed_two_out[...] = mixed_two
    after_time = after_tanner + dot(mixed_two, w_temporal_out[...])

    hidden = (after_time * inverse_rms(after_time) * gain_ffn[...]).astype(BF)
    outer = cotangent[...]
    transposed[...] = hidden.T
    grad_three = None
    befores = []
    for block in range(FF // WIDTH):
        cols = slice(block * WIDTH, (block + 1) * WIDTH)
        before = dot(hidden, w_up[:, cols])
        square = before * before
        bend = jnp.tanh(GELU_A * before * (1.0 + GELU_B * square))
        upper = 0.5 * (1.0 + bend)
        activated = (before * upper).astype(BF)
        slope = upper + 0.5 * before * (1.0 - bend * bend) * (GELU_A * (1.0 + 3.0 * GELU_B * square))
        grad_before = (dot_nt(outer, w_down[cols, :]) * slope).astype(BF)
        befores.append(grad_before)
        part = dot_nt(grad_before, w_up[:, cols])
        grad_three = part if grad_three is None else grad_three + part
        transposed_act[cols, :] = activated.T
    for ref, which in ((keep, core), (send, 1 - core)):
        half = pl.ds(pl.multiple_of(which * HALF, HALF), HALF)
        lead = transposed[half, :]
        for block in range(FF // WIDTH):
            ref[block * HALF : (block + 1) * HALF, :] = dot(lead, befores[block]).astype(BF)
            part = transposed_act[pl.ds(pl.multiple_of(block * WIDTH + which * HALF, HALF), HALF), :]
            base = (FF // WIDTH + block) * HALF
            ref[base : base + HALF, :] = dot(part, outer).astype(BF)
    grad_norm, grad_gain = norm_back(after_time, gain_ffn[...], grad_three)
    grad_time_out[...] = outer.astype(F32) + grad_norm
    grad_gain_out[...] = grad_gain


def backward_kernel(
    offsets, grad_time_in, tanner_in, packed_in, query_in, kv_in, row_kv, col_kv,
    bent_one, probs_one, bent_two, probs_two, w_merge, gain_time, w_temporal, w_temporal_out,
    grad_query_out, grad_kv_out, grad_rows_out, grad_cols_out, grad_packed_out, grad_tanner_out, grad_gain_out,
    extended, columns, grad_extended,
):
    rounds, twice, width, features = extended.shape
    rows = twice // 2
    tokens = grad_time_in.shape[0]
    sites = tokens // rounds
    grad_time = grad_time_in[...]
    grad_mixed = dot_nt(grad_time.astype(BF), w_temporal_out[...]).reshape(rounds, sites, WIDTH)
    packed = packed_in[...].astype(F32).reshape(rounds, sites, 3 * WIDTH)
    grad_probs = None
    for earlier in range(rounds):
        product = grad_mixed[earlier:] * packed[earlier][None, :, 2 * WIDTH :]
        part = dot(product.reshape(-1, WIDTH).astype(BF), gather_heads(earlier, 32))
        if earlier:
            part = jnp.concatenate([jnp.zeros((earlier * sites, LANES), F32), part], axis=0)
        grad_probs = part if grad_probs is None else grad_probs + part
    probs = probs_two[...]
    prob_parts = two_parts(probs, 32)
    score_parts = two_parts(softmax_back(bent_two[...], probs, grad_probs, 32), 32)
    grad_queries = None
    grad_keys = []
    grad_values = []
    for earlier in range(rounds):
        spread = spread_heads(earlier, 32)
        shape = (rounds - earlier, sites, WIDTH)
        weight = dot(prob_parts[earlier * sites :], spread).reshape(shape)
        slope = dot(score_parts[earlier * sites :], spread).reshape(shape)
        grad_values.append(jnp.sum(weight * grad_mixed[earlier:], axis=0))
        grad_keys.append(jnp.sum(slope * packed[earlier:, :, :WIDTH], axis=0))
        part = (slope * packed[earlier][None, :, WIDTH : 2 * WIDTH]).reshape(-1, WIDTH)
        if earlier:
            part = jnp.concatenate([jnp.zeros((earlier * sites, WIDTH), F32), part], axis=0)
        grad_queries = part if grad_queries is None else grad_queries + part
    grad_packed = jnp.concatenate(
        [grad_queries, jnp.concatenate(grad_keys, axis=0), jnp.concatenate(grad_values, axis=0)], axis=1
    ).astype(BF)
    grad_packed_out[...] = grad_packed
    grad_two = dot_nt(grad_packed, w_temporal[...])
    grad_norm, grad_gain = norm_back(tanner_in[...], gain_time[...], grad_two)
    grad_gain_out[...] = grad_gain
    grad_tanner = grad_time + grad_norm
    grad_tanner_out[...] = grad_tanner

    grad_mixed = dot_nt(grad_tanner.astype(BF), w_merge[...])
    extended[:, :rows] = kv_in[...].astype(F32).reshape(rounds, rows, width, features)
    extended[:, rows:] = row_kv[...].astype(F32).reshape(rounds, rows, width, features)
    columns[...] = col_kv[...].astype(F32).reshape(rounds * rows, width, features)
    grad_probs = None
    for number in range(MONOS + 1):
        values = neighbour(number, offsets, extended, columns)[:, WIDTH:]
        part = dot((grad_mixed * values).astype(BF), gather_heads(number, 64))
        grad_probs = part if grad_probs is None else grad_probs + part
    probs = probs_one[...]
    prob_parts = two_parts(probs, 64)
    score_parts = two_parts(softmax_back(bent_one[...], probs, grad_probs, 64), 64)
    query = query_in[...].astype(F32)
    grad_query = None
    grad_cols = None
    for number in (0,) + tuple(i + 1 for i in range(MONOS)):
        spread = spread_heads(number, 64)
        slope = dot(score_parts, spread)
        weight = dot(prob_parts, spread)
        keys = neighbour(number, offsets, extended, columns)[:, :WIDTH]
        part = slope * keys
        grad_query = part if grad_query is None else grad_query + part
        grad_kv = jnp.concatenate([slope * query, weight * grad_mixed], axis=1)
        if number == 0:
            grad_extended[:, :rows] = grad_kv.reshape(rounds, rows, width, features)
            grad_extended[:, rows:] = jnp.zeros((rounds, rows, width, features), F32)
            continue
        by = offset_of(offsets, number - 1)
        if number - 1 in ALONG_ROWS:
            grad_extended[:, pl.ds(by, rows)] += grad_kv.reshape(rounds, rows, width, features)
            continue
        moved = pltpu.roll(grad_kv.reshape(rounds * rows, width, features), by % width, 1)
        place = lax.broadcasted_iota(jnp.int32, moved.shape, 1)
        own = jnp.where(place >= by, moved, 0.0)
        grad_extended[:, :rows] += own.reshape(rounds, rows, width, features)
        grad_cols = moved - own if grad_cols is None else grad_cols + (moved - own)
    grad_query_out[...] = grad_query.astype(BF)
    grad_kv_out[...] = grad_extended[:, :rows].reshape(tokens, features).astype(BF)
    grad_rows_out[...] = grad_extended[:, rows:].reshape(tokens, features).astype(BF)
    grad_cols_out[...] = grad_cols.reshape(tokens, features).astype(BF)


def weights_kernel(
    place, mixed_two, grad_time, hidden_two, grad_packed, mixed_one, grad_tanner, grad_query, w_query, w_key_value, gain,
    x_own, x_row, x_col, hidden_own, hidden_row, hidden_col, onehot_own, onehot_row, onehot_col,
    grad_own, grad_row, grad_col, grad_gain_time, grad_gain_ffn,
    grad_out, row_out, col_out, keep, send, transposed, transposed_own,
):
    core = place[0]
    tokens = x_own.shape[0]
    transposed[0] = hidden_two[...].T
    transposed[1] = mixed_two[...].T
    transposed[2] = mixed_one[...].T
    small = None
    grad_gain = None
    for number, (x, hidden, onehot, grad_kv, out) in enumerate((
        (x_own, hidden_own, onehot_own, grad_own, grad_out),
        (x_row, hidden_row, onehot_row, grad_row, row_out),
        (x_col, hidden_col, onehot_col, grad_col, col_out),
    )):
        transposed_own[:, number * tokens : (number + 1) * tokens] = hidden[...].T
        grad_one = dot_nt(grad_kv[...], w_key_value[...])
        if number == 0:
            grad_one = grad_one + dot_nt(grad_query[...], w_query[...])
        grad, part = norm_back(x[...], gain[...], grad_one)
        grad_gain = part if grad_gain is None else grad_gain + part
        if number == 0:
            grad = grad + grad_tanner[...]
        out[...] = grad.astype(out.dtype)
        high = grad.astype(BF)
        low = (grad - high.astype(F32)).astype(BF)
        part = dot(onehot[...], jnp.concatenate([high, low], axis=1), ((0,), (0,)))[:16]
        part = part[:, :WIDTH] + part[:, WIDTH:]
        small = part if small is None else small + part
    row = lax.broadcasted_iota(jnp.int32, small.shape, 0)
    small = jnp.where(row == 9, grad_gain, small)
    small = jnp.where(row == 10, grad_gain_time[...], small)
    small = jnp.where(row == 11, grad_gain_ffn[...], small).astype(BF)
    grad_time_low = grad_time[...].astype(BF)
    grad_tanner_low = grad_tanner[...].astype(BF)
    grad_all = jnp.concatenate([grad_own[...], grad_row[...], grad_col[...]], axis=0)
    for ref, which in ((keep, core), (send, 1 - core)):
        half = pl.ds(pl.multiple_of(which * HALF, HALF), HALF)
        products = []
        for block in range(3):
            cols = slice(block * WIDTH, (block + 1) * WIDTH)
            products.append(dot(transposed[0, half, :], grad_packed[:, cols]))
        products.append(dot(transposed[1, half, :], grad_time_low))
        products.append(dot(transposed[2, half, :], grad_tanner_low))
        products.append(dot(transposed_own[half, :tokens], grad_query[...]))
        for block in range(2):
            cols = slice(block * WIDTH, (block + 1) * WIDTH)
            products.append(dot(transposed_own[half, :], grad_all[:, cols]))
        ref[:16, :] = small
        for block, product in enumerate(products):
            ref[16 + block * HALF : 16 + (block + 1) * HALF, :] = product.astype(BF)


def finish_kernel(grad, row, col, out):
    out[...] = (grad[...] + row[...].astype(F32) + col[...].astype(F32)).astype(BF)


def split_kernel(extra, bit, place, kept, received, keep, send, total):
    value = kept[...].astype(F32) + received[...].astype(F32)
    total[...] = value[extra:]
    rows = keep.shape[0] - extra
    for ref, which in ((keep, place[bit]), (send, 1 - place[bit])):
        if extra:
            ref[:extra, :] = value[:extra].astype(BF)
        ref[extra:, :] = total[pl.ds(pl.multiple_of(which * rows, rows), rows), :].astype(BF)


def end_kernel(extra, scale, kept, received, out, *small):
    value = kept[...].astype(F32) + received[...].astype(F32)
    out[...] = value[extra:].astype(BF)
    if extra:
        value = value[:extra] * scale
        small[0][...] = value[:8]
        for number in range(4):
            small[1 + number][...] = value[8 + number : 9 + number]


def join_kernel(bit, place, own, received, out):
    out[place[bit]] = own[...]
    out[1 - place[bit]] = received[...]


def unpack_kernel(blocks, scale, place, own, other, *refs):
    outs, halves = refs[:-1], refs[-1]
    halves[place[0]] = own[...].astype(F32) * scale
    halves[1 - place[0]] = other[...].astype(F32) * scale
    block = 0
    for out, (down, across) in zip(outs, blocks):
        for index in range(down * across):
            for half in range(2):
                top = (index if down > 1 else 0) * WIDTH + half * HALF
                left = (index if across > 1 else 0) * WIDTH
                out[top : top + HALF, left : left + WIDTH] = halves[half, block * HALF : (block + 1) * HALF, :]
            block += 1


def call(kernel, outs, args, scratch=(), smem=0, limit=16):
    vmem = pl.BlockSpec(memory_space=pltpu.VMEM)
    return pl.pallas_call(
        kernel,
        out_shape=[jax.ShapeDtypeStruct(shape, dtype) for shape, dtype in outs],
        in_specs=[pl.BlockSpec(memory_space=pltpu.SMEM)] * smem + [vmem] * (len(args) - smem),
        out_specs=[vmem] * len(outs),
        scratch_shapes=list(scratch),
        compiler_params=pltpu.CompilerParams(vmem_limit_bytes=limit * MIB),
    )(*args)


def shifted(x, axis, by):
    count = lax.axis_size(axis)
    return lax.ppermute(x, axis, [(i, (i + by) % count) for i in range(count)])


class Layout:
    def __init__(self):
        self.nx = lax.axis_size("gx")
        self.ny = lax.axis_size("gy")
        self.many = self.ny.bit_length() - 1
        self.bits = self.many + self.nx.bit_length() - 1
        assert 1 << self.bits == self.nx * self.ny

    def place(self):
        gx = lax.axis_index("gx")
        gy = lax.axis_index("gy")
        bits = [(gy >> b) & 1 for b in range(self.many)] + [(gx >> b) & 1 for b in range(self.bits - self.many)]
        return jnp.stack(bits).astype(jnp.int32)

    def swap(self, x, bit):
        flip = 1 << bit if bit < self.many else self.ny << (bit - self.many)
        return lax.ppermute(x, ("gx", "gy"), [(i, i ^ flip) for i in range(self.nx * self.ny)])


def reduce_tree(layout, place, keep, send, extra, order, scale):
    for stage, bit in enumerate(order):
        received = layout.swap(send, bit)
        rows = keep.shape[0] - extra
        if stage + 1 < len(order):
            half = ((rows // 2 + extra, WIDTH), BF)
            keep, send = call(
                functools.partial(split_kernel, extra, order[stage + 1]),
                [half, half],
                [place, keep, received],
                [pltpu.VMEM((rows, WIDTH), F32)],
                smem=1,
            )
    small = [((8, WIDTH), F32)] + [((1, WIDTH), F32)] * 4 if extra else []
    return call(functools.partial(end_kernel, extra, scale), [((rows, WIDTH), BF)] + small, [keep, received])


def gather_tree(layout, place, own, order, blocks, scale):
    for bit in order[:0:-1]:
        received = layout.swap(own, bit)
        rows = own.shape[0]
        own = call(
            functools.partial(join_kernel, bit), [((2, rows, WIDTH), BF)], [place, own, received], smem=1
        )[0].reshape(2 * rows, WIDTH)
    other = layout.swap(own, order[0])
    return call(
        functools.partial(unpack_kernel, blocks, scale),
        [((down * WIDTH, across * WIDTH), F32) for down, across in blocks],
        [place, own, other],
        [pltpu.VMEM((2,) + own.shape, F32)],
        smem=1,
    )


def on_device(
    tokens,
    syndrome,
    check_plan_step,
    offsets,
    flip_vector,
    plan_step_embedding,
    gain_tanner,
    w_query,
    w_key_value,
    w_merge,
    gain_time,
    w_temporal,
    w_temporal_out,
    gain_ffn,
    w_ffn_up,
    w_ffn_down,
    cotangent,
):
    layout = Layout()
    place = layout.place()
    rounds, rows, cols = tokens.shape[:3]
    count = rounds * rows * cols
    scale = 1.0 / math.sqrt(count * layout.nx * layout.ny)
    flat = (count, WIDTH)
    act = (flat, BF)
    stream = (flat, F32)
    wide = ((count, 2 * WIDTH), BF)
    lanes = ((count, LANES), F32)
    onehot = ((count, LANES), BF)
    row = ((1, WIDTH), F32)
    vmem = pl.BlockSpec(memory_space=pltpu.VMEM)
    hbm = pl.BlockSpec(memory_space=pltpu.HBM)

    sites = pltpu.VMEM((rounds, rows, cols), jnp.int32)
    packed_tokens = pl.pallas_call(
        pack_kernel,
        out_shape=jax.ShapeDtypeStruct((count + rounds * rows, WIDTH), BF),
        in_specs=[hbm] * 3,
        out_specs=vmem,
        scratch_shapes=[sites, sites, pltpu.SemaphoreType.DMA((3,))],
    )(tokens.reshape(flat), syndrome, check_plan_step)
    row_packed = shifted(packed_tokens, "gx", -1)
    col_packed = shifted(packed_tokens, "gy", -1)
    given = [
        plan_step_embedding, flip_vector.reshape(1, WIDTH), gain_tanner.reshape(1, WIDTH), w_query, w_key_value,
        gain_time.reshape(1, WIDTH), gain_ffn.reshape(1, WIDTH), w_merge, w_temporal, w_temporal_out, w_ffn_up,
        w_ffn_down, cotangent.reshape(flat),
    ]
    outs = [stream, onehot, act, act, wide] + [(value.shape, value.dtype) for value in given]
    (
        x, onehot_own, hidden_one, query, key_value, plan, flip, gain_one, w_query, w_key_value,
        gain_two, gain_three, w_merge, w_temporal, w_temporal_out, w_ffn_up, w_ffn_down, outer,
    ) = pl.pallas_call(
        functools.partial(start_kernel, cols),
        out_shape=[jax.ShapeDtypeStruct(shape, dtype) for shape, dtype in outs],
        in_specs=[vmem] + [hbm] * len(given),
        out_specs=[vmem] * len(outs),
        scratch_shapes=[pltpu.SemaphoreType.DMA((len(given),))],
        compiler_params=pltpu.CompilerParams(vmem_limit_bytes=16 * MIB),
    )(packed_tokens, *given)
    extended = pltpu.VMEM((rounds, 2 * rows, cols, 2 * WIDTH), F32)
    columns = pltpu.VMEM((rounds * rows, cols, 2 * WIDTH), F32)
    half_one = ((2 * (FF // WIDTH) * HALF, WIDTH), BF)
    (
        keep_one, send_one, grad_time, after_tanner, mixed_one, mixed_two, packed, hidden_two,
        row_kv, col_kv, row_x, col_x, row_hidden, col_hidden, row_onehot, col_onehot,
        bent_one, probs_one, bent_two, probs_two, grad_gain_ffn,
    ) = call(
        forward_kernel,
        [half_one, half_one, stream, stream, act, act, ((count, 3 * WIDTH), BF), act,
         wide, wide, stream, stream, act, act, onehot, onehot, lanes, lanes, lanes, lanes, row],
        [place, offsets, x, query, key_value, row_packed, col_packed, plan, flip,
         gain_one, w_key_value, w_merge, gain_two, w_temporal, w_temporal_out, gain_three, w_ffn_up, w_ffn_down,
         outer],
        [extended, columns, pltpu.VMEM((WIDTH, count), BF), pltpu.VMEM((FF, count), BF)],
        smem=2,
        limit=32,
    )
    grad_query, grad_kv, grad_rows, grad_cols, grad_packed, grad_tanner, grad_gain_time = call(
        backward_kernel,
        [act, wide, wide, wide, ((count, 3 * WIDTH), BF), stream, row],
        [offsets, grad_time, after_tanner, packed, query, key_value, row_kv, col_kv,
         bent_one, probs_one, bent_two, probs_two, w_merge, gain_two, w_temporal, w_temporal_out],
        [extended, columns, extended],
        smem=1,
        limit=32,
    )
    half_two = ((16 + 8 * HALF, WIDTH), BF)
    grad_own, lent_rows, lent_cols, keep_two, send_two = call(
        weights_kernel,
        [stream, act, act, half_two, half_two],
        [place, mixed_two, grad_time, hidden_two, grad_packed, mixed_one, grad_tanner, grad_query, w_query, w_key_value,
         gain_one, x, row_x, col_x, hidden_one, row_hidden, col_hidden, onehot_own, row_onehot, col_onehot,
         grad_kv, grad_rows, grad_cols, grad_gain_time, grad_gain_ffn],
        [pltpu.VMEM((3, WIDTH, count), BF), pltpu.VMEM((WIDTH, 3 * count), BF)],
        smem=1,
        limit=32,
    )
    back_rows = shifted(lent_rows, "gx", 1)
    back_cols = shifted(lent_cols, "gy", 1)
    token_grad = call(finish_kernel, [act], [grad_own, back_rows, back_cols])[0]

    many, bits = layout.many, layout.bits
    order_one = list(range(many)) + list(range(many, bits))
    order_two = [0, many] + list(range(1, many)) + list(range(many + 1, bits))
    shard_one = reduce_tree(layout, place, keep_one, send_one, 0, order_one, scale)[0]
    shard_two, plan_grad, grad_flip, sum_gain_tanner, sum_gain_time, sum_gain_ffn = reduce_tree(
        layout, place, keep_two, send_two, 16, order_two, scale
    )
    grad_up, grad_down = gather_tree(
        layout, place, shard_one, order_one, ((1, FF // WIDTH), (FF // WIDTH, 1)), scale
    )
    grad_temporal, grad_temporal_out, grad_merge, grad_w_query, grad_key_value = gather_tree(
        layout, place, shard_two, order_two, ((1, 3), (1, 1), (1, 1), (1, 1), (1, 2)), scale
    )
    return (
        token_grad.reshape(tokens.shape),
        grad_flip.reshape(WIDTH),
        plan_grad,
        sum_gain_tanner.reshape(WIDTH),
        grad_w_query,
        grad_key_value,
        grad_merge,
        sum_gain_time.reshape(WIDTH),
        grad_temporal,
        grad_temporal_out,
        sum_gain_ffn.reshape(WIDTH),
        grad_up,
        grad_down,
    )


def solution(mesh):
    tiled = P(None, "gx", "gy", None)
    sites = P(None, "gx", "gy")
    return jax.shard_map(
        on_device,
        mesh=mesh,
        in_specs=(tiled, sites, sites) + (P(),) * 13 + (tiled,),
        out_specs=(tiled,) + (P(),) * 12,
        check_vma=False,
    )
```

```python
import functools
import math

import jax
import jax.numpy as jnp
from jax import lax
from jax.experimental import pallas as pl
from jax.experimental.pallas import tpu as pltpu
from jax.sharding import PartitionSpec as P

WIDTH = 256
HEADDIM = 32
HEADS = WIDTH // HEADDIM
FF = 1024
PLAN_STEP_COUNT = 8
MONOS = 6
MAXEXP = 8
LANES = 128
HALF = WIDTH // 2

EPS = 1e-05
CAP = 4.0
ALONG_ROWS = (0, 4, 5)
BF = jnp.bfloat16
F32 = jnp.float32
SCORE = 1.0 / math.sqrt(HEADDIM)
GELU_A = math.sqrt(2.0 / math.pi)
GELU_B = 0.044715
MIB = 1 << 20


def dot(a, b, dims=((1,), (0,))):
    return lax.dot_general(a, b, (dims, ((), ())), preferred_element_type=F32)


def dot_nt(a, b):
    return dot(a, b, ((1,), (1,)))


def embed(packed, plan, flip, width):
    count = packed.shape[0]
    lines = count // (width + 1)
    tokens = lines * width
    codes = packed[tokens:, :LANES]
    token = lax.broadcasted_iota(jnp.int32, (tokens, lines), 0)
    line = lax.broadcasted_iota(jnp.int32, (tokens, lines), 1)
    spread = dot(jnp.where(token // width == line, 1.0, 0.0).astype(BF), codes)
    token = lax.broadcasted_iota(jnp.int32, (tokens, LANES), 0)
    lane = lax.broadcasted_iota(jnp.int32, (tokens, LANES), 1)
    picked = jnp.where(token % width == lane, spread, 0.0).astype(BF)
    code = dot(picked, jnp.ones((LANES, LANES), BF))
    flipped = code >= PLAN_STEP_COUNT
    step = jnp.where(flipped, code - PLAN_STEP_COUNT, code)
    slot = lane % 16
    chosen = (slot.astype(F32) == step) | ((slot == PLAN_STEP_COUNT) & flipped)
    onehot = jnp.where(chosen & (lane < 48), 1.0, 0.0).astype(BF)
    row = lax.broadcasted_iota(jnp.int32, (8, WIDTH), 0)
    table = jnp.concatenate([plan, jnp.where(row == 0, flip, 0.0)], axis=0)
    high = table.astype(BF)
    rest = table - high.astype(F32)
    middle = rest.astype(BF)
    low = (rest - middle.astype(F32)).astype(BF)
    empty = jnp.zeros((LANES - 48, WIDTH), BF)
    vectors = dot(onehot, jnp.concatenate([high, middle, low, empty], axis=0))
    return packed[:tokens].astype(F32) + vectors, onehot


def inverse_rms(stream):
    return lax.rsqrt(jnp.mean(stream * stream, axis=-1, keepdims=True) + EPS)


def norm_back(stream, gain, grad):
    inverse = inverse_rms(stream)
    normed = stream * inverse
    scaled = grad * gain
    mean = jnp.mean(scaled * normed, axis=-1, keepdims=True)
    return inverse * (scaled - normed * mean), jnp.sum(grad * normed, axis=0, keepdims=True)


def gather_heads(slot, period):
    feature = lax.broadcasted_iota(jnp.int32, (WIDTH, LANES), 0) // HEADDIM
    lane = lax.broadcasted_iota(jnp.int32, (WIDTH, LANES), 1) % period
    return jnp.where(lane - feature == slot * HEADS, 1.0, 0.0).astype(BF)


def spread_heads(slot, period):
    lane = lax.broadcasted_iota(jnp.int32, (LANES, WIDTH), 0)
    feature = lax.broadcasted_iota(jnp.int32, (LANES, WIDTH), 1) // HEADDIM
    at = (lane < 2 * period) & (lane % period - feature == slot * HEADS)
    return jnp.where(at, 1.0, 0.0).astype(BF)


def two_parts(value, period):
    lane = lax.broadcasted_iota(jnp.int32, value.shape, 1)
    high = value.astype(BF).astype(F32)
    return jnp.where(lane < period, high, value - high).astype(BF)


def slot_total(value, period):
    shift = HEADS
    while shift < period:
        value = value + pltpu.roll(value, shift, 1)
        shift *= 2
    return value


def softmax_parts(scores, valid, period):
    bent = jnp.tanh(scores * (SCORE / CAP))
    weights = jnp.where(valid, jnp.exp(CAP * bent), 0.0)
    return bent, weights / slot_total(weights, period)


def softmax_back(bent, probs, grad, period):
    inner = probs * grad
    return (inner - probs * slot_total(inner, period)) * (1.0 - bent * bent) * SCORE


def tanner_valid(tokens):
    lane = lax.broadcasted_iota(jnp.int32, (tokens, LANES), 1)
    return lane % 64 < HEADS * (MONOS + 1)


def time_valid(tokens, rounds):
    lane = lax.broadcasted_iota(jnp.int32, (tokens, LANES), 1)
    row = lax.broadcasted_iota(jnp.int32, (tokens, LANES), 0)
    return (lane % 32) // HEADS <= row // (tokens // rounds)


def offset_of(offsets, index):
    return offsets[index, 0] if index in ALONG_ROWS else offsets[index, 1]


def neighbour(number, offsets, extended, columns):
    rounds, twice, width, features = extended.shape
    rows = twice // 2
    tokens = rounds * rows * width
    if number == 0:
        return extended[:, :rows].reshape(tokens, features)
    by = offset_of(offsets, number - 1)
    if number - 1 in ALONG_ROWS:
        return extended[:, pl.ds(by, rows)].reshape(tokens, features)
    own = extended[:, :rows].reshape(rounds * rows, width, features)
    place = lax.broadcasted_iota(jnp.int32, own.shape, 1)
    joined = jnp.where(place >= by, own, columns[...])
    return pltpu.roll(joined, width - by, 1).reshape(tokens, features)


def pack_kernel(tokens, syndrome, step, out, flips, steps, done):
    count = tokens.shape[0]
    rounds, rows, width = syndrome.shape
    moves = [
        pltpu.make_async_copy(tokens, out.at[pl.ds(0, count)], done.at[0]),
        pltpu.make_async_copy(syndrome, flips, done.at[1]),
        pltpu.make_async_copy(step, steps, done.at[2]),
    ]
    for move in moves:
        move.start()
    out[count:, :] = jnp.zeros((rounds * rows, WIDTH), BF)
    moves[1].wait()
    moves[2].wait()
    code = flips[...] * PLAN_STEP_COUNT + steps[...]
    out[count:, :width] = code.reshape(rounds * rows, width).astype(F32).astype(BF)
    moves[0].wait()


def start_kernel(width, packed, plan, flip, gain, w_query, w_key_value, x_out, onehot_out, hidden_out, query_out, kv_out):
    x, onehot = embed(packed[...], plan[...], flip[...], width)
    hidden = (x * inverse_rms(x) * gain[...]).astype(BF)
    x_out[...] = x
    onehot_out[...] = onehot
    hidden_out[...] = hidden
    query_out[...] = dot(hidden, w_query[...]).astype(BF)
    kv_out[...] = dot(hidden, w_key_value[...]).astype(BF)


def forward_kernel(
    offsets, x_in, query_in, kv_in, row_packed, col_packed, plan, flip,
    gain_tanner, w_key_value, w_merge, gain_time, w_temporal, w_temporal_out, gain_ffn, w_up, w_down, cotangent,
    keep, send, grad_time_out, tanner_out, mixed_one_out, mixed_two_out, packed_out, hidden_two_out,
    row_kv_out, col_kv_out, row_x_out, col_x_out, row_hidden_out, col_hidden_out, row_onehot_out, col_onehot_out,
    bent_one_out, probs_one_out, bent_two_out, probs_two_out, grad_gain_out,
    extended, columns, transposed, transposed_act,
):
    rounds, twice, width, features = extended.shape
    rows = twice // 2
    tokens = x_in.shape[0]
    core = my_bit(0)
    borrowed = []
    for other, x_out, hidden_out, onehot_out, kv_out in (
        (row_packed, row_x_out, row_hidden_out, row_onehot_out, row_kv_out),
        (col_packed, col_x_out, col_hidden_out, col_onehot_out, col_kv_out),
    ):
        x, onehot = embed(other[...], plan[...], flip[...], width)
        hidden = (x * inverse_rms(x) * gain_tanner[...]).astype(BF)
        kv = dot(hidden, w_key_value[...]).astype(BF)
        x_out[...] = x
        onehot_out[...] = onehot
        hidden_out[...] = hidden
        kv_out[...] = kv
        borrowed.append(kv.astype(F32))
    extended[:, :rows] = kv_in[...].astype(F32).reshape(rounds, rows, width, features)
    extended[:, rows:] = borrowed[0].reshape(rounds, rows, width, features)
    columns[...] = borrowed[1].reshape(rounds * rows, width, features)
    query = query_in[...].astype(F32)
    scores = None
    for number in range(MONOS + 1):
        keys = neighbour(number, offsets, extended, columns)[:, :WIDTH]
        part = dot((query * keys).astype(BF), gather_heads(number, 64))
        scores = part if scores is None else scores + part
    bent, probs = softmax_parts(scores, tanner_valid(tokens), 64)
    bent_one_out[...] = bent
    probs_one_out[...] = probs
    parts = two_parts(probs, 64)
    mixed = None
    for number in range(MONOS + 1):
        values = neighbour(number, offsets, extended, columns)[:, WIDTH:]
        part = dot(parts, spread_heads(number, 64)) * values
        mixed = part if mixed is None else mixed + part
    mixed_one = mixed.astype(BF)
    mixed_one_out[...] = mixed_one
    after_tanner = x_in[...] + dot(mixed_one, w_merge[...])
    tanner_out[...] = after_tanner

    hidden_two = (after_tanner * inverse_rms(after_tanner) * gain_time[...]).astype(BF)
    hidden_two_out[...] = hidden_two
    packed_low = dot(hidden_two, w_temporal[...]).astype(BF)
    packed_out[...] = packed_low
    packed = packed_low.astype(F32).reshape(rounds, tokens // rounds, 3 * WIDTH)
    sites = tokens // rounds
    scores = None
    for earlier in range(rounds):
        product = packed[earlier:, :, :WIDTH] * packed[earlier][None, :, WIDTH : 2 * WIDTH]
        part = dot(product.reshape(-1, WIDTH).astype(BF), gather_heads(earlier, 32))
        if earlier:
            part = jnp.concatenate([jnp.zeros((earlier * sites, LANES), F32), part], axis=0)
        scores = part if scores is None else scores + part
    bent, probs = softmax_parts(scores, time_valid(tokens, rounds), 32)
    bent_two_out[...] = bent
    probs_two_out[...] = probs
    parts = two_parts(probs, 32)
    mixed = None
    for earlier in range(rounds):
        weight = dot(parts[earlier * sites :], spread_heads(earlier, 32)).reshape(rounds - earlier, sites, WIDTH)
        part = (weight * packed[earlier][None, :, 2 * WIDTH :]).reshape(-1, WIDTH)
        if earlier:
            part = jnp.concatenate([jnp.zeros((earlier * sites, WIDTH), F32), part], axis=0)
        mixed = part if mixed is None else mixed + part
    mixed_two = mixed.astype(BF)
    mixed_two_out[...] = mixed_two
    after_time = after_tanner + dot(mixed_two, w_temporal_out[...])

    hidden = (after_time * inverse_rms(after_time) * gain_ffn[...]).astype(BF)
    outer = cotangent[...]
    transposed[...] = hidden.T
    grad_three = None
    befores = []
    for block in range(FF // WIDTH):
        cols = slice(block * WIDTH, (block + 1) * WIDTH)
        before = dot(hidden, w_up[:, cols])
        square = before * before
        bend = jnp.tanh(GELU_A * before * (1.0 + GELU_B * square))
        upper = 0.5 * (1.0 + bend)
        activated = (before * upper).astype(BF)
        slope = upper + 0.5 * before * (1.0 - bend * bend) * (GELU_A * (1.0 + 3.0 * GELU_B * square))
        grad_before = (dot_nt(outer, w_down[cols, :]) * slope).astype(BF)
        befores.append(grad_before)
        part = dot_nt(grad_before, w_up[:, cols])
        grad_three = part if grad_three is None else grad_three + part
        transposed_act[cols, :] = activated.T
    for ref, which in ((keep, core), (send, 1 - core)):
        half = pl.ds(pl.multiple_of(which * HALF, HALF), HALF)
        lead = transposed[half, :]
        for block in range(FF // WIDTH):
            ref[block * HALF : (block + 1) * HALF, :] = dot(lead, befores[block]).astype(BF)
            part = transposed_act[pl.ds(pl.multiple_of(block * WIDTH + which * HALF, HALF), HALF), :]
            base = (FF // WIDTH + block) * HALF
            ref[base : base + HALF, :] = dot(part, outer).astype(BF)
    grad_norm, grad_gain = norm_back(after_time, gain_ffn[...], grad_three)
    grad_time_out[...] = outer.astype(F32) + grad_norm
    grad_gain_out[...] = grad_gain


def backward_kernel(
    offsets, grad_time_in, tanner_in, packed_in, query_in, kv_in, row_kv, col_kv,
    bent_one, probs_one, bent_two, probs_two, w_merge, gain_time, w_temporal, w_temporal_out,
    grad_query_out, grad_kv_out, grad_rows_out, grad_cols_out, grad_packed_out, grad_tanner_out, grad_gain_out,
    extended, columns, grad_extended,
):
    rounds, twice, width, features = extended.shape
    rows = twice // 2
    tokens = grad_time_in.shape[0]
    sites = tokens // rounds
    grad_time = grad_time_in[...]
    grad_mixed = dot_nt(grad_time.astype(BF), w_temporal_out[...]).reshape(rounds, sites, WIDTH)
    packed = packed_in[...].astype(F32).reshape(rounds, sites, 3 * WIDTH)
    grad_probs = None
    for earlier in range(rounds):
        product = grad_mixed[earlier:] * packed[earlier][None, :, 2 * WIDTH :]
        part = dot(product.reshape(-1, WIDTH).astype(BF), gather_heads(earlier, 32))
        if earlier:
            part = jnp.concatenate([jnp.zeros((earlier * sites, LANES), F32), part], axis=0)
        grad_probs = part if grad_probs is None else grad_probs + part
    probs = probs_two[...]
    prob_parts = two_parts(probs, 32)
    score_parts = two_parts(softmax_back(bent_two[...], probs, grad_probs, 32), 32)
    grad_queries = None
    grad_keys = []
    grad_values = []
    for earlier in range(rounds):
        spread = spread_heads(earlier, 32)
        shape = (rounds - earlier, sites, WIDTH)
        weight = dot(prob_parts[earlier * sites :], spread).reshape(shape)
        slope = dot(score_parts[earlier * sites :], spread).reshape(shape)
        grad_values.append(jnp.sum(weight * grad_mixed[earlier:], axis=0))
        grad_keys.append(jnp.sum(slope * packed[earlier:, :, :WIDTH], axis=0))
        part = (slope * packed[earlier][None, :, WIDTH : 2 * WIDTH]).reshape(-1, WIDTH)
        if earlier:
            part = jnp.concatenate([jnp.zeros((earlier * sites, WIDTH), F32), part], axis=0)
        grad_queries = part if grad_queries is None else grad_queries + part
    grad_packed = jnp.concatenate(
        [grad_queries, jnp.concatenate(grad_keys, axis=0), jnp.concatenate(grad_values, axis=0)], axis=1
    ).astype(BF)
    grad_packed_out[...] = grad_packed
    grad_two = dot_nt(grad_packed, w_temporal[...])
    grad_norm, grad_gain = norm_back(tanner_in[...], gain_time[...], grad_two)
    grad_gain_out[...] = grad_gain
    grad_tanner = grad_time + grad_norm
    grad_tanner_out[...] = grad_tanner

    grad_mixed = dot_nt(grad_tanner.astype(BF), w_merge[...])
    extended[:, :rows] = kv_in[...].astype(F32).reshape(rounds, rows, width, features)
    extended[:, rows:] = row_kv[...].astype(F32).reshape(rounds, rows, width, features)
    columns[...] = col_kv[...].astype(F32).reshape(rounds * rows, width, features)
    grad_probs = None
    for number in range(MONOS + 1):
        values = neighbour(number, offsets, extended, columns)[:, WIDTH:]
        part = dot((grad_mixed * values).astype(BF), gather_heads(number, 64))
        grad_probs = part if grad_probs is None else grad_probs + part
    probs = probs_one[...]
    prob_parts = two_parts(probs, 64)
    score_parts = two_parts(softmax_back(bent_one[...], probs, grad_probs, 64), 64)
    query = query_in[...].astype(F32)
    grad_query = None
    grad_cols = None
    for number in (0,) + tuple(i + 1 for i in range(MONOS)):
        spread = spread_heads(number, 64)
        slope = dot(score_parts, spread)
        weight = dot(prob_parts, spread)
        keys = neighbour(number, offsets, extended, columns)[:, :WIDTH]
        part = slope * keys
        grad_query = part if grad_query is None else grad_query + part
        grad_kv = jnp.concatenate([slope * query, weight * grad_mixed], axis=1)
        if number == 0:
            grad_extended[:, :rows] = grad_kv.reshape(rounds, rows, width, features)
            grad_extended[:, rows:] = jnp.zeros((rounds, rows, width, features), F32)
            continue
        by = offset_of(offsets, number - 1)
        if number - 1 in ALONG_ROWS:
            grad_extended[:, pl.ds(by, rows)] += grad_kv.reshape(rounds, rows, width, features)
            continue
        moved = pltpu.roll(grad_kv.reshape(rounds * rows, width, features), by % width, 1)
        place = lax.broadcasted_iota(jnp.int32, moved.shape, 1)
        own = jnp.where(place >= by, moved, 0.0)
        grad_extended[:, :rows] += own.reshape(rounds, rows, width, features)
        grad_cols = moved - own if grad_cols is None else grad_cols + (moved - own)
    grad_query_out[...] = grad_query.astype(BF)
    grad_kv_out[...] = grad_extended[:, :rows].reshape(tokens, features).astype(BF)
    grad_rows_out[...] = grad_extended[:, rows:].reshape(tokens, features).astype(BF)
    grad_cols_out[...] = grad_cols.reshape(tokens, features).astype(BF)


def weights_kernel(
    mixed_two, grad_time, hidden_two, grad_packed, mixed_one, grad_tanner, grad_query, w_query, w_key_value, gain,
    x_own, x_row, x_col, hidden_own, hidden_row, hidden_col, onehot_own, onehot_row, onehot_col,
    grad_own, grad_row, grad_col, grad_gain_time, grad_gain_ffn,
    grad_out, row_out, col_out, keep, send, transposed, transposed_own,
):
    core = my_bit(0)
    tokens = x_own.shape[0]
    transposed[0] = hidden_two[...].T
    transposed[1] = mixed_two[...].T
    transposed[2] = mixed_one[...].T
    small = None
    grad_gain = None
    for number, (x, hidden, onehot, grad_kv, out) in enumerate((
        (x_own, hidden_own, onehot_own, grad_own, grad_out),
        (x_row, hidden_row, onehot_row, grad_row, row_out),
        (x_col, hidden_col, onehot_col, grad_col, col_out),
    )):
        transposed_own[:, number * tokens : (number + 1) * tokens] = hidden[...].T
        grad_one = dot_nt(grad_kv[...], w_key_value[...])
        if number == 0:
            grad_one = grad_one + dot_nt(grad_query[...], w_query[...])
        grad, part = norm_back(x[...], gain[...], grad_one)
        grad_gain = part if grad_gain is None else grad_gain + part
        if number == 0:
            grad = grad + grad_tanner[...]
        out[...] = grad.astype(out.dtype)
        high = grad.astype(BF)
        low = (grad - high.astype(F32)).astype(BF)
        part = dot(onehot[...], jnp.concatenate([high, low], axis=1), ((0,), (0,)))[:16]
        part = part[:, :WIDTH] + part[:, WIDTH:]
        small = part if small is None else small + part
    row = lax.broadcasted_iota(jnp.int32, small.shape, 0)
    small = jnp.where(row == 9, grad_gain, small)
    small = jnp.where(row == 10, grad_gain_time[...], small)
    small = jnp.where(row == 11, grad_gain_ffn[...], small).astype(BF)
    grad_time_low = grad_time[...].astype(BF)
    grad_tanner_low = grad_tanner[...].astype(BF)
    grad_all = jnp.concatenate([grad_own[...], grad_row[...], grad_col[...]], axis=0)
    for ref, which in ((keep, core), (send, 1 - core)):
        half = pl.ds(pl.multiple_of(which * HALF, HALF), HALF)
        products = []
        for block in range(3):
            cols = slice(block * WIDTH, (block + 1) * WIDTH)
            products.append(dot(transposed[0, half, :], grad_packed[:, cols]))
        products.append(dot(transposed[1, half, :], grad_time_low))
        products.append(dot(transposed[2, half, :], grad_tanner_low))
        products.append(dot(transposed_own[half, :tokens], grad_query[...]))
        for block in range(2):
            cols = slice(block * WIDTH, (block + 1) * WIDTH)
            products.append(dot(transposed_own[half, :], grad_all[:, cols]))
        ref[:16, :] = small
        for block, product in enumerate(products):
            ref[16 + block * HALF : 16 + (block + 1) * HALF, :] = product.astype(BF)


def finish_kernel(grad, row, col, out):
    out[...] = (grad[...] + row[...].astype(F32) + col[...].astype(F32)).astype(BF)


def my_bit(bit):
    many = lax.axis_size("gy").bit_length() - 1
    if bit < many:
        return (lax.axis_index("gy") >> bit) & 1
    return (lax.axis_index("gx") >> (bit - many)) & 1


def split_kernel(extra, bit, kept, received, keep, send, total):
    mine = my_bit(bit)
    value = kept[...].astype(F32) + received[...].astype(F32)
    total[...] = value[extra:]
    rows = keep.shape[0] - extra
    for ref, which in ((keep, mine), (send, 1 - mine)):
        if extra:
            ref[:extra, :] = value[:extra].astype(BF)
        ref[extra:, :] = total[pl.ds(pl.multiple_of(which * rows, rows), rows), :].astype(BF)


def end_kernel(extra, scale, kept, received, out, *small):
    value = kept[...].astype(F32) + received[...].astype(F32)
    out[...] = value[extra:].astype(BF)
    if extra:
        value = value[:extra] * scale
        small[0][...] = value[:8]
        for number in range(4):
            small[1 + number][...] = value[8 + number : 9 + number]


def join_kernel(bit, own, received, out):
    mine = my_bit(bit)
    out[mine] = own[...]
    out[1 - mine] = received[...]


def unpack_kernel(blocks, scale, own, other, *refs):
    outs, halves = refs[:-1], refs[-1]
    core = my_bit(0)
    halves[core] = own[...].astype(F32) * scale
    halves[1 - core] = other[...].astype(F32) * scale
    block = 0
    for out, (down, across) in zip(outs, blocks):
        for index in range(down * across):
            for half in range(2):
                top = (index if down > 1 else 0) * WIDTH + half * HALF
                left = (index if across > 1 else 0) * WIDTH
                out[top : top + HALF, left : left + WIDTH] = halves[half, block * HALF : (block + 1) * HALF, :]
            block += 1


def estimate(work):
    return pl.CostEstimate(flops=int(work * 1.1e9), transcendentals=0, bytes_accessed=0)


def call(kernel, outs, args, scratch=(), smem=0, limit=16, work=None):
    vmem = pl.BlockSpec(memory_space=pltpu.VMEM)
    return pl.pallas_call(
        kernel,
        out_shape=[jax.ShapeDtypeStruct(shape, dtype) for shape, dtype in outs],
        in_specs=[pl.BlockSpec(memory_space=pltpu.SMEM)] * smem + [vmem] * (len(args) - smem),
        out_specs=[vmem] * len(outs),
        scratch_shapes=list(scratch),
        compiler_params=pltpu.CompilerParams(vmem_limit_bytes=limit * MIB),
        cost_estimate=None if work is None else estimate(work),
    )(*args)


def shifted(x, axis, by):
    count = lax.axis_size(axis)
    return lax.ppermute(x, axis, [(i, (i + by) % count) for i in range(count)])


class Layout:
    def __init__(self):
        self.nx = lax.axis_size("gx")
        self.ny = lax.axis_size("gy")
        self.many = self.ny.bit_length() - 1
        self.bits = self.many + self.nx.bit_length() - 1
        assert 1 << self.bits == self.nx * self.ny

    def swap(self, x, bit):
        flip = 1 << bit if bit < self.many else self.ny << (bit - self.many)
        return lax.ppermute(x, ("gx", "gy"), [(i, i ^ flip) for i in range(self.nx * self.ny)])


def reduce_tree(layout, keep, send, extra, order, scale, beside=()):
    for stage, bit in enumerate(order):
        received = layout.swap(send, bit)
        if stage == 2 and beside:
            received, *beside = lax.optimization_barrier((received, *beside))
        rows = keep.shape[0] - extra
        if stage + 1 < len(order):
            half = ((rows // 2 + extra, WIDTH), BF)
            keep, send = call(
                functools.partial(split_kernel, extra, order[stage + 1]),
                [half, half],
                [keep, received],
                [pltpu.VMEM((rows, WIDTH), F32)],
            )
    small = [((8, WIDTH), F32)] + [((1, WIDTH), F32)] * 4 if extra else []
    outs = call(functools.partial(end_kernel, extra, scale), [((rows, WIDTH), BF)] + small, [keep, received])
    return (*outs, *beside)


def gather_tree(layout, own, order, blocks, scale):
    for bit in order[:0:-1]:
        received = layout.swap(own, bit)
        rows = own.shape[0]
        own = call(
            functools.partial(join_kernel, bit), [((2, rows, WIDTH), BF)], [own, received]
        )[0].reshape(2 * rows, WIDTH)
    other = layout.swap(own, order[0])
    return call(
        functools.partial(unpack_kernel, blocks, scale),
        [((down * WIDTH, across * WIDTH), F32) for down, across in blocks],
        [own, other],
        [pltpu.VMEM((2,) + own.shape, F32)],

    )


def on_device(
    tokens,
    syndrome,
    check_plan_step,
    offsets,
    flip_vector,
    plan_step_embedding,
    gain_tanner,
    w_query,
    w_key_value,
    w_merge,
    gain_time,
    w_temporal,
    w_temporal_out,
    gain_ffn,
    w_ffn_up,
    w_ffn_down,
    cotangent,
):
    layout = Layout()
    rounds, rows, cols = tokens.shape[:3]
    count = rounds * rows * cols
    scale = 1.0 / math.sqrt(count * layout.nx * layout.ny)
    flat = (count, WIDTH)
    act = (flat, BF)
    stream = (flat, F32)
    wide = ((count, 2 * WIDTH), BF)
    lanes = ((count, LANES), F32)
    onehot = ((count, LANES), BF)
    row = ((1, WIDTH), F32)
    hbm = pl.BlockSpec(memory_space=pltpu.HBM)

    sites = pltpu.VMEM((rounds, rows, cols), jnp.int32)
    packed_tokens = pl.pallas_call(
        pack_kernel,
        out_shape=jax.ShapeDtypeStruct((count + rounds * rows, WIDTH), BF),
        in_specs=[hbm] * 3,
        out_specs=pl.BlockSpec(memory_space=pltpu.VMEM),
        scratch_shapes=[sites, sites, pltpu.SemaphoreType.DMA((3,))],
        cost_estimate=estimate(12),
    )(tokens.reshape(flat), syndrome, check_plan_step)
    row_packed = shifted(packed_tokens, "gx", -1)
    col_packed = shifted(packed_tokens, "gy", -1)
    plan = plan_step_embedding
    flip = flip_vector.reshape(1, WIDTH)
    gain_one = gain_tanner.reshape(1, WIDTH)
    gain_two = gain_time.reshape(1, WIDTH)
    gain_three = gain_ffn.reshape(1, WIDTH)
    outer = cotangent.reshape(flat)
    x, onehot_own, hidden_one, query, key_value = call(
        functools.partial(start_kernel, cols),
        [stream, onehot, act, act, wide],
        [packed_tokens, plan, flip, gain_one, w_query, w_key_value],

    )
    extended = pltpu.VMEM((rounds, 2 * rows, cols, 2 * WIDTH), F32)
    columns = pltpu.VMEM((rounds * rows, cols, 2 * WIDTH), F32)
    half_one = ((2 * (FF // WIDTH) * HALF, WIDTH), BF)
    (
        keep_one, send_one, grad_time, after_tanner, mixed_one, mixed_two, packed, hidden_two,
        row_kv, col_kv, row_x, col_x, row_hidden, col_hidden, row_onehot, col_onehot,
        bent_one, probs_one, bent_two, probs_two, grad_gain_ffn,
    ) = call(
        forward_kernel,
        [half_one, half_one, stream, stream, act, act, ((count, 3 * WIDTH), BF), act,
         wide, wide, stream, stream, act, act, onehot, onehot, lanes, lanes, lanes, lanes, row],
        [offsets, x, query, key_value, row_packed, col_packed, plan, flip,
         gain_one, w_key_value, w_merge, gain_two, w_temporal, w_temporal_out, gain_three, w_ffn_up, w_ffn_down,
         outer],
        [extended, columns, pltpu.VMEM((WIDTH, count), BF), pltpu.VMEM((FF, count), BF)],
        smem=1,
        limit=32,

    )
    grad_query, grad_kv, grad_rows, grad_cols, grad_packed, grad_tanner, grad_gain_time = call(
        backward_kernel,
        [act, wide, wide, wide, ((count, 3 * WIDTH), BF), stream, row],
        [offsets, grad_time, after_tanner, packed, query, key_value, row_kv, col_kv,
         bent_one, probs_one, bent_two, probs_two, w_merge, gain_two, w_temporal, w_temporal_out],
        [extended, columns, extended],
        smem=1,
        limit=32,
        work=None,
    )
    half_two = ((16 + 8 * HALF, WIDTH), BF)
    grad_own, lent_rows, lent_cols, keep_two, send_two = call(
        weights_kernel,
        [stream, act, act, half_two, half_two],
        [mixed_two, grad_time, hidden_two, grad_packed, mixed_one, grad_tanner, grad_query, w_query, w_key_value,
         gain_one, x, row_x, col_x, hidden_one, row_hidden, col_hidden, onehot_own, row_onehot, col_onehot,
         grad_kv, grad_rows, grad_cols, grad_gain_time, grad_gain_ffn],
        [pltpu.VMEM((3, WIDTH, count), BF), pltpu.VMEM((WIDTH, 3 * count), BF)],
        limit=32,
        work=None,
    )
    back_rows = shifted(lent_rows, "gx", 1)
    back_cols = shifted(lent_cols, "gy", 1)
    many, bits = layout.many, layout.bits
    order_one = list(range(many)) + list(range(many, bits))
    order_two = [0, many] + list(range(1, many)) + list(range(many + 1, bits))
    shard_one, back_rows, back_cols = reduce_tree(
        layout, keep_one, send_one, 0, order_one, scale, (back_rows, back_cols)
    )
    token_grad = call(finish_kernel, [act], [grad_own, back_rows, back_cols])[0]
    shard_two, plan_grad, grad_flip, sum_gain_tanner, sum_gain_time, sum_gain_ffn = reduce_tree(
        layout, keep_two, send_two, 16, order_two, scale
    )
    grad_up, grad_down = gather_tree(
        layout, shard_one, order_one, ((1, FF // WIDTH), (FF // WIDTH, 1)), scale
    )
    grad_temporal, grad_temporal_out, grad_merge, grad_w_query, grad_key_value = gather_tree(
        layout, shard_two, order_two, ((1, 3), (1, 1), (1, 1), (1, 1), (1, 2)), scale
    )
    return (
        token_grad.reshape(tokens.shape),
        grad_flip.reshape(WIDTH),
        plan_grad,
        sum_gain_tanner.reshape(WIDTH),
        grad_w_query,
        grad_key_value,
        grad_merge,
        sum_gain_time.reshape(WIDTH),
        grad_temporal,
        grad_temporal_out,
        sum_gain_ffn.reshape(WIDTH),
        grad_up,
        grad_down,
    )


def solution(mesh):
    tiled = P(None, "gx", "gy", None)
    sites = P(None, "gx", "gy")
    return jax.shard_map(
        on_device,
        mesh=mesh,
        in_specs=(tiled, sites, sites) + (P(),) * 13 + (tiled,),
        out_specs=(tiled,) + (P(),) * 12,
        check_vma=False,
    )
```

```python
import functools
import math

import jax
import jax.numpy as jnp
from jax import lax
from jax.experimental import pallas as pl
from jax.experimental.pallas import tpu as pltpu
from jax.sharding import PartitionSpec as P

WIDTH = 256
HEADDIM = 32
HEADS = WIDTH // HEADDIM
FF = 1024
PLAN_STEP_COUNT = 8
MONOS = 6
MAXEXP = 8
LANES = 128
HALF = WIDTH // 2

EPS = 1e-05
CAP = 4.0
ALONG_ROWS = (0, 4, 5)
BF = jnp.bfloat16
F32 = jnp.float32
SCORE = 1.0 / math.sqrt(HEADDIM)
GELU_A = math.sqrt(2.0 / math.pi)
GELU_B = 0.044715
MIB = 1 << 20


def dot(a, b, dims=((1,), (0,))):
    return lax.dot_general(a, b, (dims, ((), ())), preferred_element_type=F32)


def dot_nt(a, b):
    return dot(a, b, ((1,), (1,)))


def embed(packed, plan, flip, width):
    count = packed.shape[0]
    lines = count // (width + 1)
    tokens = lines * width
    codes = packed[tokens:, :LANES]
    token = lax.broadcasted_iota(jnp.int32, (tokens, lines), 0)
    line = lax.broadcasted_iota(jnp.int32, (tokens, lines), 1)
    spread = dot(jnp.where(token // width == line, 1.0, 0.0).astype(BF), codes)
    token = lax.broadcasted_iota(jnp.int32, (tokens, LANES), 0)
    lane = lax.broadcasted_iota(jnp.int32, (tokens, LANES), 1)
    picked = jnp.where(token % width == lane, spread, 0.0).astype(BF)
    code = dot(picked, jnp.ones((LANES, LANES), BF))
    flipped = code >= PLAN_STEP_COUNT
    step = jnp.where(flipped, code - PLAN_STEP_COUNT, code)
    slot = lane % 16
    chosen = (slot.astype(F32) == step) | ((slot == PLAN_STEP_COUNT) & flipped)
    onehot = jnp.where(chosen & (lane < 48), 1.0, 0.0).astype(BF)
    row = lax.broadcasted_iota(jnp.int32, (8, WIDTH), 0)
    table = jnp.concatenate([plan, jnp.where(row == 0, flip, 0.0)], axis=0)
    high = table.astype(BF)
    rest = table - high.astype(F32)
    middle = rest.astype(BF)
    low = (rest - middle.astype(F32)).astype(BF)
    empty = jnp.zeros((LANES - 48, WIDTH), BF)
    vectors = dot(onehot, jnp.concatenate([high, middle, low, empty], axis=0))
    return packed[:tokens].astype(F32) + vectors, onehot


def inverse_rms(stream):
    return lax.rsqrt(jnp.mean(stream * stream, axis=-1, keepdims=True) + EPS)


def norm_back(stream, gain, grad):
    inverse = inverse_rms(stream)
    normed = stream * inverse
    scaled = grad * gain
    mean = jnp.mean(scaled * normed, axis=-1, keepdims=True)
    return inverse * (scaled - normed * mean), jnp.sum(grad * normed, axis=0, keepdims=True)


def gather_heads(slot, period):
    feature = lax.broadcasted_iota(jnp.int32, (WIDTH, LANES), 0) // HEADDIM
    lane = lax.broadcasted_iota(jnp.int32, (WIDTH, LANES), 1) % period
    return jnp.where(lane - feature == slot * HEADS, 1.0, 0.0).astype(BF)


def spread_heads(slot, period):
    lane = lax.broadcasted_iota(jnp.int32, (LANES, WIDTH), 0)
    feature = lax.broadcasted_iota(jnp.int32, (LANES, WIDTH), 1) // HEADDIM
    at = (lane < 2 * period) & (lane % period - feature == slot * HEADS)
    return jnp.where(at, 1.0, 0.0).astype(BF)


def two_parts(value, period):
    lane = lax.broadcasted_iota(jnp.int32, value.shape, 1)
    high = value.astype(BF).astype(F32)
    return jnp.where(lane < period, high, value - high).astype(BF)


def slot_total(value, period):
    shift = HEADS
    while shift < period:
        value = value + pltpu.roll(value, shift, 1)
        shift *= 2
    return value


def softmax_parts(scores, valid, period):
    bent = jnp.tanh(scores * (SCORE / CAP))
    weights = jnp.where(valid, jnp.exp(CAP * bent), 0.0)
    return bent, weights / slot_total(weights, period)


def softmax_back(bent, probs, grad, period):
    inner = probs * grad
    return (inner - probs * slot_total(inner, period)) * (1.0 - bent * bent) * SCORE


def tanner_valid(tokens):
    lane = lax.broadcasted_iota(jnp.int32, (tokens, LANES), 1)
    return lane % 64 < HEADS * (MONOS + 1)


def time_valid(tokens, rounds):
    lane = lax.broadcasted_iota(jnp.int32, (tokens, LANES), 1)
    row = lax.broadcasted_iota(jnp.int32, (tokens, LANES), 0)
    return (lane % 32) // HEADS <= row // (tokens // rounds)


def offset_of(offsets, index):
    return offsets[index, 0] if index in ALONG_ROWS else offsets[index, 1]


def neighbour(number, offsets, extended, columns):
    rounds, twice, width, features = extended.shape
    rows = twice // 2
    tokens = rounds * rows * width
    if number == 0:
        return extended[:, :rows].reshape(tokens, features)
    by = offset_of(offsets, number - 1)
    if number - 1 in ALONG_ROWS:
        return extended[:, pl.ds(by, rows)].reshape(tokens, features)
    own = extended[:, :rows].reshape(rounds * rows, width, features)
    place = lax.broadcasted_iota(jnp.int32, own.shape, 1)
    joined = jnp.where(place >= by, own, columns[...])
    return pltpu.roll(joined, width - by, 1).reshape(tokens, features)


def pack_kernel(tokens, syndrome, step, out, flips, steps, done):
    count = tokens.shape[0]
    rounds, rows, width = syndrome.shape
    moves = [
        pltpu.make_async_copy(tokens, out.at[pl.ds(0, count)], done.at[0]),
        pltpu.make_async_copy(syndrome, flips, done.at[1]),
        pltpu.make_async_copy(step, steps, done.at[2]),
    ]
    for move in moves:
        move.start()
    out[count:, :] = jnp.zeros((rounds * rows, WIDTH), BF)
    moves[1].wait()
    moves[2].wait()
    code = flips[...] * PLAN_STEP_COUNT + steps[...]
    out[count:, :width] = code.reshape(rounds * rows, width).astype(F32).astype(BF)
    moves[0].wait()


def start_kernel(width, packed, plan, flip, gain, w_query, w_key_value, x_out, onehot_out, hidden_out, query_out, kv_out):
    x, onehot = embed(packed[...], plan[...], flip[...], width)
    hidden = (x * inverse_rms(x) * gain[...]).astype(BF)
    x_out[...] = x
    onehot_out[...] = onehot
    hidden_out[...] = hidden
    query_out[...] = dot(hidden, w_query[...]).astype(BF)
    kv_out[...] = dot(hidden, w_key_value[...]).astype(BF)


def forward_kernel(
    offsets, x_in, query_in, kv_in, col_packed, row_packed, plan, flip,
    gain_tanner, w_key_value, w_merge, gain_time, w_temporal, w_temporal_out, gain_ffn, w_up, w_down, cotangent,
    keep, send, grad_time_out, tanner_out, mixed_one_out, mixed_two_out, packed_out, hidden_two_out,
    row_kv_out, col_kv_out, row_x_out, col_x_out, row_hidden_out, col_hidden_out, row_onehot_out, col_onehot_out,
    bent_one_out, probs_one_out, bent_two_out, probs_two_out, grad_gain_out,
    extended, columns, transposed, transposed_act,
):
    rounds, twice, width, features = extended.shape
    rows = twice // 2
    tokens = x_in.shape[0]
    core = my_bit(0)
    borrowed = []
    for other, x_out, hidden_out, onehot_out, kv_out in (
        (row_packed, row_x_out, row_hidden_out, row_onehot_out, row_kv_out),
        (col_packed, col_x_out, col_hidden_out, col_onehot_out, col_kv_out),
    ):
        x, onehot = embed(other[...], plan[...], flip[...], width)
        hidden = (x * inverse_rms(x) * gain_tanner[...]).astype(BF)
        kv = dot(hidden, w_key_value[...]).astype(BF)
        x_out[...] = x
        onehot_out[...] = onehot
        hidden_out[...] = hidden
        kv_out[...] = kv
        borrowed.append(kv.astype(F32))
    extended[:, :rows] = kv_in[...].astype(F32).reshape(rounds, rows, width, features)
    extended[:, rows:] = borrowed[0].reshape(rounds, rows, width, features)
    columns[...] = borrowed[1].reshape(rounds * rows, width, features)
    query = query_in[...].astype(F32)
    scores = None
    for number in range(MONOS + 1):
        keys = neighbour(number, offsets, extended, columns)[:, :WIDTH]
        part = dot((query * keys).astype(BF), gather_heads(number, 64))
        scores = part if scores is None else scores + part
    bent, probs = softmax_parts(scores, tanner_valid(tokens), 64)
    bent_one_out[...] = bent
    probs_one_out[...] = probs
    parts = two_parts(probs, 64)
    mixed = None
    for number in range(MONOS + 1):
        values = neighbour(number, offsets, extended, columns)[:, WIDTH:]
        part = dot(parts, spread_heads(number, 64)) * values
        mixed = part if mixed is None else mixed + part
    mixed_one = mixed.astype(BF)
    mixed_one_out[...] = mixed_one
    after_tanner = x_in[...] + dot(mixed_one, w_merge[...])
    tanner_out[...] = after_tanner

    hidden_two = (after_tanner * inverse_rms(after_tanner) * gain_time[...]).astype(BF)
    hidden_two_out[...] = hidden_two
    packed_low = dot(hidden_two, w_temporal[...]).astype(BF)
    packed_out[...] = packed_low
    packed = packed_low.astype(F32).reshape(rounds, tokens // rounds, 3 * WIDTH)
    sites = tokens // rounds
    scores = None
    for earlier in range(rounds):
        product = packed[earlier:, :, :WIDTH] * packed[earlier][None, :, WIDTH : 2 * WIDTH]
        part = dot(product.reshape(-1, WIDTH).astype(BF), gather_heads(earlier, 32))
        if earlier:
            part = jnp.concatenate([jnp.zeros((earlier * sites, LANES), F32), part], axis=0)
        scores = part if scores is None else scores + part
    bent, probs = softmax_parts(scores, time_valid(tokens, rounds), 32)
    bent_two_out[...] = bent
    probs_two_out[...] = probs
    parts = two_parts(probs, 32)
    mixed = None
    for earlier in range(rounds):
        weight = dot(parts[earlier * sites :], spread_heads(earlier, 32)).reshape(rounds - earlier, sites, WIDTH)
        part = (weight * packed[earlier][None, :, 2 * WIDTH :]).reshape(-1, WIDTH)
        if earlier:
            part = jnp.concatenate([jnp.zeros((earlier * sites, WIDTH), F32), part], axis=0)
        mixed = part if mixed is None else mixed + part
    mixed_two = mixed.astype(BF)
    mixed_two_out[...] = mixed_two
    after_time = after_tanner + dot(mixed_two, w_temporal_out[...])

    hidden = (after_time * inverse_rms(after_time) * gain_ffn[...]).astype(BF)
    outer = cotangent[...]
    transposed[...] = hidden.T
    grad_three = None
    befores = []
    for block in range(FF // WIDTH):
        cols = slice(block * WIDTH, (block + 1) * WIDTH)
        before = dot(hidden, w_up[:, cols])
        square = before * before
        bend = jnp.tanh(GELU_A * before * (1.0 + GELU_B * square))
        upper = 0.5 * (1.0 + bend)
        activated = (before * upper).astype(BF)
        slope = upper + 0.5 * before * (1.0 - bend * bend) * (GELU_A * (1.0 + 3.0 * GELU_B * square))
        grad_before = (dot_nt(outer, w_down[cols, :]) * slope).astype(BF)
        befores.append(grad_before)
        part = dot_nt(grad_before, w_up[:, cols])
        grad_three = part if grad_three is None else grad_three + part
        transposed_act[cols, :] = activated.T
    mine = pl.multiple_of(core * HALF, HALF)
    other = pl.multiple_of((1 - core) * HALF, HALF)
    blocks = FF // WIDTH
    lead = jnp.concatenate([transposed[pl.ds(start, HALF), :] for start in (mine, other)], axis=0)
    for block in range(blocks):
        product = dot(lead, befores[block]).astype(BF)
        keep[block * HALF : (block + 1) * HALF, :] = product[:HALF]
        send[block * HALF : (block + 1) * HALF, :] = product[HALF:]
    lead = jnp.concatenate(
        [transposed_act[pl.ds(block * WIDTH + start, HALF), :] for start in (mine, other) for block in range(blocks)],
        axis=0,
    )
    product = dot(lead, outer).astype(BF)
    keep[blocks * HALF :, :] = product[: blocks * HALF]
    send[blocks * HALF :, :] = product[blocks * HALF :]
    grad_norm, grad_gain = norm_back(after_time, gain_ffn[...], grad_three)
    grad_time_out[...] = outer.astype(F32) + grad_norm
    grad_gain_out[...] = grad_gain


def backward_kernel(
    offsets, grad_time_in, tanner_in, packed_in, query_in, kv_in, row_kv, col_kv,
    bent_one, probs_one, bent_two, probs_two, w_merge, gain_time, w_temporal, w_temporal_out,
    grad_query_out, grad_kv_out, grad_rows_out, grad_cols_out, grad_packed_out, grad_tanner_out, grad_gain_out,
    extended, columns, grad_extended,
):
    rounds, twice, width, features = extended.shape
    rows = twice // 2
    tokens = grad_time_in.shape[0]
    sites = tokens // rounds
    grad_time = grad_time_in[...]
    grad_mixed = dot_nt(grad_time.astype(BF), w_temporal_out[...]).reshape(rounds, sites, WIDTH)
    packed = packed_in[...].astype(F32).reshape(rounds, sites, 3 * WIDTH)
    grad_probs = None
    for earlier in range(rounds):
        product = grad_mixed[earlier:] * packed[earlier][None, :, 2 * WIDTH :]
        part = dot(product.reshape(-1, WIDTH).astype(BF), gather_heads(earlier, 32))
        if earlier:
            part = jnp.concatenate([jnp.zeros((earlier * sites, LANES), F32), part], axis=0)
        grad_probs = part if grad_probs is None else grad_probs + part
    probs = probs_two[...]
    prob_parts = two_parts(probs, 32)
    score_parts = two_parts(softmax_back(bent_two[...], probs, grad_probs, 32), 32)
    grad_queries = None
    grad_keys = []
    grad_values = []
    for earlier in range(rounds):
        spread = spread_heads(earlier, 32)
        shape = (rounds - earlier, sites, WIDTH)
        weight = dot(prob_parts[earlier * sites :], spread).reshape(shape)
        slope = dot(score_parts[earlier * sites :], spread).reshape(shape)
        grad_values.append(jnp.sum(weight * grad_mixed[earlier:], axis=0))
        grad_keys.append(jnp.sum(slope * packed[earlier:, :, :WIDTH], axis=0))
        part = (slope * packed[earlier][None, :, WIDTH : 2 * WIDTH]).reshape(-1, WIDTH)
        if earlier:
            part = jnp.concatenate([jnp.zeros((earlier * sites, WIDTH), F32), part], axis=0)
        grad_queries = part if grad_queries is None else grad_queries + part
    grad_packed = jnp.concatenate(
        [grad_queries, jnp.concatenate(grad_keys, axis=0), jnp.concatenate(grad_values, axis=0)], axis=1
    ).astype(BF)
    grad_packed_out[...] = grad_packed
    grad_two = dot_nt(grad_packed, w_temporal[...])
    grad_norm, grad_gain = norm_back(tanner_in[...], gain_time[...], grad_two)
    grad_gain_out[...] = grad_gain
    grad_tanner = grad_time + grad_norm
    grad_tanner_out[...] = grad_tanner

    grad_mixed = dot_nt(grad_tanner.astype(BF), w_merge[...])
    extended[:, :rows] = kv_in[...].astype(F32).reshape(rounds, rows, width, features)
    extended[:, rows:] = row_kv[...].astype(F32).reshape(rounds, rows, width, features)
    columns[...] = col_kv[...].astype(F32).reshape(rounds * rows, width, features)
    grad_probs = None
    for number in range(MONOS + 1):
        values = neighbour(number, offsets, extended, columns)[:, WIDTH:]
        part = dot((grad_mixed * values).astype(BF), gather_heads(number, 64))
        grad_probs = part if grad_probs is None else grad_probs + part
    probs = probs_one[...]
    prob_parts = two_parts(probs, 64)
    score_parts = two_parts(softmax_back(bent_one[...], probs, grad_probs, 64), 64)
    query = query_in[...].astype(F32)
    grad_query = None
    grad_cols = None
    for number in (0,) + tuple(i + 1 for i in range(MONOS)):
        spread = spread_heads(number, 64)
        slope = dot(score_parts, spread)
        weight = dot(prob_parts, spread)
        keys = neighbour(number, offsets, extended, columns)[:, :WIDTH]
        part = slope * keys
        grad_query = part if grad_query is None else grad_query + part
        grad_kv = jnp.concatenate([slope * query, weight * grad_mixed], axis=1)
        if number == 0:
            grad_extended[:, :rows] = grad_kv.reshape(rounds, rows, width, features)
            grad_extended[:, rows:] = jnp.zeros((rounds, rows, width, features), F32)
            continue
        by = offset_of(offsets, number - 1)
        if number - 1 in ALONG_ROWS:
            grad_extended[:, pl.ds(by, rows)] += grad_kv.reshape(rounds, rows, width, features)
            continue
        moved = pltpu.roll(grad_kv.reshape(rounds * rows, width, features), by % width, 1)
        place = lax.broadcasted_iota(jnp.int32, moved.shape, 1)
        own = jnp.where(place >= by, moved, 0.0)
        grad_extended[:, :rows] += own.reshape(rounds, rows, width, features)
        grad_cols = moved - own if grad_cols is None else grad_cols + (moved - own)
    grad_query_out[...] = grad_query.astype(BF)
    grad_kv_out[...] = grad_extended[:, :rows].reshape(tokens, features).astype(BF)
    grad_rows_out[...] = grad_extended[:, rows:].reshape(tokens, features).astype(BF)
    grad_cols_out[...] = grad_cols.reshape(tokens, features).astype(BF)


def weights_kernel(
    mixed_two, grad_time, hidden_two, grad_packed, mixed_one, grad_tanner, grad_query, w_query, w_key_value, gain,
    x_own, x_row, x_col, hidden_own, hidden_row, hidden_col, onehot_own, onehot_row, onehot_col,
    grad_own, grad_row, grad_col, grad_gain_time, grad_gain_ffn,
    grad_out, row_out, col_out, keep, send, transposed, transposed_own,
):
    core = my_bit(0)
    tokens = x_own.shape[0]
    transposed[0] = hidden_two[...].T
    transposed[1] = mixed_two[...].T
    transposed[2] = mixed_one[...].T
    small = None
    grad_gain = None
    for number, (x, hidden, onehot, grad_kv, out) in enumerate((
        (x_own, hidden_own, onehot_own, grad_own, grad_out),
        (x_row, hidden_row, onehot_row, grad_row, row_out),
        (x_col, hidden_col, onehot_col, grad_col, col_out),
    )):
        transposed_own[:, number * tokens : (number + 1) * tokens] = hidden[...].T
        grad_one = dot_nt(grad_kv[...], w_key_value[...])
        if number == 0:
            grad_one = grad_one + dot_nt(grad_query[...], w_query[...])
        grad, part = norm_back(x[...], gain[...], grad_one)
        grad_gain = part if grad_gain is None else grad_gain + part
        if number == 0:
            grad = grad + grad_tanner[...]
        out[...] = grad.astype(out.dtype)
        high = grad.astype(BF)
        low = (grad - high.astype(F32)).astype(BF)
        part = dot(onehot[...], jnp.concatenate([high, low], axis=1), ((0,), (0,)))[:16]
        part = part[:, :WIDTH] + part[:, WIDTH:]
        small = part if small is None else small + part
    row = lax.broadcasted_iota(jnp.int32, small.shape, 0)
    small = jnp.where(row == 9, grad_gain, small)
    small = jnp.where(row == 10, grad_gain_time[...], small)
    small = jnp.where(row == 11, grad_gain_ffn[...], small).astype(BF)
    grad_time_low = grad_time[...].astype(BF)
    grad_tanner_low = grad_tanner[...].astype(BF)
    grad_all = jnp.concatenate([grad_own[...], grad_row[...], grad_col[...]], axis=0)
    mine = pl.ds(pl.multiple_of(core * HALF, HALF), HALF)
    other = pl.ds(pl.multiple_of((1 - core) * HALF, HALF), HALF)
    keep[:16, :] = small
    send[:16, :] = small
    pairs = [(transposed.at[0], grad_packed[:, block * WIDTH : (block + 1) * WIDTH]) for block in range(3)]
    pairs.append((transposed.at[1], grad_time_low))
    pairs.append((transposed.at[2], grad_tanner_low))
    pairs.append((transposed_own.at[:, pl.ds(0, tokens)], grad_query[...]))
    pairs += [(transposed_own, grad_all[:, block * WIDTH : (block + 1) * WIDTH]) for block in range(2)]
    for block, (lead, grad) in enumerate(pairs):
        product = dot(jnp.concatenate([lead[mine, :], lead[other, :]], axis=0), grad).astype(BF)
        rows = slice(16 + block * HALF, 16 + (block + 1) * HALF)
        keep[rows, :] = product[:HALF]
        send[rows, :] = product[HALF:]


def finish_kernel(grad, row, col, out):
    out[...] = (grad[...] + row[...].astype(F32) + col[...].astype(F32)).astype(BF)


def my_bit(bit):
    many = lax.axis_size("gy").bit_length() - 1
    if bit < many:
        return (lax.axis_index("gy") >> bit) & 1
    return (lax.axis_index("gx") >> (bit - many)) & 1


def split_kernel(extra, bit, kept, received, keep, send, total):
    mine = my_bit(bit)
    value = kept[...].astype(F32) + received[...].astype(F32)
    total[...] = value[extra:]
    rows = keep.shape[0] - extra
    for ref, which in ((keep, mine), (send, 1 - mine)):
        if extra:
            ref[:extra, :] = value[:extra].astype(BF)
        ref[extra:, :] = total[pl.ds(pl.multiple_of(which * rows, rows), rows), :].astype(BF)


def end_kernel(extra, scale, kept, received, out, *small):
    value = kept[...].astype(F32) + received[...].astype(F32)
    out[...] = value[extra:].astype(BF)
    if extra:
        value = value[:extra] * scale
        small[0][...] = value[:8]
        for number in range(4):
            small[1 + number][...] = value[8 + number : 9 + number]


def join_kernel(bit, own, received, out):
    mine = my_bit(bit)
    out[mine] = own[...]
    out[1 - mine] = received[...]


def unpack_kernel(blocks, scale, own, other, *refs):
    outs, wides, done = refs[: len(blocks)], refs[len(blocks) : -1], refs[-1]
    core = my_bit(0)
    moves = []
    for side, (ref, which) in enumerate(((own, core), (other, 1 - core))):
        block = 0
        half = pl.multiple_of(which * HALF, HALF)
        for out, wide, (down, across) in zip(outs, wides, blocks):
            for index in range(down * across):
                value = ref[block * HALF : (block + 1) * HALF, :].astype(F32) * scale
                left = (index if across > 1 else 0) * WIDTH
                wide[side, index if down > 1 else 0, :, left : left + WIDTH] = value
                block += 1
            for index in range(down):
                target = out.at[pl.ds(index * WIDTH + half, HALF)]
                moves.append(pltpu.make_async_copy(wide.at[side, index], target, done.at[len(moves)]))
                moves[-1].start()
    for move in moves:
        move.wait()


def estimate(work, outs=(), args=()):
    moved = sum(math.prod(shape) * jnp.dtype(dtype).itemsize for shape, dtype in outs)
    moved += sum(math.prod(arg.shape) * arg.dtype.itemsize for arg in args)
    return pl.CostEstimate(flops=int(work * 1.1e9), transcendentals=0, bytes_accessed=moved)


def call(kernel, outs, args, scratch=(), smem=0, limit=16, work=0.1):
    vmem = pl.BlockSpec(memory_space=pltpu.VMEM)
    return pl.pallas_call(
        kernel,
        out_shape=[jax.ShapeDtypeStruct(shape, dtype) for shape, dtype in outs],
        in_specs=[pl.BlockSpec(memory_space=pltpu.SMEM)] * smem + [vmem] * (len(args) - smem),
        out_specs=[vmem] * len(outs),
        scratch_shapes=list(scratch),
        compiler_params=pltpu.CompilerParams(vmem_limit_bytes=limit * MIB),
        cost_estimate=estimate(work, outs, args),
    )(*args)


def shifted(x, axis, by):
    count = lax.axis_size(axis)
    return lax.ppermute(x, axis, [(i, (i + by) % count) for i in range(count)])


class Layout:
    def __init__(self):
        self.nx = lax.axis_size("gx")
        self.ny = lax.axis_size("gy")
        self.many = self.ny.bit_length() - 1
        self.bits = self.many + self.nx.bit_length() - 1
        assert 1 << self.bits == self.nx * self.ny

    def swap(self, x, bit):
        flip = 1 << bit if bit < self.many else self.ny << (bit - self.many)
        return lax.ppermute(x, ("gx", "gy"), [(i, i ^ flip) for i in range(self.nx * self.ny)])


def reduce_tree(layout, keep, send, extra, order, scale, first=0, until=None):
    for stage in range(first, len(order) if until is None else until):
        received = layout.swap(send, order[stage])
        rows = keep.shape[0] - extra
        if stage + 1 < len(order):
            half = ((rows // 2 + extra, WIDTH), BF)
            keep, send = call(
                functools.partial(split_kernel, extra, order[stage + 1]),
                [half, half],
                [keep, received],
                [pltpu.VMEM((rows, WIDTH), F32)],
            )
    if until is not None:
        return keep, send
    small = [((8, WIDTH), F32)] + [((1, WIDTH), F32)] * 4 if extra else []
    return call(functools.partial(end_kernel, extra, scale), [((rows, WIDTH), BF)] + small, [keep, received])


def gather_tree(layout, own, order, blocks, scale, beside=()):
    for bit in order[:0:-1]:
        received = layout.swap(own, bit)
        if bit == order[1] and beside:
            received, *beside = lax.optimization_barrier((received, *beside))
        rows = own.shape[0]
        own = call(
            functools.partial(join_kernel, bit), [((2, rows, WIDTH), BF)], [own, received]
        )[0].reshape(2 * rows, WIDTH)
    other = layout.swap(own, order[0])
    copies = 2 * sum(down for down, _ in blocks)
    outs = pl.pallas_call(
        functools.partial(unpack_kernel, blocks, scale),
        out_shape=[jax.ShapeDtypeStruct((down * WIDTH, across * WIDTH), F32) for down, across in blocks],
        in_specs=[pl.BlockSpec(memory_space=pltpu.VMEM)] * 2,
        out_specs=[pl.BlockSpec(memory_space=pltpu.HBM)] * len(blocks),
        scratch_shapes=[pltpu.VMEM((2, down, HALF, across * WIDTH), F32) for down, across in blocks]
        + [pltpu.SemaphoreType.DMA((copies,))],
        compiler_params=pltpu.CompilerParams(vmem_limit_bytes=16 * MIB),
    )(own, other)
    return (*outs, *beside)


def on_device(
    tokens,
    syndrome,
    check_plan_step,
    offsets,
    flip_vector,
    plan_step_embedding,
    gain_tanner,
    w_query,
    w_key_value,
    w_merge,
    gain_time,
    w_temporal,
    w_temporal_out,
    gain_ffn,
    w_ffn_up,
    w_ffn_down,
    cotangent,
):
    layout = Layout()
    rounds, rows, cols = tokens.shape[:3]
    count = rounds * rows * cols
    scale = 1.0 / math.sqrt(count * layout.nx * layout.ny)
    flat = (count, WIDTH)
    act = (flat, BF)
    stream = (flat, F32)
    wide = ((count, 2 * WIDTH), BF)
    lanes = ((count, LANES), F32)
    onehot = ((count, LANES), BF)
    row = ((1, WIDTH), F32)
    hbm = pl.BlockSpec(memory_space=pltpu.HBM)

    sites = pltpu.VMEM((rounds, rows, cols), jnp.int32)
    packed_tokens = pl.pallas_call(
        pack_kernel,
        out_shape=jax.ShapeDtypeStruct((count + rounds * rows, WIDTH), BF),
        in_specs=[hbm] * 3,
        out_specs=pl.BlockSpec(memory_space=pltpu.VMEM),
        scratch_shapes=[sites, sites, pltpu.SemaphoreType.DMA((3,))],
        cost_estimate=estimate(12),
    )(tokens.reshape(flat), syndrome, check_plan_step)
    row_packed = shifted(packed_tokens, "gx", -1)
    col_packed = shifted(packed_tokens, "gy", -1)
    plan = plan_step_embedding
    flip = flip_vector.reshape(1, WIDTH)
    gain_one = gain_tanner.reshape(1, WIDTH)
    gain_two = gain_time.reshape(1, WIDTH)
    gain_three = gain_ffn.reshape(1, WIDTH)
    outer = cotangent.reshape(flat)
    x, onehot_own, hidden_one, query, key_value = call(
        functools.partial(start_kernel, cols),
        [stream, onehot, act, act, wide],
        [packed_tokens, plan, flip, gain_one, w_query, w_key_value],

    )
    extended = pltpu.VMEM((rounds, 2 * rows, cols, 2 * WIDTH), F32)
    columns = pltpu.VMEM((rounds * rows, cols, 2 * WIDTH), F32)
    half_one = ((2 * (FF // WIDTH) * HALF, WIDTH), BF)
    (
        keep_one, send_one, grad_time, after_tanner, mixed_one, mixed_two, packed, hidden_two,
        row_kv, col_kv, row_x, col_x, row_hidden, col_hidden, row_onehot, col_onehot,
        bent_one, probs_one, bent_two, probs_two, grad_gain_ffn,
    ) = call(
        forward_kernel,
        [half_one, half_one, stream, stream, act, act, ((count, 3 * WIDTH), BF), act,
         wide, wide, stream, stream, act, act, onehot, onehot, lanes, lanes, lanes, lanes, row],
        [offsets, x, query, key_value, col_packed, row_packed, plan, flip,
         gain_one, w_key_value, w_merge, gain_two, w_temporal, w_temporal_out, gain_three, w_ffn_up, w_ffn_down,
         outer],
        [extended, columns, pltpu.VMEM((WIDTH, count), BF), pltpu.VMEM((FF, count), BF)],
        smem=1,
        limit=32,

    )
    grad_query, grad_kv, grad_rows, grad_cols, grad_packed, grad_tanner, grad_gain_time = call(
        backward_kernel,
        [act, wide, wide, wide, ((count, 3 * WIDTH), BF), stream, row],
        [offsets, grad_time, after_tanner, packed, query, key_value, row_kv, col_kv,
         bent_one, probs_one, bent_two, probs_two, w_merge, gain_two, w_temporal, w_temporal_out],
        [extended, columns, extended],
        smem=1,
        limit=32,
        work=3,
    )
    many, bits = layout.many, layout.bits
    order_one = list(range(many)) + list(range(many, bits))
    order_two = [0, many] + list(range(1, many)) + list(range(many + 1, bits))
    keep_one, send_one = reduce_tree(layout, keep_one, send_one, 0, order_one, scale, until=1)
    keep_one, grad_tanner = lax.optimization_barrier((keep_one, grad_tanner))
    half_two = ((16 + 8 * HALF, WIDTH), BF)
    grad_own, lent_rows, lent_cols, keep_two, send_two = call(
        weights_kernel,
        [stream, act, act, half_two, half_two],
        [mixed_two, grad_time, hidden_two, grad_packed, mixed_one, grad_tanner, grad_query, w_query, w_key_value,
         gain_one, x, row_x, col_x, hidden_one, row_hidden, col_hidden, onehot_own, row_onehot, col_onehot,
         grad_kv, grad_rows, grad_cols, grad_gain_time, grad_gain_ffn],
        [pltpu.VMEM((3, WIDTH, count), BF), pltpu.VMEM((WIDTH, 3 * count), BF)],
        limit=32,
        work=3,
    )
    back_rows = shifted(lent_rows, "gx", 1)
    back_cols = shifted(lent_cols, "gy", 1)
    shard_one = reduce_tree(layout, keep_one, send_one, 0, order_one, scale, first=1)[0]
    shard_two, plan_grad, grad_flip, sum_gain_tanner, sum_gain_time, sum_gain_ffn = reduce_tree(
        layout, keep_two, send_two, 16, order_two, scale
    )
    grad_up, grad_down, back_rows, back_cols = gather_tree(
        layout, shard_one, order_one, ((1, FF // WIDTH), (FF // WIDTH, 1)), scale, (back_rows, back_cols)
    )
    token_grad = call(finish_kernel, [act], [grad_own, back_rows, back_cols])[0]
    grad_temporal, grad_temporal_out, grad_merge, grad_w_query, grad_key_value = gather_tree(
        layout, shard_two, order_two, ((1, 3), (1, 1), (1, 1), (1, 1), (1, 2)), scale
    )
    return (
        token_grad.reshape(tokens.shape),
        grad_flip.reshape(WIDTH),
        plan_grad,
        sum_gain_tanner.reshape(WIDTH),
        grad_w_query,
        grad_key_value,
        grad_merge,
        sum_gain_time.reshape(WIDTH),
        grad_temporal,
        grad_temporal_out,
        sum_gain_ffn.reshape(WIDTH),
        grad_up,
        grad_down,
    )


def solution(mesh):
    tiled = P(None, "gx", "gy", None)
    sites = P(None, "gx", "gy")
    return jax.shard_map(
        on_device,
        mesh=mesh,
        in_specs=(tiled, sites, sites) + (P(),) * 13 + (tiled,),
        out_specs=(tiled,) + (P(),) * 12,
        check_vma=False,
    )
```

```python
import functools
import math

import jax
import jax.numpy as jnp
from jax import lax
from jax.experimental import pallas as pl
from jax.experimental.pallas import tpu as pltpu
from jax.sharding import PartitionSpec as P

WIDTH = 256
HEADDIM = 32
HEADS = WIDTH // HEADDIM
FF = 1024
PLAN_STEP_COUNT = 8
MONOS = 6
MAXEXP = 8
LANES = 128
HALF = WIDTH // 2

EPS = 1e-05
CAP = 4.0
ALONG_ROWS = (0, 4, 5)
BF = jnp.bfloat16
F32 = jnp.float32
SCORE = 1.0 / math.sqrt(HEADDIM)
GELU_A = math.sqrt(2.0 / math.pi)
GELU_B = 0.044715
MIB = 1 << 20


def dot(a, b, dims=((1,), (0,))):
    return lax.dot_general(a, b, (dims, ((), ())), preferred_element_type=F32)


def dot_nt(a, b):
    return dot(a, b, ((1,), (1,)))


def embed(packed, plan, flip, width):
    count = packed.shape[0]
    lines = count // (width + 1)
    tokens = lines * width
    codes = packed[tokens:, :LANES]
    token = lax.broadcasted_iota(jnp.int32, (tokens, lines), 0)
    line = lax.broadcasted_iota(jnp.int32, (tokens, lines), 1)
    spread = dot(jnp.where(token // width == line, 1.0, 0.0).astype(BF), codes)
    token = lax.broadcasted_iota(jnp.int32, (tokens, LANES), 0)
    lane = lax.broadcasted_iota(jnp.int32, (tokens, LANES), 1)
    picked = jnp.where(token % width == lane, spread, 0.0).astype(BF)
    code = dot(picked, jnp.ones((LANES, LANES), BF))
    flipped = code >= PLAN_STEP_COUNT
    step = jnp.where(flipped, code - PLAN_STEP_COUNT, code)
    slot = lane % 16
    chosen = (slot.astype(F32) == step) | ((slot == PLAN_STEP_COUNT) & flipped)
    onehot = jnp.where(chosen & (lane < 48), 1.0, 0.0).astype(BF)
    row = lax.broadcasted_iota(jnp.int32, (8, WIDTH), 0)
    table = jnp.concatenate([plan, jnp.where(row == 0, flip, 0.0)], axis=0)
    high = table.astype(BF)
    rest = table - high.astype(F32)
    middle = rest.astype(BF)
    low = (rest - middle.astype(F32)).astype(BF)
    empty = jnp.zeros((LANES - 48, WIDTH), BF)
    vectors = dot(onehot, jnp.concatenate([high, middle, low, empty], axis=0))
    return packed[:tokens].astype(F32) + vectors, onehot


def inverse_rms(stream):
    return lax.rsqrt(jnp.mean(stream * stream, axis=-1, keepdims=True) + EPS)


def norm_back(stream, gain, grad):
    inverse = inverse_rms(stream)
    normed = stream * inverse
    scaled = grad * gain
    mean = jnp.mean(scaled * normed, axis=-1, keepdims=True)
    return inverse * (scaled - normed * mean), jnp.sum(grad * normed, axis=0, keepdims=True)


def gather_heads(slot, period):
    feature = lax.broadcasted_iota(jnp.int32, (WIDTH, LANES), 0) // HEADDIM
    lane = lax.broadcasted_iota(jnp.int32, (WIDTH, LANES), 1) % period
    return jnp.where(lane - feature == slot * HEADS, 1.0, 0.0).astype(BF)


def spread_heads(slot, period):
    lane = lax.broadcasted_iota(jnp.int32, (LANES, WIDTH), 0)
    feature = lax.broadcasted_iota(jnp.int32, (LANES, WIDTH), 1) // HEADDIM
    at = (lane < 2 * period) & (lane % period - feature == slot * HEADS)
    return jnp.where(at, 1.0, 0.0).astype(BF)


def two_parts(value, period):
    lane = lax.broadcasted_iota(jnp.int32, value.shape, 1)
    high = value.astype(BF).astype(F32)
    return jnp.where(lane < period, high, value - high).astype(BF)


def slot_total(value, period):
    shift = HEADS
    while shift < period:
        value = value + pltpu.roll(value, shift, 1)
        shift *= 2
    return value


def softmax_parts(scores, valid, period):
    bent = jnp.tanh(scores * (SCORE / CAP))
    weights = jnp.where(valid, jnp.exp(CAP * bent), 0.0)
    return bent, weights / slot_total(weights, period)


def softmax_back(bent, probs, grad, period):
    inner = probs * grad
    return (inner - probs * slot_total(inner, period)) * (1.0 - bent * bent) * SCORE


def tanner_valid(tokens):
    lane = lax.broadcasted_iota(jnp.int32, (tokens, LANES), 1)
    return lane % 64 < HEADS * (MONOS + 1)


def time_valid(tokens, rounds):
    lane = lax.broadcasted_iota(jnp.int32, (tokens, LANES), 1)
    row = lax.broadcasted_iota(jnp.int32, (tokens, LANES), 0)
    return (lane % 32) // HEADS <= row // (tokens // rounds)


def offset_of(offsets, index):
    return offsets[index, 0] if index in ALONG_ROWS else offsets[index, 1]


def neighbour(number, offsets, extended, columns):
    rounds, twice, width, features = extended.shape
    rows = twice // 2
    tokens = rounds * rows * width
    if number == 0:
        return extended[:, :rows].reshape(tokens, features)
    by = offset_of(offsets, number - 1)
    if number - 1 in ALONG_ROWS:
        return extended[:, pl.ds(by, rows)].reshape(tokens, features)
    own = extended[:, :rows].reshape(rounds * rows, width, features)
    place = lax.broadcasted_iota(jnp.int32, own.shape, 1)
    joined = jnp.where(place >= by, own, columns[...])
    return pltpu.roll(joined, width - by, 1).reshape(tokens, features)


def pack_kernel(tokens, syndrome, step, out, flips, steps, done):
    count = tokens.shape[0]
    rounds, rows, width = syndrome.shape
    moves = [
        pltpu.make_async_copy(tokens, out.at[pl.ds(0, count)], done.at[0]),
        pltpu.make_async_copy(syndrome, flips, done.at[1]),
        pltpu.make_async_copy(step, steps, done.at[2]),
    ]
    for move in moves:
        move.start()
    out[count:, :] = jnp.zeros((rounds * rows, WIDTH), BF)
    moves[1].wait()
    moves[2].wait()
    code = flips[...] * PLAN_STEP_COUNT + steps[...]
    out[count:, :width] = code.reshape(rounds * rows, width).astype(F32).astype(BF)
    moves[0].wait()


def start_kernel(width, packed, plan, flip, gain, w_query, w_key_value, x_out, onehot_out, hidden_out, query_out, kv_out):
    x, onehot = embed(packed[...], plan[...], flip[...], width)
    hidden = (x * inverse_rms(x) * gain[...]).astype(BF)
    x_out[...] = x
    onehot_out[...] = onehot
    hidden_out[...] = hidden
    query_out[...] = dot(hidden, w_query[...]).astype(BF)
    kv_out[...] = dot(hidden, w_key_value[...]).astype(BF)


def forward_kernel(
    offsets, x_in, query_in, kv_in, col_packed, row_packed, plan, flip,
    gain_tanner, w_key_value, w_merge, gain_time, w_temporal, w_temporal_out, gain_ffn, w_up, w_down, cotangent,
    keep, send, grad_time_out, tanner_out, mixed_one_out, mixed_two_out, packed_out, hidden_two_out,
    row_kv_out, col_kv_out, row_x_out, col_x_out, row_hidden_out, col_hidden_out, row_onehot_out, col_onehot_out,
    bent_one_out, probs_one_out, bent_two_out, probs_two_out, grad_gain_out,
    extended, columns, transposed, transposed_act,
):
    rounds, twice, width, features = extended.shape
    rows = twice // 2
    tokens = x_in.shape[0]
    core = my_bit(0)
    borrowed = []
    for other, x_out, hidden_out, onehot_out, kv_out in (
        (row_packed, row_x_out, row_hidden_out, row_onehot_out, row_kv_out),
        (col_packed, col_x_out, col_hidden_out, col_onehot_out, col_kv_out),
    ):
        x, onehot = embed(other[...], plan[...], flip[...], width)
        hidden = (x * inverse_rms(x) * gain_tanner[...]).astype(BF)
        kv = dot(hidden, w_key_value[...]).astype(BF)
        x_out[...] = x
        onehot_out[...] = onehot
        hidden_out[...] = hidden
        kv_out[...] = kv
        borrowed.append(kv.astype(F32))
    extended[:, :rows] = kv_in[...].astype(F32).reshape(rounds, rows, width, features)
    extended[:, rows:] = borrowed[0].reshape(rounds, rows, width, features)
    columns[...] = borrowed[1].reshape(rounds * rows, width, features)
    query = query_in[...].astype(F32)
    scores = None
    for number in range(MONOS + 1):
        keys = neighbour(number, offsets, extended, columns)[:, :WIDTH]
        part = dot((query * keys).astype(BF), gather_heads(number, 64))
        scores = part if scores is None else scores + part
    bent, probs = softmax_parts(scores, tanner_valid(tokens), 64)
    bent_one_out[...] = bent
    probs_one_out[...] = probs
    parts = two_parts(probs, 64)
    mixed = None
    for number in range(MONOS + 1):
        values = neighbour(number, offsets, extended, columns)[:, WIDTH:]
        part = dot(parts, spread_heads(number, 64)) * values
        mixed = part if mixed is None else mixed + part
    mixed_one = mixed.astype(BF)
    mixed_one_out[...] = mixed_one
    after_tanner = x_in[...] + dot(mixed_one, w_merge[...])
    tanner_out[...] = after_tanner

    hidden_two = (after_tanner * inverse_rms(after_tanner) * gain_time[...]).astype(BF)
    hidden_two_out[...] = hidden_two
    packed_low = dot(hidden_two, w_temporal[...]).astype(BF)
    packed_out[...] = packed_low
    packed = packed_low.astype(F32).reshape(rounds, tokens // rounds, 3 * WIDTH)
    sites = tokens // rounds
    scores = None
    for earlier in range(rounds):
        product = packed[earlier:, :, :WIDTH] * packed[earlier][None, :, WIDTH : 2 * WIDTH]
        part = dot(product.reshape(-1, WIDTH).astype(BF), gather_heads(earlier, 32))
        if earlier:
            part = jnp.concatenate([jnp.zeros((earlier * sites, LANES), F32), part], axis=0)
        scores = part if scores is None else scores + part
    bent, probs = softmax_parts(scores, time_valid(tokens, rounds), 32)
    bent_two_out[...] = bent
    probs_two_out[...] = probs
    parts = two_parts(probs, 32)
    mixed = None
    for earlier in range(rounds):
        weight = dot(parts[earlier * sites :], spread_heads(earlier, 32)).reshape(rounds - earlier, sites, WIDTH)
        part = (weight * packed[earlier][None, :, 2 * WIDTH :]).reshape(-1, WIDTH)
        if earlier:
            part = jnp.concatenate([jnp.zeros((earlier * sites, WIDTH), F32), part], axis=0)
        mixed = part if mixed is None else mixed + part
    mixed_two = mixed.astype(BF)
    mixed_two_out[...] = mixed_two
    after_time = after_tanner + dot(mixed_two, w_temporal_out[...])

    hidden = (after_time * inverse_rms(after_time) * gain_ffn[...]).astype(BF)
    outer = cotangent[...]
    transposed[...] = hidden.T
    grad_three = None
    befores = []
    for block in range(FF // WIDTH):
        cols = slice(block * WIDTH, (block + 1) * WIDTH)
        before = dot(hidden, w_up[:, cols])
        square = before * before
        bend = jnp.tanh(GELU_A * before * (1.0 + GELU_B * square))
        upper = 0.5 * (1.0 + bend)
        activated = (before * upper).astype(BF)
        slope = upper + 0.5 * before * (1.0 - bend * bend) * (GELU_A * (1.0 + 3.0 * GELU_B * square))
        grad_before = (dot_nt(outer, w_down[cols, :]) * slope).astype(BF)
        befores.append(grad_before)
        part = dot_nt(grad_before, w_up[:, cols])
        grad_three = part if grad_three is None else grad_three + part
        transposed_act[cols, :] = activated.T
    mine = pl.multiple_of(core * HALF, HALF)
    other = pl.multiple_of((1 - core) * HALF, HALF)
    blocks = FF // WIDTH
    lead = jnp.concatenate([transposed[pl.ds(start, HALF), :] for start in (mine, other)], axis=0)
    for block in range(blocks):
        product = dot(lead, befores[block]).astype(BF)
        keep[block * HALF : (block + 1) * HALF, :] = product[:HALF]
        send[block * HALF : (block + 1) * HALF, :] = product[HALF:]
    lead = jnp.concatenate(
        [transposed_act[pl.ds(block * WIDTH + start, HALF), :] for start in (mine, other) for block in range(blocks)],
        axis=0,
    )
    product = dot(lead, outer).astype(BF)
    keep[blocks * HALF :, :] = product[: blocks * HALF]
    send[blocks * HALF :, :] = product[blocks * HALF :]
    grad_norm, grad_gain = norm_back(after_time, gain_ffn[...], grad_three)
    grad_time_out[...] = outer.astype(F32) + grad_norm
    grad_gain_out[...] = grad_gain


def backward_kernel(
    offsets, grad_time_in, tanner_in, packed_in, query_in, kv_in, row_kv, col_kv,
    bent_one, probs_one, bent_two, probs_two, w_merge, gain_time, w_temporal, w_temporal_out,
    grad_query_out, grad_kv_out, grad_rows_out, grad_cols_out, grad_packed_out, grad_tanner_out, grad_gain_out,
    extended, columns, grad_extended,
):
    rounds, twice, width, features = extended.shape
    rows = twice // 2
    tokens = grad_time_in.shape[0]
    sites = tokens // rounds
    grad_time = grad_time_in[...]
    grad_mixed = dot_nt(grad_time.astype(BF), w_temporal_out[...]).reshape(rounds, sites, WIDTH)
    packed = packed_in[...].astype(F32).reshape(rounds, sites, 3 * WIDTH)
    grad_probs = None
    for earlier in range(rounds):
        product = grad_mixed[earlier:] * packed[earlier][None, :, 2 * WIDTH :]
        part = dot(product.reshape(-1, WIDTH).astype(BF), gather_heads(earlier, 32))
        if earlier:
            part = jnp.concatenate([jnp.zeros((earlier * sites, LANES), F32), part], axis=0)
        grad_probs = part if grad_probs is None else grad_probs + part
    probs = probs_two[...]
    prob_parts = two_parts(probs, 32)
    score_parts = two_parts(softmax_back(bent_two[...], probs, grad_probs, 32), 32)
    grad_queries = None
    grad_keys = []
    grad_values = []
    for earlier in range(rounds):
        spread = spread_heads(earlier, 32)
        shape = (rounds - earlier, sites, WIDTH)
        weight = dot(prob_parts[earlier * sites :], spread).reshape(shape)
        slope = dot(score_parts[earlier * sites :], spread).reshape(shape)
        grad_values.append(jnp.sum(weight * grad_mixed[earlier:], axis=0))
        grad_keys.append(jnp.sum(slope * packed[earlier:, :, :WIDTH], axis=0))
        part = (slope * packed[earlier][None, :, WIDTH : 2 * WIDTH]).reshape(-1, WIDTH)
        if earlier:
            part = jnp.concatenate([jnp.zeros((earlier * sites, WIDTH), F32), part], axis=0)
        grad_queries = part if grad_queries is None else grad_queries + part
    grad_packed = jnp.concatenate(
        [grad_queries, jnp.concatenate(grad_keys, axis=0), jnp.concatenate(grad_values, axis=0)], axis=1
    ).astype(BF)
    grad_packed_out[...] = grad_packed
    grad_two = dot_nt(grad_packed, w_temporal[...])
    grad_norm, grad_gain = norm_back(tanner_in[...], gain_time[...], grad_two)
    grad_gain_out[...] = grad_gain
    grad_tanner = grad_time + grad_norm
    grad_tanner_out[...] = grad_tanner

    grad_mixed = dot_nt(grad_tanner.astype(BF), w_merge[...])
    extended[:, :rows] = kv_in[...].astype(F32).reshape(rounds, rows, width, features)
    extended[:, rows:] = row_kv[...].astype(F32).reshape(rounds, rows, width, features)
    columns[...] = col_kv[...].astype(F32).reshape(rounds * rows, width, features)
    grad_probs = None
    for number in range(MONOS + 1):
        values = neighbour(number, offsets, extended, columns)[:, WIDTH:]
        part = dot((grad_mixed * values).astype(BF), gather_heads(number, 64))
        grad_probs = part if grad_probs is None else grad_probs + part
    probs = probs_one[...]
    prob_parts = two_parts(probs, 64)
    score_parts = two_parts(softmax_back(bent_one[...], probs, grad_probs, 64), 64)
    query = query_in[...].astype(F32)
    grad_query = None
    grad_cols = None
    for number in (0,) + tuple(i + 1 for i in range(MONOS)):
        spread = spread_heads(number, 64)
        slope = dot(score_parts, spread)
        weight = dot(prob_parts, spread)
        keys = neighbour(number, offsets, extended, columns)[:, :WIDTH]
        part = slope * keys
        grad_query = part if grad_query is None else grad_query + part
        grad_kv = jnp.concatenate([slope * query, weight * grad_mixed], axis=1)
        if number == 0:
            grad_extended[:, :rows] = grad_kv.reshape(rounds, rows, width, features)
            grad_extended[:, rows:] = jnp.zeros((rounds, rows, width, features), F32)
            continue
        by = offset_of(offsets, number - 1)
        if number - 1 in ALONG_ROWS:
            grad_extended[:, pl.ds(by, rows)] += grad_kv.reshape(rounds, rows, width, features)
            continue
        moved = pltpu.roll(grad_kv.reshape(rounds * rows, width, features), by % width, 1)
        place = lax.broadcasted_iota(jnp.int32, moved.shape, 1)
        own = jnp.where(place >= by, moved, 0.0)
        grad_extended[:, :rows] += own.reshape(rounds, rows, width, features)
        grad_cols = moved - own if grad_cols is None else grad_cols + (moved - own)
    grad_query_out[...] = grad_query.astype(BF)
    grad_kv_out[...] = grad_extended[:, :rows].reshape(tokens, features).astype(BF)
    grad_rows_out[...] = grad_extended[:, rows:].reshape(tokens, features).astype(BF)
    grad_cols_out[...] = grad_cols.reshape(tokens, features).astype(BF)


def weights_kernel(
    mixed_two, grad_time, hidden_two, grad_packed, mixed_one, grad_tanner, grad_query, w_query, w_key_value, gain,
    x_own, x_row, x_col, hidden_own, hidden_row, hidden_col, onehot_own, onehot_row, onehot_col,
    grad_own, grad_row, grad_col, grad_gain_time, grad_gain_ffn,
    grad_out, row_out, col_out, keep, send, transposed, transposed_own,
):
    core = my_bit(0)
    tokens = x_own.shape[0]
    transposed[0] = hidden_two[...].T
    transposed[1] = mixed_two[...].T
    transposed[2] = mixed_one[...].T
    small = None
    grad_gain = None
    for number, (x, hidden, onehot, grad_kv, out) in enumerate((
        (x_own, hidden_own, onehot_own, grad_own, grad_out),
        (x_row, hidden_row, onehot_row, grad_row, row_out),
        (x_col, hidden_col, onehot_col, grad_col, col_out),
    )):
        transposed_own[:, number * tokens : (number + 1) * tokens] = hidden[...].T
        grad_one = dot_nt(grad_kv[...], w_key_value[...])
        if number == 0:
            grad_one = grad_one + dot_nt(grad_query[...], w_query[...])
        grad, part = norm_back(x[...], gain[...], grad_one)
        grad_gain = part if grad_gain is None else grad_gain + part
        if number == 0:
            grad = grad + grad_tanner[...]
        out[...] = grad.astype(out.dtype)
        high = grad.astype(BF)
        low = (grad - high.astype(F32)).astype(BF)
        part = dot(onehot[...], jnp.concatenate([high, low], axis=1), ((0,), (0,)))[:16]
        part = part[:, :WIDTH] + part[:, WIDTH:]
        small = part if small is None else small + part
    row = lax.broadcasted_iota(jnp.int32, small.shape, 0)
    small = jnp.where(row == 9, grad_gain, small)
    small = jnp.where(row == 10, grad_gain_time[...], small)
    small = jnp.where(row == 11, grad_gain_ffn[...], small).astype(BF)
    grad_time_low = grad_time[...].astype(BF)
    grad_tanner_low = grad_tanner[...].astype(BF)
    grad_all = jnp.concatenate([grad_own[...], grad_row[...], grad_col[...]], axis=0)
    mine = pl.ds(pl.multiple_of(core * HALF, HALF), HALF)
    other = pl.ds(pl.multiple_of((1 - core) * HALF, HALF), HALF)
    keep[:16, :] = small
    send[:16, :] = small
    pairs = [(transposed.at[0], grad_packed[:, block * WIDTH : (block + 1) * WIDTH]) for block in range(3)]
    pairs.append((transposed.at[1], grad_time_low))
    pairs.append((transposed.at[2], grad_tanner_low))
    pairs.append((transposed_own.at[:, pl.ds(0, tokens)], grad_query[...]))
    pairs += [(transposed_own, grad_all[:, block * WIDTH : (block + 1) * WIDTH]) for block in range(2)]
    for block, (lead, grad) in enumerate(pairs):
        product = dot(jnp.concatenate([lead[mine, :], lead[other, :]], axis=0), grad).astype(BF)
        rows = slice(16 + block * HALF, 16 + (block + 1) * HALF)
        keep[rows, :] = product[:HALF]
        send[rows, :] = product[HALF:]


def finish_kernel(grad, row, col, out):
    out[...] = (grad[...] + row[...].astype(F32) + col[...].astype(F32)).astype(BF)


def my_bit(bit):
    many = lax.axis_size("gy").bit_length() - 1
    if bit < many:
        return (lax.axis_index("gy") >> bit) & 1
    return (lax.axis_index("gx") >> (bit - many)) & 1


def split_kernel(extra, bit, kept, received, keep, send, total):
    mine = my_bit(bit)
    value = kept[...].astype(F32) + received[...].astype(F32)
    total[...] = value[extra:]
    rows = keep.shape[0] - extra
    for ref, which in ((keep, mine), (send, 1 - mine)):
        if extra:
            ref[:extra, :] = value[:extra].astype(BF)
        ref[extra:, :] = total[pl.ds(pl.multiple_of(which * rows, rows), rows), :].astype(BF)


def sum_kernel(first, second, out):
    out[...] = (first[...].astype(F32) + second[...].astype(F32)).astype(BF)


def end_kernel(extra, scale, inner, ours, theirs, out, *small):
    if inner is None:
        value = (ours[...].astype(F32) + theirs[...].astype(F32)).astype(BF)
    else:
        line = lax.axis_index("gx") // 2
        inside = jnp.where((line == inner[0]) | (line == inner[1]), 1.0, 0.0)
        value = (ours[...].astype(F32) * inside + theirs[...].astype(F32) * (1.0 - inside)).astype(BF)
    out[...] = value[extra:]
    if extra:
        value = value[:extra].astype(F32) * scale
        small[0][...] = value[:8]
        for number in range(4):
            small[1 + number][...] = value[8 + number : 9 + number]


def join_kernel(bit, own, received, out):
    mine = my_bit(bit)
    out[mine] = own[...]
    out[1 - mine] = received[...]


def unpack_kernel(blocks, scale, own, other, *refs):
    outs, wides, done = refs[: len(blocks)], refs[len(blocks) : -1], refs[-1]
    core = my_bit(0)
    moves = []
    for side, (ref, which) in enumerate(((own, core), (other, 1 - core))):
        block = 0
        half = pl.multiple_of(which * HALF, HALF)
        for out, wide, (down, across) in zip(outs, wides, blocks):
            for index in range(down * across):
                value = ref[block * HALF : (block + 1) * HALF, :].astype(F32) * scale
                left = (index if across > 1 else 0) * WIDTH
                wide[side, index if down > 1 else 0, :, left : left + WIDTH] = value
                block += 1
            for index in range(down):
                target = out.at[pl.ds(index * WIDTH + half, HALF)]
                moves.append(pltpu.make_async_copy(wide.at[side, index], target, done.at[len(moves)]))
                moves[-1].start()
    for move in moves:
        move.wait()


def estimate(work, outs=(), args=()):
    moved = sum(math.prod(shape) * jnp.dtype(dtype).itemsize for shape, dtype in outs)
    moved += sum(math.prod(arg.shape) * arg.dtype.itemsize for arg in args)
    return pl.CostEstimate(flops=int(work * 1.1e9), transcendentals=0, bytes_accessed=moved)


def call(kernel, outs, args, scratch=(), smem=0, limit=16, work=0.1):
    vmem = pl.BlockSpec(memory_space=pltpu.VMEM)
    return pl.pallas_call(
        kernel,
        out_shape=[jax.ShapeDtypeStruct(shape, dtype) for shape, dtype in outs],
        in_specs=[pl.BlockSpec(memory_space=pltpu.SMEM)] * smem + [vmem] * (len(args) - smem),
        out_specs=[vmem] * len(outs),
        scratch_shapes=list(scratch),
        compiler_params=pltpu.CompilerParams(vmem_limit_bytes=limit * MIB),
        cost_estimate=estimate(work, outs, args),
    )(*args)


def shifted(x, axis, by):
    count = lax.axis_size(axis)
    return lax.ppermute(x, axis, [(i, (i + by) % count) for i in range(count)])


class Layout:
    def __init__(self):
        self.nx = lax.axis_size("gx")
        self.ny = lax.axis_size("gy")
        self.many = self.ny.bit_length() - 1
        self.bits = self.many + self.nx.bit_length() - 1
        assert 1 << self.bits == self.nx * self.ny
        self.short = self.nx == 8

    def along(self, x, pairs):
        columns = [(side, gy) for side in range(2) for gy in range(self.ny)]
        return lax.ppermute(
            x,
            ("gx", "gy"),
            [((a * 2 + side) * self.ny + gy, (b * 2 + side) * self.ny + gy) for a, b in pairs for side, gy in columns],
        )

    def swap(self, x, bit):
        flip = 1 << bit if bit < self.many else self.ny << (bit - self.many)
        return lax.ppermute(x, ("gx", "gy"), [(i, i ^ flip) for i in range(self.nx * self.ny)])


def reduce_tree(layout, keep, send, extra, order, scale, first=0, until=None, beside=()):
    for stage in range(first, len(order) if until is None else until):
        received = layout.swap(send, order[stage])
        if stage == 2 and beside:
            received, *beside = lax.optimization_barrier((received, *beside))
        rows = keep.shape[0] - extra
        if stage + 1 < len(order):
            half = ((rows // 2 + extra, WIDTH), BF)
            keep, send = call(
                functools.partial(split_kernel, extra, order[stage + 1]),
                [half, half],
                [keep, received],
                [pltpu.VMEM((rows, WIDTH), F32)],
            )
    if until is not None:
        return keep, send
    inner = None
    if layout.short:
        inner = (1, 2)
        total = [(keep.shape, BF)]
        keep = call(sum_kernel, total, [keep, received])[0]
        keep = call(sum_kernel, total, [keep, layout.along(keep, ((0, 1), (3, 2)))])[0]
        keep = call(sum_kernel, total, [keep, layout.along(keep, ((1, 2), (2, 1)))])[0]
        received = layout.along(keep, ((1, 0), (2, 3)))
    small = [((8, WIDTH), F32)] + [((1, WIDTH), F32)] * 4 if extra else []
    outs = call(functools.partial(end_kernel, extra, scale, inner), [((rows, WIDTH), BF)] + small, [keep, received])
    return (*outs, *beside)


def gather_tree(layout, own, order, blocks, scale, beside=()):
    for bit in order[:0:-1]:
        received = layout.swap(own, bit)
        if bit == order[1] and beside:
            received, *beside = lax.optimization_barrier((received, *beside))
        rows = own.shape[0]
        own = call(
            functools.partial(join_kernel, bit), [((2, rows, WIDTH), BF)], [own, received]
        )[0].reshape(2 * rows, WIDTH)
    other = layout.swap(own, order[0])
    copies = 2 * sum(down for down, _ in blocks)
    outs = pl.pallas_call(
        functools.partial(unpack_kernel, blocks, scale),
        out_shape=[jax.ShapeDtypeStruct((down * WIDTH, across * WIDTH), F32) for down, across in blocks],
        in_specs=[pl.BlockSpec(memory_space=pltpu.VMEM)] * 2,
        out_specs=[pl.BlockSpec(memory_space=pltpu.HBM)] * len(blocks),
        scratch_shapes=[pltpu.VMEM((2, down, HALF, across * WIDTH), F32) for down, across in blocks]
        + [pltpu.SemaphoreType.DMA((copies,))],
        compiler_params=pltpu.CompilerParams(vmem_limit_bytes=16 * MIB),
    )(own, other)
    return (*outs, *beside)


def on_device(
    tokens,
    syndrome,
    check_plan_step,
    offsets,
    flip_vector,
    plan_step_embedding,
    gain_tanner,
    w_query,
    w_key_value,
    w_merge,
    gain_time,
    w_temporal,
    w_temporal_out,
    gain_ffn,
    w_ffn_up,
    w_ffn_down,
    cotangent,
):
    layout = Layout()
    rounds, rows, cols = tokens.shape[:3]
    count = rounds * rows * cols
    scale = 1.0 / math.sqrt(count * layout.nx * layout.ny)
    flat = (count, WIDTH)
    act = (flat, BF)
    stream = (flat, F32)
    wide = ((count, 2 * WIDTH), BF)
    lanes = ((count, LANES), F32)
    onehot = ((count, LANES), BF)
    row = ((1, WIDTH), F32)
    hbm = pl.BlockSpec(memory_space=pltpu.HBM)

    sites = pltpu.VMEM((rounds, rows, cols), jnp.int32)
    packed_tokens = pl.pallas_call(
        pack_kernel,
        out_shape=jax.ShapeDtypeStruct((count + rounds * rows, WIDTH), BF),
        in_specs=[hbm] * 3,
        out_specs=pl.BlockSpec(memory_space=pltpu.VMEM),
        scratch_shapes=[sites, sites, pltpu.SemaphoreType.DMA((3,))],
        cost_estimate=estimate(12),
    )(tokens.reshape(flat), syndrome, check_plan_step)
    row_packed = shifted(packed_tokens, "gx", -1)
    col_packed = shifted(packed_tokens, "gy", -1)
    plan = plan_step_embedding
    flip = flip_vector.reshape(1, WIDTH)
    gain_one = gain_tanner.reshape(1, WIDTH)
    gain_two = gain_time.reshape(1, WIDTH)
    gain_three = gain_ffn.reshape(1, WIDTH)
    outer = cotangent.reshape(flat)
    x, onehot_own, hidden_one, query, key_value = call(
        functools.partial(start_kernel, cols),
        [stream, onehot, act, act, wide],
        [packed_tokens, plan, flip, gain_one, w_query, w_key_value],

    )
    extended = pltpu.VMEM((rounds, 2 * rows, cols, 2 * WIDTH), F32)
    columns = pltpu.VMEM((rounds * rows, cols, 2 * WIDTH), F32)
    half_one = ((2 * (FF // WIDTH) * HALF, WIDTH), BF)
    (
        keep_one, send_one, grad_time, after_tanner, mixed_one, mixed_two, packed, hidden_two,
        row_kv, col_kv, row_x, col_x, row_hidden, col_hidden, row_onehot, col_onehot,
        bent_one, probs_one, bent_two, probs_two, grad_gain_ffn,
    ) = call(
        forward_kernel,
        [half_one, half_one, stream, stream, act, act, ((count, 3 * WIDTH), BF), act,
         wide, wide, stream, stream, act, act, onehot, onehot, lanes, lanes, lanes, lanes, row],
        [offsets, x, query, key_value, col_packed, row_packed, plan, flip,
         gain_one, w_key_value, w_merge, gain_two, w_temporal, w_temporal_out, gain_three, w_ffn_up, w_ffn_down,
         outer],
        [extended, columns, pltpu.VMEM((WIDTH, count), BF), pltpu.VMEM((FF, count), BF)],
        smem=1,
        limit=32,

    )
    grad_query, grad_kv, grad_rows, grad_cols, grad_packed, grad_tanner, grad_gain_time = call(
        backward_kernel,
        [act, wide, wide, wide, ((count, 3 * WIDTH), BF), stream, row],
        [offsets, grad_time, after_tanner, packed, query, key_value, row_kv, col_kv,
         bent_one, probs_one, bent_two, probs_two, w_merge, gain_two, w_temporal, w_temporal_out],
        [extended, columns, extended],
        smem=1,
        limit=32,
        work=3,
    )
    many, bits = layout.many, layout.bits
    far = [] if layout.short else list(range(many + 1, bits))
    order_one = list(range(many)) + [many] + far
    order_two = [0, many] + list(range(1, many)) + far
    keep_one, send_one = reduce_tree(layout, keep_one, send_one, 0, order_one, scale, until=1)
    keep_one, grad_tanner = lax.optimization_barrier((keep_one, grad_tanner))
    half_two = ((16 + 8 * HALF, WIDTH), BF)
    grad_own, lent_rows, lent_cols, keep_two, send_two = call(
        weights_kernel,
        [stream, act, act, half_two, half_two],
        [mixed_two, grad_time, hidden_two, grad_packed, mixed_one, grad_tanner, grad_query, w_query, w_key_value,
         gain_one, x, row_x, col_x, hidden_one, row_hidden, col_hidden, onehot_own, row_onehot, col_onehot,
         grad_kv, grad_rows, grad_cols, grad_gain_time, grad_gain_ffn],
        [pltpu.VMEM((3, WIDTH, count), BF), pltpu.VMEM((WIDTH, 3 * count), BF)],
        limit=32,
        work=3,
    )
    back_rows = shifted(lent_rows, "gx", 1)
    back_cols = shifted(lent_cols, "gy", 1)
    shard_one, back_rows, back_cols = reduce_tree(
        layout, keep_one, send_one, 0, order_one, scale, first=1, beside=(back_rows, back_cols)
    )
    shard_two, plan_grad, grad_flip, sum_gain_tanner, sum_gain_time, sum_gain_ffn = reduce_tree(
        layout, keep_two, send_two, 16, order_two, scale
    )
    grad_up, grad_down = gather_tree(
        layout, shard_one, order_one, ((1, FF // WIDTH), (FF // WIDTH, 1)), scale
    )
    token_grad = call(finish_kernel, [act], [grad_own, back_rows, back_cols])[0]
    grad_temporal, grad_temporal_out, grad_merge, grad_w_query, grad_key_value = gather_tree(
        layout, shard_two, order_two, ((1, 3), (1, 1), (1, 1), (1, 1), (1, 2)), scale
    )
    return (
        token_grad.reshape(tokens.shape),
        grad_flip.reshape(WIDTH),
        plan_grad,
        sum_gain_tanner.reshape(WIDTH),
        grad_w_query,
        grad_key_value,
        grad_merge,
        sum_gain_time.reshape(WIDTH),
        grad_temporal,
        grad_temporal_out,
        sum_gain_ffn.reshape(WIDTH),
        grad_up,
        grad_down,
    )


def solution(mesh):
    tiled = P(None, "gx", "gy", None)
    sites = P(None, "gx", "gy")
    return jax.shard_map(
        on_device,
        mesh=mesh,
        in_specs=(tiled, sites, sites) + (P(),) * 13 + (tiled,),
        out_specs=(tiled,) + (P(),) * 12,
        check_vma=False,
    )
```

```python
import functools
import math

import jax
import jax.numpy as jnp
from jax import lax
from jax.experimental import pallas as pl
from jax.experimental.pallas import tpu as pltpu
from jax.sharding import PartitionSpec as P

WIDTH = 256
HEADDIM = 32
HEADS = WIDTH // HEADDIM
FF = 1024
PLAN_STEP_COUNT = 8
MONOS = 6
MAXEXP = 8
LANES = 128
HALF = WIDTH // 2

EPS = 1e-05
CAP = 4.0
ALONG_ROWS = (0, 4, 5)
BF = jnp.bfloat16
F32 = jnp.float32
SCORE = 1.0 / math.sqrt(HEADDIM)
GELU_A = math.sqrt(2.0 / math.pi)
GELU_B = 0.044715
MIB = 1 << 20


def dot(a, b, dims=((1,), (0,))):
    return lax.dot_general(a, b, (dims, ((), ())), preferred_element_type=F32)


def dot_nt(a, b):
    return dot(a, b, ((1,), (1,)))


def embed(packed, plan, flip, width):
    count = packed.shape[0]
    lines = count // (width + 1)
    tokens = lines * width
    codes = packed[tokens:, :LANES]
    token = lax.broadcasted_iota(jnp.int32, (tokens, lines), 0)
    line = lax.broadcasted_iota(jnp.int32, (tokens, lines), 1)
    spread = dot(jnp.where(token // width == line, 1.0, 0.0).astype(BF), codes)
    token = lax.broadcasted_iota(jnp.int32, (tokens, LANES), 0)
    lane = lax.broadcasted_iota(jnp.int32, (tokens, LANES), 1)
    picked = jnp.where(token % width == lane, spread, 0.0).astype(BF)
    code = dot(picked, jnp.ones((LANES, LANES), BF))
    flipped = code >= PLAN_STEP_COUNT
    step = jnp.where(flipped, code - PLAN_STEP_COUNT, code)
    slot = lane % 16
    chosen = (slot.astype(F32) == step) | ((slot == PLAN_STEP_COUNT) & flipped)
    onehot = jnp.where(chosen & (lane < 48), 1.0, 0.0).astype(BF)
    row = lax.broadcasted_iota(jnp.int32, (8, WIDTH), 0)
    table = jnp.concatenate([plan, jnp.where(row == 0, flip, 0.0)], axis=0)
    high = table.astype(BF)
    rest = table - high.astype(F32)
    middle = rest.astype(BF)
    low = (rest - middle.astype(F32)).astype(BF)
    empty = jnp.zeros((LANES - 48, WIDTH), BF)
    vectors = dot(onehot, jnp.concatenate([high, middle, low, empty], axis=0))
    return packed[:tokens].astype(F32) + vectors, onehot


def inverse_rms(stream):
    return lax.rsqrt(jnp.mean(stream * stream, axis=-1, keepdims=True) + EPS)


def norm_back(stream, gain, grad):
    inverse = inverse_rms(stream)
    normed = stream * inverse
    scaled = grad * gain
    mean = jnp.mean(scaled * normed, axis=-1, keepdims=True)
    return inverse * (scaled - normed * mean), jnp.sum(grad * normed, axis=0, keepdims=True)


def gather_heads(slot, period):
    feature = lax.broadcasted_iota(jnp.int32, (WIDTH, LANES), 0) // HEADDIM
    lane = lax.broadcasted_iota(jnp.int32, (WIDTH, LANES), 1) % period
    return jnp.where(lane - feature == slot * HEADS, 1.0, 0.0).astype(BF)


def spread_heads(slot, period):
    lane = lax.broadcasted_iota(jnp.int32, (LANES, WIDTH), 0)
    feature = lax.broadcasted_iota(jnp.int32, (LANES, WIDTH), 1) // HEADDIM
    at = (lane < 2 * period) & (lane % period - feature == slot * HEADS)
    return jnp.where(at, 1.0, 0.0).astype(BF)


def two_parts(value, period):
    lane = lax.broadcasted_iota(jnp.int32, value.shape, 1)
    high = value.astype(BF).astype(F32)
    return jnp.where(lane < period, high, value - high).astype(BF)


def slot_total(value, period):
    shift = HEADS
    while shift < period:
        value = value + pltpu.roll(value, shift, 1)
        shift *= 2
    return value


def softmax_parts(scores, valid, period):
    bent = jnp.tanh(scores * (SCORE / CAP))
    weights = jnp.where(valid, jnp.exp(CAP * bent), 0.0)
    return bent, weights / slot_total(weights, period)


def softmax_back(bent, probs, grad, period):
    inner = probs * grad
    return (inner - probs * slot_total(inner, period)) * (1.0 - bent * bent) * SCORE


def tanner_valid(tokens):
    lane = lax.broadcasted_iota(jnp.int32, (tokens, LANES), 1)
    return lane % 64 < HEADS * (MONOS + 1)


def time_valid(tokens, rounds):
    lane = lax.broadcasted_iota(jnp.int32, (tokens, LANES), 1)
    row = lax.broadcasted_iota(jnp.int32, (tokens, LANES), 0)
    return (lane % 32) // HEADS <= row // (tokens // rounds)


def offset_of(offsets, index):
    return offsets[index, 0] if index in ALONG_ROWS else offsets[index, 1]


def neighbour(number, offsets, extended, columns):
    rounds, twice, width, features = extended.shape
    rows = twice // 2
    tokens = rounds * rows * width
    if number == 0:
        return extended[:, :rows].reshape(tokens, features)
    by = offset_of(offsets, number - 1)
    if number - 1 in ALONG_ROWS:
        return extended[:, pl.ds(by, rows)].reshape(tokens, features)
    own = extended[:, :rows].reshape(rounds * rows, width, features)
    place = lax.broadcasted_iota(jnp.int32, own.shape, 1)
    joined = jnp.where(place >= by, own, columns[...])
    return pltpu.roll(joined, width - by, 1).reshape(tokens, features)


def pack_kernel(tokens, syndrome, step, out, flips, steps, done):
    count = tokens.shape[0]
    rounds, rows, width = syndrome.shape
    moves = [
        pltpu.make_async_copy(tokens, out.at[pl.ds(0, count)], done.at[0]),
        pltpu.make_async_copy(syndrome, flips, done.at[1]),
        pltpu.make_async_copy(step, steps, done.at[2]),
    ]
    for move in moves:
        move.start()
    out[count:, :] = jnp.zeros((rounds * rows, WIDTH), BF)
    moves[1].wait()
    moves[2].wait()
    code = flips[...] * PLAN_STEP_COUNT + steps[...]
    out[count:, :width] = code.reshape(rounds * rows, width).astype(F32).astype(BF)
    moves[0].wait()


def start_kernel(width, packed, plan, flip, gain, *refs):
    count = (len(refs) - 5) // 2
    weights, (x_out, onehot_out, hidden_out, query_out, kv_out), flipped = refs[:count], refs[count : count + 5], refs[count + 5 :]
    w_query, w_key_value = weights[:2]
    for weight, out in zip(weights, flipped):
        out[...] = weight[...].T
    x, onehot = embed(packed[...], plan[...], flip[...], width)
    hidden = (x * inverse_rms(x) * gain[...]).astype(BF)
    x_out[...] = x
    onehot_out[...] = onehot
    hidden_out[...] = hidden
    query_out[...] = dot(hidden, w_query[...]).astype(BF)
    kv_out[...] = dot(hidden, w_key_value[...]).astype(BF)


def forward_kernel(
    offsets, x_in, query_in, kv_in, row_packed, col_packed, plan, flip,
    gain_tanner, w_key_value, w_merge, gain_time, w_temporal, w_temporal_out, gain_ffn, w_up, w_up_t, w_down_t, cotangent,
    keep, send, grad_time_out, tanner_out, mixed_one_out, mixed_two_out, packed_out, hidden_two_out,
    row_kv_out, col_kv_out, row_x_out, col_x_out, row_hidden_out, col_hidden_out, row_onehot_out, col_onehot_out,
    bent_one_out, probs_one_out, bent_two_out, probs_two_out, grad_gain_out,
    extended, columns, transposed, transposed_act,
):
    rounds, twice, width, features = extended.shape
    rows = twice // 2
    tokens = x_in.shape[0]
    core = my_bit(0)
    borrowed = []
    for other, x_out, hidden_out, onehot_out, kv_out in (
        (row_packed, row_x_out, row_hidden_out, row_onehot_out, row_kv_out),
        (col_packed, col_x_out, col_hidden_out, col_onehot_out, col_kv_out),
    ):
        x, onehot = embed(other[...], plan[...], flip[...], width)
        hidden = (x * inverse_rms(x) * gain_tanner[...]).astype(BF)
        kv = dot(hidden, w_key_value[...]).astype(BF)
        x_out[...] = x
        onehot_out[...] = onehot
        hidden_out[...] = hidden
        kv_out[...] = kv
        borrowed.append(kv.astype(F32))
    extended[:, :rows] = kv_in[...].astype(F32).reshape(rounds, rows, width, features)
    extended[:, rows:] = borrowed[0].reshape(rounds, rows, width, features)
    columns[...] = borrowed[1].reshape(rounds * rows, width, features)
    query = query_in[...].astype(F32)
    scores = None
    for number in range(MONOS + 1):
        keys = neighbour(number, offsets, extended, columns)[:, :WIDTH]
        part = dot((query * keys).astype(BF), gather_heads(number, 64))
        scores = part if scores is None else scores + part
    bent, probs = softmax_parts(scores, tanner_valid(tokens), 64)
    bent_one_out[...] = bent
    probs_one_out[...] = probs
    parts = two_parts(probs, 64)
    mixed = None
    for number in range(MONOS + 1):
        values = neighbour(number, offsets, extended, columns)[:, WIDTH:]
        part = dot(parts, spread_heads(number, 64)) * values
        mixed = part if mixed is None else mixed + part
    mixed_one = mixed.astype(BF)
    mixed_one_out[...] = mixed_one
    after_tanner = x_in[...] + dot(mixed_one, w_merge[...])
    tanner_out[...] = after_tanner

    hidden_two = (after_tanner * inverse_rms(after_tanner) * gain_time[...]).astype(BF)
    hidden_two_out[...] = hidden_two
    packed_low = dot(hidden_two, w_temporal[...]).astype(BF)
    packed_out[...] = packed_low
    packed = packed_low.astype(F32).reshape(rounds, tokens // rounds, 3 * WIDTH)
    sites = tokens // rounds
    scores = None
    for earlier in range(rounds):
        product = packed[earlier:, :, :WIDTH] * packed[earlier][None, :, WIDTH : 2 * WIDTH]
        part = dot(product.reshape(-1, WIDTH).astype(BF), gather_heads(earlier, 32))
        if earlier:
            part = jnp.concatenate([jnp.zeros((earlier * sites, LANES), F32), part], axis=0)
        scores = part if scores is None else scores + part
    bent, probs = softmax_parts(scores, time_valid(tokens, rounds), 32)
    bent_two_out[...] = bent
    probs_two_out[...] = probs
    parts = two_parts(probs, 32)
    mixed = None
    for earlier in range(rounds):
        weight = dot(parts[earlier * sites :], spread_heads(earlier, 32)).reshape(rounds - earlier, sites, WIDTH)
        part = (weight * packed[earlier][None, :, 2 * WIDTH :]).reshape(-1, WIDTH)
        if earlier:
            part = jnp.concatenate([jnp.zeros((earlier * sites, WIDTH), F32), part], axis=0)
        mixed = part if mixed is None else mixed + part
    mixed_two = mixed.astype(BF)
    mixed_two_out[...] = mixed_two
    after_time = after_tanner + dot(mixed_two, w_temporal_out[...])

    hidden = (after_time * inverse_rms(after_time) * gain_ffn[...]).astype(BF)
    outer = cotangent[...]
    transposed[...] = hidden.T
    grad_three = None
    befores = []
    for block in range(FF // WIDTH):
        cols = slice(block * WIDTH, (block + 1) * WIDTH)
        before = dot(hidden, w_up[:, cols])
        square = before * before
        bend = jnp.tanh(GELU_A * before * (1.0 + GELU_B * square))
        upper = 0.5 * (1.0 + bend)
        activated = (before * upper).astype(BF)
        slope = upper + 0.5 * before * (1.0 - bend * bend) * (GELU_A * (1.0 + 3.0 * GELU_B * square))
        grad_before = (dot(outer, w_down_t[:, cols]) * slope).astype(BF)
        befores.append(grad_before)
        part = dot(grad_before, w_up_t[cols, :])
        grad_three = part if grad_three is None else grad_three + part
        transposed_act[cols, :] = activated.T
    mine = pl.multiple_of(core * HALF, HALF)
    other = pl.multiple_of((1 - core) * HALF, HALF)
    blocks = FF // WIDTH
    lead = jnp.concatenate([transposed[pl.ds(start, HALF), :] for start in (mine, other)], axis=0)
    for block in range(blocks):
        product = dot(lead, befores[block]).astype(BF)
        keep[block * HALF : (block + 1) * HALF, :] = product[:HALF]
        send[block * HALF : (block + 1) * HALF, :] = product[HALF:]
    lead = jnp.concatenate(
        [transposed_act[pl.ds(block * WIDTH + start, HALF), :] for start in (mine, other) for block in range(blocks)],
        axis=0,
    )
    product = dot(lead, outer).astype(BF)
    keep[blocks * HALF :, :] = product[: blocks * HALF]
    send[blocks * HALF :, :] = product[blocks * HALF :]
    grad_norm, grad_gain = norm_back(after_time, gain_ffn[...], grad_three)
    grad_time_out[...] = outer.astype(F32) + grad_norm
    grad_gain_out[...] = grad_gain


def backward_kernel(
    offsets, grad_time_in, tanner_in, packed_in, query_in, kv_in, row_kv, col_kv,
    bent_one, probs_one, bent_two, probs_two, w_merge, gain_time, w_temporal, w_temporal_out,
    grad_query_out, grad_kv_out, grad_rows_out, grad_cols_out, grad_packed_out, grad_tanner_out, grad_gain_out,
    extended, columns, grad_extended,
):
    rounds, twice, width, features = extended.shape
    rows = twice // 2
    tokens = grad_time_in.shape[0]
    sites = tokens // rounds
    grad_time = grad_time_in[...]
    grad_mixed = dot(grad_time.astype(BF), w_temporal_out[...]).reshape(rounds, sites, WIDTH)
    packed = packed_in[...].astype(F32).reshape(rounds, sites, 3 * WIDTH)
    grad_probs = None
    for earlier in range(rounds):
        product = grad_mixed[earlier:] * packed[earlier][None, :, 2 * WIDTH :]
        part = dot(product.reshape(-1, WIDTH).astype(BF), gather_heads(earlier, 32))
        if earlier:
            part = jnp.concatenate([jnp.zeros((earlier * sites, LANES), F32), part], axis=0)
        grad_probs = part if grad_probs is None else grad_probs + part
    probs = probs_two[...]
    prob_parts = two_parts(probs, 32)
    score_parts = two_parts(softmax_back(bent_two[...], probs, grad_probs, 32), 32)
    grad_queries = None
    grad_keys = []
    grad_values = []
    for earlier in range(rounds):
        spread = spread_heads(earlier, 32)
        shape = (rounds - earlier, sites, WIDTH)
        weight = dot(prob_parts[earlier * sites :], spread).reshape(shape)
        slope = dot(score_parts[earlier * sites :], spread).reshape(shape)
        grad_values.append(jnp.sum(weight * grad_mixed[earlier:], axis=0))
        grad_keys.append(jnp.sum(slope * packed[earlier:, :, :WIDTH], axis=0))
        part = (slope * packed[earlier][None, :, WIDTH : 2 * WIDTH]).reshape(-1, WIDTH)
        if earlier:
            part = jnp.concatenate([jnp.zeros((earlier * sites, WIDTH), F32), part], axis=0)
        grad_queries = part if grad_queries is None else grad_queries + part
    grad_packed = jnp.concatenate(
        [grad_queries, jnp.concatenate(grad_keys, axis=0), jnp.concatenate(grad_values, axis=0)], axis=1
    ).astype(BF)
    grad_packed_out[...] = grad_packed
    grad_two = dot(grad_packed, w_temporal[...])
    grad_norm, grad_gain = norm_back(tanner_in[...], gain_time[...], grad_two)
    grad_gain_out[...] = grad_gain
    grad_tanner = grad_time + grad_norm
    grad_tanner_out[...] = grad_tanner

    grad_mixed = dot(grad_tanner.astype(BF), w_merge[...])
    extended[:, :rows] = kv_in[...].astype(F32).reshape(rounds, rows, width, features)
    extended[:, rows:] = row_kv[...].astype(F32).reshape(rounds, rows, width, features)
    columns[...] = col_kv[...].astype(F32).reshape(rounds * rows, width, features)
    grad_probs = None
    for number in range(MONOS + 1):
        values = neighbour(number, offsets, extended, columns)[:, WIDTH:]
        part = dot((grad_mixed * values).astype(BF), gather_heads(number, 64))
        grad_probs = part if grad_probs is None else grad_probs + part
    probs = probs_one[...]
    prob_parts = two_parts(probs, 64)
    score_parts = two_parts(softmax_back(bent_one[...], probs, grad_probs, 64), 64)
    query = query_in[...].astype(F32)
    grad_query = None
    grad_cols = None
    for number in (0,) + tuple(i + 1 for i in range(MONOS)):
        spread = spread_heads(number, 64)
        slope = dot(score_parts, spread)
        weight = dot(prob_parts, spread)
        keys = neighbour(number, offsets, extended, columns)[:, :WIDTH]
        part = slope * keys
        grad_query = part if grad_query is None else grad_query + part
        grad_kv = jnp.concatenate([slope * query, weight * grad_mixed], axis=1)
        if number == 0:
            grad_extended[:, :rows] = grad_kv.reshape(rounds, rows, width, features)
            grad_extended[:, rows:] = jnp.zeros((rounds, rows, width, features), F32)
            continue
        by = offset_of(offsets, number - 1)
        if number - 1 in ALONG_ROWS:
            grad_extended[:, pl.ds(by, rows)] += grad_kv.reshape(rounds, rows, width, features)
            continue
        moved = pltpu.roll(grad_kv.reshape(rounds * rows, width, features), by % width, 1)
        place = lax.broadcasted_iota(jnp.int32, moved.shape, 1)
        own = jnp.where(place >= by, moved, 0.0)
        grad_extended[:, :rows] += own.reshape(rounds, rows, width, features)
        grad_cols = moved - own if grad_cols is None else grad_cols + (moved - own)
    grad_query_out[...] = grad_query.astype(BF)
    grad_kv_out[...] = grad_extended[:, :rows].reshape(tokens, features).astype(BF)
    grad_rows_out[...] = grad_extended[:, rows:].reshape(tokens, features).astype(BF)
    grad_cols_out[...] = grad_cols.reshape(tokens, features).astype(BF)


def weights_kernel(
    mixed_two, grad_time, hidden_two, grad_packed, mixed_one, grad_tanner, grad_query, w_query, w_key_value, gain,
    x_own, x_row, x_col, hidden_own, hidden_row, hidden_col, onehot_own, onehot_row, onehot_col,
    grad_own, grad_row, grad_col, grad_gain_time, grad_gain_ffn,
    grad_out, row_out, col_out, keep, send, transposed, transposed_own,
):
    core = my_bit(0)
    tokens = x_own.shape[0]
    transposed[0] = hidden_two[...].T
    transposed[1] = mixed_two[...].T
    transposed[2] = mixed_one[...].T
    small = None
    grad_gain = None
    for number, (x, hidden, onehot, grad_kv, out) in enumerate((
        (x_own, hidden_own, onehot_own, grad_own, grad_out),
        (x_row, hidden_row, onehot_row, grad_row, row_out),
        (x_col, hidden_col, onehot_col, grad_col, col_out),
    )):
        transposed_own[:, number * tokens : (number + 1) * tokens] = hidden[...].T
        grad_one = dot(grad_kv[...], w_key_value[...])
        if number == 0:
            grad_one = grad_one + dot(grad_query[...], w_query[...])
        grad, part = norm_back(x[...], gain[...], grad_one)
        grad_gain = part if grad_gain is None else grad_gain + part
        if number == 0:
            grad = grad + grad_tanner[...]
        out[...] = grad.astype(out.dtype)
        high = grad.astype(BF)
        low = (grad - high.astype(F32)).astype(BF)
        part = dot(onehot[...], jnp.concatenate([high, low], axis=1), ((0,), (0,)))[:16]
        part = part[:, :WIDTH] + part[:, WIDTH:]
        small = part if small is None else small + part
    row = lax.broadcasted_iota(jnp.int32, small.shape, 0)
    small = jnp.where(row == 9, grad_gain, small)
    small = jnp.where(row == 10, grad_gain_time[...], small)
    small = jnp.where(row == 11, grad_gain_ffn[...], small).astype(BF)
    grad_time_low = grad_time[...].astype(BF)
    grad_tanner_low = grad_tanner[...].astype(BF)
    grad_all = jnp.concatenate([grad_own[...], grad_row[...], grad_col[...]], axis=0)
    mine = pl.ds(pl.multiple_of(core * HALF, HALF), HALF)
    other = pl.ds(pl.multiple_of((1 - core) * HALF, HALF), HALF)
    keep[:16, :] = small
    send[:16, :] = small
    pairs = [(transposed.at[0], grad_packed[:, block * WIDTH : (block + 1) * WIDTH]) for block in range(3)]
    pairs.append((transposed.at[1], grad_time_low))
    pairs.append((transposed.at[2], grad_tanner_low))
    pairs.append((transposed_own.at[:, pl.ds(0, tokens)], grad_query[...]))
    pairs += [(transposed_own, grad_all[:, block * WIDTH : (block + 1) * WIDTH]) for block in range(2)]
    for block, (lead, grad) in enumerate(pairs):
        product = dot(jnp.concatenate([lead[mine, :], lead[other, :]], axis=0), grad).astype(BF)
        rows = slice(16 + block * HALF, 16 + (block + 1) * HALF)
        keep[rows, :] = product[:HALF]
        send[rows, :] = product[HALF:]


def finish_kernel(grad, row, col, out):
    out[...] = (grad[...] + row[...].astype(F32) + col[...].astype(F32)).astype(BF)


def my_bit(bit):
    many = lax.axis_size("gy").bit_length() - 1
    if bit < many:
        return (lax.axis_index("gy") >> bit) & 1
    return (lax.axis_index("gx") >> (bit - many)) & 1


def split_kernel(extra, bit, kept, received, keep, send, total):
    mine = my_bit(bit)
    value = kept[...].astype(F32) + received[...].astype(F32)
    total[...] = value[extra:]
    rows = keep.shape[0] - extra
    for ref, which in ((keep, mine), (send, 1 - mine)):
        if extra:
            ref[:extra, :] = value[:extra].astype(BF)
        ref[extra:, :] = total[pl.ds(pl.multiple_of(which * rows, rows), rows), :].astype(BF)


def end_kernel(extra, scale, kept, received, out, *small):
    value = kept[...].astype(F32) + received[...].astype(F32)
    out[...] = value[extra:].astype(BF)
    if extra:
        value = value[:extra] * scale
        small[0][...] = value[:8]
        for number in range(4):
            small[1 + number][...] = value[8 + number : 9 + number]


def join_kernel(bit, own, received, out):
    mine = my_bit(bit)
    out[mine] = own[...]
    out[1 - mine] = received[...]


def unpack_kernel(blocks, scale, side, source, *refs):
    refs = refs[-2 * len(blocks) - 1 :]
    outs, wides, done = refs[: len(blocks)], refs[len(blocks) : -1], refs[-1]
    half = pl.multiple_of((my_bit(0) ^ side) * HALF, HALF)
    moves = []
    block = 0
    for out, wide, (down, across) in zip(outs, wides, blocks):
        for index in range(down * across):
            value = source[block * HALF : (block + 1) * HALF, :].astype(F32) * scale
            left = (index if across > 1 else 0) * WIDTH
            wide[index if down > 1 else 0, :, left : left + WIDTH] = value
            block += 1
        for index in range(down):
            target = out.at[pl.ds(index * WIDTH + half, HALF)]
            moves.append(pltpu.make_async_copy(wide.at[index], target, done.at[len(moves)]))
            moves[-1].start()
    for move in moves:
        move.wait()


def unpack(blocks, scale, side, source, partial):
    hbm = pl.BlockSpec(memory_space=pltpu.HBM)
    return pl.pallas_call(
        functools.partial(unpack_kernel, blocks, scale, side),
        out_shape=[jax.ShapeDtypeStruct((down * WIDTH, across * WIDTH), F32) for down, across in blocks],
        in_specs=[pl.BlockSpec(memory_space=pltpu.VMEM)] + [hbm] * len(partial),
        out_specs=[hbm] * len(blocks),
        scratch_shapes=[pltpu.VMEM((down, HALF, across * WIDTH), F32) for down, across in blocks]
        + [pltpu.SemaphoreType.DMA((sum(down for down, _ in blocks),))],
        input_output_aliases={1 + i: i for i in range(len(partial))},
        compiler_params=pltpu.CompilerParams(vmem_limit_bytes=16 * MIB),
    )(source, *partial)


def estimate(work, outs=(), args=()):
    moved = sum(math.prod(shape) * jnp.dtype(dtype).itemsize for shape, dtype in outs)
    moved += sum(math.prod(arg.shape) * arg.dtype.itemsize for arg in args)
    return pl.CostEstimate(flops=int(work * 1.1e9), transcendentals=0, bytes_accessed=moved)


def call(kernel, outs, args, scratch=(), smem=0, limit=16, work=0.1):
    vmem = pl.BlockSpec(memory_space=pltpu.VMEM)
    return pl.pallas_call(
        kernel,
        out_shape=[jax.ShapeDtypeStruct(shape, dtype) for shape, dtype in outs],
        in_specs=[pl.BlockSpec(memory_space=pltpu.SMEM)] * smem + [vmem] * (len(args) - smem),
        out_specs=[vmem] * len(outs),
        scratch_shapes=list(scratch),
        compiler_params=pltpu.CompilerParams(vmem_limit_bytes=limit * MIB),
        cost_estimate=estimate(work, outs, args),
    )(*args)


def shifted(x, axis, by):
    count = lax.axis_size(axis)
    return lax.ppermute(x, axis, [(i, (i + by) % count) for i in range(count)])


class Layout:
    def __init__(self):
        self.nx = lax.axis_size("gx")
        self.ny = lax.axis_size("gy")
        self.many = self.ny.bit_length() - 1
        self.bits = self.many + self.nx.bit_length() - 1
        assert 1 << self.bits == self.nx * self.ny

    def swap(self, x, bit):
        flip = 1 << bit if bit < self.many else self.ny << (bit - self.many)
        return lax.ppermute(x, ("gx", "gy"), [(i, i ^ flip) for i in range(self.nx * self.ny)])


def reduce_tree(layout, keep, send, extra, order, scale, first=0, until=None, beside=()):
    for stage in range(first, len(order) if until is None else until):
        received = layout.swap(send, order[stage])
        if stage == 2 and beside:
            received, *beside = lax.optimization_barrier((received, *beside))
        rows = keep.shape[0] - extra
        if stage + 1 < len(order):
            half = ((rows // 2 + extra, WIDTH), BF)
            keep, send = call(
                functools.partial(split_kernel, extra, order[stage + 1]),
                [half, half],
                [keep, received],
                [pltpu.VMEM((rows, WIDTH), F32)],
            )
    if until is not None:
        return keep, send
    small = [((8, WIDTH), F32)] + [((1, WIDTH), F32)] * 4 if extra else []
    outs = call(functools.partial(end_kernel, extra, scale), [((rows, WIDTH), BF)] + small, [keep, received])
    return (*outs, *beside)


def gather_tree(layout, own, order, blocks, scale, beside=()):
    for bit in order[:0:-1]:
        received = layout.swap(own, bit)
        if bit == order[1] and beside:
            received, *beside = lax.optimization_barrier((received, *beside))
        rows = own.shape[0]
        own = call(
            functools.partial(join_kernel, bit), [((2, rows, WIDTH), BF)], [own, received]
        )[0].reshape(2 * rows, WIDTH)
    other = layout.swap(own, order[0])
    outs = unpack(blocks, scale, 1, other, unpack(blocks, scale, 0, own, ()))
    return (*outs, *beside)


def on_device(
    tokens,
    syndrome,
    check_plan_step,
    offsets,
    flip_vector,
    plan_step_embedding,
    gain_tanner,
    w_query,
    w_key_value,
    w_merge,
    gain_time,
    w_temporal,
    w_temporal_out,
    gain_ffn,
    w_ffn_up,
    w_ffn_down,
    cotangent,
):
    layout = Layout()
    rounds, rows, cols = tokens.shape[:3]
    count = rounds * rows * cols
    scale = 1.0 / math.sqrt(count * layout.nx * layout.ny)
    flat = (count, WIDTH)
    act = (flat, BF)
    stream = (flat, F32)
    wide = ((count, 2 * WIDTH), BF)
    lanes = ((count, LANES), F32)
    onehot = ((count, LANES), BF)
    row = ((1, WIDTH), F32)
    hbm = pl.BlockSpec(memory_space=pltpu.HBM)

    sites = pltpu.VMEM((rounds, rows, cols), jnp.int32)
    packed_tokens = pl.pallas_call(
        pack_kernel,
        out_shape=jax.ShapeDtypeStruct((count + rounds * rows, WIDTH), BF),
        in_specs=[hbm] * 3,
        out_specs=pl.BlockSpec(memory_space=pltpu.VMEM),
        scratch_shapes=[sites, sites, pltpu.SemaphoreType.DMA((3,))],
        cost_estimate=estimate(12),
    )(tokens.reshape(flat), syndrome, check_plan_step)
    row_packed = shifted(packed_tokens, "gx", -1)
    col_packed = shifted(packed_tokens, "gy", -1)
    plan = plan_step_embedding
    flip = flip_vector.reshape(1, WIDTH)
    gain_one = gain_tanner.reshape(1, WIDTH)
    gain_two = gain_time.reshape(1, WIDTH)
    gain_three = gain_ffn.reshape(1, WIDTH)
    outer = cotangent.reshape(flat)
    weights = [w_query, w_key_value, w_merge, w_temporal, w_temporal_out, w_ffn_up, w_ffn_down]
    x, onehot_own, hidden_one, query, key_value, *flipped = call(
        functools.partial(start_kernel, cols),
        [stream, onehot, act, act, wide] + [(weight.shape[::-1], BF) for weight in weights],
        [packed_tokens, plan, flip, gain_one, *weights],

    )
    extended = pltpu.VMEM((rounds, 2 * rows, cols, 2 * WIDTH), F32)
    columns = pltpu.VMEM((rounds * rows, cols, 2 * WIDTH), F32)
    half_one = ((2 * (FF // WIDTH) * HALF, WIDTH), BF)
    (
        keep_one, send_one, grad_time, after_tanner, mixed_one, mixed_two, packed, hidden_two,
        row_kv, col_kv, row_x, col_x, row_hidden, col_hidden, row_onehot, col_onehot,
        bent_one, probs_one, bent_two, probs_two, grad_gain_ffn,
    ) = call(
        forward_kernel,
        [half_one, half_one, stream, stream, act, act, ((count, 3 * WIDTH), BF), act,
         wide, wide, stream, stream, act, act, onehot, onehot, lanes, lanes, lanes, lanes, row],
        [offsets, x, query, key_value, row_packed, col_packed, plan, flip,
         gain_one, w_key_value, w_merge, gain_two, w_temporal, w_temporal_out, gain_three, w_ffn_up, flipped[5], flipped[6],
         outer],
        [extended, columns, pltpu.VMEM((WIDTH, count), BF), pltpu.VMEM((FF, count), BF)],
        smem=1,
        limit=32,

    )
    grad_query, grad_kv, grad_rows, grad_cols, grad_packed, grad_tanner, grad_gain_time = call(
        backward_kernel,
        [act, wide, wide, wide, ((count, 3 * WIDTH), BF), stream, row],
        [offsets, grad_time, after_tanner, packed, query, key_value, row_kv, col_kv,
         bent_one, probs_one, bent_two, probs_two, flipped[2], gain_two, flipped[3], flipped[4]],
        [extended, columns, extended],
        smem=1,
        limit=32,
        work=3,
    )
    many, bits = layout.many, layout.bits
    order_one = list(range(many)) + list(range(many, bits))
    order_two = [0, many] + list(range(1, many)) + list(range(many + 1, bits))
    keep_one, send_one = reduce_tree(layout, keep_one, send_one, 0, order_one, scale, until=1)
    keep_one, grad_tanner = lax.optimization_barrier((keep_one, grad_tanner))
    half_two = ((16 + 8 * HALF, WIDTH), BF)
    grad_own, lent_rows, lent_cols, keep_two, send_two = call(
        weights_kernel,
        [stream, act, act, half_two, half_two],
        [mixed_two, grad_time, hidden_two, grad_packed, mixed_one, grad_tanner, grad_query, flipped[0], flipped[1],
         gain_one, x, row_x, col_x, hidden_one, row_hidden, col_hidden, onehot_own, row_onehot, col_onehot,
         grad_kv, grad_rows, grad_cols, grad_gain_time, grad_gain_ffn],
        [pltpu.VMEM((3, WIDTH, count), BF), pltpu.VMEM((WIDTH, 3 * count), BF)],
        limit=32,
        work=3,
    )
    back_rows = shifted(lent_rows, "gx", 1)
    back_cols = shifted(lent_cols, "gy", 1)
    shard_one, back_rows, back_cols = reduce_tree(
        layout, keep_one, send_one, 0, order_one, scale, first=1, beside=(back_rows, back_cols)
    )
    shard_two, plan_grad, grad_flip, sum_gain_tanner, sum_gain_time, sum_gain_ffn = reduce_tree(
        layout, keep_two, send_two, 16, order_two, scale
    )
    grad_up, grad_down = gather_tree(
        layout, shard_one, order_one, ((1, FF // WIDTH), (FF // WIDTH, 1)), scale
    )
    token_grad = call(finish_kernel, [act], [grad_own, back_rows, back_cols])[0]
    grad_temporal, grad_temporal_out, grad_merge, grad_w_query, grad_key_value = gather_tree(
        layout, shard_two, order_two, ((1, 3), (1, 1), (1, 1), (1, 1), (1, 2)), scale
    )
    return (
        token_grad.reshape(tokens.shape),
        grad_flip.reshape(WIDTH),
        plan_grad,
        sum_gain_tanner.reshape(WIDTH),
        grad_w_query,
        grad_key_value,
        grad_merge,
        sum_gain_time.reshape(WIDTH),
        grad_temporal,
        grad_temporal_out,
        sum_gain_ffn.reshape(WIDTH),
        grad_up,
        grad_down,
    )


def solution(mesh):
    tiled = P(None, "gx", "gy", None)
    sites = P(None, "gx", "gy")
    return jax.shard_map(
        on_device,
        mesh=mesh,
        in_specs=(tiled, sites, sites) + (P(),) * 13 + (tiled,),
        out_specs=(tiled,) + (P(),) * 12,
        check_vma=False,
    )
```

```python
import functools
import math

import jax
import jax.numpy as jnp
from jax import lax
from jax.experimental import pallas as pl
from jax.experimental.pallas import tpu as pltpu
from jax.sharding import PartitionSpec as P

WIDTH = 256
HEADDIM = 32
HEADS = WIDTH // HEADDIM
FF = 1024
PLAN_STEP_COUNT = 8
MONOS = 6
MAXEXP = 8
LANES = 128
HALF = WIDTH // 2

EPS = 1e-05
CAP = 4.0
ALONG_ROWS = (0, 4, 5)
BF = jnp.bfloat16
F32 = jnp.float32
SCORE = 1.0 / math.sqrt(HEADDIM)
GELU_A = math.sqrt(2.0 / math.pi)
GELU_B = 0.044715
MIB = 1 << 20


def dot(a, b, dims=((1,), (0,))):
    return lax.dot_general(a, b, (dims, ((), ())), preferred_element_type=F32)


def dot_nt(a, b):
    return dot(a, b, ((1,), (1,)))


def embed(packed, plan, flip, width):
    count = packed.shape[0]
    lines = count // (width + 1)
    tokens = lines * width
    codes = packed[tokens:, :LANES]
    token = lax.broadcasted_iota(jnp.int32, (tokens, lines), 0)
    line = lax.broadcasted_iota(jnp.int32, (tokens, lines), 1)
    spread = dot(jnp.where(token // width == line, 1.0, 0.0).astype(BF), codes)
    token = lax.broadcasted_iota(jnp.int32, (tokens, LANES), 0)
    lane = lax.broadcasted_iota(jnp.int32, (tokens, LANES), 1)
    picked = jnp.where(token % width == lane, spread, 0.0).astype(BF)
    code = dot(picked, jnp.ones((LANES, LANES), BF))
    flipped = code >= PLAN_STEP_COUNT
    step = jnp.where(flipped, code - PLAN_STEP_COUNT, code)
    slot = lane % 16
    chosen = (slot.astype(F32) == step) | ((slot == PLAN_STEP_COUNT) & flipped)
    onehot = jnp.where(chosen & (lane < 48), 1.0, 0.0).astype(BF)
    row = lax.broadcasted_iota(jnp.int32, (8, WIDTH), 0)
    table = jnp.concatenate([plan, jnp.where(row == 0, flip, 0.0)], axis=0)
    high = table.astype(BF)
    rest = table - high.astype(F32)
    middle = rest.astype(BF)
    low = (rest - middle.astype(F32)).astype(BF)
    empty = jnp.zeros((LANES - 48, WIDTH), BF)
    vectors = dot(onehot, jnp.concatenate([high, middle, low, empty], axis=0))
    return packed[:tokens].astype(F32) + vectors, onehot


def inverse_rms(stream):
    return lax.rsqrt(jnp.mean(stream * stream, axis=-1, keepdims=True) + EPS)


def norm_back(stream, gain, grad):
    inverse = inverse_rms(stream)
    normed = stream * inverse
    scaled = grad * gain
    mean = jnp.mean(scaled * normed, axis=-1, keepdims=True)
    return inverse * (scaled - normed * mean), jnp.sum(grad * normed, axis=0, keepdims=True)


def gather_heads(slot, period):
    feature = lax.broadcasted_iota(jnp.int32, (WIDTH, LANES), 0) // HEADDIM
    lane = lax.broadcasted_iota(jnp.int32, (WIDTH, LANES), 1) % period
    return jnp.where(lane - feature == slot * HEADS, 1.0, 0.0).astype(BF)


def spread_heads(slot, period):
    lane = lax.broadcasted_iota(jnp.int32, (LANES, WIDTH), 0)
    feature = lax.broadcasted_iota(jnp.int32, (LANES, WIDTH), 1) // HEADDIM
    at = (lane < 2 * period) & (lane % period - feature == slot * HEADS)
    return jnp.where(at, 1.0, 0.0).astype(BF)


def two_parts(value, period):
    lane = lax.broadcasted_iota(jnp.int32, value.shape, 1)
    high = value.astype(BF).astype(F32)
    return jnp.where(lane < period, high, value - high).astype(BF)


def slot_total(value, period):
    shift = HEADS
    while shift < period:
        value = value + pltpu.roll(value, shift, 1)
        shift *= 2
    return value


def softmax_parts(scores, valid, period):
    bent = jnp.tanh(scores * (SCORE / CAP))
    weights = jnp.where(valid, jnp.exp(CAP * bent), 0.0)
    return bent, weights / slot_total(weights, period)


def softmax_back(bent, probs, grad, period):
    inner = probs * grad
    return (inner - probs * slot_total(inner, period)) * (1.0 - bent * bent) * SCORE


def tanner_valid(tokens):
    lane = lax.broadcasted_iota(jnp.int32, (tokens, LANES), 1)
    return lane % 64 < HEADS * (MONOS + 1)


def time_valid(tokens, rounds):
    lane = lax.broadcasted_iota(jnp.int32, (tokens, LANES), 1)
    row = lax.broadcasted_iota(jnp.int32, (tokens, LANES), 0)
    return (lane % 32) // HEADS <= row // (tokens // rounds)


def offset_of(offsets, index):
    return offsets[index, 0] if index in ALONG_ROWS else offsets[index, 1]


def neighbour(number, offsets, extended, columns):
    rounds, twice, width, features = extended.shape
    rows = twice // 2
    tokens = rounds * rows * width
    if number == 0:
        return extended[:, :rows].reshape(tokens, features)
    by = offset_of(offsets, number - 1)
    if number - 1 in ALONG_ROWS:
        return extended[:, pl.ds(by, rows)].reshape(tokens, features)
    own = extended[:, :rows].reshape(rounds * rows, width, features)
    place = lax.broadcasted_iota(jnp.int32, own.shape, 1)
    joined = jnp.where(place >= by, own, columns[...])
    return pltpu.roll(joined, width - by, 1).reshape(tokens, features)


def pack_kernel(tokens, syndrome, step, out, flips, steps, done):
    count = tokens.shape[0]
    rounds, rows, width = syndrome.shape
    moves = [
        pltpu.make_async_copy(tokens, out.at[pl.ds(0, count)], done.at[0]),
        pltpu.make_async_copy(syndrome, flips, done.at[1]),
        pltpu.make_async_copy(step, steps, done.at[2]),
    ]
    for move in moves:
        move.start()
    out[count:, :] = jnp.zeros((rounds * rows, WIDTH), BF)
    moves[1].wait()
    moves[2].wait()
    code = flips[...] * PLAN_STEP_COUNT + steps[...]
    out[count:, :width] = code.reshape(rounds * rows, width).astype(F32).astype(BF)
    moves[0].wait()


def start_kernel(width, packed, plan, flip, gain, *refs):
    count = (len(refs) - 5) // 2
    weights, (x_out, onehot_out, hidden_out, query_out, kv_out), flipped = refs[:count], refs[count : count + 5], refs[count + 5 :]
    w_query, w_key_value = weights[:2]
    for weight, out in zip(weights, flipped):
        out[...] = weight[...].T
    x, onehot = embed(packed[...], plan[...], flip[...], width)
    hidden = (x * inverse_rms(x) * gain[...]).astype(BF)
    x_out[...] = x
    onehot_out[...] = onehot
    hidden_out[...] = hidden
    query_out[...] = dot(hidden, w_query[...]).astype(BF)
    kv_out[...] = dot(hidden, w_key_value[...]).astype(BF)


def forward_kernel(
    offsets, x_in, query_in, kv_in, row_packed, col_packed, plan, flip,
    gain_tanner, w_key_value, w_merge, gain_time, w_temporal, w_temporal_out, gain_ffn, w_up, w_up_t, w_down_t, cotangent,
    keep, send, grad_time_out, tanner_out, mixed_one_out, mixed_two_out, packed_out, hidden_two_out,
    row_kv_out, col_kv_out, row_x_out, col_x_out, row_hidden_out, col_hidden_out, row_onehot_out, col_onehot_out,
    bent_one_out, probs_one_out, bent_two_out, probs_two_out, grad_gain_out,
    extended, columns, transposed, transposed_act,
):
    rounds, twice, width, features = extended.shape
    rows = twice // 2
    tokens = x_in.shape[0]
    core = my_bit(0)
    borrowed = []
    for other, x_out, hidden_out, onehot_out, kv_out in (
        (row_packed, row_x_out, row_hidden_out, row_onehot_out, row_kv_out),
        (col_packed, col_x_out, col_hidden_out, col_onehot_out, col_kv_out),
    ):
        x, onehot = embed(other[...], plan[...], flip[...], width)
        hidden = (x * inverse_rms(x) * gain_tanner[...]).astype(BF)
        kv = dot(hidden, w_key_value[...]).astype(BF)
        x_out[...] = x
        onehot_out[...] = onehot
        hidden_out[...] = hidden
        kv_out[...] = kv
        borrowed.append(kv.astype(F32))
    extended[:, :rows] = kv_in[...].astype(F32).reshape(rounds, rows, width, features)
    extended[:, rows:] = borrowed[0].reshape(rounds, rows, width, features)
    columns[...] = borrowed[1].reshape(rounds * rows, width, features)
    query = query_in[...].astype(F32)
    scores = None
    for number in range(MONOS + 1):
        keys = neighbour(number, offsets, extended, columns)[:, :WIDTH]
        part = dot((query * keys).astype(BF), gather_heads(number, 64))
        scores = part if scores is None else scores + part
    bent, probs = softmax_parts(scores, tanner_valid(tokens), 64)
    bent_one_out[...] = bent
    probs_one_out[...] = probs
    parts = two_parts(probs, 64)
    mixed = None
    for number in range(MONOS + 1):
        values = neighbour(number, offsets, extended, columns)[:, WIDTH:]
        part = dot(parts, spread_heads(number, 64)) * values
        mixed = part if mixed is None else mixed + part
    mixed_one = mixed.astype(BF)
    mixed_one_out[...] = mixed_one
    after_tanner = x_in[...] + dot(mixed_one, w_merge[...])
    tanner_out[...] = after_tanner

    hidden_two = (after_tanner * inverse_rms(after_tanner) * gain_time[...]).astype(BF)
    hidden_two_out[...] = hidden_two
    packed_low = dot(hidden_two, w_temporal[...]).astype(BF)
    packed_out[...] = packed_low
    packed = packed_low.astype(F32).reshape(rounds, tokens // rounds, 3 * WIDTH)
    sites = tokens // rounds
    scores = None
    for earlier in range(rounds):
        product = packed[earlier:, :, :WIDTH] * packed[earlier][None, :, WIDTH : 2 * WIDTH]
        part = dot(product.reshape(-1, WIDTH).astype(BF), gather_heads(earlier, 32))
        if earlier:
            part = jnp.concatenate([jnp.zeros((earlier * sites, LANES), F32), part], axis=0)
        scores = part if scores is None else scores + part
    bent, probs = softmax_parts(scores, time_valid(tokens, rounds), 32)
    bent_two_out[...] = bent
    probs_two_out[...] = probs
    parts = two_parts(probs, 32)
    mixed = None
    for earlier in range(rounds):
        weight = dot(parts[earlier * sites :], spread_heads(earlier, 32)).reshape(rounds - earlier, sites, WIDTH)
        part = (weight * packed[earlier][None, :, 2 * WIDTH :]).reshape(-1, WIDTH)
        if earlier:
            part = jnp.concatenate([jnp.zeros((earlier * sites, WIDTH), F32), part], axis=0)
        mixed = part if mixed is None else mixed + part
    mixed_two = mixed.astype(BF)
    mixed_two_out[...] = mixed_two
    after_time = after_tanner + dot(mixed_two, w_temporal_out[...])

    hidden = (after_time * inverse_rms(after_time) * gain_ffn[...]).astype(BF)
    outer = cotangent[...]
    transposed[...] = hidden.T
    grad_three = None
    befores = []
    for block in range(FF // WIDTH):
        cols = slice(block * WIDTH, (block + 1) * WIDTH)
        before = dot(hidden, w_up[:, cols])
        square = before * before
        bend = jnp.tanh(GELU_A * before * (1.0 + GELU_B * square))
        upper = 0.5 * (1.0 + bend)
        activated = (before * upper).astype(BF)
        slope = upper + 0.5 * before * (1.0 - bend * bend) * (GELU_A * (1.0 + 3.0 * GELU_B * square))
        grad_before = (dot(outer, w_down_t[:, cols]) * slope).astype(BF)
        befores.append(grad_before)
        part = dot(grad_before, w_up_t[cols, :])
        grad_three = part if grad_three is None else grad_three + part
        transposed_act[cols, :] = activated.T
    mine = pl.multiple_of(core * HALF, HALF)
    other = pl.multiple_of((1 - core) * HALF, HALF)
    blocks = FF // WIDTH
    lead = jnp.concatenate([transposed[pl.ds(start, HALF), :] for start in (mine, other)], axis=0)
    for block in range(blocks):
        product = dot(lead, befores[block]).astype(BF)
        keep[block * HALF : (block + 1) * HALF, :] = product[:HALF]
        send[block * HALF : (block + 1) * HALF, :] = product[HALF:]
    lead = jnp.concatenate(
        [transposed_act[pl.ds(block * WIDTH + start, HALF), :] for start in (mine, other) for block in range(blocks)],
        axis=0,
    )
    product = dot(lead, outer).astype(BF)
    keep[blocks * HALF :, :] = product[: blocks * HALF]
    send[blocks * HALF :, :] = product[blocks * HALF :]
    grad_norm, grad_gain = norm_back(after_time, gain_ffn[...], grad_three)
    grad_time_out[...] = outer.astype(F32) + grad_norm
    grad_gain_out[...] = grad_gain


def backward_kernel(
    offsets, grad_time_in, tanner_in, packed_in, query_in, kv_in, row_kv, col_kv,
    bent_one, probs_one, bent_two, probs_two, w_merge, gain_time, w_temporal, w_temporal_out,
    grad_query_out, grad_kv_out, grad_rows_out, grad_cols_out, grad_packed_out, grad_tanner_out, grad_gain_out,
    extended, columns, grad_extended,
):
    rounds, twice, width, features = extended.shape
    rows = twice // 2
    tokens = grad_time_in.shape[0]
    sites = tokens // rounds
    grad_time = grad_time_in[...]
    grad_mixed = dot(grad_time.astype(BF), w_temporal_out[...]).reshape(rounds, sites, WIDTH)
    packed = packed_in[...].astype(F32).reshape(rounds, sites, 3 * WIDTH)
    grad_probs = None
    for earlier in range(rounds):
        product = grad_mixed[earlier:] * packed[earlier][None, :, 2 * WIDTH :]
        part = dot(product.reshape(-1, WIDTH).astype(BF), gather_heads(earlier, 32))
        if earlier:
            part = jnp.concatenate([jnp.zeros((earlier * sites, LANES), F32), part], axis=0)
        grad_probs = part if grad_probs is None else grad_probs + part
    probs = probs_two[...]
    prob_parts = two_parts(probs, 32)
    score_parts = two_parts(softmax_back(bent_two[...], probs, grad_probs, 32), 32)
    grad_queries = None
    grad_keys = []
    grad_values = []
    for earlier in range(rounds):
        spread = spread_heads(earlier, 32)
        shape = (rounds - earlier, sites, WIDTH)
        weight = dot(prob_parts[earlier * sites :], spread).reshape(shape)
        slope = dot(score_parts[earlier * sites :], spread).reshape(shape)
        grad_values.append(jnp.sum(weight * grad_mixed[earlier:], axis=0))
        grad_keys.append(jnp.sum(slope * packed[earlier:, :, :WIDTH], axis=0))
        part = (slope * packed[earlier][None, :, WIDTH : 2 * WIDTH]).reshape(-1, WIDTH)
        if earlier:
            part = jnp.concatenate([jnp.zeros((earlier * sites, WIDTH), F32), part], axis=0)
        grad_queries = part if grad_queries is None else grad_queries + part
    grad_packed = jnp.concatenate(
        [grad_queries, jnp.concatenate(grad_keys, axis=0), jnp.concatenate(grad_values, axis=0)], axis=1
    ).astype(BF)
    grad_packed_out[...] = grad_packed
    grad_two = dot(grad_packed, w_temporal[...])
    grad_norm, grad_gain = norm_back(tanner_in[...], gain_time[...], grad_two)
    grad_gain_out[...] = grad_gain
    grad_tanner = grad_time + grad_norm
    grad_tanner_out[...] = grad_tanner

    grad_mixed = dot(grad_tanner.astype(BF), w_merge[...])
    extended[:, :rows] = kv_in[...].astype(F32).reshape(rounds, rows, width, features)
    extended[:, rows:] = row_kv[...].astype(F32).reshape(rounds, rows, width, features)
    columns[...] = col_kv[...].astype(F32).reshape(rounds * rows, width, features)
    grad_probs = None
    for number in range(MONOS + 1):
        values = neighbour(number, offsets, extended, columns)[:, WIDTH:]
        part = dot((grad_mixed * values).astype(BF), gather_heads(number, 64))
        grad_probs = part if grad_probs is None else grad_probs + part
    probs = probs_one[...]
    prob_parts = two_parts(probs, 64)
    score_parts = two_parts(softmax_back(bent_one[...], probs, grad_probs, 64), 64)
    query = query_in[...].astype(F32)
    grad_query = None
    grad_cols = None
    for number in (0,) + tuple(i + 1 for i in range(MONOS)):
        spread = spread_heads(number, 64)
        slope = dot(score_parts, spread)
        weight = dot(prob_parts, spread)
        keys = neighbour(number, offsets, extended, columns)[:, :WIDTH]
        part = slope * keys
        grad_query = part if grad_query is None else grad_query + part
        grad_kv = jnp.concatenate([slope * query, weight * grad_mixed], axis=1)
        if number == 0:
            grad_extended[:, :rows] = grad_kv.reshape(rounds, rows, width, features)
            grad_extended[:, rows:] = jnp.zeros((rounds, rows, width, features), F32)
            continue
        by = offset_of(offsets, number - 1)
        if number - 1 in ALONG_ROWS:
            grad_extended[:, pl.ds(by, rows)] += grad_kv.reshape(rounds, rows, width, features)
            continue
        moved = pltpu.roll(grad_kv.reshape(rounds * rows, width, features), by % width, 1)
        place = lax.broadcasted_iota(jnp.int32, moved.shape, 1)
        own = jnp.where(place >= by, moved, 0.0)
        grad_extended[:, :rows] += own.reshape(rounds, rows, width, features)
        grad_cols = moved - own if grad_cols is None else grad_cols + (moved - own)
    grad_query_out[...] = grad_query.astype(BF)
    grad_kv_out[...] = grad_extended[:, :rows].reshape(tokens, features).astype(BF)
    grad_rows_out[...] = grad_extended[:, rows:].reshape(tokens, features).astype(BF)
    grad_cols_out[...] = grad_cols.reshape(tokens, features).astype(BF)


def weights_kernel(
    mixed_two, grad_time, hidden_two, grad_packed, mixed_one, grad_tanner, grad_query, w_query, w_key_value, gain,
    x_own, x_row, x_col, hidden_own, hidden_row, hidden_col, onehot_own, onehot_row, onehot_col,
    grad_own, grad_row, grad_col, grad_gain_time, grad_gain_ffn,
    grad_out, row_out, col_out, keep, send, transposed, transposed_own,
):
    core = my_bit(0)
    tokens = x_own.shape[0]
    transposed[0] = hidden_two[...].T
    transposed[1] = mixed_two[...].T
    transposed[2] = mixed_one[...].T
    small = None
    grad_gain = None
    for number, (x, hidden, onehot, grad_kv, out) in enumerate((
        (x_own, hidden_own, onehot_own, grad_own, grad_out),
        (x_row, hidden_row, onehot_row, grad_row, row_out),
        (x_col, hidden_col, onehot_col, grad_col, col_out),
    )):
        transposed_own[:, number * tokens : (number + 1) * tokens] = hidden[...].T
        grad_one = dot(grad_kv[...], w_key_value[...])
        if number == 0:
            grad_one = grad_one + dot(grad_query[...], w_query[...])
        grad, part = norm_back(x[...], gain[...], grad_one)
        grad_gain = part if grad_gain is None else grad_gain + part
        if number == 0:
            grad = grad + grad_tanner[...]
        out[...] = grad.astype(out.dtype)
        high = grad.astype(BF)
        low = (grad - high.astype(F32)).astype(BF)
        part = dot(onehot[...], jnp.concatenate([high, low], axis=1), ((0,), (0,)))[:16]
        part = part[:, :WIDTH] + part[:, WIDTH:]
        small = part if small is None else small + part
    row = lax.broadcasted_iota(jnp.int32, small.shape, 0)
    small = jnp.where(row == 9, grad_gain, small)
    small = jnp.where(row == 10, grad_gain_time[...], small)
    small = jnp.where(row == 11, grad_gain_ffn[...], small).astype(BF)
    grad_time_low = grad_time[...].astype(BF)
    grad_tanner_low = grad_tanner[...].astype(BF)
    grad_all = jnp.concatenate([grad_own[...], grad_row[...], grad_col[...]], axis=0)
    mine = pl.ds(pl.multiple_of(core * HALF, HALF), HALF)
    other = pl.ds(pl.multiple_of((1 - core) * HALF, HALF), HALF)
    keep[:16, :] = small
    send[:16, :] = small
    pairs = [(transposed.at[0], grad_packed[:, block * WIDTH : (block + 1) * WIDTH]) for block in range(3)]
    pairs.append((transposed.at[1], grad_time_low))
    pairs.append((transposed.at[2], grad_tanner_low))
    pairs.append((transposed_own.at[:, pl.ds(0, tokens)], grad_query[...]))
    pairs += [(transposed_own, grad_all[:, block * WIDTH : (block + 1) * WIDTH]) for block in range(2)]
    for block, (lead, grad) in enumerate(pairs):
        product = dot(jnp.concatenate([lead[mine, :], lead[other, :]], axis=0), grad).astype(BF)
        rows = slice(16 + block * HALF, 16 + (block + 1) * HALF)
        keep[rows, :] = product[:HALF]
        send[rows, :] = product[HALF:]


def my_bit(bit):
    many = lax.axis_size("gy").bit_length() - 1
    if bit < many:
        return (lax.axis_index("gy") >> bit) & 1
    return (lax.axis_index("gx") >> (bit - many)) & 1


def split_kernel(extra, bit, kept, received, keep, send, total):
    mine = my_bit(bit)
    value = kept[...].astype(F32) + received[...].astype(F32)
    total[...] = value[extra:]
    rows = keep.shape[0] - extra
    for ref, which in ((keep, mine), (send, 1 - mine)):
        if extra:
            ref[:extra, :] = value[:extra].astype(BF)
        ref[extra:, :] = total[pl.ds(pl.multiple_of(which * rows, rows), rows), :].astype(BF)


def sum_kernel(first, second, out):
    out[...] = (first[...].astype(F32) + second[...].astype(F32)).astype(BF)


def end_kernel(extra, scale, kept, received, out, *small):
    value = kept[...].astype(F32) + received[...].astype(F32)
    out[...] = value[extra:].astype(BF)
    if extra:
        value = value[:extra] * scale
        small[0][...] = value[:8]
        for number in range(4):
            small[1 + number][...] = value[8 + number : 9 + number]


def join_kernel(bit, own, received, out):
    mine = my_bit(bit)
    out[mine] = own[...]
    out[1 - mine] = received[...]


def unpack_kernel(groups, scale, grad, row, col, *refs):
    sources, refs = refs[: 2 * len(groups)], refs[2 * len(groups) :]
    token_out, *outs = refs[: len(refs) // 2]
    token_low, *wides = refs[len(refs) // 2 : -1]
    done = refs[-1]
    moves = []

    def move(source, target):
        moves.append(pltpu.make_async_copy(source, target, done.at[len(moves)]))
        moves[-1].start()

    for number, blocks in enumerate(groups):
        for side in range(2):
            source = sources[2 * number + side]
            half = pl.multiple_of((my_bit(0) ^ side) * HALF, HALF)
            block = 0
            first = sum(len(group) for group in groups[:number])
            for out, wide, (down, across) in zip(outs[first:], wides[first:], blocks):
                for index in range(down * across):
                    value = source[block * HALF : (block + 1) * HALF, :].astype(F32) * scale
                    left = (index if across > 1 else 0) * WIDTH
                    wide[side, index if down > 1 else 0, :, left : left + WIDTH] = value
                    block += 1
                for index in range(down):
                    move(wide.at[side, index], out.at[pl.ds(index * WIDTH + half, HALF)])
    token_low[...] = (grad[...] + row[...].astype(F32) + col[...].astype(F32)).astype(BF)
    move(token_low, token_out)
    for one in moves:
        one.wait()


def unpack(groups, scale, sources, grad, row, col):
    hbm = pl.BlockSpec(memory_space=pltpu.HBM)
    blocks = [block for group in groups for block in group]
    return pl.pallas_call(
        functools.partial(unpack_kernel, groups, scale),
        out_shape=[jax.ShapeDtypeStruct(grad.shape, BF)]
        + [jax.ShapeDtypeStruct((down * WIDTH, across * WIDTH), F32) for down, across in blocks],
        in_specs=[pl.BlockSpec(memory_space=pltpu.VMEM)] * (3 + len(sources)),
        out_specs=[hbm] * (1 + len(blocks)),
        scratch_shapes=[pltpu.VMEM(grad.shape, BF)]
        + [pltpu.VMEM((2, down, HALF, across * WIDTH), F32) for down, across in blocks]
        + [pltpu.SemaphoreType.DMA((1 + 2 * sum(down for down, _ in blocks),))],
        compiler_params=pltpu.CompilerParams(vmem_limit_bytes=16 * MIB),
    )(grad, row, col, *sources)


def estimate(work, outs=(), args=()):
    moved = sum(math.prod(shape) * jnp.dtype(dtype).itemsize for shape, dtype in outs)
    moved += sum(math.prod(arg.shape) * arg.dtype.itemsize for arg in args)
    return pl.CostEstimate(flops=int(work * 1.1e9), transcendentals=0, bytes_accessed=moved)


def call(kernel, outs, args, scratch=(), smem=0, limit=16, work=0.1):
    vmem = pl.BlockSpec(memory_space=pltpu.VMEM)
    return pl.pallas_call(
        kernel,
        out_shape=[jax.ShapeDtypeStruct(shape, dtype) for shape, dtype in outs],
        in_specs=[pl.BlockSpec(memory_space=pltpu.SMEM)] * smem + [vmem] * (len(args) - smem),
        out_specs=[vmem] * len(outs),
        scratch_shapes=list(scratch),
        compiler_params=pltpu.CompilerParams(vmem_limit_bytes=limit * MIB),
        cost_estimate=estimate(work, outs, args),
    )(*args)


def shifted(x, axis, by):
    count = lax.axis_size(axis)
    return lax.ppermute(x, axis, [(i, (i + by) % count) for i in range(count)])


class Layout:
    def __init__(self):
        self.nx = lax.axis_size("gx")
        self.ny = lax.axis_size("gy")
        self.many = self.ny.bit_length() - 1
        self.bits = self.many + self.nx.bit_length() - 1
        assert 1 << self.bits == self.nx * self.ny

    def swap(self, x, bit):
        flip = 1 << bit if bit < self.many else self.ny << (bit - self.many)
        return lax.ppermute(x, ("gx", "gy"), [(i, i ^ flip) for i in range(self.nx * self.ny)])


def reduce_tree(layout, keep, send, extra, order, scale, first=0, until=None, beside=()):
    halving = order[:-1]
    for stage in range(first, len(halving) if until is None else until):
        received = layout.swap(send, halving[stage])
        if stage == 2 and beside:
            received, *beside = lax.optimization_barrier((received, *beside))
        rows = keep.shape[0] - extra
        if stage + 1 < len(halving):
            half = ((rows // 2 + extra, WIDTH), BF)
            keep, send = call(
                functools.partial(split_kernel, extra, halving[stage + 1]),
                [half, half],
                [keep, received],
                [pltpu.VMEM((rows, WIDTH), F32)],
            )
    if until is not None:
        return keep, send
    total = call(sum_kernel, [(keep.shape, BF)], [keep, received])[0]
    received = layout.swap(total, order[-1])
    small = [((8, WIDTH), F32)] + [((1, WIDTH), F32)] * 4 if extra else []
    outs = call(functools.partial(end_kernel, extra, scale), [((rows, WIDTH), BF)] + small, [total, received])
    return (*outs, *beside)


def gather_tree(layout, own, order):
    for bit in order[-2:0:-1]:
        received = layout.swap(own, bit)
        rows = own.shape[0]
        own = call(
            functools.partial(join_kernel, bit), [((2, rows, WIDTH), BF)], [own, received]
        )[0].reshape(2 * rows, WIDTH)
    return own, layout.swap(own, order[0])


def on_device(
    tokens,
    syndrome,
    check_plan_step,
    offsets,
    flip_vector,
    plan_step_embedding,
    gain_tanner,
    w_query,
    w_key_value,
    w_merge,
    gain_time,
    w_temporal,
    w_temporal_out,
    gain_ffn,
    w_ffn_up,
    w_ffn_down,
    cotangent,
):
    layout = Layout()
    rounds, rows, cols = tokens.shape[:3]
    count = rounds * rows * cols
    scale = 1.0 / math.sqrt(count * layout.nx * layout.ny)
    flat = (count, WIDTH)
    act = (flat, BF)
    stream = (flat, F32)
    wide = ((count, 2 * WIDTH), BF)
    lanes = ((count, LANES), F32)
    onehot = ((count, LANES), BF)
    row = ((1, WIDTH), F32)
    hbm = pl.BlockSpec(memory_space=pltpu.HBM)

    sites = pltpu.VMEM((rounds, rows, cols), jnp.int32)
    packed_tokens = pl.pallas_call(
        pack_kernel,
        out_shape=jax.ShapeDtypeStruct((count + rounds * rows, WIDTH), BF),
        in_specs=[hbm] * 3,
        out_specs=pl.BlockSpec(memory_space=pltpu.VMEM),
        scratch_shapes=[sites, sites, pltpu.SemaphoreType.DMA((3,))],
        cost_estimate=estimate(12),
    )(tokens.reshape(flat), syndrome, check_plan_step)
    row_packed = shifted(packed_tokens, "gx", -1)
    col_packed = shifted(packed_tokens, "gy", -1)
    plan = plan_step_embedding
    flip = flip_vector.reshape(1, WIDTH)
    gain_one = gain_tanner.reshape(1, WIDTH)
    gain_two = gain_time.reshape(1, WIDTH)
    gain_three = gain_ffn.reshape(1, WIDTH)
    outer = cotangent.reshape(flat)
    weights = [w_query, w_key_value, w_merge, w_temporal, w_temporal_out, w_ffn_up, w_ffn_down]
    x, onehot_own, hidden_one, query, key_value, *flipped = call(
        functools.partial(start_kernel, cols),
        [stream, onehot, act, act, wide] + [(weight.shape[::-1], BF) for weight in weights],
        [packed_tokens, plan, flip, gain_one, *weights],

    )
    extended = pltpu.VMEM((rounds, 2 * rows, cols, 2 * WIDTH), F32)
    columns = pltpu.VMEM((rounds * rows, cols, 2 * WIDTH), F32)
    half_one = ((2 * (FF // WIDTH) * HALF, WIDTH), BF)
    (
        keep_one, send_one, grad_time, after_tanner, mixed_one, mixed_two, packed, hidden_two,
        row_kv, col_kv, row_x, col_x, row_hidden, col_hidden, row_onehot, col_onehot,
        bent_one, probs_one, bent_two, probs_two, grad_gain_ffn,
    ) = call(
        forward_kernel,
        [half_one, half_one, stream, stream, act, act, ((count, 3 * WIDTH), BF), act,
         wide, wide, stream, stream, act, act, onehot, onehot, lanes, lanes, lanes, lanes, row],
        [offsets, x, query, key_value, row_packed, col_packed, plan, flip,
         gain_one, w_key_value, w_merge, gain_two, w_temporal, w_temporal_out, gain_three, w_ffn_up, flipped[5], flipped[6],
         outer],
        [extended, columns, pltpu.VMEM((WIDTH, count), BF), pltpu.VMEM((FF, count), BF)],
        smem=1,
        limit=32,

    )
    grad_query, grad_kv, grad_rows, grad_cols, grad_packed, grad_tanner, grad_gain_time = call(
        backward_kernel,
        [act, wide, wide, wide, ((count, 3 * WIDTH), BF), stream, row],
        [offsets, grad_time, after_tanner, packed, query, key_value, row_kv, col_kv,
         bent_one, probs_one, bent_two, probs_two, flipped[2], gain_two, flipped[3], flipped[4]],
        [extended, columns, extended],
        smem=1,
        limit=32,
        work=3,
    )
    many, bits = layout.many, layout.bits
    order_one = list(range(many)) + list(range(many, bits))
    order_two = [0, many] + list(range(1, many)) + list(range(many + 1, bits))
    keep_one, send_one = reduce_tree(layout, keep_one, send_one, 0, order_one, scale, until=1)
    keep_one, grad_tanner = lax.optimization_barrier((keep_one, grad_tanner))
    half_two = ((16 + 8 * HALF, WIDTH), BF)
    grad_own, lent_rows, lent_cols, keep_two, send_two = call(
        weights_kernel,
        [stream, act, act, half_two, half_two],
        [mixed_two, grad_time, hidden_two, grad_packed, mixed_one, grad_tanner, grad_query, flipped[0], flipped[1],
         gain_one, x, row_x, col_x, hidden_one, row_hidden, col_hidden, onehot_own, row_onehot, col_onehot,
         grad_kv, grad_rows, grad_cols, grad_gain_time, grad_gain_ffn],
        [pltpu.VMEM((3, WIDTH, count), BF), pltpu.VMEM((WIDTH, 3 * count), BF)],
        limit=32,
        work=3,
    )
    back_rows = shifted(lent_rows, "gx", 1)
    back_cols = shifted(lent_cols, "gy", 1)
    shard_one, back_rows, back_cols = reduce_tree(
        layout, keep_one, send_one, 0, order_one, scale, first=1, beside=(back_rows, back_cols)
    )
    shard_two, plan_grad, grad_flip, sum_gain_tanner, sum_gain_time, sum_gain_ffn = reduce_tree(
        layout, keep_two, send_two, 16, order_two, scale
    )
    sources = [*gather_tree(layout, shard_one, order_one), *gather_tree(layout, shard_two, order_two)]
    groups = (((1, FF // WIDTH), (FF // WIDTH, 1)), ((1, 3), (1, 1), (1, 1), (1, 1), (1, 2)))
    (
        token_grad, grad_up, grad_down, grad_temporal, grad_temporal_out, grad_merge, grad_w_query, grad_key_value,
    ) = unpack(groups, scale, sources, grad_own, back_rows, back_cols)
    return (
        token_grad.reshape(tokens.shape),
        grad_flip.reshape(WIDTH),
        plan_grad,
        sum_gain_tanner.reshape(WIDTH),
        grad_w_query,
        grad_key_value,
        grad_merge,
        sum_gain_time.reshape(WIDTH),
        grad_temporal,
        grad_temporal_out,
        sum_gain_ffn.reshape(WIDTH),
        grad_up,
        grad_down,
    )


def solution(mesh):
    tiled = P(None, "gx", "gy", None)
    sites = P(None, "gx", "gy")
    return jax.shard_map(
        on_device,
        mesh=mesh,
        in_specs=(tiled, sites, sites) + (P(),) * 13 + (tiled,),
        out_specs=(tiled,) + (P(),) * 12,
        check_vma=False,
    )
```

```python
import functools
import math

import jax
import jax.numpy as jnp
from jax import lax
from jax.experimental import pallas as pl
from jax.experimental.pallas import tpu as pltpu
from jax.sharding import PartitionSpec as P

WIDTH = 256
HEADDIM = 32
HEADS = WIDTH // HEADDIM
FF = 1024
PLAN_STEP_COUNT = 8
MONOS = 6
MAXEXP = 8
LANES = 128
HALF = WIDTH // 2

EPS = 1e-05
CAP = 4.0
ALONG_ROWS = (0, 4, 5)
BF = jnp.bfloat16
F32 = jnp.float32
SCORE = 1.0 / math.sqrt(HEADDIM)
GELU_A = math.sqrt(2.0 / math.pi)
GELU_B = 0.044715
MIB = 1 << 20


def dot(a, b, dims=((1,), (0,))):
    return lax.dot_general(a, b, (dims, ((), ())), preferred_element_type=F32)


def dot_nt(a, b):
    return dot(a, b, ((1,), (1,)))


def embed(values, codes, plan, flip):
    tokens = values.shape[0]
    lines = codes.shape[0]
    width = tokens // lines
    token = lax.broadcasted_iota(jnp.int32, (tokens, lines), 0)
    line = lax.broadcasted_iota(jnp.int32, (tokens, lines), 1)
    spread = dot(jnp.where(token // width == line, 1.0, 0.0).astype(BF), codes)
    token = lax.broadcasted_iota(jnp.int32, (tokens, LANES), 0)
    lane = lax.broadcasted_iota(jnp.int32, (tokens, LANES), 1)
    picked = jnp.where(token % width == lane, spread, 0.0).astype(BF)
    code = dot(picked, jnp.ones((LANES, LANES), BF))
    flipped = code >= PLAN_STEP_COUNT
    step = jnp.where(flipped, code - PLAN_STEP_COUNT, code)
    slot = lane % 16
    chosen = (slot.astype(F32) == step) | ((slot == PLAN_STEP_COUNT) & flipped)
    onehot = jnp.where(chosen & (lane < 48), 1.0, 0.0).astype(BF)
    row = lax.broadcasted_iota(jnp.int32, (8, WIDTH), 0)
    table = jnp.concatenate([plan, jnp.where(row == 0, flip, 0.0)], axis=0)
    high = table.astype(BF)
    rest = table - high.astype(F32)
    middle = rest.astype(BF)
    low = (rest - middle.astype(F32)).astype(BF)
    empty = jnp.zeros((LANES - 48, WIDTH), BF)
    vectors = dot(onehot, jnp.concatenate([high, middle, low, empty], axis=0))
    return values.astype(F32) + vectors, onehot


def inverse_rms(stream):
    return lax.rsqrt(jnp.mean(stream * stream, axis=-1, keepdims=True) + EPS)


def norm_back(stream, gain, grad):
    inverse = inverse_rms(stream)
    normed = stream * inverse
    scaled = grad * gain
    mean = jnp.mean(scaled * normed, axis=-1, keepdims=True)
    return inverse * (scaled - normed * mean), jnp.sum(grad * normed, axis=0, keepdims=True)


def gather_heads(slot, period):
    feature = lax.broadcasted_iota(jnp.int32, (WIDTH, LANES), 0) // HEADDIM
    lane = lax.broadcasted_iota(jnp.int32, (WIDTH, LANES), 1) % period
    return jnp.where(lane - feature == slot * HEADS, 1.0, 0.0).astype(BF)


def spread_heads(slot, period):
    lane = lax.broadcasted_iota(jnp.int32, (LANES, WIDTH), 0)
    feature = lax.broadcasted_iota(jnp.int32, (LANES, WIDTH), 1) // HEADDIM
    at = (lane < 2 * period) & (lane % period - feature == slot * HEADS)
    return jnp.where(at, 1.0, 0.0).astype(BF)


def two_parts(value, period):
    lane = lax.broadcasted_iota(jnp.int32, value.shape, 1)
    high = value.astype(BF).astype(F32)
    return jnp.where(lane < period, high, value - high).astype(BF)


def slot_total(value, period):
    shift = HEADS
    while shift < period:
        value = value + pltpu.roll(value, shift, 1)
        shift *= 2
    return value


def softmax_parts(scores, valid, period):
    bent = jnp.tanh(scores * (SCORE / CAP))
    weights = jnp.where(valid, jnp.exp(CAP * bent), 0.0)
    return bent, weights / slot_total(weights, period)


def softmax_back(bent, probs, grad, period):
    inner = probs * grad
    return (inner - probs * slot_total(inner, period)) * (1.0 - bent * bent) * SCORE


def tanner_valid(tokens):
    lane = lax.broadcasted_iota(jnp.int32, (tokens, LANES), 1)
    return lane % 64 < HEADS * (MONOS + 1)


def time_valid(tokens, rounds):
    lane = lax.broadcasted_iota(jnp.int32, (tokens, LANES), 1)
    row = lax.broadcasted_iota(jnp.int32, (tokens, LANES), 0)
    return (lane % 32) // HEADS <= row // (tokens // rounds)


def offset_of(offsets, index):
    return offsets[index, 0] if index in ALONG_ROWS else offsets[index, 1]


def neighbour(number, offsets, extended, columns):
    rounds, twice, width, features = extended.shape
    rows = twice // 2
    tokens = rounds * rows * width
    if number == 0:
        return extended[:, :rows].reshape(tokens, features)
    by = offset_of(offsets, number - 1)
    if number - 1 in ALONG_ROWS:
        return extended[:, pl.ds(by, rows)].reshape(tokens, features)
    own = extended[:, :rows].reshape(rounds * rows, width, features)
    place = lax.broadcasted_iota(jnp.int32, own.shape, 1)
    joined = jnp.where(place >= by, own, columns[...])
    return pltpu.roll(joined, width - by, 1).reshape(tokens, features)


def code_kernel(syndrome, step, out, flips, steps, done):
    rounds, rows, width = syndrome.shape
    moves = [pltpu.make_async_copy(syndrome, flips, done.at[0]), pltpu.make_async_copy(step, steps, done.at[1])]
    for move in moves:
        move.start()
    out[...] = jnp.zeros(out.shape, BF)
    for move in moves:
        move.wait()
    code = flips[...] * PLAN_STEP_COUNT + steps[...]
    out[:, :width] = code.reshape(rounds * rows, width).astype(F32).astype(BF)


def start_kernel(tokens, codes, plan, flip, gain, *refs):
    count = (len(refs) - 5) // 2
    weights, (x_out, onehot_out, hidden_out, query_out, kv_out), flipped = refs[:count], refs[count : count + 5], refs[count + 5 :]
    w_query, w_key_value = weights[:2]
    for weight, out in zip(weights, flipped):
        out[...] = weight[...].T
    x, onehot = embed(tokens[...], codes[...], plan[...], flip[...])
    hidden = (x * inverse_rms(x) * gain[...]).astype(BF)
    x_out[...] = x
    onehot_out[...] = onehot
    hidden_out[...] = hidden
    query_out[...] = dot(hidden, w_query[...]).astype(BF)
    kv_out[...] = dot(hidden, w_key_value[...]).astype(BF)


def forward_kernel(
    offsets, x_in, query_in, kv_in, row_tokens, row_codes, col_tokens, col_codes, plan, flip,
    gain_tanner, w_key_value, w_merge, gain_time, w_temporal, w_temporal_out, gain_ffn, w_up, w_up_t, w_down_t, cotangent,
    keep, send, grad_time_out, tanner_out, mixed_one_out, mixed_two_out, packed_out, hidden_two_out,
    row_kv_out, col_kv_out, row_x_out, col_x_out, row_hidden_out, col_hidden_out, row_onehot_out, col_onehot_out,
    bent_one_out, probs_one_out, bent_two_out, probs_two_out, grad_gain_out,
    extended, columns, transposed, transposed_act,
):
    rounds, twice, width, features = extended.shape
    rows = twice // 2
    tokens = x_in.shape[0]
    core = my_bit(0)
    borrowed = []
    for other, codes, x_out, hidden_out, onehot_out, kv_out in (
        (row_tokens, row_codes, row_x_out, row_hidden_out, row_onehot_out, row_kv_out),
        (col_tokens, col_codes, col_x_out, col_hidden_out, col_onehot_out, col_kv_out),
    ):
        x, onehot = embed(other[...], codes[...], plan[...], flip[...])
        hidden = (x * inverse_rms(x) * gain_tanner[...]).astype(BF)
        kv = dot(hidden, w_key_value[...]).astype(BF)
        x_out[...] = x
        onehot_out[...] = onehot
        hidden_out[...] = hidden
        kv_out[...] = kv
        borrowed.append(kv.astype(F32))
    extended[:, :rows] = kv_in[...].astype(F32).reshape(rounds, rows, width, features)
    extended[:, rows:] = borrowed[0].reshape(rounds, rows, width, features)
    columns[...] = borrowed[1].reshape(rounds * rows, width, features)
    query = query_in[...].astype(F32)
    scores = None
    for number in range(MONOS + 1):
        keys = neighbour(number, offsets, extended, columns)[:, :WIDTH]
        part = dot((query * keys).astype(BF), gather_heads(number, 64))
        scores = part if scores is None else scores + part
    bent, probs = softmax_parts(scores, tanner_valid(tokens), 64)
    bent_one_out[...] = bent
    probs_one_out[...] = probs
    parts = two_parts(probs, 64)
    mixed = None
    for number in range(MONOS + 1):
        values = neighbour(number, offsets, extended, columns)[:, WIDTH:]
        part = dot(parts, spread_heads(number, 64)) * values
        mixed = part if mixed is None else mixed + part
    mixed_one = mixed.astype(BF)
    mixed_one_out[...] = mixed_one
    after_tanner = x_in[...] + dot(mixed_one, w_merge[...])
    tanner_out[...] = after_tanner

    hidden_two = (after_tanner * inverse_rms(after_tanner) * gain_time[...]).astype(BF)
    hidden_two_out[...] = hidden_two
    packed_low = dot(hidden_two, w_temporal[...]).astype(BF)
    packed_out[...] = packed_low
    packed = packed_low.astype(F32).reshape(rounds, tokens // rounds, 3 * WIDTH)
    sites = tokens // rounds
    scores = None
    for earlier in range(rounds):
        product = packed[earlier:, :, :WIDTH] * packed[earlier][None, :, WIDTH : 2 * WIDTH]
        part = dot(product.reshape(-1, WIDTH).astype(BF), gather_heads(earlier, 32))
        if earlier:
            part = jnp.concatenate([jnp.zeros((earlier * sites, LANES), F32), part], axis=0)
        scores = part if scores is None else scores + part
    bent, probs = softmax_parts(scores, time_valid(tokens, rounds), 32)
    bent_two_out[...] = bent
    probs_two_out[...] = probs
    parts = two_parts(probs, 32)
    mixed = None
    for earlier in range(rounds):
        weight = dot(parts[earlier * sites :], spread_heads(earlier, 32)).reshape(rounds - earlier, sites, WIDTH)
        part = (weight * packed[earlier][None, :, 2 * WIDTH :]).reshape(-1, WIDTH)
        if earlier:
            part = jnp.concatenate([jnp.zeros((earlier * sites, WIDTH), F32), part], axis=0)
        mixed = part if mixed is None else mixed + part
    mixed_two = mixed.astype(BF)
    mixed_two_out[...] = mixed_two
    after_time = after_tanner + dot(mixed_two, w_temporal_out[...])

    hidden = (after_time * inverse_rms(after_time) * gain_ffn[...]).astype(BF)
    outer = cotangent[...]
    transposed[...] = hidden.T
    grad_three = None
    befores = []
    for block in range(FF // WIDTH):
        cols = slice(block * WIDTH, (block + 1) * WIDTH)
        before = dot(hidden, w_up[:, cols])
        square = before * before
        bend = jnp.tanh(GELU_A * before * (1.0 + GELU_B * square))
        upper = 0.5 * (1.0 + bend)
        activated = (before * upper).astype(BF)
        slope = upper + 0.5 * before * (1.0 - bend * bend) * (GELU_A * (1.0 + 3.0 * GELU_B * square))
        grad_before = (dot(outer, w_down_t[:, cols]) * slope).astype(BF)
        befores.append(grad_before)
        part = dot(grad_before, w_up_t[cols, :])
        grad_three = part if grad_three is None else grad_three + part
        transposed_act[cols, :] = activated.T
    mine = pl.multiple_of(core * HALF, HALF)
    other = pl.multiple_of((1 - core) * HALF, HALF)
    blocks = FF // WIDTH
    lead = jnp.concatenate([transposed[pl.ds(start, HALF), :] for start in (mine, other)], axis=0)
    for block in range(blocks):
        product = dot(lead, befores[block]).astype(BF)
        keep[block * HALF : (block + 1) * HALF, :] = product[:HALF]
        send[block * HALF : (block + 1) * HALF, :] = product[HALF:]
    lead = jnp.concatenate(
        [transposed_act[pl.ds(block * WIDTH + start, HALF), :] for start in (mine, other) for block in range(blocks)],
        axis=0,
    )
    product = dot(lead, outer).astype(BF)
    keep[blocks * HALF :, :] = product[: blocks * HALF]
    send[blocks * HALF :, :] = product[blocks * HALF :]
    grad_norm, grad_gain = norm_back(after_time, gain_ffn[...], grad_three)
    grad_time_out[...] = outer.astype(F32) + grad_norm
    grad_gain_out[...] = grad_gain


def backward_kernel(
    offsets, grad_time_in, tanner_in, packed_in, query_in, kv_in, row_kv, col_kv,
    bent_one, probs_one, bent_two, probs_two, w_merge, gain_time, w_temporal, w_temporal_out,
    grad_query_out, grad_kv_out, grad_rows_out, grad_cols_out, grad_packed_out, grad_tanner_out, grad_gain_out,
    extended, columns, grad_extended,
):
    rounds, twice, width, features = extended.shape
    rows = twice // 2
    tokens = grad_time_in.shape[0]
    sites = tokens // rounds
    grad_time = grad_time_in[...]
    grad_mixed = dot(grad_time.astype(BF), w_temporal_out[...]).reshape(rounds, sites, WIDTH)
    packed = packed_in[...].astype(F32).reshape(rounds, sites, 3 * WIDTH)
    grad_probs = None
    for earlier in range(rounds):
        product = grad_mixed[earlier:] * packed[earlier][None, :, 2 * WIDTH :]
        part = dot(product.reshape(-1, WIDTH).astype(BF), gather_heads(earlier, 32))
        if earlier:
            part = jnp.concatenate([jnp.zeros((earlier * sites, LANES), F32), part], axis=0)
        grad_probs = part if grad_probs is None else grad_probs + part
    probs = probs_two[...]
    prob_parts = two_parts(probs, 32)
    score_parts = two_parts(softmax_back(bent_two[...], probs, grad_probs, 32), 32)
    grad_queries = None
    grad_keys = []
    grad_values = []
    for earlier in range(rounds):
        spread = spread_heads(earlier, 32)
        shape = (rounds - earlier, sites, WIDTH)
        weight = dot(prob_parts[earlier * sites :], spread).reshape(shape)
        slope = dot(score_parts[earlier * sites :], spread).reshape(shape)
        grad_values.append(jnp.sum(weight * grad_mixed[earlier:], axis=0))
        grad_keys.append(jnp.sum(slope * packed[earlier:, :, :WIDTH], axis=0))
        part = (slope * packed[earlier][None, :, WIDTH : 2 * WIDTH]).reshape(-1, WIDTH)
        if earlier:
            part = jnp.concatenate([jnp.zeros((earlier * sites, WIDTH), F32), part], axis=0)
        grad_queries = part if grad_queries is None else grad_queries + part
    grad_packed = jnp.concatenate(
        [grad_queries, jnp.concatenate(grad_keys, axis=0), jnp.concatenate(grad_values, axis=0)], axis=1
    ).astype(BF)
    grad_packed_out[...] = grad_packed
    grad_two = dot(grad_packed, w_temporal[...])
    grad_norm, grad_gain = norm_back(tanner_in[...], gain_time[...], grad_two)
    grad_gain_out[...] = grad_gain
    grad_tanner = grad_time + grad_norm
    grad_tanner_out[...] = grad_tanner

    grad_mixed = dot(grad_tanner.astype(BF), w_merge[...])
    extended[:, :rows] = kv_in[...].astype(F32).reshape(rounds, rows, width, features)
    extended[:, rows:] = row_kv[...].astype(F32).reshape(rounds, rows, width, features)
    columns[...] = col_kv[...].astype(F32).reshape(rounds * rows, width, features)
    grad_probs = None
    for number in range(MONOS + 1):
        values = neighbour(number, offsets, extended, columns)[:, WIDTH:]
        part = dot((grad_mixed * values).astype(BF), gather_heads(number, 64))
        grad_probs = part if grad_probs is None else grad_probs + part
    probs = probs_one[...]
    prob_parts = two_parts(probs, 64)
    score_parts = two_parts(softmax_back(bent_one[...], probs, grad_probs, 64), 64)
    query = query_in[...].astype(F32)
    grad_query = None
    grad_cols = None
    for number in (0,) + tuple(i + 1 for i in range(MONOS)):
        spread = spread_heads(number, 64)
        slope = dot(score_parts, spread)
        weight = dot(prob_parts, spread)
        keys = neighbour(number, offsets, extended, columns)[:, :WIDTH]
        part = slope * keys
        grad_query = part if grad_query is None else grad_query + part
        grad_kv = jnp.concatenate([slope * query, weight * grad_mixed], axis=1)
        if number == 0:
            grad_extended[:, :rows] = grad_kv.reshape(rounds, rows, width, features)
            grad_extended[:, rows:] = jnp.zeros((rounds, rows, width, features), F32)
            continue
        by = offset_of(offsets, number - 1)
        if number - 1 in ALONG_ROWS:
            grad_extended[:, pl.ds(by, rows)] += grad_kv.reshape(rounds, rows, width, features)
            continue
        moved = pltpu.roll(grad_kv.reshape(rounds * rows, width, features), by % width, 1)
        place = lax.broadcasted_iota(jnp.int32, moved.shape, 1)
        own = jnp.where(place >= by, moved, 0.0)
        grad_extended[:, :rows] += own.reshape(rounds, rows, width, features)
        grad_cols = moved - own if grad_cols is None else grad_cols + (moved - own)
    grad_query_out[...] = grad_query.astype(BF)
    grad_kv_out[...] = grad_extended[:, :rows].reshape(tokens, features).astype(BF)
    grad_rows_out[...] = grad_extended[:, rows:].reshape(tokens, features).astype(BF)
    grad_cols_out[...] = grad_cols.reshape(tokens, features).astype(BF)


def weights_kernel(
    mixed_two, grad_time, hidden_two, grad_packed, mixed_one, grad_tanner, grad_query, w_query, w_key_value, gain,
    x_own, x_row, x_col, hidden_own, hidden_row, hidden_col, onehot_own, onehot_row, onehot_col,
    grad_own, grad_row, grad_col, grad_gain_time, grad_gain_ffn,
    grad_out, row_out, col_out, keep, send, transposed, transposed_own,
):
    core = my_bit(0)
    tokens = x_own.shape[0]
    transposed[0] = hidden_two[...].T
    transposed[1] = mixed_two[...].T
    transposed[2] = mixed_one[...].T
    small = None
    grad_gain = None
    for number, (x, hidden, onehot, grad_kv, out) in enumerate((
        (x_own, hidden_own, onehot_own, grad_own, grad_out),
        (x_row, hidden_row, onehot_row, grad_row, row_out),
        (x_col, hidden_col, onehot_col, grad_col, col_out),
    )):
        transposed_own[:, number * tokens : (number + 1) * tokens] = hidden[...].T
        grad_one = dot(grad_kv[...], w_key_value[...])
        if number == 0:
            grad_one = grad_one + dot(grad_query[...], w_query[...])
        grad, part = norm_back(x[...], gain[...], grad_one)
        grad_gain = part if grad_gain is None else grad_gain + part
        if number == 0:
            grad = grad + grad_tanner[...]
        out[...] = grad.astype(out.dtype)
        high = grad.astype(BF)
        low = (grad - high.astype(F32)).astype(BF)
        part = dot(onehot[...], jnp.concatenate([high, low], axis=1), ((0,), (0,)))[:16]
        part = part[:, :WIDTH] + part[:, WIDTH:]
        small = part if small is None else small + part
    row = lax.broadcasted_iota(jnp.int32, small.shape, 0)
    small = jnp.where(row == 9, grad_gain, small)
    small = jnp.where(row == 10, grad_gain_time[...], small)
    small = jnp.where(row == 11, grad_gain_ffn[...], small).astype(BF)
    grad_time_low = grad_time[...].astype(BF)
    grad_tanner_low = grad_tanner[...].astype(BF)
    grad_all = jnp.concatenate([grad_own[...], grad_row[...], grad_col[...]], axis=0)
    mine = pl.ds(pl.multiple_of(core * HALF, HALF), HALF)
    other = pl.ds(pl.multiple_of((1 - core) * HALF, HALF), HALF)
    keep[:16, :] = small
    send[:16, :] = small
    pairs = [(transposed.at[0], grad_packed[:, block * WIDTH : (block + 1) * WIDTH]) for block in range(3)]
    pairs.append((transposed.at[1], grad_time_low))
    pairs.append((transposed.at[2], grad_tanner_low))
    pairs.append((transposed_own.at[:, pl.ds(0, tokens)], grad_query[...]))
    pairs += [(transposed_own, grad_all[:, block * WIDTH : (block + 1) * WIDTH]) for block in range(2)]
    for block, (lead, grad) in enumerate(pairs):
        product = dot(jnp.concatenate([lead[mine, :], lead[other, :]], axis=0), grad).astype(BF)
        rows = slice(16 + block * HALF, 16 + (block + 1) * HALF)
        keep[rows, :] = product[:HALF]
        send[rows, :] = product[HALF:]


def my_bit(bit):
    many = lax.axis_size("gy").bit_length() - 1
    if bit < many:
        return (lax.axis_index("gy") >> bit) & 1
    return (lax.axis_index("gx") >> (bit - many)) & 1


def split_kernel(extra, bit, kept, received, keep, send, total):
    mine = my_bit(bit)
    value = kept[...].astype(F32) + received[...].astype(F32)
    total[...] = value[extra:]
    rows = keep.shape[0] - extra
    for ref, which in ((keep, mine), (send, 1 - mine)):
        if extra:
            ref[:extra, :] = value[:extra].astype(BF)
        ref[extra:, :] = total[pl.ds(pl.multiple_of(which * rows, rows), rows), :].astype(BF)


def sum_kernel(first, second, out):
    out[...] = (first[...].astype(F32) + second[...].astype(F32)).astype(BF)


def end_kernel(extra, scale, kept, received, out, *small):
    value = kept[...].astype(F32) + received[...].astype(F32)
    out[...] = value[extra:].astype(BF)
    if extra:
        value = value[:extra] * scale
        small[0][...] = value[:8]
        for number in range(4):
            small[1 + number][...] = value[8 + number : 9 + number]


def join_kernel(bit, own, received, out):
    mine = my_bit(bit)
    out[mine] = own[...]
    out[1 - mine] = received[...]


def unpack_kernel(groups, scale, grad, row, col, *refs):
    sources, refs = refs[: 2 * len(groups)], refs[2 * len(groups) :]
    token_out, *outs = refs[: len(refs) // 2]
    token_low, *wides = refs[len(refs) // 2 : -1]
    done = refs[-1]
    moves = []

    def move(source, target):
        moves.append(pltpu.make_async_copy(source, target, done.at[len(moves)]))
        moves[-1].start()

    for number, blocks in enumerate(groups):
        for side in range(2):
            source = sources[2 * number + side]
            half = pl.multiple_of((my_bit(0) ^ side) * HALF, HALF)
            block = 0
            first = sum(len(group) for group in groups[:number])
            for out, wide, (down, across) in zip(outs[first:], wides[first:], blocks):
                for index in range(down * across):
                    value = source[block * HALF : (block + 1) * HALF, :].astype(F32) * scale
                    left = (index if across > 1 else 0) * WIDTH
                    wide[side, index if down > 1 else 0, :, left : left + WIDTH] = value
                    block += 1
                for index in range(down):
                    move(wide.at[side, index], out.at[pl.ds(index * WIDTH + half, HALF)])
    token_low[...] = (grad[...] + row[...].astype(F32) + col[...].astype(F32)).astype(BF)
    move(token_low, token_out)
    for one in moves:
        one.wait()


def unpack(groups, scale, sources, grad, row, col):
    hbm = pl.BlockSpec(memory_space=pltpu.HBM)
    blocks = [block for group in groups for block in group]
    return pl.pallas_call(
        functools.partial(unpack_kernel, groups, scale),
        out_shape=[jax.ShapeDtypeStruct(grad.shape, BF)]
        + [jax.ShapeDtypeStruct((down * WIDTH, across * WIDTH), F32) for down, across in blocks],
        in_specs=[pl.BlockSpec(memory_space=pltpu.VMEM)] * (3 + len(sources)),
        out_specs=[hbm] * (1 + len(blocks)),
        scratch_shapes=[pltpu.VMEM(grad.shape, BF)]
        + [pltpu.VMEM((2, down, HALF, across * WIDTH), F32) for down, across in blocks]
        + [pltpu.SemaphoreType.DMA((1 + 2 * sum(down for down, _ in blocks),))],
        compiler_params=pltpu.CompilerParams(vmem_limit_bytes=16 * MIB),
    )(grad, row, col, *sources)


def estimate(work, outs=(), args=()):
    moved = sum(math.prod(shape) * jnp.dtype(dtype).itemsize for shape, dtype in outs)
    moved += sum(math.prod(arg.shape) * arg.dtype.itemsize for arg in args)
    return pl.CostEstimate(flops=int(work * 1.1e9), transcendentals=0, bytes_accessed=moved)


def call(kernel, outs, args, scratch=(), smem=0, limit=16, work=0.1):
    vmem = pl.BlockSpec(memory_space=pltpu.VMEM)
    return pl.pallas_call(
        kernel,
        out_shape=[jax.ShapeDtypeStruct(shape, dtype) for shape, dtype in outs],
        in_specs=[pl.BlockSpec(memory_space=pltpu.SMEM)] * smem + [vmem] * (len(args) - smem),
        out_specs=[vmem] * len(outs),
        scratch_shapes=list(scratch),
        compiler_params=pltpu.CompilerParams(vmem_limit_bytes=limit * MIB),
        cost_estimate=estimate(work, outs, args),
    )(*args)


def shifted(x, axis, by):
    count = lax.axis_size(axis)
    return lax.ppermute(x, axis, [(i, (i + by) % count) for i in range(count)])


class Layout:
    def __init__(self):
        self.nx = lax.axis_size("gx")
        self.ny = lax.axis_size("gy")
        self.many = self.ny.bit_length() - 1
        self.bits = self.many + self.nx.bit_length() - 1
        assert 1 << self.bits == self.nx * self.ny

    def swap(self, x, bit):
        flip = 1 << bit if bit < self.many else self.ny << (bit - self.many)
        return lax.ppermute(x, ("gx", "gy"), [(i, i ^ flip) for i in range(self.nx * self.ny)])


def reduce_tree(layout, keep, send, extra, order, scale, first=0, until=None, beside=()):
    halving = order[:-1]
    for stage in range(first, len(halving) if until is None else until):
        received = layout.swap(send, halving[stage])
        if stage == 2 and beside:
            received, *beside = lax.optimization_barrier((received, *beside))
        rows = keep.shape[0] - extra
        if stage + 1 < len(halving):
            half = ((rows // 2 + extra, WIDTH), BF)
            keep, send = call(
                functools.partial(split_kernel, extra, halving[stage + 1]),
                [half, half],
                [keep, received],
                [pltpu.VMEM((rows, WIDTH), F32)],
            )
    if until is not None:
        return keep, send
    total = call(sum_kernel, [(keep.shape, BF)], [keep, received])[0]
    received = layout.swap(total, order[-1])
    small = [((8, WIDTH), F32)] + [((1, WIDTH), F32)] * 4 if extra else []
    outs = call(functools.partial(end_kernel, extra, scale), [((rows, WIDTH), BF)] + small, [total, received])
    return (*outs, *beside)


def gather_tree(layout, own, order):
    for bit in order[-2:0:-1]:
        received = layout.swap(own, bit)
        rows = own.shape[0]
        own = call(
            functools.partial(join_kernel, bit), [((2, rows, WIDTH), BF)], [own, received]
        )[0].reshape(2 * rows, WIDTH)
    return own, layout.swap(own, order[0])


def on_device(
    tokens,
    syndrome,
    check_plan_step,
    offsets,
    flip_vector,
    plan_step_embedding,
    gain_tanner,
    w_query,
    w_key_value,
    w_merge,
    gain_time,
    w_temporal,
    w_temporal_out,
    gain_ffn,
    w_ffn_up,
    w_ffn_down,
    cotangent,
):
    layout = Layout()
    rounds, rows, cols = tokens.shape[:3]
    count = rounds * rows * cols
    scale = 1.0 / math.sqrt(count * layout.nx * layout.ny)
    flat = (count, WIDTH)
    act = (flat, BF)
    stream = (flat, F32)
    wide = ((count, 2 * WIDTH), BF)
    lanes = ((count, LANES), F32)
    onehot = ((count, LANES), BF)
    row = ((1, WIDTH), F32)
    hbm = pl.BlockSpec(memory_space=pltpu.HBM)

    sites = pltpu.VMEM((rounds, rows, cols), jnp.int32)
    codes = pl.pallas_call(
        code_kernel,
        out_shape=jax.ShapeDtypeStruct((rounds * rows, LANES), BF),
        in_specs=[hbm] * 2,
        out_specs=pl.BlockSpec(memory_space=pltpu.VMEM),
        scratch_shapes=[sites, sites, pltpu.SemaphoreType.DMA((2,))],
        cost_estimate=estimate(12),
    )(syndrome, check_plan_step)
    row_tokens = shifted(tokens, "gx", -1).reshape(flat)
    col_tokens = shifted(tokens, "gy", -1).reshape(flat)
    row_codes = shifted(codes, "gx", -1)
    col_codes = shifted(codes, "gy", -1)
    plan = plan_step_embedding
    flip = flip_vector.reshape(1, WIDTH)
    gain_one = gain_tanner.reshape(1, WIDTH)
    gain_two = gain_time.reshape(1, WIDTH)
    gain_three = gain_ffn.reshape(1, WIDTH)
    outer = cotangent.reshape(flat)
    weights = [w_query, w_key_value, w_merge, w_temporal, w_temporal_out, w_ffn_up, w_ffn_down]
    x, onehot_own, hidden_one, query, key_value, *flipped = call(
        start_kernel,
        [stream, onehot, act, act, wide] + [(weight.shape[::-1], BF) for weight in weights],
        [tokens.reshape(flat), codes, plan, flip, gain_one, *weights],

    )
    extended = pltpu.VMEM((rounds, 2 * rows, cols, 2 * WIDTH), F32)
    columns = pltpu.VMEM((rounds * rows, cols, 2 * WIDTH), F32)
    half_one = ((2 * (FF // WIDTH) * HALF, WIDTH), BF)
    (
        keep_one, send_one, grad_time, after_tanner, mixed_one, mixed_two, packed, hidden_two,
        row_kv, col_kv, row_x, col_x, row_hidden, col_hidden, row_onehot, col_onehot,
        bent_one, probs_one, bent_two, probs_two, grad_gain_ffn,
    ) = call(
        forward_kernel,
        [half_one, half_one, stream, stream, act, act, ((count, 3 * WIDTH), BF), act,
         wide, wide, stream, stream, act, act, onehot, onehot, lanes, lanes, lanes, lanes, row],
        [offsets, x, query, key_value, row_tokens, row_codes, col_tokens, col_codes, plan, flip,
         gain_one, w_key_value, w_merge, gain_two, w_temporal, w_temporal_out, gain_three, w_ffn_up, flipped[5], flipped[6],
         outer],
        [extended, columns, pltpu.VMEM((WIDTH, count), BF), pltpu.VMEM((FF, count), BF)],
        smem=1,
        limit=32,

    )
    grad_query, grad_kv, grad_rows, grad_cols, grad_packed, grad_tanner, grad_gain_time = call(
        backward_kernel,
        [act, wide, wide, wide, ((count, 3 * WIDTH), BF), stream, row],
        [offsets, grad_time, after_tanner, packed, query, key_value, row_kv, col_kv,
         bent_one, probs_one, bent_two, probs_two, flipped[2], gain_two, flipped[3], flipped[4]],
        [extended, columns, extended],
        smem=1,
        limit=32,
        work=3,
    )
    many, bits = layout.many, layout.bits
    order_one = list(range(many)) + list(range(many, bits))
    order_two = [0, many] + list(range(1, many)) + list(range(many + 1, bits))
    keep_one, send_one = reduce_tree(layout, keep_one, send_one, 0, order_one, scale, until=1)
    keep_one, grad_tanner = lax.optimization_barrier((keep_one, grad_tanner))
    half_two = ((16 + 8 * HALF, WIDTH), BF)
    grad_own, lent_rows, lent_cols, keep_two, send_two = call(
        weights_kernel,
        [stream, act, act, half_two, half_two],
        [mixed_two, grad_time, hidden_two, grad_packed, mixed_one, grad_tanner, grad_query, flipped[0], flipped[1],
         gain_one, x, row_x, col_x, hidden_one, row_hidden, col_hidden, onehot_own, row_onehot, col_onehot,
         grad_kv, grad_rows, grad_cols, grad_gain_time, grad_gain_ffn],
        [pltpu.VMEM((3, WIDTH, count), BF), pltpu.VMEM((WIDTH, 3 * count), BF)],
        limit=32,
        work=3,
    )
    back_rows = shifted(lent_rows, "gx", 1)
    back_cols = shifted(lent_cols, "gy", 1)
    shard_one, back_rows, back_cols = reduce_tree(
        layout, keep_one, send_one, 0, order_one, scale, first=1, beside=(back_rows, back_cols)
    )
    shard_two, plan_grad, grad_flip, sum_gain_tanner, sum_gain_time, sum_gain_ffn = reduce_tree(
        layout, keep_two, send_two, 16, order_two, scale
    )
    sources = [*gather_tree(layout, shard_one, order_one), *gather_tree(layout, shard_two, order_two)]
    groups = (((1, FF // WIDTH), (FF // WIDTH, 1)), ((1, 3), (1, 1), (1, 1), (1, 1), (1, 2)))
    (
        token_grad, grad_up, grad_down, grad_temporal, grad_temporal_out, grad_merge, grad_w_query, grad_key_value,
    ) = unpack(groups, scale, sources, grad_own, back_rows, back_cols)
    return (
        token_grad.reshape(tokens.shape),
        grad_flip.reshape(WIDTH),
        plan_grad,
        sum_gain_tanner.reshape(WIDTH),
        grad_w_query,
        grad_key_value,
        grad_merge,
        sum_gain_time.reshape(WIDTH),
        grad_temporal,
        grad_temporal_out,
        sum_gain_ffn.reshape(WIDTH),
        grad_up,
        grad_down,
    )


def solution(mesh):
    tiled = P(None, "gx", "gy", None)
    sites = P(None, "gx", "gy")
    return jax.shard_map(
        on_device,
        mesh=mesh,
        in_specs=(tiled, sites, sites) + (P(),) * 13 + (tiled,),
        out_specs=(tiled,) + (P(),) * 12,
        check_vma=False,
    )
```

```python
import functools
import math

import jax
import jax.numpy as jnp
from jax import lax
from jax.experimental import pallas as pl
from jax.experimental.pallas import tpu as pltpu
from jax.sharding import PartitionSpec as P

WIDTH = 256
HEADDIM = 32
HEADS = WIDTH // HEADDIM
FF = 1024
PLAN_STEP_COUNT = 8
MONOS = 6
MAXEXP = 8
LANES = 128
HALF = WIDTH // 2

EPS = 1e-05
CAP = 4.0
ALONG_ROWS = (0, 4, 5)
BF = jnp.bfloat16
F32 = jnp.float32
SCORE = 1.0 / math.sqrt(HEADDIM)
GELU_A = math.sqrt(2.0 / math.pi)
GELU_B = 0.044715
MIB = 1 << 20


def dot(a, b, dims=((1,), (0,))):
    return lax.dot_general(a, b, (dims, ((), ())), preferred_element_type=F32)


def dot_nt(a, b):
    return dot(a, b, ((1,), (1,)))


def embed(values, codes, plan, flip):
    tokens = values.shape[0]
    lines = codes.shape[0]
    width = tokens // lines
    token = lax.broadcasted_iota(jnp.int32, (tokens, lines), 0)
    line = lax.broadcasted_iota(jnp.int32, (tokens, lines), 1)
    spread = dot(jnp.where(token // width == line, 1.0, 0.0).astype(BF), codes)
    token = lax.broadcasted_iota(jnp.int32, (tokens, LANES), 0)
    lane = lax.broadcasted_iota(jnp.int32, (tokens, LANES), 1)
    picked = jnp.where(token % width == lane, spread, 0.0).astype(BF)
    code = dot(picked, jnp.ones((LANES, LANES), BF))
    flipped = code >= PLAN_STEP_COUNT
    step = jnp.where(flipped, code - PLAN_STEP_COUNT, code)
    slot = lane % 16
    chosen = (slot.astype(F32) == step) | ((slot == PLAN_STEP_COUNT) & flipped)
    onehot = jnp.where(chosen & (lane < 48), 1.0, 0.0).astype(BF)
    row = lax.broadcasted_iota(jnp.int32, (8, WIDTH), 0)
    table = jnp.concatenate([plan, jnp.where(row == 0, flip, 0.0)], axis=0)
    high = table.astype(BF)
    rest = table - high.astype(F32)
    middle = rest.astype(BF)
    low = (rest - middle.astype(F32)).astype(BF)
    empty = jnp.zeros((LANES - 48, WIDTH), BF)
    vectors = dot(onehot, jnp.concatenate([high, middle, low, empty], axis=0))
    return values.astype(F32) + vectors, onehot


def inverse_rms(stream):
    return lax.rsqrt(jnp.mean(stream * stream, axis=-1, keepdims=True) + EPS)


def norm_back(stream, gain, grad):
    inverse = inverse_rms(stream)
    normed = stream * inverse
    scaled = grad * gain
    mean = jnp.mean(scaled * normed, axis=-1, keepdims=True)
    return inverse * (scaled - normed * mean), jnp.sum(grad * normed, axis=0, keepdims=True)


def gather_heads(slot, period):
    feature = lax.broadcasted_iota(jnp.int32, (WIDTH, LANES), 0) // HEADDIM
    lane = lax.broadcasted_iota(jnp.int32, (WIDTH, LANES), 1) % period
    return jnp.where(lane - feature == slot * HEADS, 1.0, 0.0).astype(BF)


def spread_heads(slot, period):
    lane = lax.broadcasted_iota(jnp.int32, (LANES, WIDTH), 0)
    feature = lax.broadcasted_iota(jnp.int32, (LANES, WIDTH), 1) // HEADDIM
    at = (lane < 2 * period) & (lane % period - feature == slot * HEADS)
    return jnp.where(at, 1.0, 0.0).astype(BF)


def two_parts(value, period):
    lane = lax.broadcasted_iota(jnp.int32, value.shape, 1)
    high = value.astype(BF).astype(F32)
    return jnp.where(lane < period, high, value - high).astype(BF)


def slot_total(value, period):
    shift = HEADS
    while shift < period:
        value = value + pltpu.roll(value, shift, 1)
        shift *= 2
    return value


def softmax_parts(scores, valid, period):
    bent = jnp.tanh(scores * (SCORE / CAP))
    weights = jnp.where(valid, jnp.exp(CAP * bent), 0.0)
    return bent, weights / slot_total(weights, period)


def softmax_back(bent, probs, grad, period):
    inner = probs * grad
    return (inner - probs * slot_total(inner, period)) * (1.0 - bent * bent) * SCORE


def tanner_valid(tokens):
    lane = lax.broadcasted_iota(jnp.int32, (tokens, LANES), 1)
    return lane % 64 < HEADS * (MONOS + 1)


def time_valid(tokens, rounds):
    lane = lax.broadcasted_iota(jnp.int32, (tokens, LANES), 1)
    row = lax.broadcasted_iota(jnp.int32, (tokens, LANES), 0)
    return (lane % 32) // HEADS <= row // (tokens // rounds)


def offset_of(offsets, index):
    return offsets[index, 0] if index in ALONG_ROWS else offsets[index, 1]


def neighbour(number, offsets, extended, columns):
    rounds, twice, width, features = extended.shape
    rows = twice // 2
    tokens = rounds * rows * width
    if number == 0:
        return extended[:, :rows].reshape(tokens, features)
    by = offset_of(offsets, number - 1)
    if number - 1 in ALONG_ROWS:
        return extended[:, pl.ds(by, rows)].reshape(tokens, features)
    own = extended[:, :rows].reshape(rounds * rows, width, features)
    place = lax.broadcasted_iota(jnp.int32, own.shape, 1)
    joined = jnp.where(place >= by, own, columns[...])
    return pltpu.roll(joined, width - by, 1).reshape(tokens, features)


def code_kernel(syndrome, step, out, flips, steps, done):
    rounds, rows, width = syndrome.shape
    moves = [pltpu.make_async_copy(syndrome, flips, done.at[0]), pltpu.make_async_copy(step, steps, done.at[1])]
    for move in moves:
        move.start()
    out[...] = jnp.zeros(out.shape, BF)
    for move in moves:
        move.wait()
    code = flips[...] * PLAN_STEP_COUNT + steps[...]
    out[:, :width] = code.reshape(rounds * rows, width).astype(F32).astype(BF)


def start_kernel(tokens, codes, plan, flip, gain, gain_two, gain_three, *refs):
    count = (len(refs) - 12) // 2
    weights, outs = refs[:count], refs[count:]
    x_out, onehot_out, hidden_out, query_out, kv_out, *passed = outs[:8]
    gathers, spreads, gathers_time, spreads_time = outs[8:12]
    w_query, w_key_value = weights[:2]
    for weight, out in zip(weights, outs[12:]):
        out[...] = weight[...].T
    for source, out in zip((gain, gain_two, gain_three), passed):
        out[...] = source[...]
    for number in range(MONOS + 1):
        gathers[number * WIDTH : (number + 1) * WIDTH, :] = gather_heads(number, 64)
        spreads[:, number * WIDTH : (number + 1) * WIDTH] = spread_heads(number, 64)
    for number in range(gathers_time.shape[0] // WIDTH):
        gathers_time[number * WIDTH : (number + 1) * WIDTH, :] = gather_heads(number, 32)
        spreads_time[:, number * WIDTH : (number + 1) * WIDTH] = spread_heads(number, 32)
    x, onehot = embed(tokens[...], codes[...], plan[...], flip[...])
    hidden = (x * inverse_rms(x) * gain[...]).astype(BF)
    x_out[...] = x
    onehot_out[...] = onehot
    hidden_out[...] = hidden
    query_out[...] = dot(hidden, w_query[...]).astype(BF)
    kv_out[...] = dot(hidden, w_key_value[...]).astype(BF)


def forward_kernel(
    offsets, x_in, query_in, kv_in, row_tokens, row_codes, col_tokens, col_codes, plan, flip,
    gathers, spreads, gathers_time, spreads_time, gain_tanner, w_key_value, w_merge, gain_time, w_temporal, w_temporal_out, gain_ffn, w_up, w_up_t, w_down_t, cotangent,
    keep, send, grad_time_out, tanner_out, mixed_one_out, mixed_two_out, packed_out, hidden_two_out,
    row_kv_out, col_kv_out, row_x_out, col_x_out, row_hidden_out, col_hidden_out, row_onehot_out, col_onehot_out,
    bent_one_out, probs_one_out, bent_two_out, probs_two_out, grad_gain_out,
    extended, columns, transposed, transposed_act,
):
    rounds, twice, width, features = extended.shape
    rows = twice // 2
    tokens = x_in.shape[0]
    core = my_bit(0)
    borrowed = []
    for other, codes, x_out, hidden_out, onehot_out, kv_out in (
        (row_tokens, row_codes, row_x_out, row_hidden_out, row_onehot_out, row_kv_out),
        (col_tokens, col_codes, col_x_out, col_hidden_out, col_onehot_out, col_kv_out),
    ):
        x, onehot = embed(other[...], codes[...], plan[...], flip[...])
        hidden = (x * inverse_rms(x) * gain_tanner[...]).astype(BF)
        kv = dot(hidden, w_key_value[...]).astype(BF)
        x_out[...] = x
        onehot_out[...] = onehot
        hidden_out[...] = hidden
        kv_out[...] = kv
        borrowed.append(kv.astype(F32))
    extended[:, :rows] = kv_in[...].astype(F32).reshape(rounds, rows, width, features)
    extended[:, rows:] = borrowed[0].reshape(rounds, rows, width, features)
    columns[...] = borrowed[1].reshape(rounds * rows, width, features)
    query = query_in[...].astype(F32)
    products = []
    for number in range(MONOS + 1):
        keys = neighbour(number, offsets, extended, columns)[:, :WIDTH]
        products.append((query * keys).astype(BF))
    scores = dot(jnp.concatenate(products, axis=1), gathers[...])
    bent, probs = softmax_parts(scores, tanner_valid(tokens), 64)
    bent_one_out[...] = bent
    probs_one_out[...] = probs
    parts = two_parts(probs, 64)
    mixed = None
    for number in range(MONOS + 1):
        values = neighbour(number, offsets, extended, columns)[:, WIDTH:]
        part = dot(parts, spreads[:, number * WIDTH : (number + 1) * WIDTH]) * values
        mixed = part if mixed is None else mixed + part
    mixed_one = mixed.astype(BF)
    mixed_one_out[...] = mixed_one
    after_tanner = x_in[...] + dot(mixed_one, w_merge[...])
    tanner_out[...] = after_tanner

    hidden_two = (after_tanner * inverse_rms(after_tanner) * gain_time[...]).astype(BF)
    hidden_two_out[...] = hidden_two
    packed_low = dot(hidden_two, w_temporal[...]).astype(BF)
    packed_out[...] = packed_low
    packed = packed_low.astype(F32).reshape(rounds, tokens // rounds, 3 * WIDTH)
    sites = tokens // rounds
    scores = None
    for earlier in range(rounds):
        product = packed[earlier:, :, :WIDTH] * packed[earlier][None, :, WIDTH : 2 * WIDTH]
        part = dot(product.reshape(-1, WIDTH).astype(BF), gathers_time[earlier * WIDTH : (earlier + 1) * WIDTH, :])
        if earlier:
            part = jnp.concatenate([jnp.zeros((earlier * sites, LANES), F32), part], axis=0)
        scores = part if scores is None else scores + part
    bent, probs = softmax_parts(scores, time_valid(tokens, rounds), 32)
    bent_two_out[...] = bent
    probs_two_out[...] = probs
    parts = two_parts(probs, 32)
    mixed = None
    for earlier in range(rounds):
        spread = spreads_time[:, earlier * WIDTH : (earlier + 1) * WIDTH]
        weight = dot(parts[earlier * sites :], spread).reshape(rounds - earlier, sites, WIDTH)
        part = (weight * packed[earlier][None, :, 2 * WIDTH :]).reshape(-1, WIDTH)
        if earlier:
            part = jnp.concatenate([jnp.zeros((earlier * sites, WIDTH), F32), part], axis=0)
        mixed = part if mixed is None else mixed + part
    mixed_two = mixed.astype(BF)
    mixed_two_out[...] = mixed_two
    after_time = after_tanner + dot(mixed_two, w_temporal_out[...])

    hidden = (after_time * inverse_rms(after_time) * gain_ffn[...]).astype(BF)
    outer = cotangent[...]
    transposed[...] = hidden.T
    grad_three = None
    befores = []
    for block in range(FF // WIDTH):
        cols = slice(block * WIDTH, (block + 1) * WIDTH)
        before = dot(hidden, w_up[:, cols])
        square = before * before
        bend = jnp.tanh(GELU_A * before * (1.0 + GELU_B * square))
        upper = 0.5 * (1.0 + bend)
        activated = (before * upper).astype(BF)
        slope = upper + 0.5 * before * (1.0 - bend * bend) * (GELU_A * (1.0 + 3.0 * GELU_B * square))
        grad_before = (dot(outer, w_down_t[:, cols]) * slope).astype(BF)
        befores.append(grad_before)
        part = dot(grad_before, w_up_t[cols, :])
        grad_three = part if grad_three is None else grad_three + part
        transposed_act[cols, :] = activated.T
    mine = pl.multiple_of(core * HALF, HALF)
    other = pl.multiple_of((1 - core) * HALF, HALF)
    blocks = FF // WIDTH
    lead = jnp.concatenate([transposed[pl.ds(start, HALF), :] for start in (mine, other)], axis=0)
    for block in range(blocks):
        product = dot(lead, befores[block]).astype(BF)
        keep[block * HALF : (block + 1) * HALF, :] = product[:HALF]
        send[block * HALF : (block + 1) * HALF, :] = product[HALF:]
    lead = jnp.concatenate(
        [transposed_act[pl.ds(block * WIDTH + start, HALF), :] for start in (mine, other) for block in range(blocks)],
        axis=0,
    )
    product = dot(lead, outer).astype(BF)
    keep[blocks * HALF :, :] = product[: blocks * HALF]
    send[blocks * HALF :, :] = product[blocks * HALF :]
    grad_norm, grad_gain = norm_back(after_time, gain_ffn[...], grad_three)
    grad_time_out[...] = outer.astype(F32) + grad_norm
    grad_gain_out[...] = grad_gain


def backward_kernel(
    offsets, grad_time_in, tanner_in, packed_in, query_in, kv_in, row_kv, col_kv,
    bent_one, probs_one, bent_two, probs_two, gathers, spreads, gathers_time, spreads_time,
    w_merge, gain_time, w_temporal, w_temporal_out,
    grad_query_out, grad_kv_out, grad_rows_out, grad_cols_out, grad_packed_out, grad_tanner_out, grad_gain_out,
    extended, columns, grad_extended,
):
    rounds, twice, width, features = extended.shape
    rows = twice // 2
    tokens = grad_time_in.shape[0]
    sites = tokens // rounds
    grad_time = grad_time_in[...]
    grad_mixed = dot(grad_time.astype(BF), w_temporal_out[...]).reshape(rounds, sites, WIDTH)
    packed = packed_in[...].astype(F32).reshape(rounds, sites, 3 * WIDTH)
    grad_probs = None
    for earlier in range(rounds):
        product = grad_mixed[earlier:] * packed[earlier][None, :, 2 * WIDTH :]
        part = dot(product.reshape(-1, WIDTH).astype(BF), gathers_time[earlier * WIDTH : (earlier + 1) * WIDTH, :])
        if earlier:
            part = jnp.concatenate([jnp.zeros((earlier * sites, LANES), F32), part], axis=0)
        grad_probs = part if grad_probs is None else grad_probs + part
    probs = probs_two[...]
    prob_parts = two_parts(probs, 32)
    score_parts = two_parts(softmax_back(bent_two[...], probs, grad_probs, 32), 32)
    grad_queries = None
    grad_keys = []
    grad_values = []
    for earlier in range(rounds):
        spread = spreads_time[:, earlier * WIDTH : (earlier + 1) * WIDTH]
        shape = (2, rounds - earlier, sites, WIDTH)
        both = [prob_parts[earlier * sites :], score_parts[earlier * sites :]]
        weight, slope = dot(jnp.concatenate(both, axis=0), spread).reshape(shape)
        grad_values.append(jnp.sum(weight * grad_mixed[earlier:], axis=0))
        grad_keys.append(jnp.sum(slope * packed[earlier:, :, :WIDTH], axis=0))
        part = (slope * packed[earlier][None, :, WIDTH : 2 * WIDTH]).reshape(-1, WIDTH)
        if earlier:
            part = jnp.concatenate([jnp.zeros((earlier * sites, WIDTH), F32), part], axis=0)
        grad_queries = part if grad_queries is None else grad_queries + part
    grad_packed = jnp.concatenate(
        [grad_queries, jnp.concatenate(grad_keys, axis=0), jnp.concatenate(grad_values, axis=0)], axis=1
    ).astype(BF)
    grad_packed_out[...] = grad_packed
    grad_two = dot(grad_packed, w_temporal[...])
    grad_norm, grad_gain = norm_back(tanner_in[...], gain_time[...], grad_two)
    grad_gain_out[...] = grad_gain
    grad_tanner = grad_time + grad_norm
    grad_tanner_out[...] = grad_tanner

    grad_mixed = dot(grad_tanner.astype(BF), w_merge[...])
    extended[:, :rows] = kv_in[...].astype(F32).reshape(rounds, rows, width, features)
    extended[:, rows:] = row_kv[...].astype(F32).reshape(rounds, rows, width, features)
    columns[...] = col_kv[...].astype(F32).reshape(rounds * rows, width, features)
    products = []
    for number in range(MONOS + 1):
        values = neighbour(number, offsets, extended, columns)[:, WIDTH:]
        products.append((grad_mixed * values).astype(BF))
    grad_probs = dot(jnp.concatenate(products, axis=1), gathers[...])
    probs = probs_one[...]
    prob_parts = two_parts(probs, 64)
    score_parts = two_parts(softmax_back(bent_one[...], probs, grad_probs, 64), 64)
    parts = jnp.concatenate([score_parts, prob_parts], axis=0)
    query = query_in[...].astype(F32)
    grad_query = None
    grad_cols = None
    for number in (0,) + tuple(i + 1 for i in range(MONOS)):
        both = dot(parts, spreads[:, number * WIDTH : (number + 1) * WIDTH])
        slope, weight = both[:tokens], both[tokens:]
        keys = neighbour(number, offsets, extended, columns)[:, :WIDTH]
        part = slope * keys
        grad_query = part if grad_query is None else grad_query + part
        grad_kv = jnp.concatenate([slope * query, weight * grad_mixed], axis=1)
        if number == 0:
            grad_extended[:, :rows] = grad_kv.reshape(rounds, rows, width, features)
            grad_extended[:, rows:] = jnp.zeros((rounds, rows, width, features), F32)
            continue
        by = offset_of(offsets, number - 1)
        if number - 1 in ALONG_ROWS:
            grad_extended[:, pl.ds(by, rows)] += grad_kv.reshape(rounds, rows, width, features)
            continue
        moved = pltpu.roll(grad_kv.reshape(rounds * rows, width, features), by % width, 1)
        place = lax.broadcasted_iota(jnp.int32, moved.shape, 1)
        own = jnp.where(place >= by, moved, 0.0)
        grad_extended[:, :rows] += own.reshape(rounds, rows, width, features)
        grad_cols = moved - own if grad_cols is None else grad_cols + (moved - own)
    grad_query_out[...] = grad_query.astype(BF)
    grad_kv_out[...] = grad_extended[:, :rows].reshape(tokens, features).astype(BF)
    grad_rows_out[...] = grad_extended[:, rows:].reshape(tokens, features).astype(BF)
    grad_cols_out[...] = grad_cols.reshape(tokens, features).astype(BF)


def weights_kernel(
    mixed_two, grad_time, hidden_two, grad_packed, mixed_one, grad_tanner, grad_query, w_query, w_key_value, gain,
    x_own, x_row, x_col, hidden_own, hidden_row, hidden_col, onehot_own, onehot_row, onehot_col,
    grad_own, grad_row, grad_col, grad_gain_time, grad_gain_ffn,
    grad_out, row_out, col_out, keep, send, transposed, transposed_own,
):
    core = my_bit(0)
    tokens = x_own.shape[0]
    transposed[0] = hidden_two[...].T
    transposed[1] = mixed_two[...].T
    transposed[2] = mixed_one[...].T
    small = None
    grad_gain = None
    for number, (x, hidden, onehot, grad_kv, out) in enumerate((
        (x_own, hidden_own, onehot_own, grad_own, grad_out),
        (x_row, hidden_row, onehot_row, grad_row, row_out),
        (x_col, hidden_col, onehot_col, grad_col, col_out),
    )):
        transposed_own[:, number * tokens : (number + 1) * tokens] = hidden[...].T
        grad_one = dot(grad_kv[...], w_key_value[...])
        if number == 0:
            grad_one = grad_one + dot(grad_query[...], w_query[...])
        grad, part = norm_back(x[...], gain[...], grad_one)
        grad_gain = part if grad_gain is None else grad_gain + part
        if number == 0:
            grad = grad + grad_tanner[...]
        out[...] = grad.astype(out.dtype)
        high = grad.astype(BF)
        low = (grad - high.astype(F32)).astype(BF)
        part = dot(onehot[...], jnp.concatenate([high, low], axis=1), ((0,), (0,)))[:16]
        part = part[:, :WIDTH] + part[:, WIDTH:]
        small = part if small is None else small + part
    row = lax.broadcasted_iota(jnp.int32, small.shape, 0)
    small = jnp.where(row == 9, grad_gain, small)
    small = jnp.where(row == 10, grad_gain_time[...], small)
    small = jnp.where(row == 11, grad_gain_ffn[...], small).astype(BF)
    grad_time_low = grad_time[...].astype(BF)
    grad_tanner_low = grad_tanner[...].astype(BF)
    grad_all = jnp.concatenate([grad_own[...], grad_row[...], grad_col[...]], axis=0)
    mine = pl.ds(pl.multiple_of(core * HALF, HALF), HALF)
    other = pl.ds(pl.multiple_of((1 - core) * HALF, HALF), HALF)
    keep[:16, :] = small
    send[:16, :] = small
    pairs = [(transposed.at[0], grad_packed[:, block * WIDTH : (block + 1) * WIDTH]) for block in range(3)]
    pairs.append((transposed.at[1], grad_time_low))
    pairs.append((transposed.at[2], grad_tanner_low))
    pairs.append((transposed_own.at[:, pl.ds(0, tokens)], grad_query[...]))
    pairs += [(transposed_own, grad_all[:, block * WIDTH : (block + 1) * WIDTH]) for block in range(2)]
    for block, (lead, grad) in enumerate(pairs):
        product = dot(jnp.concatenate([lead[mine, :], lead[other, :]], axis=0), grad).astype(BF)
        rows = slice(16 + block * HALF, 16 + (block + 1) * HALF)
        keep[rows, :] = product[:HALF]
        send[rows, :] = product[HALF:]


def my_bit(bit):
    many = lax.axis_size("gy").bit_length() - 1
    if bit < many:
        return (lax.axis_index("gy") >> bit) & 1
    return (lax.axis_index("gx") >> (bit - many)) & 1


def split_kernel(extra, bit, kept, received, keep, send, total):
    mine = my_bit(bit)
    value = kept[...].astype(F32) + received[...].astype(F32)
    total[...] = value[extra:]
    rows = keep.shape[0] - extra
    for ref, which in ((keep, mine), (send, 1 - mine)):
        if extra:
            ref[:extra, :] = value[:extra].astype(BF)
        ref[extra:, :] = total[pl.ds(pl.multiple_of(which * rows, rows), rows), :].astype(BF)


def sum_kernel(first, second, out):
    out[...] = (first[...].astype(F32) + second[...].astype(F32)).astype(BF)


def end_kernel(extra, scale, kept, received, out, *small):
    value = kept[...].astype(F32) + received[...].astype(F32)
    out[...] = value[extra:].astype(BF)
    if extra:
        value = value[:extra] * scale
        small[0][...] = value[:8]
        for number in range(4):
            small[1 + number][...] = value[8 + number : 9 + number]


def join_kernel(bit, own, received, out):
    mine = my_bit(bit)
    out[mine] = own[...]
    out[1 - mine] = received[...]


def unpack_kernel(groups, scale, grad, row, col, *refs):
    sources, refs = refs[: 2 * len(groups)], refs[2 * len(groups) :]
    token_out, *outs = refs[: len(refs) // 2]
    token_low, *wides = refs[len(refs) // 2 : -1]
    done = refs[-1]
    moves = []

    def move(source, target):
        moves.append(pltpu.make_async_copy(source, target, done.at[len(moves)]))
        moves[-1].start()

    for number, blocks in enumerate(groups):
        for side in range(2):
            source = sources[2 * number + side]
            half = pl.multiple_of((my_bit(0) ^ side) * HALF, HALF)
            block = 0
            first = sum(len(group) for group in groups[:number])
            for out, wide, (down, across) in zip(outs[first:], wides[first:], blocks):
                for index in range(down * across):
                    value = source[block * HALF : (block + 1) * HALF, :].astype(F32) * scale
                    left = (index if across > 1 else 0) * WIDTH
                    wide[side, index if down > 1 else 0, :, left : left + WIDTH] = value
                    block += 1
                for index in range(down):
                    move(wide.at[side, index], out.at[pl.ds(index * WIDTH + half, HALF)])
    token_low[...] = (grad[...] + row[...].astype(F32) + col[...].astype(F32)).astype(BF)
    move(token_low, token_out)
    for one in moves:
        one.wait()


def unpack(groups, scale, sources, grad, row, col):
    hbm = pl.BlockSpec(memory_space=pltpu.HBM)
    blocks = [block for group in groups for block in group]
    return pl.pallas_call(
        functools.partial(unpack_kernel, groups, scale),
        out_shape=[jax.ShapeDtypeStruct(grad.shape, BF)]
        + [jax.ShapeDtypeStruct((down * WIDTH, across * WIDTH), F32) for down, across in blocks],
        in_specs=[pl.BlockSpec(memory_space=pltpu.VMEM)] * (3 + len(sources)),
        out_specs=[hbm] * (1 + len(blocks)),
        scratch_shapes=[pltpu.VMEM(grad.shape, BF)]
        + [pltpu.VMEM((2, down, HALF, across * WIDTH), F32) for down, across in blocks]
        + [pltpu.SemaphoreType.DMA((1 + 2 * sum(down for down, _ in blocks),))],
        compiler_params=pltpu.CompilerParams(vmem_limit_bytes=16 * MIB),
    )(grad, row, col, *sources)


def estimate(work, outs=(), args=()):
    moved = sum(math.prod(shape) * jnp.dtype(dtype).itemsize for shape, dtype in outs)
    moved += sum(math.prod(arg.shape) * arg.dtype.itemsize for arg in args)
    return pl.CostEstimate(flops=int(work * 1.1e9), transcendentals=0, bytes_accessed=moved)


def call(kernel, outs, args, scratch=(), smem=0, limit=16, work=0.1):
    vmem = pl.BlockSpec(memory_space=pltpu.VMEM)
    return pl.pallas_call(
        kernel,
        out_shape=[jax.ShapeDtypeStruct(shape, dtype) for shape, dtype in outs],
        in_specs=[pl.BlockSpec(memory_space=pltpu.SMEM)] * smem + [vmem] * (len(args) - smem),
        out_specs=[vmem] * len(outs),
        scratch_shapes=list(scratch),
        compiler_params=pltpu.CompilerParams(vmem_limit_bytes=limit * MIB),
        cost_estimate=estimate(work, outs, args),
    )(*args)


def shifted(x, axis, by):
    count = lax.axis_size(axis)
    return lax.ppermute(x, axis, [(i, (i + by) % count) for i in range(count)])


class Layout:
    def __init__(self):
        self.nx = lax.axis_size("gx")
        self.ny = lax.axis_size("gy")
        self.many = self.ny.bit_length() - 1
        self.bits = self.many + self.nx.bit_length() - 1
        assert 1 << self.bits == self.nx * self.ny

    def swap(self, x, bit):
        flip = 1 << bit if bit < self.many else self.ny << (bit - self.many)
        return lax.ppermute(x, ("gx", "gy"), [(i, i ^ flip) for i in range(self.nx * self.ny)])


def reduce_tree(layout, keep, send, extra, order, scale, first=0, until=None, beside=()):
    halving = order[:-1]
    for stage in range(first, len(halving) if until is None else until):
        received = layout.swap(send, halving[stage])
        if stage == 2 and beside:
            received, *beside = lax.optimization_barrier((received, *beside))
        rows = keep.shape[0] - extra
        if stage + 1 < len(halving):
            half = ((rows // 2 + extra, WIDTH), BF)
            keep, send = call(
                functools.partial(split_kernel, extra, halving[stage + 1]),
                [half, half],
                [keep, received],
                [pltpu.VMEM((rows, WIDTH), F32)],
            )
    if until is not None:
        return keep, send
    total = call(sum_kernel, [(keep.shape, BF)], [keep, received])[0]
    received = layout.swap(total, order[-1])
    small = [((8, WIDTH), F32)] + [((1, WIDTH), F32)] * 4 if extra else []
    outs = call(functools.partial(end_kernel, extra, scale), [((rows, WIDTH), BF)] + small, [total, received])
    return (*outs, *beside)


def gather_tree(layout, own, order):
    for bit in order[-2:0:-1]:
        received = layout.swap(own, bit)
        rows = own.shape[0]
        own = call(
            functools.partial(join_kernel, bit), [((2, rows, WIDTH), BF)], [own, received]
        )[0].reshape(2 * rows, WIDTH)
    return own, layout.swap(own, order[0])


def on_device(
    tokens,
    syndrome,
    check_plan_step,
    offsets,
    flip_vector,
    plan_step_embedding,
    gain_tanner,
    w_query,
    w_key_value,
    w_merge,
    gain_time,
    w_temporal,
    w_temporal_out,
    gain_ffn,
    w_ffn_up,
    w_ffn_down,
    cotangent,
):
    layout = Layout()
    rounds, rows, cols = tokens.shape[:3]
    count = rounds * rows * cols
    scale = 1.0 / math.sqrt(count * layout.nx * layout.ny)
    flat = (count, WIDTH)
    act = (flat, BF)
    stream = (flat, F32)
    wide = ((count, 2 * WIDTH), BF)
    lanes = ((count, LANES), F32)
    onehot = ((count, LANES), BF)
    row = ((1, WIDTH), F32)
    hbm = pl.BlockSpec(memory_space=pltpu.HBM)

    sites = pltpu.VMEM((rounds, rows, cols), jnp.int32)
    codes = pl.pallas_call(
        code_kernel,
        out_shape=jax.ShapeDtypeStruct((rounds * rows, LANES), BF),
        in_specs=[hbm] * 2,
        out_specs=pl.BlockSpec(memory_space=pltpu.VMEM),
        scratch_shapes=[sites, sites, pltpu.SemaphoreType.DMA((2,))],
        cost_estimate=estimate(12),
    )(syndrome, check_plan_step)
    row_tokens = shifted(tokens, "gx", -1).reshape(flat)
    col_tokens = shifted(tokens, "gy", -1).reshape(flat)
    row_codes = shifted(codes, "gx", -1)
    col_codes = shifted(codes, "gy", -1)
    plan = plan_step_embedding
    flip = flip_vector.reshape(1, WIDTH)
    gain_one = gain_tanner.reshape(1, WIDTH)
    gain_two = gain_time.reshape(1, WIDTH)
    gain_three = gain_ffn.reshape(1, WIDTH)
    outer = cotangent.reshape(flat)
    weights = [w_query, w_key_value, w_merge, w_temporal, w_temporal_out, w_ffn_up, w_ffn_down]
    heads = [
        (((MONOS + 1) * WIDTH, LANES), BF), ((LANES, (MONOS + 1) * WIDTH), BF),
        ((rounds * WIDTH, LANES), BF), ((LANES, rounds * WIDTH), BF),
    ]
    (
        x, onehot_own, hidden_one, query, key_value, gain_one, gain_two, gain_three,
        gathers, spreads, gathers_time, spreads_time, *flipped,
    ) = call(
        start_kernel,
        [stream, onehot, act, act, wide, row, row, row] + heads + [(weight.shape[::-1], BF) for weight in weights],
        [tokens.reshape(flat), codes, plan, flip, gain_one, gain_two, gain_three, *weights],

    )
    extended = pltpu.VMEM((rounds, 2 * rows, cols, 2 * WIDTH), F32)
    columns = pltpu.VMEM((rounds * rows, cols, 2 * WIDTH), F32)
    half_one = ((2 * (FF // WIDTH) * HALF, WIDTH), BF)
    (
        keep_one, send_one, grad_time, after_tanner, mixed_one, mixed_two, packed, hidden_two,
        row_kv, col_kv, row_x, col_x, row_hidden, col_hidden, row_onehot, col_onehot,
        bent_one, probs_one, bent_two, probs_two, grad_gain_ffn,
    ) = call(
        forward_kernel,
        [half_one, half_one, stream, stream, act, act, ((count, 3 * WIDTH), BF), act,
         wide, wide, stream, stream, act, act, onehot, onehot, lanes, lanes, lanes, lanes, row],
        [offsets, x, query, key_value, row_tokens, row_codes, col_tokens, col_codes, plan, flip,
         gathers, spreads, gathers_time, spreads_time, gain_one, w_key_value, w_merge, gain_two, w_temporal, w_temporal_out, gain_three, w_ffn_up, flipped[5], flipped[6],
         outer],
        [extended, columns, pltpu.VMEM((WIDTH, count), BF), pltpu.VMEM((FF, count), BF)],
        smem=1,
        limit=32,

    )
    grad_query, grad_kv, grad_rows, grad_cols, grad_packed, grad_tanner, grad_gain_time = call(
        backward_kernel,
        [act, wide, wide, wide, ((count, 3 * WIDTH), BF), stream, row],
        [offsets, grad_time, after_tanner, packed, query, key_value, row_kv, col_kv,
         bent_one, probs_one, bent_two, probs_two, gathers, spreads, gathers_time, spreads_time, flipped[2], gain_two, flipped[3], flipped[4]],
        [extended, columns, extended],
        smem=1,
        limit=32,
        work=3,
    )
    many, bits = layout.many, layout.bits
    order_one = list(range(many)) + list(range(many, bits))
    order_two = [0, many] + list(range(1, many)) + list(range(many + 1, bits))
    keep_one, send_one = reduce_tree(layout, keep_one, send_one, 0, order_one, scale, until=1)
    keep_one, grad_tanner = lax.optimization_barrier((keep_one, grad_tanner))
    half_two = ((16 + 8 * HALF, WIDTH), BF)
    grad_own, lent_rows, lent_cols, keep_two, send_two = call(
        weights_kernel,
        [stream, act, act, half_two, half_two],
        [mixed_two, grad_time, hidden_two, grad_packed, mixed_one, grad_tanner, grad_query, flipped[0], flipped[1],
         gain_one, x, row_x, col_x, hidden_one, row_hidden, col_hidden, onehot_own, row_onehot, col_onehot,
         grad_kv, grad_rows, grad_cols, grad_gain_time, grad_gain_ffn],
        [pltpu.VMEM((3, WIDTH, count), BF), pltpu.VMEM((WIDTH, 3 * count), BF)],
        limit=32,
        work=3,
    )
    back_rows = shifted(lent_rows, "gx", 1)
    back_cols = shifted(lent_cols, "gy", 1)
    shard_one, back_rows, back_cols = reduce_tree(
        layout, keep_one, send_one, 0, order_one, scale, first=1, beside=(back_rows, back_cols)
    )
    shard_two, plan_grad, grad_flip, sum_gain_tanner, sum_gain_time, sum_gain_ffn = reduce_tree(
        layout, keep_two, send_two, 16, order_two, scale
    )
    sources = [*gather_tree(layout, shard_one, order_one), *gather_tree(layout, shard_two, order_two)]
    groups = (((1, FF // WIDTH), (FF // WIDTH, 1)), ((1, 3), (1, 1), (1, 1), (1, 1), (1, 2)))
    (
        token_grad, grad_up, grad_down, grad_temporal, grad_temporal_out, grad_merge, grad_w_query, grad_key_value,
    ) = unpack(groups, scale, sources, grad_own, back_rows, back_cols)
    return (
        token_grad.reshape(tokens.shape),
        grad_flip.reshape(WIDTH),
        plan_grad,
        sum_gain_tanner.reshape(WIDTH),
        grad_w_query,
        grad_key_value,
        grad_merge,
        sum_gain_time.reshape(WIDTH),
        grad_temporal,
        grad_temporal_out,
        sum_gain_ffn.reshape(WIDTH),
        grad_up,
        grad_down,
    )


def solution(mesh):
    tiled = P(None, "gx", "gy", None)
    sites = P(None, "gx", "gy")
    return jax.shard_map(
        on_device,
        mesh=mesh,
        in_specs=(tiled, sites, sites) + (P(),) * 13 + (tiled,),
        out_specs=(tiled,) + (P(),) * 12,
        check_vma=False,
    )
```

```python
import functools
import math

import jax
import jax.numpy as jnp
from jax import lax
from jax.experimental import pallas as pl
from jax.experimental.pallas import tpu as pltpu
from jax.sharding import PartitionSpec as P

WIDTH = 256
HEADDIM = 32
HEADS = WIDTH // HEADDIM
FF = 1024
PLAN_STEP_COUNT = 8
MONOS = 6
MAXEXP = 8
LANES = 128
HALF = WIDTH // 2

EPS = 1e-05
CAP = 4.0
ALONG_ROWS = (0, 4, 5)
BF = jnp.bfloat16
F32 = jnp.float32
SCORE = 1.0 / math.sqrt(HEADDIM)
GELU_A = math.sqrt(2.0 / math.pi)
GELU_B = 0.044715
MIB = 1 << 20


def dot(a, b, dims=((1,), (0,))):
    return lax.dot_general(a, b, (dims, ((), ())), preferred_element_type=F32)


def dot_nt(a, b):
    return dot(a, b, ((1,), (1,)))


def embed(values, codes, plan, flip):
    tokens = values.shape[0]
    lines = codes.shape[0]
    width = tokens // lines
    token = lax.broadcasted_iota(jnp.int32, (tokens, lines), 0)
    line = lax.broadcasted_iota(jnp.int32, (tokens, lines), 1)
    spread = dot(jnp.where(token // width == line, 1.0, 0.0).astype(BF), codes)
    token = lax.broadcasted_iota(jnp.int32, (tokens, LANES), 0)
    lane = lax.broadcasted_iota(jnp.int32, (tokens, LANES), 1)
    picked = jnp.where(token % width == lane, spread, 0.0).astype(BF)
    code = dot(picked, jnp.ones((LANES, LANES), BF))
    flipped = code >= PLAN_STEP_COUNT
    step = jnp.where(flipped, code - PLAN_STEP_COUNT, code)
    slot = lane % 16
    chosen = (slot.astype(F32) == step) | ((slot == PLAN_STEP_COUNT) & flipped)
    onehot = jnp.where(chosen & (lane < 48), 1.0, 0.0).astype(BF)
    row = lax.broadcasted_iota(jnp.int32, (8, WIDTH), 0)
    table = jnp.concatenate([plan, jnp.where(row == 0, flip, 0.0)], axis=0)
    high = table.astype(BF)
    rest = table - high.astype(F32)
    middle = rest.astype(BF)
    low = (rest - middle.astype(F32)).astype(BF)
    empty = jnp.zeros((LANES - 48, WIDTH), BF)
    vectors = dot(onehot, jnp.concatenate([high, middle, low, empty], axis=0))
    return values.astype(F32) + vectors, onehot


def inverse_rms(stream):
    return lax.rsqrt(jnp.mean(stream * stream, axis=-1, keepdims=True) + EPS)


def norm_back(stream, gain, grad):
    inverse = inverse_rms(stream)
    normed = stream * inverse
    scaled = grad * gain
    mean = jnp.mean(scaled * normed, axis=-1, keepdims=True)
    return inverse * (scaled - normed * mean), jnp.sum(grad * normed, axis=0, keepdims=True)


def gather_heads(slot, period):
    feature = lax.broadcasted_iota(jnp.int32, (WIDTH, LANES), 0) // HEADDIM
    lane = lax.broadcasted_iota(jnp.int32, (WIDTH, LANES), 1) % period
    return jnp.where(lane - feature == slot * HEADS, 1.0, 0.0).astype(BF)


def spread_heads(slot, period):
    lane = lax.broadcasted_iota(jnp.int32, (LANES, WIDTH), 0)
    feature = lax.broadcasted_iota(jnp.int32, (LANES, WIDTH), 1) // HEADDIM
    at = (lane < 2 * period) & (lane % period - feature == slot * HEADS)
    return jnp.where(at, 1.0, 0.0).astype(BF)


def two_parts(value, period):
    lane = lax.broadcasted_iota(jnp.int32, value.shape, 1)
    high = value.astype(BF).astype(F32)
    return jnp.where(lane < period, high, value - high).astype(BF)


def slot_total(value, period):
    shift = HEADS
    while shift < period:
        value = value + pltpu.roll(value, shift, 1)
        shift *= 2
    return value


def softmax_parts(scores, valid, period):
    bent = jnp.tanh(scores * (SCORE / CAP))
    weights = jnp.where(valid, jnp.exp(CAP * bent), 0.0)
    return bent, weights / slot_total(weights, period)


def softmax_back(bent, probs, grad, period):
    inner = probs * grad
    return (inner - probs * slot_total(inner, period)) * (1.0 - bent * bent) * SCORE


def tanner_valid(tokens):
    lane = lax.broadcasted_iota(jnp.int32, (tokens, LANES), 1)
    return lane % 64 < HEADS * (MONOS + 1)


def time_valid(tokens, rounds):
    lane = lax.broadcasted_iota(jnp.int32, (tokens, LANES), 1)
    row = lax.broadcasted_iota(jnp.int32, (tokens, LANES), 0)
    return (lane % 32) // HEADS <= row // (tokens // rounds)


def offset_of(offsets, index):
    return offsets[index, 0] if index in ALONG_ROWS else offsets[index, 1]


def neighbour(number, offsets, extended, columns):
    rounds, twice, width, features = extended.shape
    rows = twice // 2
    tokens = rounds * rows * width
    if number == 0:
        return extended[:, :rows].reshape(tokens, features)
    by = offset_of(offsets, number - 1)
    if number - 1 in ALONG_ROWS:
        return extended[:, pl.ds(by, rows)].reshape(tokens, features)
    own = extended[:, :rows].reshape(rounds * rows, width, features)
    place = lax.broadcasted_iota(jnp.int32, own.shape, 1)
    joined = jnp.where(place >= by, own, columns[...])
    return pltpu.roll(joined, width - by, 1).reshape(tokens, features)


def code_kernel(code, out):
    rounds, rows, width = code.shape
    out[...] = jnp.zeros(out.shape, BF)
    out[:, :width] = code[...].reshape(rounds * rows, width).astype(F32).astype(BF)


def start_kernel(tokens, codes, plan, flip, gain, gain_two, gain_three, *refs):
    count = (len(refs) - 8) // 2
    weights, outs = refs[:count], refs[count:]
    x_out, onehot_out, hidden_out, query_out, kv_out, *passed = outs[:8]
    w_query, w_key_value = weights[:2]
    for weight, out in zip(weights, outs[8:]):
        out[...] = weight[...].T
    for source, out in zip((gain, gain_two, gain_three), passed):
        out[...] = source[...]
    x, onehot = embed(tokens[...], codes[...], plan[...], flip[...])
    hidden = (x * inverse_rms(x) * gain[...]).astype(BF)
    x_out[...] = x
    onehot_out[...] = onehot
    hidden_out[...] = hidden
    query_out[...] = dot(hidden, w_query[...]).astype(BF)
    kv_out[...] = dot(hidden, w_key_value[...]).astype(BF)


def forward_kernel(
    offsets, x_in, query_in, kv_in, row_tokens, row_codes, col_tokens, col_codes, plan, flip,
    gain_tanner, w_key_value, w_merge, gain_time, w_temporal, w_temporal_out, gain_ffn, w_up, w_up_t, w_down_t, cotangent,
    keep, send, grad_time_out, tanner_out, mixed_one_out, mixed_two_out, packed_out, hidden_two_out,
    row_kv_out, col_kv_out, row_x_out, col_x_out, row_hidden_out, col_hidden_out, row_onehot_out, col_onehot_out,
    bent_one_out, probs_one_out, bent_two_out, probs_two_out, grad_gain_out,
    extended, columns, transposed, transposed_act,
):
    rounds, twice, width, features = extended.shape
    rows = twice // 2
    tokens = x_in.shape[0]
    core = my_bit(0)
    borrowed = []
    for other, codes, x_out, hidden_out, onehot_out, kv_out in (
        (row_tokens, row_codes, row_x_out, row_hidden_out, row_onehot_out, row_kv_out),
        (col_tokens, col_codes, col_x_out, col_hidden_out, col_onehot_out, col_kv_out),
    ):
        x, onehot = embed(other[...], codes[...], plan[...], flip[...])
        hidden = (x * inverse_rms(x) * gain_tanner[...]).astype(BF)
        kv = dot(hidden, w_key_value[...]).astype(BF)
        x_out[...] = x
        onehot_out[...] = onehot
        hidden_out[...] = hidden
        kv_out[...] = kv
        borrowed.append(kv.astype(F32))
    extended[:, :rows] = kv_in[...].astype(F32).reshape(rounds, rows, width, features)
    extended[:, rows:] = borrowed[0].reshape(rounds, rows, width, features)
    columns[...] = borrowed[1].reshape(rounds * rows, width, features)
    query = query_in[...].astype(F32)
    scores = None
    for number in range(MONOS + 1):
        keys = neighbour(number, offsets, extended, columns)[:, :WIDTH]
        part = dot((query * keys).astype(BF), gather_heads(number, 64))
        scores = part if scores is None else scores + part
    bent, probs = softmax_parts(scores, tanner_valid(tokens), 64)
    bent_one_out[...] = bent
    probs_one_out[...] = probs
    parts = two_parts(probs, 64)
    mixed = None
    for number in range(MONOS + 1):
        values = neighbour(number, offsets, extended, columns)[:, WIDTH:]
        part = dot(parts, spread_heads(number, 64)) * values
        mixed = part if mixed is None else mixed + part
    mixed_one = mixed.astype(BF)
    mixed_one_out[...] = mixed_one
    after_tanner = x_in[...] + dot(mixed_one, w_merge[...])
    tanner_out[...] = after_tanner

    hidden_two = (after_tanner * inverse_rms(after_tanner) * gain_time[...]).astype(BF)
    hidden_two_out[...] = hidden_two
    packed_low = dot(hidden_two, w_temporal[...]).astype(BF)
    packed_out[...] = packed_low
    packed = packed_low.astype(F32).reshape(rounds, tokens // rounds, 3 * WIDTH)
    sites = tokens // rounds
    scores = None
    for earlier in range(rounds):
        product = packed[earlier:, :, :WIDTH] * packed[earlier][None, :, WIDTH : 2 * WIDTH]
        part = dot(product.reshape(-1, WIDTH).astype(BF), gather_heads(earlier, 32))
        if earlier:
            part = jnp.concatenate([jnp.zeros((earlier * sites, LANES), F32), part], axis=0)
        scores = part if scores is None else scores + part
    bent, probs = softmax_parts(scores, time_valid(tokens, rounds), 32)
    bent_two_out[...] = bent
    probs_two_out[...] = probs
    parts = two_parts(probs, 32)
    mixed = None
    for earlier in range(rounds):
        weight = dot(parts[earlier * sites :], spread_heads(earlier, 32)).reshape(rounds - earlier, sites, WIDTH)
        part = (weight * packed[earlier][None, :, 2 * WIDTH :]).reshape(-1, WIDTH)
        if earlier:
            part = jnp.concatenate([jnp.zeros((earlier * sites, WIDTH), F32), part], axis=0)
        mixed = part if mixed is None else mixed + part
    mixed_two = mixed.astype(BF)
    mixed_two_out[...] = mixed_two
    after_time = after_tanner + dot(mixed_two, w_temporal_out[...])

    hidden = (after_time * inverse_rms(after_time) * gain_ffn[...]).astype(BF)
    outer = cotangent[...]
    transposed[...] = hidden.T
    grad_three = None
    befores = []
    for block in range(FF // WIDTH):
        cols = slice(block * WIDTH, (block + 1) * WIDTH)
        before = dot(hidden, w_up[:, cols])
        square = before * before
        bend = jnp.tanh(GELU_A * before * (1.0 + GELU_B * square))
        upper = 0.5 * (1.0 + bend)
        activated = (before * upper).astype(BF)
        slope = upper + 0.5 * before * (1.0 - bend * bend) * (GELU_A * (1.0 + 3.0 * GELU_B * square))
        grad_before = (dot(outer, w_down_t[:, cols]) * slope).astype(BF)
        befores.append(grad_before)
        part = dot(grad_before, w_up_t[cols, :])
        grad_three = part if grad_three is None else grad_three + part
        transposed_act[cols, :] = activated.T
    mine = pl.multiple_of(core * HALF, HALF)
    other = pl.multiple_of((1 - core) * HALF, HALF)
    blocks = FF // WIDTH
    lead = jnp.concatenate([transposed[pl.ds(start, HALF), :] for start in (mine, other)], axis=0)
    for block in range(blocks):
        product = dot(lead, befores[block]).astype(BF)
        keep[block * HALF : (block + 1) * HALF, :] = product[:HALF]
        send[block * HALF : (block + 1) * HALF, :] = product[HALF:]
    lead = jnp.concatenate(
        [transposed_act[pl.ds(block * WIDTH + start, HALF), :] for start in (mine, other) for block in range(blocks)],
        axis=0,
    )
    product = dot(lead, outer).astype(BF)
    keep[blocks * HALF :, :] = product[: blocks * HALF]
    send[blocks * HALF :, :] = product[blocks * HALF :]
    grad_norm, grad_gain = norm_back(after_time, gain_ffn[...], grad_three)
    grad_time_out[...] = outer.astype(F32) + grad_norm
    grad_gain_out[...] = grad_gain


def backward_kernel(
    offsets, grad_time_in, tanner_in, packed_in, query_in, kv_in, row_kv, col_kv,
    bent_one, probs_one, bent_two, probs_two, w_merge, gain_time, w_temporal, w_temporal_out,
    grad_query_out, grad_kv_out, grad_rows_out, grad_cols_out, grad_packed_out, grad_tanner_out, grad_gain_out,
    extended, columns, grad_extended,
):
    rounds, twice, width, features = extended.shape
    rows = twice // 2
    tokens = grad_time_in.shape[0]
    sites = tokens // rounds
    grad_time = grad_time_in[...]
    grad_mixed = dot(grad_time.astype(BF), w_temporal_out[...]).reshape(rounds, sites, WIDTH)
    packed = packed_in[...].astype(F32).reshape(rounds, sites, 3 * WIDTH)
    grad_probs = None
    for earlier in range(rounds):
        product = grad_mixed[earlier:] * packed[earlier][None, :, 2 * WIDTH :]
        part = dot(product.reshape(-1, WIDTH).astype(BF), gather_heads(earlier, 32))
        if earlier:
            part = jnp.concatenate([jnp.zeros((earlier * sites, LANES), F32), part], axis=0)
        grad_probs = part if grad_probs is None else grad_probs + part
    probs = probs_two[...]
    prob_parts = two_parts(probs, 32)
    score_parts = two_parts(softmax_back(bent_two[...], probs, grad_probs, 32), 32)
    grad_queries = None
    grad_keys = []
    grad_values = []
    for earlier in range(rounds):
        spread = spread_heads(earlier, 32)
        shape = (rounds - earlier, sites, WIDTH)
        weight = dot(prob_parts[earlier * sites :], spread).reshape(shape)
        slope = dot(score_parts[earlier * sites :], spread).reshape(shape)
        grad_values.append(jnp.sum(weight * grad_mixed[earlier:], axis=0))
        grad_keys.append(jnp.sum(slope * packed[earlier:, :, :WIDTH], axis=0))
        part = (slope * packed[earlier][None, :, WIDTH : 2 * WIDTH]).reshape(-1, WIDTH)
        if earlier:
            part = jnp.concatenate([jnp.zeros((earlier * sites, WIDTH), F32), part], axis=0)
        grad_queries = part if grad_queries is None else grad_queries + part
    grad_packed = jnp.concatenate(
        [grad_queries, jnp.concatenate(grad_keys, axis=0), jnp.concatenate(grad_values, axis=0)], axis=1
    ).astype(BF)
    grad_packed_out[...] = grad_packed
    grad_two = dot(grad_packed, w_temporal[...])
    grad_norm, grad_gain = norm_back(tanner_in[...], gain_time[...], grad_two)
    grad_gain_out[...] = grad_gain
    grad_tanner = grad_time + grad_norm
    grad_tanner_out[...] = grad_tanner

    grad_mixed = dot(grad_tanner.astype(BF), w_merge[...])
    extended[:, :rows] = kv_in[...].astype(F32).reshape(rounds, rows, width, features)
    extended[:, rows:] = row_kv[...].astype(F32).reshape(rounds, rows, width, features)
    columns[...] = col_kv[...].astype(F32).reshape(rounds * rows, width, features)
    grad_probs = None
    for number in range(MONOS + 1):
        values = neighbour(number, offsets, extended, columns)[:, WIDTH:]
        part = dot((grad_mixed * values).astype(BF), gather_heads(number, 64))
        grad_probs = part if grad_probs is None else grad_probs + part
    probs = probs_one[...]
    prob_parts = two_parts(probs, 64)
    score_parts = two_parts(softmax_back(bent_one[...], probs, grad_probs, 64), 64)
    query = query_in[...].astype(F32)
    grad_query = None
    grad_cols = None
    for number in (0,) + tuple(i + 1 for i in range(MONOS)):
        spread = spread_heads(number, 64)
        slope = dot(score_parts, spread)
        weight = dot(prob_parts, spread)
        keys = neighbour(number, offsets, extended, columns)[:, :WIDTH]
        part = slope * keys
        grad_query = part if grad_query is None else grad_query + part
        grad_kv = jnp.concatenate([slope * query, weight * grad_mixed], axis=1)
        if number == 0:
            grad_extended[:, :rows] = grad_kv.reshape(rounds, rows, width, features)
            grad_extended[:, rows:] = jnp.zeros((rounds, rows, width, features), F32)
            continue
        by = offset_of(offsets, number - 1)
        if number - 1 in ALONG_ROWS:
            grad_extended[:, pl.ds(by, rows)] += grad_kv.reshape(rounds, rows, width, features)
            continue
        moved = pltpu.roll(grad_kv.reshape(rounds * rows, width, features), by % width, 1)
        place = lax.broadcasted_iota(jnp.int32, moved.shape, 1)
        own = jnp.where(place >= by, moved, 0.0)
        grad_extended[:, :rows] += own.reshape(rounds, rows, width, features)
        grad_cols = moved - own if grad_cols is None else grad_cols + (moved - own)
    grad_query_out[...] = grad_query.astype(BF)
    grad_kv_out[...] = grad_extended[:, :rows].reshape(tokens, features).astype(BF)
    grad_rows_out[...] = grad_extended[:, rows:].reshape(tokens, features).astype(BF)
    grad_cols_out[...] = grad_cols.reshape(tokens, features).astype(BF)


def weights_kernel(
    mixed_two, grad_time, hidden_two, grad_packed, mixed_one, grad_tanner, grad_query, w_query, w_key_value, gain,
    x_own, x_row, x_col, hidden_own, hidden_row, hidden_col, onehot_own, onehot_row, onehot_col,
    grad_own, grad_row, grad_col, grad_gain_time, grad_gain_ffn,
    grad_out, row_out, col_out, keep, send, transposed, transposed_own,
):
    core = my_bit(0)
    tokens = x_own.shape[0]
    transposed[0] = hidden_two[...].T
    transposed[1] = mixed_two[...].T
    transposed[2] = mixed_one[...].T
    small = None
    grad_gain = None
    for number, (x, hidden, onehot, grad_kv, out) in enumerate((
        (x_own, hidden_own, onehot_own, grad_own, grad_out),
        (x_row, hidden_row, onehot_row, grad_row, row_out),
        (x_col, hidden_col, onehot_col, grad_col, col_out),
    )):
        transposed_own[:, number * tokens : (number + 1) * tokens] = hidden[...].T
        grad_one = dot(grad_kv[...], w_key_value[...])
        if number == 0:
            grad_one = grad_one + dot(grad_query[...], w_query[...])
        grad, part = norm_back(x[...], gain[...], grad_one)
        grad_gain = part if grad_gain is None else grad_gain + part
        if number == 0:
            grad = grad + grad_tanner[...]
        out[...] = grad.astype(out.dtype)
        high = grad.astype(BF)
        low = (grad - high.astype(F32)).astype(BF)
        part = dot(onehot[...], jnp.concatenate([high, low], axis=1), ((0,), (0,)))[:16]
        part = part[:, :WIDTH] + part[:, WIDTH:]
        small = part if small is None else small + part
    row = lax.broadcasted_iota(jnp.int32, small.shape, 0)
    small = jnp.where(row == 9, grad_gain, small)
    small = jnp.where(row == 10, grad_gain_time[...], small)
    small = jnp.where(row == 11, grad_gain_ffn[...], small).astype(BF)
    grad_time_low = grad_time[...].astype(BF)
    grad_tanner_low = grad_tanner[...].astype(BF)
    grad_all = jnp.concatenate([grad_own[...], grad_row[...], grad_col[...]], axis=0)
    mine = pl.ds(pl.multiple_of(core * HALF, HALF), HALF)
    other = pl.ds(pl.multiple_of((1 - core) * HALF, HALF), HALF)
    keep[:16, :] = small
    send[:16, :] = small
    pairs = [(transposed.at[0], grad_packed[:, block * WIDTH : (block + 1) * WIDTH]) for block in range(3)]
    pairs.append((transposed.at[1], grad_time_low))
    pairs.append((transposed.at[2], grad_tanner_low))
    pairs.append((transposed_own.at[:, pl.ds(0, tokens)], grad_query[...]))
    pairs += [(transposed_own, grad_all[:, block * WIDTH : (block + 1) * WIDTH]) for block in range(2)]
    for block, (lead, grad) in enumerate(pairs):
        product = dot(jnp.concatenate([lead[mine, :], lead[other, :]], axis=0), grad).astype(BF)
        rows = slice(16 + block * HALF, 16 + (block + 1) * HALF)
        keep[rows, :] = product[:HALF]
        send[rows, :] = product[HALF:]


def my_bit(bit):
    many = lax.axis_size("gy").bit_length() - 1
    if bit < many:
        return (lax.axis_index("gy") >> bit) & 1
    return (lax.axis_index("gx") >> (bit - many)) & 1


def split_kernel(extra, bit, kept, received, keep, send, total):
    mine = my_bit(bit)
    value = kept[...].astype(F32) + received[...].astype(F32)
    total[...] = value[extra:]
    rows = keep.shape[0] - extra
    for ref, which in ((keep, mine), (send, 1 - mine)):
        if extra:
            ref[:extra, :] = value[:extra].astype(BF)
        ref[extra:, :] = total[pl.ds(pl.multiple_of(which * rows, rows), rows), :].astype(BF)


def sum_kernel(first, second, out):
    out[...] = (first[...].astype(F32) + second[...].astype(F32)).astype(BF)


def end_kernel(extra, scale, kept, received, out, *small):
    value = kept[...].astype(F32) + received[...].astype(F32)
    out[...] = value[extra:].astype(BF)
    if extra:
        value = value[:extra] * scale
        small[0][...] = value[:8]
        for number in range(4):
            small[1 + number][...] = value[8 + number : 9 + number]


def join_kernel(bit, own, received, out):
    mine = my_bit(bit)
    out[mine] = own[...]
    out[1 - mine] = received[...]


def unpack_kernel(groups, scale, grad, row, col, *refs):
    sources, refs = refs[: 2 * len(groups)], refs[2 * len(groups) :]
    token_out, *outs = refs[: len(refs) // 2]
    token_low, *wides = refs[len(refs) // 2 : -1]
    done = refs[-1]
    moves = []

    def move(source, target):
        moves.append(pltpu.make_async_copy(source, target, done.at[len(moves)]))
        moves[-1].start()

    for number, blocks in enumerate(groups):
        for side in range(2):
            source = sources[2 * number + side]
            half = pl.multiple_of((my_bit(0) ^ side) * HALF, HALF)
            block = 0
            first = sum(len(group) for group in groups[:number])
            for out, wide, (down, across) in zip(outs[first:], wides[first:], blocks):
                for index in range(down * across):
                    value = source[block * HALF : (block + 1) * HALF, :].astype(F32) * scale
                    left = (index if across > 1 else 0) * WIDTH
                    wide[side, index if down > 1 else 0, :, left : left + WIDTH] = value
                    block += 1
                for index in range(down):
                    move(wide.at[side, index], out.at[pl.ds(index * WIDTH + half, HALF)])
    token_low[...] = (grad[...] + row[...].astype(F32) + col[...].astype(F32)).astype(BF)
    move(token_low, token_out)
    for one in moves:
        one.wait()


def unpack(groups, scale, sources, grad, row, col):
    hbm = pl.BlockSpec(memory_space=pltpu.HBM)
    blocks = [block for group in groups for block in group]
    return pl.pallas_call(
        functools.partial(unpack_kernel, groups, scale),
        out_shape=[jax.ShapeDtypeStruct(grad.shape, BF)]
        + [jax.ShapeDtypeStruct((down * WIDTH, across * WIDTH), F32) for down, across in blocks],
        in_specs=[pl.BlockSpec(memory_space=pltpu.VMEM)] * (3 + len(sources)),
        out_specs=[hbm] * (1 + len(blocks)),
        scratch_shapes=[pltpu.VMEM(grad.shape, BF)]
        + [pltpu.VMEM((2, down, HALF, across * WIDTH), F32) for down, across in blocks]
        + [pltpu.SemaphoreType.DMA((1 + 2 * sum(down for down, _ in blocks),))],
        compiler_params=pltpu.CompilerParams(vmem_limit_bytes=16 * MIB),
    )(grad, row, col, *sources)


def estimate(work, outs=(), args=()):
    moved = sum(math.prod(shape) * jnp.dtype(dtype).itemsize for shape, dtype in outs)
    moved += sum(math.prod(arg.shape) * arg.dtype.itemsize for arg in args)
    return pl.CostEstimate(flops=int(work * 1.1e9), transcendentals=0, bytes_accessed=moved)


def call(kernel, outs, args, scratch=(), smem=0, limit=16, work=0.1):
    vmem = pl.BlockSpec(memory_space=pltpu.VMEM)
    return pl.pallas_call(
        kernel,
        out_shape=[jax.ShapeDtypeStruct(shape, dtype) for shape, dtype in outs],
        in_specs=[pl.BlockSpec(memory_space=pltpu.SMEM)] * smem + [vmem] * (len(args) - smem),
        out_specs=[vmem] * len(outs),
        scratch_shapes=list(scratch),
        compiler_params=pltpu.CompilerParams(vmem_limit_bytes=limit * MIB),
        cost_estimate=estimate(work, outs, args),
    )(*args)


def shifted(x, axis, by):
    count = lax.axis_size(axis)
    return lax.ppermute(x, axis, [(i, (i + by) % count) for i in range(count)])


class Layout:
    def __init__(self):
        self.nx = lax.axis_size("gx")
        self.ny = lax.axis_size("gy")
        self.many = self.ny.bit_length() - 1
        self.bits = self.many + self.nx.bit_length() - 1
        assert 1 << self.bits == self.nx * self.ny

    def swap(self, x, bit):
        flip = 1 << bit if bit < self.many else self.ny << (bit - self.many)
        return lax.ppermute(x, ("gx", "gy"), [(i, i ^ flip) for i in range(self.nx * self.ny)])


def reduce_tree(layout, keep, send, extra, order, scale, first=0, until=None, beside=()):
    halving = order[:-1]
    for stage in range(first, len(halving) if until is None else until):
        received = layout.swap(send, halving[stage])
        if stage == 2 and beside:
            received, *beside = lax.optimization_barrier((received, *beside))
        rows = keep.shape[0] - extra
        if stage + 1 < len(halving):
            half = ((rows // 2 + extra, WIDTH), BF)
            keep, send = call(
                functools.partial(split_kernel, extra, halving[stage + 1]),
                [half, half],
                [keep, received],
                [pltpu.VMEM((rows, WIDTH), F32)],
            )
    if until is not None:
        return keep, send
    total = call(sum_kernel, [(keep.shape, BF)], [keep, received])[0]
    received = layout.swap(total, order[-1])
    small = [((8, WIDTH), F32)] + [((1, WIDTH), F32)] * 4 if extra else []
    outs = call(functools.partial(end_kernel, extra, scale), [((rows, WIDTH), BF)] + small, [total, received])
    return (*outs, *beside)


def gather_tree(layout, own, order):
    for bit in order[-2:0:-1]:
        received = layout.swap(own, bit)
        rows = own.shape[0]
        own = call(
            functools.partial(join_kernel, bit), [((2, rows, WIDTH), BF)], [own, received]
        )[0].reshape(2 * rows, WIDTH)
    return own, layout.swap(own, order[0])


def on_device(
    tokens,
    syndrome,
    check_plan_step,
    offsets,
    flip_vector,
    plan_step_embedding,
    gain_tanner,
    w_query,
    w_key_value,
    w_merge,
    gain_time,
    w_temporal,
    w_temporal_out,
    gain_ffn,
    w_ffn_up,
    w_ffn_down,
    cotangent,
):
    layout = Layout()
    rounds, rows, cols = tokens.shape[:3]
    count = rounds * rows * cols
    scale = 1.0 / math.sqrt(count * layout.nx * layout.ny)
    flat = (count, WIDTH)
    act = (flat, BF)
    stream = (flat, F32)
    wide = ((count, 2 * WIDTH), BF)
    lanes = ((count, LANES), F32)
    onehot = ((count, LANES), BF)
    row = ((1, WIDTH), F32)

    code = syndrome * PLAN_STEP_COUNT + check_plan_step
    codes = call(code_kernel, [((rounds * rows, LANES), BF)], [code], work=12)[0]
    row_tokens = shifted(tokens, "gx", -1).reshape(flat)
    col_tokens = shifted(tokens, "gy", -1).reshape(flat)
    row_codes = shifted(codes, "gx", -1)
    col_codes = shifted(codes, "gy", -1)
    plan = plan_step_embedding
    flip = flip_vector.reshape(1, WIDTH)
    gain_one = gain_tanner.reshape(1, WIDTH)
    gain_two = gain_time.reshape(1, WIDTH)
    gain_three = gain_ffn.reshape(1, WIDTH)
    outer = cotangent.reshape(flat)
    weights = [w_query, w_key_value, w_merge, w_temporal, w_temporal_out, w_ffn_up, w_ffn_down]
    x, onehot_own, hidden_one, query, key_value, gain_one, gain_two, gain_three, *flipped = call(
        start_kernel,
        [stream, onehot, act, act, wide, row, row, row] + [(weight.shape[::-1], BF) for weight in weights],
        [tokens.reshape(flat), codes, plan, flip, gain_one, gain_two, gain_three, *weights],

    )
    extended = pltpu.VMEM((rounds, 2 * rows, cols, 2 * WIDTH), F32)
    columns = pltpu.VMEM((rounds * rows, cols, 2 * WIDTH), F32)
    half_one = ((2 * (FF // WIDTH) * HALF, WIDTH), BF)
    (
        keep_one, send_one, grad_time, after_tanner, mixed_one, mixed_two, packed, hidden_two,
        row_kv, col_kv, row_x, col_x, row_hidden, col_hidden, row_onehot, col_onehot,
        bent_one, probs_one, bent_two, probs_two, grad_gain_ffn,
    ) = call(
        forward_kernel,
        [half_one, half_one, stream, stream, act, act, ((count, 3 * WIDTH), BF), act,
         wide, wide, stream, stream, act, act, onehot, onehot, lanes, lanes, lanes, lanes, row],
        [offsets, x, query, key_value, row_tokens, row_codes, col_tokens, col_codes, plan, flip,
         gain_one, w_key_value, w_merge, gain_two, w_temporal, w_temporal_out, gain_three, w_ffn_up, flipped[5], flipped[6],
         outer],
        [extended, columns, pltpu.VMEM((WIDTH, count), BF), pltpu.VMEM((FF, count), BF)],
        smem=1,
        limit=32,

    )
    grad_query, grad_kv, grad_rows, grad_cols, grad_packed, grad_tanner, grad_gain_time = call(
        backward_kernel,
        [act, wide, wide, wide, ((count, 3 * WIDTH), BF), stream, row],
        [offsets, grad_time, after_tanner, packed, query, key_value, row_kv, col_kv,
         bent_one, probs_one, bent_two, probs_two, flipped[2], gain_two, flipped[3], flipped[4]],
        [extended, columns, extended],
        smem=1,
        limit=32,
        work=3,
    )
    many, bits = layout.many, layout.bits
    order_one = list(range(many)) + list(range(many, bits))
    order_two = [0, many] + list(range(1, many)) + list(range(many + 1, bits))
    keep_one, send_one = reduce_tree(layout, keep_one, send_one, 0, order_one, scale, until=1)
    keep_one, grad_tanner = lax.optimization_barrier((keep_one, grad_tanner))
    half_two = ((16 + 8 * HALF, WIDTH), BF)
    grad_own, lent_rows, lent_cols, keep_two, send_two = call(
        weights_kernel,
        [stream, act, act, half_two, half_two],
        [mixed_two, grad_time, hidden_two, grad_packed, mixed_one, grad_tanner, grad_query, flipped[0], flipped[1],
         gain_one, x, row_x, col_x, hidden_one, row_hidden, col_hidden, onehot_own, row_onehot, col_onehot,
         grad_kv, grad_rows, grad_cols, grad_gain_time, grad_gain_ffn],
        [pltpu.VMEM((3, WIDTH, count), BF), pltpu.VMEM((WIDTH, 3 * count), BF)],
        limit=32,
        work=3,
    )
    back_rows = shifted(lent_rows, "gx", 1)
    back_cols = shifted(lent_cols, "gy", 1)
    shard_one, back_rows, back_cols = reduce_tree(
        layout, keep_one, send_one, 0, order_one, scale, first=1, beside=(back_rows, back_cols)
    )
    shard_two, plan_grad, grad_flip, sum_gain_tanner, sum_gain_time, sum_gain_ffn = reduce_tree(
        layout, keep_two, send_two, 16, order_two, scale
    )
    sources = [*gather_tree(layout, shard_one, order_one), *gather_tree(layout, shard_two, order_two)]
    groups = (((1, FF // WIDTH), (FF // WIDTH, 1)), ((1, 3), (1, 1), (1, 1), (1, 1), (1, 2)))
    (
        token_grad, grad_up, grad_down, grad_temporal, grad_temporal_out, grad_merge, grad_w_query, grad_key_value,
    ) = unpack(groups, scale, sources, grad_own, back_rows, back_cols)
    return (
        token_grad.reshape(tokens.shape),
        grad_flip.reshape(WIDTH),
        plan_grad,
        sum_gain_tanner.reshape(WIDTH),
        grad_w_query,
        grad_key_value,
        grad_merge,
        sum_gain_time.reshape(WIDTH),
        grad_temporal,
        grad_temporal_out,
        sum_gain_ffn.reshape(WIDTH),
        grad_up,
        grad_down,
    )


def solution(mesh):
    tiled = P(None, "gx", "gy", None)
    sites = P(None, "gx", "gy")
    return jax.shard_map(
        on_device,
        mesh=mesh,
        in_specs=(tiled, sites, sites) + (P(),) * 13 + (tiled,),
        out_specs=(tiled,) + (P(),) * 12,
        check_vma=False,
    )
```

```python
import functools
import math

import jax
import jax.numpy as jnp
from jax import lax
from jax.experimental import pallas as pl
from jax.experimental.pallas import tpu as pltpu
from jax.sharding import PartitionSpec as P

WIDTH = 256
HEADDIM = 32
HEADS = WIDTH // HEADDIM
FF = 1024
PLAN_STEP_COUNT = 8
MONOS = 6
MAXEXP = 8
LANES = 128
HALF = WIDTH // 2

EPS = 1e-05
CAP = 4.0
ALONG_ROWS = (0, 4, 5)
BF = jnp.bfloat16
F32 = jnp.float32
SCORE = 1.0 / math.sqrt(HEADDIM)
GELU_A = math.sqrt(2.0 / math.pi)
GELU_B = 0.044715
MIB = 1 << 20


def dot(a, b, dims=((1,), (0,))):
    return lax.dot_general(a, b, (dims, ((), ())), preferred_element_type=F32)


def dot_nt(a, b):
    return dot(a, b, ((1,), (1,)))


def embed(values, codes, plan, flip):
    tokens = values.shape[0]
    lines = codes.shape[0]
    width = tokens // lines
    token = lax.broadcasted_iota(jnp.int32, (tokens, lines), 0)
    line = lax.broadcasted_iota(jnp.int32, (tokens, lines), 1)
    spread = dot(jnp.where(token // width == line, 1.0, 0.0).astype(BF), codes)
    token = lax.broadcasted_iota(jnp.int32, (tokens, LANES), 0)
    lane = lax.broadcasted_iota(jnp.int32, (tokens, LANES), 1)
    picked = jnp.where(token % width == lane, spread, 0.0).astype(BF)
    code = dot(picked, jnp.ones((LANES, LANES), BF))
    flipped = code >= PLAN_STEP_COUNT
    step = jnp.where(flipped, code - PLAN_STEP_COUNT, code)
    slot = lane % 16
    chosen = (slot.astype(F32) == step) | ((slot == PLAN_STEP_COUNT) & flipped)
    onehot = jnp.where(chosen & (lane < 48), 1.0, 0.0).astype(BF)
    row = lax.broadcasted_iota(jnp.int32, (8, WIDTH), 0)
    table = jnp.concatenate([plan, jnp.where(row == 0, flip, 0.0)], axis=0)
    high = table.astype(BF)
    rest = table - high.astype(F32)
    middle = rest.astype(BF)
    low = (rest - middle.astype(F32)).astype(BF)
    empty = jnp.zeros((LANES - 48, WIDTH), BF)
    vectors = dot(onehot, jnp.concatenate([high, middle, low, empty], axis=0))
    return values.astype(F32) + vectors, onehot


def inverse_rms(stream):
    return lax.rsqrt(jnp.mean(stream * stream, axis=-1, keepdims=True) + EPS)


def norm_back(stream, gain, grad):
    inverse = inverse_rms(stream)
    normed = stream * inverse
    scaled = grad * gain
    mean = jnp.mean(scaled * normed, axis=-1, keepdims=True)
    return inverse * (scaled - normed * mean), jnp.sum(grad * normed, axis=0, keepdims=True)


def gather_heads(slot, period):
    feature = lax.broadcasted_iota(jnp.int32, (WIDTH, LANES), 0) // HEADDIM
    lane = lax.broadcasted_iota(jnp.int32, (WIDTH, LANES), 1) % period
    return jnp.where(lane - feature == slot * HEADS, 1.0, 0.0).astype(BF)


def spread_heads(slot, period):
    lane = lax.broadcasted_iota(jnp.int32, (LANES, WIDTH), 0)
    feature = lax.broadcasted_iota(jnp.int32, (LANES, WIDTH), 1) // HEADDIM
    at = (lane < 2 * period) & (lane % period - feature == slot * HEADS)
    return jnp.where(at, 1.0, 0.0).astype(BF)


def two_parts(value, period):
    lane = lax.broadcasted_iota(jnp.int32, value.shape, 1)
    high = value.astype(BF).astype(F32)
    return jnp.where(lane < period, high, value - high).astype(BF)


def slot_total(value, period):
    shift = HEADS
    while shift < period:
        value = value + pltpu.roll(value, shift, 1)
        shift *= 2
    return value


def softmax_parts(scores, valid, period):
    bent = jnp.tanh(scores * (SCORE / CAP))
    weights = jnp.where(valid, jnp.exp(CAP * bent), 0.0)
    return bent, weights / slot_total(weights, period)


def softmax_back(bent, probs, grad, period):
    inner = probs * grad
    return (inner - probs * slot_total(inner, period)) * (1.0 - bent * bent) * SCORE


def tanner_valid(tokens):
    lane = lax.broadcasted_iota(jnp.int32, (tokens, LANES), 1)
    return lane % 64 < HEADS * (MONOS + 1)


def time_valid(tokens, rounds):
    lane = lax.broadcasted_iota(jnp.int32, (tokens, LANES), 1)
    row = lax.broadcasted_iota(jnp.int32, (tokens, LANES), 0)
    return (lane % 32) // HEADS <= row // (tokens // rounds)


def offset_of(offsets, index):
    return offsets[index, 0] if index in ALONG_ROWS else offsets[index, 1]


def neighbour(number, offsets, extended, columns):
    rounds, twice, width, features = extended.shape
    rows = twice // 2
    tokens = rounds * rows * width
    if number == 0:
        return extended[:, :rows].reshape(tokens, features)
    by = offset_of(offsets, number - 1)
    if number - 1 in ALONG_ROWS:
        return extended[:, pl.ds(by, rows)].reshape(tokens, features)
    own = extended[:, :rows].reshape(rounds * rows, width, features)
    place = lax.broadcasted_iota(jnp.int32, own.shape, 1)
    joined = jnp.where(place >= by, own, columns[...])
    return pltpu.roll(joined, width - by, 1).reshape(tokens, features)


def code_kernel(code, out):
    rounds, rows, width = code.shape
    out[...] = jnp.zeros(out.shape, BF)
    out[:, :width] = code[...].reshape(rounds * rows, width).astype(F32).astype(BF)


def start_kernel(tokens, codes, plan, flip, gain, gain_two, gain_three, *refs):
    count = (len(refs) - 8) // 2
    weights, outs = refs[:count], refs[count:]
    x_out, onehot_out, hidden_out, query_out, kv_out, *passed = outs[:8]
    w_query, w_key_value = weights[:2]
    for weight, out in zip(weights, outs[8:]):
        out[...] = weight[...].T
    for source, out in zip((gain, gain_two, gain_three), passed):
        out[...] = source[...]
    x, onehot = embed(tokens[...], codes[...], plan[...], flip[...])
    hidden = (x * inverse_rms(x) * gain[...]).astype(BF)
    x_out[...] = x
    onehot_out[...] = onehot
    hidden_out[...] = hidden
    query_out[...] = dot(hidden, w_query[...]).astype(BF)
    kv_out[...] = dot(hidden, w_key_value[...]).astype(BF)


def forward_kernel(
    offsets, x_in, query_in, kv_in, row_tokens, row_codes, col_tokens, col_codes, plan, flip,
    gain_tanner, w_key_value, w_merge, gain_time, w_temporal, w_temporal_out, gain_ffn, w_up, w_up_t, w_down_t, cotangent,
    keep, send, grad_time_out, tanner_out, mixed_one_out, mixed_two_out, packed_out, hidden_two_out,
    row_kv_out, col_kv_out, row_x_out, col_x_out, row_hidden_out, col_hidden_out, row_onehot_out, col_onehot_out,
    bent_one_out, probs_one_out, bent_two_out, probs_two_out, grad_gain_out,
    extended, columns, transposed, transposed_act,
):
    rounds, twice, width, features = extended.shape
    rows = twice // 2
    tokens = x_in.shape[0]
    core = my_bit(0)
    borrowed = []
    for other, codes, x_out, hidden_out, onehot_out, kv_out in (
        (row_tokens, row_codes, row_x_out, row_hidden_out, row_onehot_out, row_kv_out),
        (col_tokens, col_codes, col_x_out, col_hidden_out, col_onehot_out, col_kv_out),
    ):
        x, onehot = embed(other[...], codes[...], plan[...], flip[...])
        hidden = (x * inverse_rms(x) * gain_tanner[...]).astype(BF)
        kv = dot(hidden, w_key_value[...]).astype(BF)
        x_out[...] = x
        onehot_out[...] = onehot
        hidden_out[...] = hidden
        kv_out[...] = kv
        borrowed.append(kv.astype(F32))
    extended[:, :rows] = kv_in[...].astype(F32).reshape(rounds, rows, width, features)
    extended[:, rows:] = borrowed[0].reshape(rounds, rows, width, features)
    columns[...] = borrowed[1].reshape(rounds * rows, width, features)
    query = query_in[...].astype(F32)
    scores = None
    for number in range(MONOS + 1):
        keys = neighbour(number, offsets, extended, columns)[:, :WIDTH]
        part = dot((query * keys).astype(BF), gather_heads(number, 64))
        scores = part if scores is None else scores + part
    bent, probs = softmax_parts(scores, tanner_valid(tokens), 64)
    bent_one_out[...] = bent
    probs_one_out[...] = probs
    parts = two_parts(probs, 64)
    mixed = None
    for number in range(MONOS + 1):
        values = neighbour(number, offsets, extended, columns)[:, WIDTH:]
        part = dot(parts, spread_heads(number, 64)) * values
        mixed = part if mixed is None else mixed + part
    mixed_one = mixed.astype(BF)
    mixed_one_out[...] = mixed_one
    after_tanner = x_in[...] + dot(mixed_one, w_merge[...])
    tanner_out[...] = after_tanner

    hidden_two = (after_tanner * inverse_rms(after_tanner) * gain_time[...]).astype(BF)
    hidden_two_out[...] = hidden_two
    packed_low = dot(hidden_two, w_temporal[...]).astype(BF)
    packed_out[...] = packed_low
    packed = packed_low.astype(F32).reshape(rounds, tokens // rounds, 3 * WIDTH)
    sites = tokens // rounds
    scores = None
    for earlier in range(rounds):
        product = packed[earlier:, :, :WIDTH] * packed[earlier][None, :, WIDTH : 2 * WIDTH]
        part = dot(product.reshape(-1, WIDTH).astype(BF), gather_heads(earlier, 32))
        if earlier:
            part = jnp.concatenate([jnp.zeros((earlier * sites, LANES), F32), part], axis=0)
        scores = part if scores is None else scores + part
    bent, probs = softmax_parts(scores, time_valid(tokens, rounds), 32)
    bent_two_out[...] = bent
    probs_two_out[...] = probs
    parts = two_parts(probs, 32)
    mixed = None
    for earlier in range(rounds):
        weight = dot(parts[earlier * sites :], spread_heads(earlier, 32)).reshape(rounds - earlier, sites, WIDTH)
        part = (weight * packed[earlier][None, :, 2 * WIDTH :]).reshape(-1, WIDTH)
        if earlier:
            part = jnp.concatenate([jnp.zeros((earlier * sites, WIDTH), F32), part], axis=0)
        mixed = part if mixed is None else mixed + part
    mixed_two = mixed.astype(BF)
    mixed_two_out[...] = mixed_two
    after_time = after_tanner + dot(mixed_two, w_temporal_out[...])

    hidden = (after_time * inverse_rms(after_time) * gain_ffn[...]).astype(BF)
    outer = cotangent[...]
    transposed[...] = hidden.T
    grad_three = None
    befores = []
    for block in range(FF // WIDTH):
        cols = slice(block * WIDTH, (block + 1) * WIDTH)
        before = dot(hidden, w_up[:, cols])
        square = before * before
        bend = jnp.tanh(GELU_A * before * (1.0 + GELU_B * square))
        upper = 0.5 * (1.0 + bend)
        activated = (before * upper).astype(BF)
        slope = upper + 0.5 * before * (1.0 - bend * bend) * (GELU_A * (1.0 + 3.0 * GELU_B * square))
        grad_before = (dot(outer, w_down_t[:, cols]) * slope).astype(BF)
        befores.append(grad_before)
        part = dot(grad_before, w_up_t[cols, :])
        grad_three = part if grad_three is None else grad_three + part
        transposed_act[cols, :] = activated.T
    mine = pl.multiple_of(core * HALF, HALF)
    other = pl.multiple_of((1 - core) * HALF, HALF)
    blocks = FF // WIDTH
    lead = jnp.concatenate([transposed[pl.ds(start, HALF), :] for start in (mine, other)], axis=0)
    for block in range(blocks):
        product = dot(lead, befores[block]).astype(BF)
        keep[block * HALF : (block + 1) * HALF, :] = product[:HALF]
        send[block * HALF : (block + 1) * HALF, :] = product[HALF:]
    lead = jnp.concatenate(
        [transposed_act[pl.ds(block * WIDTH + start, HALF), :] for start in (mine, other) for block in range(blocks)],
        axis=0,
    )
    product = dot(lead, outer).astype(BF)
    keep[blocks * HALF :, :] = product[: blocks * HALF]
    send[blocks * HALF :, :] = product[blocks * HALF :]
    grad_norm, grad_gain = norm_back(after_time, gain_ffn[...], grad_three)
    grad_time_out[...] = outer.astype(F32) + grad_norm
    grad_gain_out[...] = grad_gain


def backward_kernel(
    offsets, grad_time_in, tanner_in, packed_in, query_in, kv_in, row_kv, col_kv,
    bent_one, probs_one, bent_two, probs_two, w_merge, gain_time, w_temporal, w_temporal_out,
    grad_query_out, grad_kv_out, grad_rows_out, grad_cols_out, grad_packed_out, grad_tanner_out, grad_gain_out,
    extended, columns, grad_extended,
):
    rounds, twice, width, features = extended.shape
    rows = twice // 2
    tokens = grad_time_in.shape[0]
    sites = tokens // rounds
    grad_time = grad_time_in[...]
    grad_mixed = dot(grad_time.astype(BF), w_temporal_out[...]).reshape(rounds, sites, WIDTH)
    packed = packed_in[...].astype(F32).reshape(rounds, sites, 3 * WIDTH)
    grad_probs = None
    for earlier in range(rounds):
        product = grad_mixed[earlier:] * packed[earlier][None, :, 2 * WIDTH :]
        part = dot(product.reshape(-1, WIDTH).astype(BF), gather_heads(earlier, 32))
        if earlier:
            part = jnp.concatenate([jnp.zeros((earlier * sites, LANES), F32), part], axis=0)
        grad_probs = part if grad_probs is None else grad_probs + part
    probs = probs_two[...]
    prob_parts = two_parts(probs, 32)
    score_parts = two_parts(softmax_back(bent_two[...], probs, grad_probs, 32), 32)
    grad_queries = None
    grad_keys = []
    grad_values = []
    for earlier in range(rounds):
        spread = spread_heads(earlier, 32)
        shape = (rounds - earlier, sites, WIDTH)
        weight = dot(prob_parts[earlier * sites :], spread).reshape(shape)
        slope = dot(score_parts[earlier * sites :], spread).reshape(shape)
        grad_values.append(jnp.sum(weight * grad_mixed[earlier:], axis=0))
        grad_keys.append(jnp.sum(slope * packed[earlier:, :, :WIDTH], axis=0))
        part = (slope * packed[earlier][None, :, WIDTH : 2 * WIDTH]).reshape(-1, WIDTH)
        if earlier:
            part = jnp.concatenate([jnp.zeros((earlier * sites, WIDTH), F32), part], axis=0)
        grad_queries = part if grad_queries is None else grad_queries + part
    grad_packed = jnp.concatenate(
        [grad_queries, jnp.concatenate(grad_keys, axis=0), jnp.concatenate(grad_values, axis=0)], axis=1
    ).astype(BF)
    grad_packed_out[...] = grad_packed
    grad_two = dot(grad_packed, w_temporal[...])
    grad_norm, grad_gain = norm_back(tanner_in[...], gain_time[...], grad_two)
    grad_gain_out[...] = grad_gain
    grad_tanner = grad_time + grad_norm
    grad_tanner_out[...] = grad_tanner

    grad_mixed = dot(grad_tanner.astype(BF), w_merge[...])
    extended[:, :rows] = kv_in[...].astype(F32).reshape(rounds, rows, width, features)
    extended[:, rows:] = row_kv[...].astype(F32).reshape(rounds, rows, width, features)
    columns[...] = col_kv[...].astype(F32).reshape(rounds * rows, width, features)
    grad_probs = None
    for number in range(MONOS + 1):
        values = neighbour(number, offsets, extended, columns)[:, WIDTH:]
        part = dot((grad_mixed * values).astype(BF), gather_heads(number, 64))
        grad_probs = part if grad_probs is None else grad_probs + part
    probs = probs_one[...]
    prob_parts = two_parts(probs, 64)
    score_parts = two_parts(softmax_back(bent_one[...], probs, grad_probs, 64), 64)
    query = query_in[...].astype(F32)
    grad_query = None
    grad_cols = None
    for number in (0,) + tuple(i + 1 for i in range(MONOS)):
        spread = spread_heads(number, 64)
        slope = dot(score_parts, spread)
        weight = dot(prob_parts, spread)
        keys = neighbour(number, offsets, extended, columns)[:, :WIDTH]
        part = slope * keys
        grad_query = part if grad_query is None else grad_query + part
        grad_kv = jnp.concatenate([slope * query, weight * grad_mixed], axis=1)
        if number == 0:
            grad_extended[:, :rows] = grad_kv.reshape(rounds, rows, width, features)
            grad_extended[:, rows:] = jnp.zeros((rounds, rows, width, features), F32)
            continue
        by = offset_of(offsets, number - 1)
        if number - 1 in ALONG_ROWS:
            grad_extended[:, pl.ds(by, rows)] += grad_kv.reshape(rounds, rows, width, features)
            continue
        moved = pltpu.roll(grad_kv.reshape(rounds * rows, width, features), by % width, 1)
        place = lax.broadcasted_iota(jnp.int32, moved.shape, 1)
        own = jnp.where(place >= by, moved, 0.0)
        grad_extended[:, :rows] += own.reshape(rounds, rows, width, features)
        grad_cols = moved - own if grad_cols is None else grad_cols + (moved - own)
    grad_query_out[...] = grad_query.astype(BF)
    grad_kv_out[...] = grad_extended[:, :rows].reshape(tokens, features).astype(BF)
    grad_rows_out[...] = grad_extended[:, rows:].reshape(tokens, features).astype(BF)
    grad_cols_out[...] = grad_cols.reshape(tokens, features).astype(BF)


def weights_kernel(
    mixed_two, grad_time, hidden_two, grad_packed, mixed_one, grad_tanner, grad_query, w_query, w_key_value, gain,
    x_own, x_row, x_col, hidden_own, hidden_row, hidden_col, onehot_own, onehot_row, onehot_col,
    grad_own, grad_row, grad_col, grad_gain_time, grad_gain_ffn,
    grad_out, row_out, col_out, keep, send, transposed, transposed_own,
):
    core = my_bit(0)
    tokens = x_own.shape[0]
    transposed[0] = hidden_two[...].T
    transposed[1] = mixed_two[...].T
    transposed[2] = mixed_one[...].T
    small = None
    grad_gain = None
    for number, (x, hidden, onehot, grad_kv, out) in enumerate((
        (x_own, hidden_own, onehot_own, grad_own, grad_out),
        (x_row, hidden_row, onehot_row, grad_row, row_out),
        (x_col, hidden_col, onehot_col, grad_col, col_out),
    )):
        transposed_own[:, number * tokens : (number + 1) * tokens] = hidden[...].T
        grad_one = dot(grad_kv[...], w_key_value[...])
        if number == 0:
            grad_one = grad_one + dot(grad_query[...], w_query[...])
        grad, part = norm_back(x[...], gain[...], grad_one)
        grad_gain = part if grad_gain is None else grad_gain + part
        if number == 0:
            grad = grad + grad_tanner[...]
        out[...] = grad.astype(out.dtype)
        high = grad.astype(BF)
        low = (grad - high.astype(F32)).astype(BF)
        part = dot(onehot[...], jnp.concatenate([high, low], axis=1), ((0,), (0,)))[:16]
        part = part[:, :WIDTH] + part[:, WIDTH:]
        small = part if small is None else small + part
    row = lax.broadcasted_iota(jnp.int32, small.shape, 0)
    small = jnp.where(row == 9, grad_gain, small)
    small = jnp.where(row == 10, grad_gain_time[...], small)
    small = jnp.where(row == 11, grad_gain_ffn[...], small).astype(BF)
    grad_time_low = grad_time[...].astype(BF)
    grad_tanner_low = grad_tanner[...].astype(BF)
    grad_all = jnp.concatenate([grad_own[...], grad_row[...], grad_col[...]], axis=0)
    mine = pl.ds(pl.multiple_of(core * HALF, HALF), HALF)
    other = pl.ds(pl.multiple_of((1 - core) * HALF, HALF), HALF)
    keep[:16, :] = small
    send[:16, :] = small
    pairs = [(transposed.at[0], grad_packed[:, block * WIDTH : (block + 1) * WIDTH]) for block in range(3)]
    pairs.append((transposed.at[1], grad_time_low))
    pairs.append((transposed.at[2], grad_tanner_low))
    pairs.append((transposed_own.at[:, pl.ds(0, tokens)], grad_query[...]))
    pairs += [(transposed_own, grad_all[:, block * WIDTH : (block + 1) * WIDTH]) for block in range(2)]
    for block, (lead, grad) in enumerate(pairs):
        product = dot(jnp.concatenate([lead[mine, :], lead[other, :]], axis=0), grad).astype(BF)
        rows = slice(16 + block * HALF, 16 + (block + 1) * HALF)
        keep[rows, :] = product[:HALF]
        send[rows, :] = product[HALF:]


def my_bit(bit):
    many = lax.axis_size("gy").bit_length() - 1
    if bit < many:
        return (lax.axis_index("gy") >> bit) & 1
    return (lax.axis_index("gx") >> (bit - many)) & 1


def split_kernel(extra, bit, kept, received, keep, send, total):
    mine = my_bit(bit)
    value = kept[...].astype(F32) + received[...].astype(F32)
    total[...] = value[extra:]
    rows = keep.shape[0] - extra
    for ref, which in ((keep, mine), (send, 1 - mine)):
        if extra:
            ref[:extra, :] = value[:extra].astype(BF)
        ref[extra:, :] = total[pl.ds(pl.multiple_of(which * rows, rows), rows), :].astype(BF)


def sum_kernel(first, second, out):
    out[...] = (first[...].astype(F32) + second[...].astype(F32)).astype(BF)


def end_kernel(extra, scale, kept, received, out, *small):
    value = kept[...].astype(F32) + received[...].astype(F32)
    out[...] = value[extra:].astype(BF)
    if extra:
        small[0][...] = value[:extra] * scale


def small_kernel(small, plan, *rows):
    plan[...] = small[:8, :]
    for number, row in enumerate(rows):
        row[...] = small[8 + number : 9 + number, :]


def join_kernel(bit, own, received, out):
    mine = my_bit(bit)
    out[mine] = own[...]
    out[1 - mine] = received[...]


def unpack_kernel(groups, scale, grad, row, col, *refs):
    sources, refs = refs[: 2 * len(groups)], refs[2 * len(groups) :]
    token_out, *outs = refs[: len(refs) // 2]
    token_low, *wides = refs[len(refs) // 2 : -1]
    done = refs[-1]
    moves = []

    def move(source, target):
        moves.append(pltpu.make_async_copy(source, target, done.at[len(moves)]))
        moves[-1].start()

    for number, blocks in enumerate(groups):
        for side in range(2):
            source = sources[2 * number + side]
            half = pl.multiple_of((my_bit(0) ^ side) * HALF, HALF)
            block = 0
            first = sum(len(group) for group in groups[:number])
            for out, wide, (down, across) in zip(outs[first:], wides[first:], blocks):
                for index in range(down * across):
                    value = source[block * HALF : (block + 1) * HALF, :].astype(F32) * scale
                    left = (index if across > 1 else 0) * WIDTH
                    wide[side, index if down > 1 else 0, :, left : left + WIDTH] = value
                    block += 1
                for index in range(down):
                    move(wide.at[side, index], out.at[pl.ds(index * WIDTH + half, HALF)])
    token_low[...] = (grad[...] + row[...].astype(F32) + col[...].astype(F32)).astype(BF)
    move(token_low, token_out)
    for one in moves:
        one.wait()


def unpack(groups, scale, sources, grad, row, col):
    hbm = pl.BlockSpec(memory_space=pltpu.HBM)
    blocks = [block for group in groups for block in group]
    return pl.pallas_call(
        functools.partial(unpack_kernel, groups, scale),
        out_shape=[jax.ShapeDtypeStruct(grad.shape, BF)]
        + [jax.ShapeDtypeStruct((down * WIDTH, across * WIDTH), F32) for down, across in blocks],
        in_specs=[pl.BlockSpec(memory_space=pltpu.VMEM)] * (3 + len(sources)),
        out_specs=[hbm] * (1 + len(blocks)),
        scratch_shapes=[pltpu.VMEM(grad.shape, BF)]
        + [pltpu.VMEM((2, down, HALF, across * WIDTH), F32) for down, across in blocks]
        + [pltpu.SemaphoreType.DMA((1 + 2 * sum(down for down, _ in blocks),))],
        compiler_params=pltpu.CompilerParams(vmem_limit_bytes=16 * MIB),
    )(grad, row, col, *sources)


def estimate(work, outs=(), args=()):
    moved = sum(math.prod(shape) * jnp.dtype(dtype).itemsize for shape, dtype in outs)
    moved += sum(math.prod(arg.shape) * arg.dtype.itemsize for arg in args)
    return pl.CostEstimate(flops=int(work * 1.1e9), transcendentals=0, bytes_accessed=moved)


def call(kernel, outs, args, scratch=(), smem=0, limit=16, work=0.1):
    vmem = pl.BlockSpec(memory_space=pltpu.VMEM)
    return pl.pallas_call(
        kernel,
        out_shape=[jax.ShapeDtypeStruct(shape, dtype) for shape, dtype in outs],
        in_specs=[pl.BlockSpec(memory_space=pltpu.SMEM)] * smem + [vmem] * (len(args) - smem),
        out_specs=[vmem] * len(outs),
        scratch_shapes=list(scratch),
        compiler_params=pltpu.CompilerParams(vmem_limit_bytes=limit * MIB),
        cost_estimate=estimate(work, outs, args),
    )(*args)


def shifted(x, axis, by):
    count = lax.axis_size(axis)
    return lax.ppermute(x, axis, [(i, (i + by) % count) for i in range(count)])


class Layout:
    def __init__(self):
        self.nx = lax.axis_size("gx")
        self.ny = lax.axis_size("gy")
        self.many = self.ny.bit_length() - 1
        self.bits = self.many + self.nx.bit_length() - 1
        assert 1 << self.bits == self.nx * self.ny

    def swap(self, x, bit):
        flip = 1 << bit if bit < self.many else self.ny << (bit - self.many)
        return lax.ppermute(x, ("gx", "gy"), [(i, i ^ flip) for i in range(self.nx * self.ny)])


def reduce_tree(layout, keep, send, extra, order, scale, first=0, until=None, beside=()):
    halving = order[:-1]
    for stage in range(first, len(halving) if until is None else until):
        received = layout.swap(send, halving[stage])
        if stage == 2 and beside:
            received, *beside = lax.optimization_barrier((received, *beside))
        rows = keep.shape[0] - extra
        if stage + 1 < len(halving):
            half = ((rows // 2 + extra, WIDTH), BF)
            keep, send = call(
                functools.partial(split_kernel, extra, halving[stage + 1]),
                [half, half],
                [keep, received],
                [pltpu.VMEM((rows, WIDTH), F32)],
            )
    if until is not None:
        return keep, send
    total = call(sum_kernel, [(keep.shape, BF)], [keep, received])[0]
    received = layout.swap(total, order[-1])
    small = [((extra, WIDTH), F32)] if extra else []
    outs = call(functools.partial(end_kernel, extra, scale), [((rows, WIDTH), BF)] + small, [total, received])
    return (*outs, *beside)


def gather_tree(layout, own, order):
    for bit in order[-2:0:-1]:
        received = layout.swap(own, bit)
        rows = own.shape[0]
        own = call(
            functools.partial(join_kernel, bit), [((2, rows, WIDTH), BF)], [own, received]
        )[0].reshape(2 * rows, WIDTH)
    return own, layout.swap(own, order[0])


def on_device(
    tokens,
    syndrome,
    check_plan_step,
    offsets,
    flip_vector,
    plan_step_embedding,
    gain_tanner,
    w_query,
    w_key_value,
    w_merge,
    gain_time,
    w_temporal,
    w_temporal_out,
    gain_ffn,
    w_ffn_up,
    w_ffn_down,
    cotangent,
):
    layout = Layout()
    rounds, rows, cols = tokens.shape[:3]
    count = rounds * rows * cols
    scale = 1.0 / math.sqrt(count * layout.nx * layout.ny)
    flat = (count, WIDTH)
    act = (flat, BF)
    stream = (flat, F32)
    wide = ((count, 2 * WIDTH), BF)
    lanes = ((count, LANES), F32)
    onehot = ((count, LANES), BF)
    row = ((1, WIDTH), F32)

    code = syndrome * PLAN_STEP_COUNT + check_plan_step
    codes = call(code_kernel, [((rounds * rows, LANES), BF)], [code], work=12)[0]
    row_tokens = shifted(tokens, "gx", -1).reshape(flat)
    col_tokens = shifted(tokens, "gy", -1).reshape(flat)
    row_codes = shifted(codes, "gx", -1)
    col_codes = shifted(codes, "gy", -1)
    plan = plan_step_embedding
    flip = flip_vector.reshape(1, WIDTH)
    gain_one = gain_tanner.reshape(1, WIDTH)
    gain_two = gain_time.reshape(1, WIDTH)
    gain_three = gain_ffn.reshape(1, WIDTH)
    outer = cotangent.reshape(flat)
    weights = [w_query, w_key_value, w_merge, w_temporal, w_temporal_out, w_ffn_up, w_ffn_down]
    x, onehot_own, hidden_one, query, key_value, gain_one, gain_two, gain_three, *flipped = call(
        start_kernel,
        [stream, onehot, act, act, wide, row, row, row] + [(weight.shape[::-1], BF) for weight in weights],
        [tokens.reshape(flat), codes, plan, flip, gain_one, gain_two, gain_three, *weights],

    )
    extended = pltpu.VMEM((rounds, 2 * rows, cols, 2 * WIDTH), F32)
    columns = pltpu.VMEM((rounds * rows, cols, 2 * WIDTH), F32)
    half_one = ((2 * (FF // WIDTH) * HALF, WIDTH), BF)
    (
        keep_one, send_one, grad_time, after_tanner, mixed_one, mixed_two, packed, hidden_two,
        row_kv, col_kv, row_x, col_x, row_hidden, col_hidden, row_onehot, col_onehot,
        bent_one, probs_one, bent_two, probs_two, grad_gain_ffn,
    ) = call(
        forward_kernel,
        [half_one, half_one, stream, stream, act, act, ((count, 3 * WIDTH), BF), act,
         wide, wide, stream, stream, act, act, onehot, onehot, lanes, lanes, lanes, lanes, row],
        [offsets, x, query, key_value, row_tokens, row_codes, col_tokens, col_codes, plan, flip,
         gain_one, w_key_value, w_merge, gain_two, w_temporal, w_temporal_out, gain_three, w_ffn_up, flipped[5], flipped[6],
         outer],
        [extended, columns, pltpu.VMEM((WIDTH, count), BF), pltpu.VMEM((FF, count), BF)],
        smem=1,
        limit=32,

    )
    grad_query, grad_kv, grad_rows, grad_cols, grad_packed, grad_tanner, grad_gain_time = call(
        backward_kernel,
        [act, wide, wide, wide, ((count, 3 * WIDTH), BF), stream, row],
        [offsets, grad_time, after_tanner, packed, query, key_value, row_kv, col_kv,
         bent_one, probs_one, bent_two, probs_two, flipped[2], gain_two, flipped[3], flipped[4]],
        [extended, columns, extended],
        smem=1,
        limit=32,
        work=3,
    )
    many, bits = layout.many, layout.bits
    order_one = list(range(many)) + list(range(many, bits))
    order_two = [0, many] + list(range(1, many)) + list(range(many + 1, bits))
    keep_one, send_one = reduce_tree(layout, keep_one, send_one, 0, order_one, scale, until=1)
    keep_one, grad_tanner = lax.optimization_barrier((keep_one, grad_tanner))
    half_two = ((16 + 8 * HALF, WIDTH), BF)
    grad_own, lent_rows, lent_cols, keep_two, send_two = call(
        weights_kernel,
        [stream, act, act, half_two, half_two],
        [mixed_two, grad_time, hidden_two, grad_packed, mixed_one, grad_tanner, grad_query, flipped[0], flipped[1],
         gain_one, x, row_x, col_x, hidden_one, row_hidden, col_hidden, onehot_own, row_onehot, col_onehot,
         grad_kv, grad_rows, grad_cols, grad_gain_time, grad_gain_ffn],
        [pltpu.VMEM((3, WIDTH, count), BF), pltpu.VMEM((WIDTH, 3 * count), BF)],
        limit=32,
        work=3,
    )
    back_rows = shifted(lent_rows, "gx", 1)
    back_cols = shifted(lent_cols, "gy", 1)
    shard_one, back_rows, back_cols = reduce_tree(
        layout, keep_one, send_one, 0, order_one, scale, first=1, beside=(back_rows, back_cols)
    )
    shard_two, small = reduce_tree(layout, keep_two, send_two, 16, order_two, scale)
    plan_grad, grad_flip, sum_gain_tanner, sum_gain_time, sum_gain_ffn = call(
        small_kernel, [((8, WIDTH), F32), row, row, row, row], [small]
    )
    sources = [*gather_tree(layout, shard_one, order_one), *gather_tree(layout, shard_two, order_two)]
    groups = (((1, FF // WIDTH), (FF // WIDTH, 1)), ((1, 3), (1, 1), (1, 1), (1, 1), (1, 2)))
    (
        token_grad, grad_up, grad_down, grad_temporal, grad_temporal_out, grad_merge, grad_w_query, grad_key_value,
    ) = unpack(groups, scale, sources, grad_own, back_rows, back_cols)
    return (
        token_grad.reshape(tokens.shape),
        grad_flip.reshape(WIDTH),
        plan_grad,
        sum_gain_tanner.reshape(WIDTH),
        grad_w_query,
        grad_key_value,
        grad_merge,
        sum_gain_time.reshape(WIDTH),
        grad_temporal,
        grad_temporal_out,
        sum_gain_ffn.reshape(WIDTH),
        grad_up,
        grad_down,
    )


def solution(mesh):
    tiled = P(None, "gx", "gy", None)
    sites = P(None, "gx", "gy")
    return jax.shard_map(
        on_device,
        mesh=mesh,
        in_specs=(tiled, sites, sites) + (P(),) * 13 + (tiled,),
        out_specs=(tiled,) + (P(),) * 12,
        check_vma=False,
    )
```
